32 devices in a mesh: section: 2 (over x), fsdp: 4 (over y, core), tensor: 4 (over z).
Axes of the slice: x: 2, y: 2, z: 4, core: 2. Of those that a mesh axis runs over, the one named last changes fastest.
Arguments:
- inputs: bfloat16 [2, 4096, 1536], P(None, ('fsdp', 'tensor')), may hold values from -6 to 6
- doc_ids: int32 [2, 4, 1024], P(None, 'fsdp'), may hold values from 0 to 3, never falling along the last dimension, each value on 1 to 512 neighbouring positions
- cotangent: bfloat16 [2, 4096, 1536], P(None, ('fsdp', 'tensor')), may hold values from -6 to 6
- query_weight: bfloat16 [2, 1536, 1536], P('section', 'fsdp', 'tensor'), may hold values from -0.15625 to 0.15625
- key_weight: bfloat16 [2, 1536, 768], P('section', 'fsdp', 'tensor'), may hold values from -0.15625 to 0.15625
- value_weight: bfloat16 [2, 1536, 768], P('section', 'fsdp', 'tensor'), may hold values from -0.15625 to 0.15625
- output_weight: bfloat16 [2, 1536, 1536], P('section', 'tensor', 'fsdp'), may hold values from -0.4375 to 0.4375
- gate_weight: bfloat16 [2, 1536, 4096], P('section', 'fsdp', 'tensor'), may hold values from -0.15625 to 0.15625
- up_weight: bfloat16 [2, 1536, 4096], P('section', 'fsdp', 'tensor'), may hold values from -0.15625 to 0.15625
- down_weight: bfloat16 [2, 4096, 1536], P('section', 'tensor', 'fsdp'), may hold values from -0.09375 to 0.09375
- gains: bfloat16 [2, 2, 1536], P('section', None, ('fsdp', 'tensor')), may hold values from 0.099609375 to 1.8984375
Outputs:
- section_out: bfloat16 [2, 2, 4096, 1536], P('section', None, ('fsdp', 'tensor'))
- input_grads: float32 [2, 2, 4096, 1536], P('section', None, ('fsdp', 'tensor'))
- query_grad: float32 [2, 1536, 1536], P('section', 'fsdp', 'tensor')
- key_grad: float32 [2, 1536, 768], P('section', 'fsdp', 'tensor')
- value_grad: float32 [2, 1536, 768], P('section', 'fsdp', 'tensor')
- output_grad: float32 [2, 1536, 1536], P('section', 'tensor', 'fsdp')
- gate_grad: float32 [2, 1536, 4096], P('section', 'fsdp', 'tensor')
- up_grad: float32 [2, 1536, 4096], P('section', 'fsdp', 'tensor')
- down_grad: float32 [2, 4096, 1536], P('section', 'tensor', 'fsdp')
- gains_grad: float32 [2, 2, 1536], P('section', None, ('fsdp', 'tensor'))
The draws below stay inside these ranges and needn't reach their ends.
Inputs may be any that keep to these rules, and one draw needn't show every extreme that they name: `doc_ids`: within each sequence the ids never fall; every document has 1 to half of 1024 tokens, and one has exactly that many.
All inputs are finite; a program needn't handle non-finite values.
Results may differ from the reference program's by a relative error of at most 0.035.
Values may be sent and summed in bfloat16 or wider, within the bound.
A program may use at most 320 MiB of HBM per device.

```python
import math
import jax
import jax.numpy as jnp
import numpy as np
from jax import lax

D = 1536
HQ = 16
HK = 8
HD = 96
FF = 4096
LEN = 1024
DOCS = 4
MICRO = 2
NSEQ = 4
ROWS = 4096


def levels(stream_key, dims, cuts, low, high):
    def one(axis_at, shards_of):
        draws = jax.random.uniform(jax.random.fold_in(jax.random.fold_in(stream_key, 6), axis_at), (shards_of,), jnp.float32, low / len(cuts), high / len(cuts))
        return jnp.repeat(jnp.exp(draws), dims[axis_at] // shards_of).reshape((-1,) + (1,) * (len(dims) - axis_at - 1))

    factor_of = one(*cuts[0])
    for cut in cuts[1:]:
        factor_of = factor_of * one(*cut)
    return factor_of


def length_profile(number_of, total, most, lean):
    weights = [(1 << 20) // math.isqrt(rank ** lean) + 1 for rank in range(2, number_of + 1)]
    surplus, holding = total - most - (number_of - 1), [1] * (number_of - 1)
    while surplus > 0:
        free = [i for i in range(number_of - 1) if holding[i] < most]
        whole, remaining = sum([weights[i] for i in free]), surplus
        for i in free:
            addition = min(most - holding[i], max(1, remaining * weights[i] // whole), surplus)
            holding[i] = holding[i] + addition
            surplus = surplus - addition
    return np.array([most] + holding)


def ragged_sizes(own_key, amount, total, limit, lean):
    if amount == 2:
        one = jax.random.randint(own_key, (), max(1, total - limit), min(limit, total - 1) + 1)
        return jnp.stack([one, total - one])
    lengths = jnp.asarray(length_profile(amount, total, limit, lean), jnp.int32)
    couples = (amount - 1) // 2
    giver, receiver = lengths[1:1 + 2 * couples:2], lengths[2:2 + 2 * couples:2]
    slack = jnp.minimum(giver - 1, limit - receiver)
    moved = jax.random.randint(jax.random.fold_in(own_key, 1), (couples,), 0, 1 << 20) % (slack + 1)
    lengths = lengths.at[1:1 + 2 * couples:2].set(giver - moved).at[2:2 + 2 * couples:2].set(receiver + moved)
    return lengths[jax.random.permutation(jax.random.fold_in(own_key, 2), amount)]


def noise(rng, shape, scale, limit, split=(), held_as=jnp.bfloat16):
    entries = scale * jax.random.normal(rng, shape, jnp.float32)
    if split:
        entries = entries * levels(rng, shape, split, -0.22, 0.18)
    return jnp.clip(entries, -limit, limit).astype(held_as)


def setup_inputs(seed: int = 0) -> dict:
    key_of = jax.random.split(jax.random.key(seed), 12)
    inputs = noise(key_of[0], (MICRO, ROWS, D), 1.0, 6.0, ((1, 16),))
    doc_ids = jax.vmap(lambda own: jnp.searchsorted(jnp.cumsum(ragged_sizes(own, DOCS, LEN, LEN // 2, 0)), jnp.arange(LEN), side="right"))(jax.random.split(key_of[1], MICRO * NSEQ)).reshape((MICRO, NSEQ, LEN)).astype(jnp.int32)
    cotangent = noise(key_of[2], (MICRO, ROWS, D), 1.0, 6.0, ((1, 16),))
    query_weight = noise(key_of[3], (2, D, HQ * HD), D ** -0.5, 0.15625, ((0, 2), (1, 4), (2, 4)))
    key_weight = noise(key_of[4], (2, D, HK * HD), D ** -0.5, 0.15625, ((0, 2), (1, 4), (2, 4)))
    value_weight = noise(key_of[5], (2, D, HK * HD), D ** -0.5, 0.15625, ((0, 2), (1, 4), (2, 4)))
    output_weight = noise(key_of[6], (2, HQ * HD, D), (HQ * HD // 8) ** -0.5, 0.4375, ((0, 2), (1, 4), (2, 4)))
    gate_weight = noise(key_of[7], (2, D, FF), D ** -0.5, 0.15625, ((0, 2), (1, 4), (2, 4)))
    up_weight = noise(key_of[8], (2, D, FF), D ** -0.5, 0.15625, ((0, 2), (1, 4), (2, 4)))
    down_weight = noise(key_of[9], (2, FF, D), FF ** -0.5, 0.09375, ((0, 2), (1, 4), (2, 4)))
    gains = jnp.clip(1.0 + 0.18 * jax.random.normal(key_of[10], (2, 2, D), jnp.float32), 0.099609375, 1.8984375).astype(jnp.bfloat16)
    return {"inputs": inputs, "doc_ids": doc_ids, "cotangent": cotangent, "query_weight": query_weight, "key_weight": key_weight, "value_weight": value_weight, "output_weight": output_weight, "gate_weight": gate_weight, "up_weight": up_weight, "down_weight": down_weight, "gains": gains}


@jax.custom_vjp
def low(v):
    return lax.optimization_barrier(v.astype(jnp.bfloat16)).astype(jnp.float32)

@jax.custom_vjp
def low_back(v):
    return v

def low_keep(v):
    return (low(v), None)

def low_pass(kept, grad):
    return (grad,)

def back_keep(v):
    return (v, None)

def back_low(kept, grad):
    return (low(grad),)
low.defvjp(low_keep, low_pass)
low_back.defvjp(back_keep, back_low)
epsilon = 1e-05
rope_base = 100000.0

def product(left_side, right_side):
    return jnp.dot(left_side, right_side, precision=lax.Precision.HIGHEST)

def normalize(values, gain_row):
    return values * lax.rsqrt(lax.optimization_barrier(jnp.mean(values * values, -1, keepdims=True)) + epsilon) * gain_row

def turning(doc_rows):
    places = jnp.arange(doc_rows.shape[-1], dtype=jnp.int32)
    begins = jnp.concatenate([jnp.ones(doc_rows.shape[:-1] + (1,), dtype=bool), doc_rows[..., 1:] != doc_rows[..., :-1]], -1)
    starts = lax.cummax(jnp.where(begins, places, 0), axis=doc_rows.ndim - 1)
    positions = (places - starts).astype(jnp.float32)
    ladder = jnp.arange(HD // 2, dtype=jnp.float32)
    frequency = rope_base ** (-2.0 * ladder / HD)
    angles = positions[..., None] * frequency
    return (jnp.cos(angles), jnp.sin(angles))

def rotate(values, cosine, sine_part):
    half_size = values.shape[-1] // 2
    first_half = values[..., :half_size]
    second_half = values[..., half_size:]
    return jnp.concatenate([first_half * cosine - second_half * sine_part, second_half * cosine + first_half * sine_part], -1)

def attend_seq(seq_block):
    query_rot, key_rot, value_low, doc_row = seq_block
    group_size = HQ // HK
    keys_wide = jnp.repeat(key_rot, group_size, axis=1)
    values_wide = jnp.repeat(value_low, group_size, axis=1)
    scores = jnp.einsum('ahd,bhd->hab', query_rot, keys_wide, precision=lax.Precision.HIGHEST) * HD ** (-0.5)
    scores = low_back(scores)
    places = jnp.arange(doc_row.shape[0], dtype=jnp.int32)
    allowed = (places[None, :] <= places[:, None]) & (doc_row[None, :] == doc_row[:, None])
    scores = jnp.where(allowed[None], scores, -1e+30)
    attn_probs = jax.nn.softmax(scores, axis=-1)
    return jnp.einsum('hab,bhd->ahd', low(attn_probs), values_wide, precision=lax.Precision.HIGHEST)

def block_layer(hidden_in, query_weight, key_weight, value_weight, output_weight, gate_weight, up_weight, down_weight, gain_pair, doc_rows):
    seq_count = doc_rows.shape[0]
    normed = low(normalize(hidden_in, gain_pair[0]))
    cosine, sine_part = turning(doc_rows)
    cosine = cosine[:, :, None, :]
    sine_part = sine_part[:, :, None, :]
    query_pre = low_back(product(normed, query_weight)).reshape(seq_count, LEN, HQ, HD)
    key_pre = low_back(product(normed, key_weight)).reshape(seq_count, LEN, HK, HD)
    value_low = low(low_back(product(normed, value_weight))).reshape(seq_count, LEN, HK, HD)
    query_rot = low(rotate(query_pre, cosine, sine_part))
    key_rot = low(rotate(key_pre, cosine, sine_part))
    mixed_all = lax.map(jax.checkpoint(attend_seq), (query_rot, key_rot, value_low, doc_rows))
    mixed_low = low(low_back(mixed_all.reshape(seq_count * LEN, HQ * HD)))
    middle = hidden_in + low_back(product(mixed_low, output_weight))
    second = low(normalize(middle, gain_pair[1]))
    gate_pre = low_back(product(second, gate_weight))
    up_pre = low_back(product(second, up_weight))
    hidden_low = low(jax.nn.silu(gate_pre) * up_pre)
    return middle + low_back(product(hidden_low, down_weight))

def reference(inputs, doc_ids, cotangent, query_weight, key_weight, value_weight, output_weight, gate_weight, up_weight, down_weight, gains):
    weight_list = (query_weight, key_weight, value_weight, output_weight, gate_weight, up_weight, down_weight, gains)
    section_params = [tuple((member[section_num].astype(jnp.float32) for member in weight_list)) for section_num in range(2)]
    totals = [[jnp.zeros(member.shape[1:], jnp.float32) for member in weight_list] for section_num in range(2)]
    first_outs, second_outs, first_grads, second_grads = ([], [], [], [])
    for micro_index in range(MICRO):
        doc_rows = doc_ids[micro_index]

        def forward(hidden_in, *params):
            return block_layer(hidden_in, *params, doc_rows)
        first_out, first_back = jax.vjp(forward, inputs[micro_index].astype(jnp.float32), *section_params[0])
        passed = low(first_out)
        second_out, second_back = jax.vjp(forward, passed, *section_params[1])
        grads_two = second_back(cotangent[micro_index].astype(jnp.float32))
        grads_one = first_back(low(grads_two[0]))
        first_outs.append(passed)
        second_outs.append(low(second_out))
        first_grads.append(grads_one[0])
        second_grads.append(grads_two[0])
        totals[0] = [acc + term for acc, term in zip(totals[0], grads_one[1:])]
        totals[1] = [acc + term for acc, term in zip(totals[1], grads_two[1:])]
    section_out = jnp.stack([jnp.stack(first_outs), jnp.stack(second_outs)]).astype(jnp.bfloat16)
    input_grads = jnp.stack([jnp.stack(first_grads), jnp.stack(second_grads)])
    merged = [jnp.stack([totals[0][number], totals[1][number]]) for number in range(8)]
    return (section_out, input_grads, merged[0], merged[1], merged[2], merged[3], merged[4], merged[5], merged[6], merged[7])
```

```python
import jax
import jax.numpy as jnp
import numpy as np
from jax import lax
from jax.sharding import PartitionSpec as P

HD = 96
epsilon = 1e-05
rope_base = 100000.0
AXES = ("section", "fsdp", "tensor")
bf16 = jnp.bfloat16
f32 = jnp.float32


class Grid:
    def __init__(self, mesh):
        self.X = mesh.shape["section"]
        self.C = 2
        self.Y = mesh.shape["fsdp"] // self.C
        self.Z = mesh.shape["tensor"]
        self.R = self.Y * self.Z
        self.places = [
            (x, y, c, z)
            for x in range(self.X)
            for y in range(self.Y)
            for c in range(self.C)
            for z in range(self.Z)
        ]

    def rank(self, place):
        x, y, c, z = place
        return ((x * self.Y + y) * self.C + c) * self.Z + z

    def send(self, block, route):
        pairs = []
        for place in self.places:
            goal = route(*place)
            if goal is not None:
                pairs.append((self.rank(place), self.rank(goal)))
        return lax.ppermute(block, AXES, pairs)

    def over_x(self, block):
        return self.send(block, lambda x, y, c, z: (1 - x, y, c, z))

    def over_c(self, block):
        return self.send(block, lambda x, y, c, z: (x, y, 1 - c, z))

    def place_of(self, p):
        p = p % self.R
        y, k = p // self.Z, p % self.Z
        return (y, k if y % 2 == 0 else self.Z - 1 - k)

    def pos_of(self, y, z):
        return y * self.Z + (z if y % 2 == 0 else self.Z - 1 - z)

    def turn(self, block, step):
        def route(x, y, c, z):
            yy, zz = self.place_of(self.pos_of(y, z) + step)
            return (x, yy, c, zz)

        return self.send(block, route)

    def me(self):
        x = lax.axis_index("section")
        f = lax.axis_index("fsdp")
        z = lax.axis_index("tensor")
        return x, f // self.C, f % self.C, z

    def my_pos(self):
        x, y, c, z = self.me()
        return y * self.Z + jnp.where(y % 2 == 0, z, self.Z - 1 - z)

    def dyn_place(self, p):
        p = (p + 2 * self.R) % self.R
        y, k = p // self.Z, p % self.Z
        return y, jnp.where(y % 2 == 0, k, self.Z - 1 - k)

    def ring_gather(self, block):
        found = [(0, block)]
        up = down = block
        ahead = self.R // 2
        for k in range(1, ahead + 1):
            up = self.turn(up, 1)
            found.append((-k, up))
            if k <= self.R - 1 - ahead:
                down = self.turn(down, -1)
                found.append((k, down))
        return found

    def ring_scatter(self, piece):
        ahead = self.R // 2
        behind = self.R - 1 - ahead
        up = down = None
        for k in range(ahead, 0, -1):
            term = piece(k)
            up = self.turn((term if up is None else term + up.astype(f32)).astype(bf16), 1)
            if k <= behind:
                term = piece(-k)
                down = self.turn((term if down is None else term + down.astype(f32)).astype(bf16), -1)
        return piece(0) + up.astype(f32) + down.astype(f32)


def matmul(a, b):
    return jnp.dot(a, b, preferred_element_type=f32)


def times_right_t(a, b):
    return lax.dot_general(a, b, (((1,), (1,)), ((), ())), preferred_element_type=f32)


def left_t_times(a, b):
    return lax.dot_general(a, b, (((0,), (0,)), ((), ())), preferred_element_type=f32)


def normalize(values, gain_row):
    return values * lax.rsqrt(jnp.mean(values * values, -1, keepdims=True) + epsilon) * gain_row


def norm_pullback(values, gain_row, upstream):
    _, pullback = jax.vjp(normalize, values, gain_row)
    return pullback(upstream)


def turning(doc_row):
    places = jnp.arange(doc_row.shape[-1], dtype=jnp.int32)
    begins = jnp.concatenate([jnp.ones((1,), dtype=bool), doc_row[1:] != doc_row[:-1]], -1)
    starts = lax.cummax(jnp.where(begins, places, 0), axis=0)
    positions = (places - starts).astype(f32)
    ladder = jnp.arange(HD // 2, dtype=f32)
    frequency = rope_base ** (-2.0 * ladder / HD)
    angles = positions[..., None] * frequency
    return jnp.cos(angles), jnp.sin(angles)


def rotate(values, cosine, sine_part):
    half = values.shape[-1] // 2
    a = values[..., :half]
    b = values[..., half:]
    return jnp.concatenate([a * cosine - b * sine_part, b * cosine + a * sine_part], -1)


def scores_of(query_rot, key_rot, allowed):
    scores = jnp.einsum("ahgd,bhd->hgab", query_rot, key_rot, preferred_element_type=f32)
    return jnp.where(allowed[None, None], scores * HD ** (-0.5), -1e30)


def attend_forward(query_rot, key_rot, value_low, allowed):
    scores = scores_of(query_rot, key_rot, allowed)
    largest = jnp.max(scores, -1, keepdims=True)
    raised = jnp.exp(scores - largest)
    row_total = jnp.sum(raised, -1, keepdims=True)
    probs = (raised / row_total).astype(bf16)
    mixed = jnp.einsum("hgab,bhd->ahgd", probs, value_low, preferred_element_type=f32)
    return mixed.astype(bf16), largest + jnp.log(row_total)


def attend_backward(query_rot, key_rot, value_low, allowed, log_total, grad_mixed):
    probs = jnp.exp(scores_of(query_rot, key_rot, allowed) - log_total)
    grad_value = jnp.einsum(
        "hgab,ahgd->bhd", probs.astype(bf16), grad_mixed, preferred_element_type=f32
    )
    grad_probs = jnp.einsum("ahgd,bhd->hgab", grad_mixed, value_low, preferred_element_type=f32)
    grad_scores = (
        probs * (grad_probs - jnp.sum(probs * grad_probs, -1, keepdims=True))
    ).astype(bf16)
    grad_query = jnp.einsum(
        "hgab,bhd->ahgd", grad_scores, key_rot, preferred_element_type=f32
    ) * HD ** (-0.5)
    grad_key = jnp.einsum(
        "hgab,ahgd->bhd", grad_scores, query_rot, preferred_element_type=f32
    ) * HD ** (-0.5)
    return grad_query, grad_key, grad_value


def spread(grid, block):
    far = grid.over_x(block)
    near = jnp.concatenate([block, grid.over_c(block)], 0)
    far = jnp.concatenate([far, grid.over_c(far)], 0)
    return near, far


def collect(grid, near, far):
    rows = near.shape[0] // 2
    passed = far[:rows] + grid.over_c(far[rows:].astype(bf16)).astype(f32)
    from_x = grid.over_x(passed.astype(bf16)).astype(f32)
    from_c = grid.over_c(near[rows:].astype(bf16)).astype(f32)
    return near[:rows] + from_c + from_x


def layer_forward(grid, hidden_in, weights, gain_pair, facts):
    cosine, sine_part, allowed = facts
    weight_qkv, weight_o, weight_g, weight_u, weight_d = weights
    heads = weight_o.shape[1] // HD
    pairs = heads // 2
    normed = normalize(hidden_in, gain_pair[0]).astype(bf16)
    near, far = spread(grid, normed)
    qkv = jnp.concatenate([matmul(near, weight_qkv), matmul(far, weight_qkv)], 0)
    length = qkv.shape[0]
    q_cols, k_cols = heads * HD, pairs * HD
    query_rot = rotate(qkv[:, :q_cols].reshape(length, heads, HD), cosine, sine_part).astype(bf16)
    key_rot = rotate(
        qkv[:, q_cols : q_cols + k_cols].reshape(length, pairs, HD), cosine, sine_part
    ).astype(bf16)
    value_low = qkv[:, q_cols + k_cols :].astype(bf16).reshape(length, pairs, HD)
    query_rot = query_rot.reshape(length, pairs, 2, HD)
    mixed, log_total = attend_forward(query_rot, key_rot, value_low, allowed)
    mixed = mixed.reshape(length, q_cols)
    half = length // 2
    part_far = times_right_t(mixed[half:], weight_o)
    part_near = times_right_t(mixed[:half], weight_o)
    middle = hidden_in + collect(grid, part_near, part_far)
    second = normalize(middle, gain_pair[1]).astype(bf16)
    near2, far2 = spread(grid, second)
    gates, ups, hiddens = [], [], []
    for part in (near2, far2):
        gate = matmul(part, weight_g)
        up = matmul(part, weight_u)
        gates.append(gate.astype(bf16))
        ups.append(up.astype(bf16))
        hiddens.append((jax.nn.silu(gate) * up).astype(bf16))
    part_far = matmul(hiddens[1], weight_d)
    part_near = matmul(hiddens[0], weight_d)
    result = middle + collect(grid, part_near, part_far)
    whole = jnp.concatenate([near, far], 0)
    whole2 = jnp.concatenate([near2, far2], 0)
    kept = (
        hidden_in, whole, query_rot, key_rot, value_low, log_total, mixed, middle, whole2,
        gates, ups, jnp.concatenate(hiddens, 0),
    )
    return result, kept


def layer_backward(grid, grad_out, kept, weights, gain_pair, facts):
    cosine, sine_part, allowed = facts
    weight_qkv, weight_o, weight_g, weight_u, weight_d = weights
    (
        hidden_in, whole, query_rot, key_rot, value_low, log_total, mixed, middle, whole2,
        gates, ups, hidden,
    ) = kept
    grad_low = grad_out.astype(bf16)
    near, far = spread(grid, grad_low)
    terms, grad_gs, grad_us = [], [], []
    for part, gate, up in zip((near, far), gates, ups):
        gate = gate.astype(f32)
        up = up.astype(f32)
        grad_hidden = times_right_t(part, weight_d)
        sig = jax.nn.sigmoid(gate)
        grad_gate = (grad_hidden * up * sig * (1.0 + gate * (1.0 - sig))).astype(bf16)
        grad_up = (grad_hidden * gate * sig).astype(bf16)
        terms.append(times_right_t(grad_gate, weight_g) + times_right_t(grad_up, weight_u))
        grad_gs.append(grad_gate)
        grad_us.append(grad_up)
    grad_second = collect(grid, terms[0], terms[1])
    down_term = left_t_times(hidden, jnp.concatenate([near, far], 0)).astype(bf16)
    gate_term = left_t_times(whole2, jnp.concatenate(grad_gs, 0)).astype(bf16)
    up_term = left_t_times(whole2, jnp.concatenate(grad_us, 0)).astype(bf16)
    grad_norm, gain_two = norm_pullback(middle, gain_pair[1], grad_second)
    grad_middle = grad_out + grad_norm
    near, far = spread(grid, grad_middle.astype(bf16))
    grad_attn = jnp.concatenate([near, far], 0)
    length = grad_attn.shape[0]
    half = length // 2
    grad_mixed = jnp.concatenate(
        [matmul(near, weight_o), matmul(far, weight_o)], 0
    ).astype(bf16)
    out_term = left_t_times(grad_attn, mixed).astype(bf16)
    pairs = key_rot.shape[1]
    grad_query, grad_key, grad_value = attend_backward(
        query_rot, key_rot, value_low, allowed, log_total,
        grad_mixed.reshape(length, pairs, 2, HD),
    )
    grad_query = rotate(grad_query.reshape(length, 2 * pairs, HD), cosine, -sine_part)
    grad_key = rotate(grad_key, cosine, -sine_part)
    grad_qkv = jnp.concatenate(
        [
            grad_query.astype(bf16).reshape(length, 2 * pairs * HD),
            grad_key.astype(bf16).reshape(length, pairs * HD),
            grad_value.astype(bf16).reshape(length, pairs * HD),
        ],
        1,
    )
    part_far = times_right_t(grad_qkv[half:], weight_qkv)
    part_near = times_right_t(grad_qkv[:half], weight_qkv)
    grad_normed = collect(grid, part_near, part_far)
    qkv_term = left_t_times(whole, grad_qkv).astype(bf16)
    grad_norm, gain_one = norm_pullback(hidden_in, gain_pair[0], grad_normed)
    grad_input = grad_middle + grad_norm
    return grad_input, (qkv_term, out_term, gate_term, up_term, down_term), jnp.stack([gain_one, gain_two])


def body(grid, inputs, doc_ids, cotangent, wq, wk, wv, wo, wg, wu, wd, gains):
    X, Y, C, Z = grid.X, grid.Y, grid.C, grid.Z
    x, y, c, z = grid.me()
    pos = grid.my_pos()
    micro, rows, width = inputs.shape
    depth = wq.shape[1]
    at_zero = x == 0

    def enter(block):
        def route(m):
            def go(x, y, c, z):
                if z % 2 != x:
                    return None
                return (x, y, z // 2, m * C + c)

            return go

        first, last = grid.send(block[0], route(0)), grid.send(block[1], route(1))
        return jnp.where(z // C == 0, first, last)

    def leave(block, section):
        def route(m):
            def go(x, y, c, z):
                if z // C != m:
                    return None
                return (section, y, z % C, 2 * c + x)

            return go

        return jnp.stack([grid.send(block, route(m)) for m in range(micro)])

    rows_in = enter(inputs)
    rows_cot = enter(cotangent)
    docs = lax.all_gather(doc_ids[:, 0], "fsdp", axis=0, tiled=False)
    doc_row = docs[y * C + z % C, z // C]
    length = doc_row.shape[0]
    places = jnp.arange(length, dtype=jnp.int32)
    cosine, sine_part = turning(doc_row)

    def in_my_order(rows_of):
        blocks = []
        for dx, dc in ((0, 0), (0, 1), (1, 0), (1, 1)):
            xx = x + dx - 2 * x * dx
            cc = c + dc - 2 * c * dc
            blocks.append(lax.dynamic_slice_in_dim(rows_of, (2 * cc + xx) * rows, rows, 0))
        return jnp.concatenate(blocks, 0)

    token = in_my_order(places)
    doc_mine = in_my_order(doc_row)
    cosine = in_my_order(cosine)[:, None, :]
    sine_part = in_my_order(sine_part)[:, None, :]
    allowed = (token[None, :] <= token[:, None]) & (doc_mine[None, :] == doc_mine[:, None])
    facts = (cosine, sine_part, allowed)

    gain_all = lax.all_gather(gains[0], AXES, axis=0, tiled=False)
    gain_all = gain_all.reshape(X, Y * C * Z, 2, -1).transpose(0, 2, 1, 3).reshape(X, 2, width).astype(f32)

    def cut(block, index, count, axis):
        size = block.shape[axis] // count
        return lax.dynamic_slice_in_dim(block, index * size, size, axis)

    def pack_attn(side):
        qkv = jnp.concatenate([cut(wq[0], side, 2, 1), cut(wk[0], side, 2, 1), cut(wv[0], side, 2, 1)], 1)
        return jnp.concatenate([qkv, cut(wo[0], side, 2, 0).T], 1)

    def pack_gu(side):
        return jnp.stack([cut(wg[0], side, 2, 1), cut(wu[0], side, 2, 1)])

    def both_layers(pack):
        kept = pack(x)
        came = grid.over_x(pack(1 - x))
        return jnp.where(at_zero, kept, came), jnp.where(at_zero, came, kept)

    attn_parts = both_layers(pack_attn)
    gu_parts = both_layers(pack_gu)
    down_parts = both_layers(lambda side: cut(wd[0], side, 2, 0))

    def sibling_join(mine, other, axis):
        came = grid.over_c(other)
        return jnp.where(
            c == 0,
            jnp.concatenate([mine, came], axis),
            jnp.concatenate([came, mine], axis),
        )

    def whole_attn(part):
        buffer = jnp.zeros((Y, Z) + part.shape, bf16)
        for offset, block in grid.ring_gather(part):
            yy, zz = grid.dyn_place(pos + offset)
            buffer = lax.dynamic_update_slice(buffer, block[None, None], (yy, zz, 0, 0))
        halves = Z // 2
        mine = lax.dynamic_slice_in_dim(buffer, c * halves, halves, 1)
        other = lax.dynamic_slice_in_dim(buffer, (1 - c) * halves, halves, 1)
        came = grid.over_c(other)
        both = jnp.where(c == 0, jnp.stack([mine, came], 1), jnp.stack([came, mine], 1))
        top = both.transpose(0, 1, 3, 2, 4).reshape(width, halves, -1)
        q_cols = wq.shape[2] // 2
        k_cols = wk.shape[2] // 2
        weight_qkv = jnp.concatenate(
            [
                top[:, :, :q_cols].reshape(width, -1),
                top[:, :, q_cols : q_cols + k_cols].reshape(width, -1),
                top[:, :, q_cols + k_cols : q_cols + 2 * k_cols].reshape(width, -1),
            ],
            1,
        )
        weight_o = top[:, :, q_cols + 2 * k_cols :].reshape(width, -1)
        return weight_qkv, weight_o

    def whole_ffn(gu_part, down_part):
        gu = sibling_join(cut(gu_part, c, 2, 2), cut(gu_part, 1 - c, 2, 2), 1)
        down = sibling_join(cut(down_part, c, 2, 0), cut(down_part, 1 - c, 2, 0), 1)
        units = down.shape[0]
        tall = C * depth
        weight_g = jnp.zeros((width, Z * units), bf16)
        weight_u = jnp.zeros((width, Z * units), bf16)
        weight_d = jnp.zeros((Z * units, width), bf16)
        for (offset, gu_block), (_, d_block) in zip(grid.ring_gather(gu), grid.ring_gather(down)):
            yy, zz = grid.dyn_place(pos + offset)
            weight_g = lax.dynamic_update_slice(weight_g, gu_block[0], (yy * tall, zz * units))
            weight_u = lax.dynamic_update_slice(weight_u, gu_block[1], (yy * tall, zz * units))
            weight_d = lax.dynamic_update_slice(weight_d, d_block, (zz * units, yy * tall))
        return weight_g, weight_u, weight_d

    weights = []
    for s in range(2):
        weights.append(whole_attn(attn_parts[s]) + whole_ffn(gu_parts[s], down_parts[s]))

    hidden = rows_in.astype(f32)
    kept, outs = [], []
    for s in range(2):
        result, keep = layer_forward(grid, hidden, weights[s], gain_all[s], facts)
        low = result.astype(bf16)
        outs.append(leave(low, s))
        kept.append(keep)
        hidden = low.astype(f32)
    produced = jnp.where(at_zero, outs[0], outs[1])

    upstream = rows_cot
    grads_in, gain_terms, sums = [None] * 2, [None] * 2, [None] * 2
    for s in (1, 0):
        grad_input, terms, gain_terms[s] = layer_backward(
            grid, upstream.astype(f32), kept[s], weights[s], gain_all[s], facts
        )
        upstream = grad_input.astype(bf16)
        grads_in[s] = leave(upstream, s)
        sums[s] = terms
    grads_in = jnp.where(at_zero, grads_in[0], grads_in[1]).astype(f32)

    def back_attn(qkv_term, out_term):
        halves = Z // 2
        q_cols = wq.shape[2] // 2
        k_cols = wk.shape[2] // 2
        nq, nk = halves * q_cols, halves * k_cols
        top = jnp.concatenate(
            [
                qkv_term[:, :nq].reshape(width, halves, q_cols),
                qkv_term[:, nq : nq + nk].reshape(width, halves, k_cols),
                qkv_term[:, nq + nk :].reshape(width, halves, k_cols),
                out_term.reshape(width, halves, q_cols),
            ],
            2,
        )
        both = top.reshape(Y, C, depth, halves, -1).transpose(0, 1, 3, 2, 4)
        mine = lax.dynamic_index_in_dim(both, c, 1, keepdims=False)
        other = lax.dynamic_index_in_dim(both, 1 - c, 1, keepdims=False)
        buffer = sibling_join(mine, other, 1)

        def piece(offset):
            yy, zz = grid.dyn_place(pos + offset)
            return lax.dynamic_slice(buffer, (yy, zz, 0, 0), (1, 1) + buffer.shape[2:])[0, 0].astype(f32)

        return grid.ring_scatter(piece)

    def back_ffn(gate_term, up_term, down_term):
        units = down_term.shape[0] // Z
        tall = C * depth

        def piece_gu(offset):
            yy, zz = grid.dyn_place(pos + offset)
            at = (yy * tall, zz * units)
            return jnp.stack(
                [lax.dynamic_slice(term, at, (tall, units)) for term in (gate_term, up_term)]
            ).astype(f32)

        def piece_d(offset):
            yy, zz = grid.dyn_place(pos + offset)
            return lax.dynamic_slice(down_term, (zz * units, yy * tall), (units, tall)).astype(f32)

        gu = grid.ring_scatter(piece_gu).astype(bf16)
        down = grid.ring_scatter(piece_d).astype(bf16)
        gu = sibling_join(cut(gu, c, 2, 1), cut(gu, 1 - c, 2, 1), 2)
        down = sibling_join(cut(down, c, 2, 1), cut(down, 1 - c, 2, 1), 0)
        return gu, down

    def home(terms, axis):
        kept_part = jnp.where(at_zero, terms[0], terms[1])
        came = grid.over_x(jnp.where(at_zero, terms[1], terms[0]))
        return jnp.where(
            at_zero,
            jnp.concatenate([kept_part, came], axis),
            jnp.concatenate([came, kept_part], axis),
        ).astype(f32)

    attn_back, gu_back, down_back = [None] * 2, [None] * 2, [None] * 2
    for s in (1, 0):
        gu_back[s], down_back[s] = back_ffn(*sums[s][2:])
        attn_back[s] = back_attn(*sums[s][:2]).astype(bf16)
    gu_home = home(gu_back, 2)
    down_home = home(down_back, 0)
    q_cols = wq.shape[2] // 2
    k_cols = wk.shape[2] // 2
    kept_part = jnp.where(at_zero, attn_back[0], attn_back[1])
    came = grid.over_x(jnp.where(at_zero, attn_back[1], attn_back[0]))
    left = jnp.where(at_zero, kept_part, came).astype(f32)
    right = jnp.where(at_zero, came, kept_part).astype(f32)
    cuts = [0, q_cols, q_cols + k_cols, q_cols + 2 * k_cols, q_cols * 2 + 2 * k_cols]
    query_home, key_home, value_home, out_home = [
        jnp.concatenate([left[:, a:b], right[:, a:b]], 1) for a, b in zip(cuts[:-1], cuts[1:])
    ]
    out_home = out_home.T

    gain_sum = jnp.stack(gain_terms)
    gain_sum = gain_sum.reshape(X, 2, Y * C * Z, -1).transpose(0, 2, 1, 3).reshape(X * Y * C * Z, -1)
    gain_share = lax.psum_scatter(gain_sum, AXES, scatter_dimension=0, tiled=True)
    gain_share = gain_share.reshape(1, 2, -1)
    return (
        produced[None],
        grads_in[None],
        query_home[None],
        key_home[None],
        value_home[None],
        out_home[None],
        gu_home[0][None],
        gu_home[1][None],
        down_home[None],
        gain_share,
    )


def solution(mesh):
    grid = Grid(mesh)

    def run(*arguments):
        return body(grid, *arguments)

    return jax.shard_map(
        run,
        mesh=mesh,
        in_specs=(
            P(None, ("fsdp", "tensor"), None),
            P(None, "fsdp", None),
            P(None, ("fsdp", "tensor"), None),
            P("section", "fsdp", "tensor"),
            P("section", "fsdp", "tensor"),
            P("section", "fsdp", "tensor"),
            P("section", "tensor", "fsdp"),
            P("section", "fsdp", "tensor"),
            P("section", "fsdp", "tensor"),
            P("section", "tensor", "fsdp"),
            P("section", None, ("fsdp", "tensor")),
        ),
        out_specs=(
            P("section", None, ("fsdp", "tensor"), None),
            P("section", None, ("fsdp", "tensor"), None),
            P("section", "fsdp", "tensor"),
            P("section", "fsdp", "tensor"),
            P("section", "fsdp", "tensor"),
            P("section", "tensor", "fsdp"),
            P("section", "fsdp", "tensor"),
            P("section", "fsdp", "tensor"),
            P("section", "tensor", "fsdp"),
            P("section", None, ("fsdp", "tensor")),
        ),
        check_vma=False,
    )
```

```python
import functools

import jax
import jax.numpy as jnp
import jax.experimental.pallas as pl
import jax.experimental.pallas.tpu as pltpu
from jax import lax
from jax.sharding import PartitionSpec as P

HD = 96
HP = 128
NEVER = -1e30
epsilon = 1e-05
rope_base = 100000.0
AXES = ("section", "fsdp", "tensor")
bf16 = jnp.bfloat16
f32 = jnp.float32


class Grid:
    def __init__(self, mesh):
        self.calls = 0
        self.X = mesh.shape["section"]
        self.C = 2
        self.Y = mesh.shape["fsdp"] // self.C
        self.Z = mesh.shape["tensor"]
        self.R = self.Y * self.Z
        self.places = [
            (x, y, c, z)
            for x in range(self.X)
            for y in range(self.Y)
            for c in range(self.C)
            for z in range(self.Z)
        ]

    def rank(self, place):
        x, y, c, z = place
        return ((x * self.Y + y) * self.C + c) * self.Z + z

    def send(self, block, route):
        pairs = []
        for place in self.places:
            goal = route(*place)
            if goal is not None:
                pairs.append((self.rank(place), self.rank(goal)))
        return lax.ppermute(block, AXES, pairs)

    def over_x(self, block):
        return self.send(block, lambda x, y, c, z: (1 - x, y, c, z))

    def over_c(self, block):
        return self.send(block, lambda x, y, c, z: (x, y, 1 - c, z))

    def hops(self):
        routes = [lambda x, y, c, z: (x, y, 1 - c, z)]
        for bit in range((self.Y - 1).bit_length()):
            routes.append(lambda x, y, c, z, bit=bit: (x, y ^ (1 << bit), c, z))
        for bit in range((self.Z - 1).bit_length()):
            routes.append(lambda x, y, c, z, bit=bit: (x, y, c, z ^ (1 << bit)))
        return routes

    def place_of(self, p):
        p = p % self.R
        y, k = p // self.Z, p % self.Z
        return (y, k if y % 2 == 0 else self.Z - 1 - k)

    def pos_of(self, y, z):
        return y * self.Z + (z if y % 2 == 0 else self.Z - 1 - z)

    def neighbour(self, way):
        yy, zz = self.dyn_place(self.my_pos() + way)
        return {"fsdp": yy * self.C + lax.axis_index("fsdp") % self.C, "tensor": zz}

    def me(self):
        x = lax.axis_index("section")
        f = lax.axis_index("fsdp")
        z = lax.axis_index("tensor")
        return x, f // self.C, f % self.C, z

    def my_pos(self):
        x, y, c, z = self.me()
        return y * self.Z + jnp.where(y % 2 == 0, z, self.Z - 1 - z)

    def dyn_place(self, p):
        p = (p + 2 * self.R) % self.R
        y, k = p // self.Z, p % self.Z
        return y, jnp.where(y % 2 == 0, k, self.Z - 1 - k)

def params(limit=56):
    return pltpu.CompilerParams(vmem_limit_bytes=limit * 1024 * 1024)


def whole_vmem(count):
    return [pl.BlockSpec(memory_space=pltpu.VMEM)] * count


def cost(micros):
    return pl.CostEstimate(flops=int(micros * 1.0e9), bytes_accessed=1 << 20, transcendentals=0)


def attn_join_kernel(grid, offsets, *refs):
    count = len(offsets)
    pieces = refs[:count]
    qkv_ref, out_ref, held, sems = refs[count:]
    pos = grid.my_pos()
    core = lax.axis_index("fsdp") % grid.C
    tall = held.shape[1]
    halves = grid.Z // 2

    def place(offset):
        yy, zz = grid.dyn_place(pos + offset)
        return yy, zz, zz // halves == core

    def fetch(i):
        return pltpu.make_async_copy(pieces[i], held.at[i], sems.at[i])

    for i, offset in enumerate(offsets):
        _, _, live = place(offset)

        @pl.when(live)
        def _():
            fetch(i).start()

    for i, offset in enumerate(offsets):
        yy, zz, live = place(offset)

        @pl.when(live)
        def _():
            fetch(i).wait()
            j = zz % halves
            rows = pl.ds(pl.multiple_of(yy * tall, tall), tall)
            q_at = pl.multiple_of(j * 2 * HP, HP)
            kv_at = pl.multiple_of(j * HP, HP)
            blank = jnp.zeros((tall, HP - HD), bf16)

            def head(n):
                return jnp.concatenate([held[i, :, n * HD : (n + 1) * HD], blank], 1)

            for h in range(2):
                qkv_ref[rows, pl.ds(q_at + h * HP, HP)] = head(h)
                out_ref[rows, pl.ds(q_at + h * HP, HP)] = head(4 + h)
            qkv_ref[rows, pl.ds(halves * 2 * HP + kv_at, HP)] = head(2)
            qkv_ref[rows, pl.ds(halves * 3 * HP + kv_at, HP)] = head(3)


def attn_join(grid, found, width):
    offsets = [o for o, _ in found]
    blocks = [b for _, b in found]
    halves = grid.Z // 2
    count = len(blocks)
    tall, cols = blocks[0].shape
    return pl.pallas_call(
        functools.partial(attn_join_kernel, grid, offsets),
        out_shape=(
            jax.ShapeDtypeStruct((width, halves * 4 * HP), bf16),
            jax.ShapeDtypeStruct((width, halves * 2 * HP), bf16),
        ),
        in_specs=[pl.BlockSpec(memory_space=pl.ANY)] * count,
        out_specs=whole_vmem(2),
        scratch_shapes=[pltpu.VMEM((count, tall, cols), bf16), pltpu.SemaphoreType.DMA((count,))],
        compiler_params=params(),
        cost_estimate=cost(5),
        name="attn_join",
    )(*blocks)


CHUNKS = 4


def add_came(term, came, n, size, starts, at=None):
    for ref, start, rows in zip(came, starts[0], starts[1]):
        first = start // size

        def added(ref=ref):
            block = ref[...] if at is None else ref[at]
            return term + block.astype(f32)

        if rows == size * CHUNKS:
            term = added()
        else:
            here = (n >= first) & (n < first + rows // size)
            block = ref[...] if at is None else ref[at]
            term = term + jnp.where(here, block.astype(f32), 0.0)
    return term


def came_spec(shape, start, size):
    lead = len(shape) - 2
    first, count = start // size, shape[-2] // size

    def index(n, at):
        return (0,) * lead + (jnp.clip(n - first, 0, count - 1), 0)

    return pl.BlockSpec(shape[:lead] + (size, shape[-1]), index)


def ffn_term_kernel(starts, at_ref, gate_ref, up_ref, down_ref, *refs):
    came, out = refs[:-1], refs[-1]
    n = pl.program_id(0)
    for m, term_ref in enumerate((gate_ref, up_ref, down_ref)):
        term = term_ref[...].astype(f32)
        out[m] = add_came(term, came, n, term.shape[0], starts, m).astype(bf16)


def ffn_term(at, terms, came, tall, units):
    size = tall // CHUNKS
    starts = ([start for _, start in came], [block.shape[1] for block, _ in came])
    return pl.pallas_call(
        functools.partial(ffn_term_kernel, starts),
        grid_spec=pltpu.PrefetchScalarGridSpec(
            num_scalar_prefetch=1,
            grid=(CHUNKS,),
            in_specs=[pl.BlockSpec((size, units), lambda n, at: (at[0] * CHUNKS + n, at[1]))] * 3
            + [came_spec(block.shape, start, size) for block, start in came],
            out_specs=pl.BlockSpec((3, size, units), lambda n, at: (0, n, 0)),
        ),
        out_shape=jax.ShapeDtypeStruct((3, tall, units), bf16),
        compiler_params=params(),
        cost_estimate=cost(3),
        name="ffn_term",
    )(at, *terms, *[block for block, _ in came])


def attn_term_kernel(halves, starts, at_ref, qkv_ref, out_ref, *refs):
    came, out = refs[:-1], refs[-1]
    n = pl.program_id(0)

    @pl.when(at_ref[2] != 0)
    def _():
        j = at_ref[1]
        q_at = pl.multiple_of(j * 2 * HP, HP)
        kv_at = pl.multiple_of(j * HP, HP)

        def part(ref, at):
            return ref[:, pl.ds(at, HP)][:, :HD].astype(f32)

        term = jnp.concatenate(
            [
                part(qkv_ref, q_at),
                part(qkv_ref, q_at + HP),
                part(qkv_ref, halves * 2 * HP + kv_at),
                part(qkv_ref, halves * 3 * HP + kv_at),
                part(out_ref, q_at),
                part(out_ref, q_at + HP),
            ],
            1,
        )
        out[...] = add_came(term, came, n, term.shape[0], starts).astype(bf16)


def attn_term(at, qkv_term, out_term, came, tall, halves):
    size = tall // CHUNKS
    starts = ([start for _, start in came], [block.shape[0] for block, _ in came])
    return pl.pallas_call(
        functools.partial(attn_term_kernel, halves, starts),
        grid_spec=pltpu.PrefetchScalarGridSpec(
            num_scalar_prefetch=1,
            grid=(CHUNKS,),
            in_specs=[
                pl.BlockSpec((size, qkv_term.shape[1]), lambda n, at: (at[0] * CHUNKS + n, 0)),
                pl.BlockSpec((size, out_term.shape[1]), lambda n, at: (at[0] * CHUNKS + n, 0)),
            ]
            + [came_spec(block.shape, start, size) for block, start in came],
            out_specs=pl.BlockSpec((size, 6 * HD), lambda n, at: (n, 0)),
        ),
        out_shape=jax.ShapeDtypeStruct((tall, 6 * HD), bf16),
        compiler_params=params(),
        cost_estimate=cost(3),
        name="attn_term",
    )(at, qkv_term, out_term, *[block for block, _ in came])


def swapped(values):
    lane = lax.broadcasted_iota(jnp.int32, values.shape, 1)
    half = HD // 2
    return jnp.where(lane < half, pltpu.roll(values, HP - half, 1), pltpu.roll(values, half, 1))


MESH = pl.DeviceIdType.MESH
NT = (((1,), (1,)), ((), ()))
PARTS = 2


def dot_nt(a, b):
    return lax.dot_general(a, b, NT, preferred_element_type=f32)


def greet(grid, sides, cycle):
    x, y, c, _ = grid.me()
    sib = {"fsdp": y * grid.C + 1 - c}
    over = {"section": 1 - x}
    others = [sib, over] if sides else []
    if cycle:
        others += [grid.neighbour(1), grid.neighbour(-1)]
    barrier = pltpu.get_barrier_semaphore()
    for other in others:
        pl.semaphore_signal(barrier, inc=1, device_id=other, device_id_type=MESH)
    pl.semaphore_wait(barrier, len(others))
    return sib, over


def remote(src, dst, sems, n, device):
    return pltpu.make_async_remote_copy(
        src_ref=src, dst_ref=dst, send_sem=sems.at[0, n], recv_sem=sems.at[1, n],
        device_id=device, device_id_type=MESH,
    )


def pieces_of(rows):
    size = rows // PARTS
    return [pl.ds(k * size, size) for k in range(PARTS)]


class Plan:
    def __init__(self):
        self.inputs, self.outs, self.stages, self.hooks = [], [], [], []

    def give(self, array):
        self.inputs.append(array)
        return ("in", len(self.inputs) - 1)

    def room(self, shape):
        self.outs.append(jax.ShapeDtypeStruct(shape, bf16))
        return ("out", len(self.outs) - 1)

    def move(self, stage, src, dst, way, offset, owned, cut=None, whole=False):
        while len(self.stages) <= stage:
            self.stages.append([])
        self.stages[stage].append((src, dst, way, offset, owned, cut, whole))

    def count(self):
        return sum(len(stage) for stage in self.stages)

    def settle(self, results):
        for hook in self.hooks:
            hook(lambda handle: self.inputs[handle[1]] if handle[0] == "in" else results[handle[1]])


class Background:
    def __init__(self, grid, plan, ins, outs, sems):
        self.stages, self.now, n = [], -1, 0
        pos = grid.my_pos()
        core = lax.axis_index("fsdp") % grid.C
        refs = {"in": ins, "out": outs}

        def live(owned, offset):
            if not owned:
                return None
            return grid.dyn_place(pos + offset)[1] // (grid.Z // 2) == core

        for stage in plan.stages:
            made = []
            for src, dst, way, offset, owned, cut, whole in stage:
                src_ref, dst_ref = refs[src[0]][src[1]], refs[dst[0]][dst[1]]
                if cut is not None:
                    src_ref = src_ref.at[cut]
                    if not whole:
                        dst_ref = dst_ref.at[cut]
                copy = remote(src_ref, dst_ref, sems, n, grid.neighbour(way))
                made.append((copy, live(owned, offset), live(owned, offset - way)))
                n += 1
            self.stages.append(made)

    @staticmethod
    def do(condition, action):
        if condition is None:
            action()
        else:
            pl.when(condition)(action)

    def advance(self):
        if 0 <= self.now < len(self.stages):
            for copy, _, come in self.stages[self.now]:
                self.do(come, copy.wait_recv)
        self.now += 1
        if self.now < len(self.stages):
            for copy, go, _ in self.stages[self.now]:
                self.do(go, copy.start)

    def finish(self):
        while self.now < len(self.stages):
            self.advance()
        for stage in self.stages:
            for copy, go, _ in stage:
                self.do(go, copy.wait_send)


class Gather:
    def __init__(self, grid, block, owned=False):
        self.grid, self.owned, self.shape = grid, owned, block.shape
        self.up = self.down = block
        self.k, self.total = 0, grid.R // 2
        self.found = [(0, block)]

    def left(self):
        return self.total - self.k

    def add(self, plan, stage, hops=None):
        hops = self.left() if hops is None else min(hops, self.left())
        if hops == 0:
            return
        one = self.up is self.down
        up = plan.give(self.up)
        down = up if one else plan.give(self.down)
        new = []
        for n in range(hops):
            self.k += 1
            k = self.k
            if k < self.total:
                to_up, to_down = plan.room(self.shape), plan.room(self.shape)
                plan.move(stage + n, up, to_up, 1, 1 - k, self.owned)
                plan.move(stage + n, down, to_down, -1, k - 1, self.owned)
                new += [(-k, to_up), (k, to_down)]
                up, down = to_up, to_down
            else:
                both = plan.room(self.shape)
                first, last = halves_cut(self.shape)
                plan.move(stage + n, up, both, 1, 1 - k, self.owned, first)
                plan.move(stage + n, down, both, -1, k - 1, self.owned, last)
                new += [(-k, both)]
                up = down = both

        def hook(get):
            self.up, self.down = get(up), get(down)
            self.found += [(offset, get(handle)) for offset, handle in new]

        plan.hooks.append(hook)


def halves_cut(shape):
    rows = shape[-2] // 2
    lead = (slice(None),) * (len(shape) - 2)
    return lead + (pl.ds(0, rows),), lead + (pl.ds(rows, rows),)


class Scatter:
    def __init__(self, grid, piece, shape, owned=False):
        self.grid, self.piece, self.shape, self.owned = grid, piece, shape, owned
        self.k = grid.R // 2
        self.up, self.down = [], []

    def left(self):
        return self.k

    def add(self, plan, stage):
        if self.k == 0:
            return
        k = self.k
        self.k -= 1
        rows = self.shape[-2] // 2
        if k == self.grid.R // 2:
            first, last = halves_cut(self.shape)
            half = self.shape[:-2] + (rows, self.shape[-1])
            block = plan.give(self.piece(k, []))
            to_up, to_down = plan.room(half), plan.room(half)
            plan.move(stage, block, to_up, 1, k, self.owned, first, True)
            plan.move(stage, block, to_down, -1, -k, self.owned, last, True)
            starts = (0, rows)
        else:
            up, down = plan.give(self.piece(k, self.up)), plan.give(self.piece(-k, self.down))
            to_up, to_down = plan.room(self.shape), plan.room(self.shape)
            plan.move(stage, up, to_up, 1, k, self.owned)
            plan.move(stage, down, to_down, -1, -k, self.owned)
            starts = (0, 0)

        def hook(get):
            self.up, self.down = [(get(to_up), starts[0])], [(get(to_down), starts[1])]

        plan.hooks.append(hook)

    def result(self):
        return self.piece(0, self.up + self.down)


def fused_call(grid, kernel, name, plan, inputs, in_specs, outs, out_specs, scratch, micros):
    plan = Plan() if plan is None else plan
    a, b, c, d = len(inputs), len(plan.inputs), len(outs), len(plan.outs)
    moves = plan.count()

    def whole(*refs):
        fg_in, bg_in = refs[:a], refs[a : a + b]
        fg_out, bg_out = refs[a + b : a + b + c], refs[a + b + c : a + b + c + d]
        rest = refs[a + b + c + d :]
        background = Background(grid, plan, bg_in, bg_out, rest[-1]) if moves else Background(grid, plan, (), (), None)
        kernel(background, bool(moves), *fg_in, *fg_out, *(rest[:-1] if moves else rest))

    number = grid.calls
    grid.calls += 1
    results = pl.pallas_call(
        whole,
        out_shape=tuple(outs) + tuple(plan.outs),
        in_specs=list(in_specs) + [ANY] * b,
        out_specs=tuple(out_specs) + (ANY,) * d,
        scratch_shapes=list(scratch) + ([pltpu.SemaphoreType.DMA((2, moves))] if moves else []),
        compiler_params=remote_params(number),
        cost_estimate=cost(micros),
        name=name,
    )(*inputs, *plan.inputs)
    plan.settle(results[c:])
    return results[:c]


def ring_call(grid, plan):
    if plan.count() == 0:
        return

    def kernel(background, cycle):
        greet(grid, False, True)
        background.advance()
        background.finish()

    fused_call(grid, kernel, "cycle", plan, (), (), (), (), (), 30 * len(plan.stages))


class Spread:
    sems = pltpu.SemaphoreType.DMA((2, 1 + 2 * PARTS))

    def __init__(self, rows_ref, sems, sib, over):
        cuts = pieces_of(rows_ref.shape[1])
        self.near = remote(rows_ref.at[0], rows_ref.at[1], sems, 0, sib)
        self.far = [
            remote(rows_ref.at[0, at], rows_ref.at[2, at], sems, 1 + k, over)
            for k, at in enumerate(cuts)
        ]
        self.relay = [
            remote(rows_ref.at[2, at], rows_ref.at[3, at], sems, 1 + PARTS + k, sib)
            for k, at in enumerate(cuts)
        ]

    def start(self):
        for copy in self.far:
            copy.start()
        self.near.start()

    def pass_on(self, k):
        self.far[k].wait_recv()
        self.relay[k].start()

    def end(self):
        self.near.wait_send()
        for copy in self.far + self.relay:
            copy.wait_send()


class Collect:
    sems = pltpu.SemaphoreType.DMA((2, 1 + 2 * PARTS))

    @staticmethod
    def scratch(rows, width):
        return [pltpu.VMEM((6, rows, width), bf16), Collect.sems]

    def __init__(self, hold, sems, sib, over):
        self.hold = hold
        self.cuts = pieces_of(hold.shape[1])
        self.near = remote(hold.at[0], hold.at[2], sems, 0, sib)
        self.side = [
            remote(hold.at[1, at], hold.at[3, at], sems, 1 + k, sib)
            for k, at in enumerate(self.cuts)
        ]
        self.over = [
            remote(hold.at[4, at], hold.at[5, at], sems, 1 + PARTS + k, over)
            for k, at in enumerate(self.cuts)
        ]

    def give_near(self, part):
        self.hold[0] = part.astype(bf16)
        self.near.start()

    def give_side(self, k, part):
        self.hold[1, self.cuts[k]] = part.astype(bf16)
        self.side[k].start()

    def give_over(self, k, part):
        self.side[k].wait_recv()
        self.hold[4, self.cuts[k]] = (part + self.hold[3, self.cuts[k]].astype(f32)).astype(bf16)
        self.over[k].start()

    def finish(self, part):
        self.near.wait_recv()
        part = part + self.hold[2].astype(f32)
        for copy in self.over:
            copy.wait_recv()
        return part + self.hold[5].astype(f32)

    def end(self):
        self.near.wait_send()
        for copy in self.side + self.over:
            copy.wait_send()


def normed_rows(values, gain_row):
    return values * lax.rsqrt(jnp.mean(values * values, -1, keepdims=True) + epsilon) * gain_row


def norm_back(values, gain_row, upstream):
    scale = lax.rsqrt(jnp.mean(values * values, -1, keepdims=True) + epsilon)
    unit = values * scale
    moved = upstream * gain_row
    grad = scale * (moved - unit * jnp.mean(moved * unit, -1, keepdims=True))
    gains = upstream * unit
    return grad, jnp.sum(gains.reshape(-1, 8, gains.shape[-1]), 0)


def remote_params(number, limit=58):
    return pltpu.CompilerParams(
        vmem_limit_bytes=limit * 1024 * 1024, collective_id=number, has_side_effects=True
    )


def shaped(*pairs):
    return tuple(jax.ShapeDtypeStruct(shape, dtype) for shape, dtype in pairs)


ANY = pl.BlockSpec(memory_space=pl.ANY)
VMEM = pl.BlockSpec(memory_space=pltpu.VMEM)


def qkv_kernel(
    grid, halves, background, cycle, h_ref, gain_ref, w_ref, cos_ref, sin_ref, all_ref, q_ref, k_ref, v_ref,
    rows_ref, sems, out_sem,
):
    rows = h_ref.shape[0]
    sib, over = greet(grid, True, cycle)
    background.advance()
    rows_ref[0] = normed_rows(h_ref[...].astype(f32), gain_ref[...]).astype(bf16)
    spread = Spread(rows_ref, sems, sib, over)
    spread.start()

    def work(slot, start, size):
        cosine, sine_part = cos_ref[slot, start : start + size], sin_ref[slot, start : start + size]
        at = slice(start, start + size)
        made = jnp.dot(rows_ref[slot, at], w_ref[...], preferred_element_type=f32)
        for h in range(3 * halves):
            one = made[:, h * HP : (h + 1) * HP]
            turned = (one * cosine + swapped(one) * sine_part).astype(bf16)
            if h < 2 * halves:
                q_ref[h, slot, at] = turned
            else:
                k_ref[h - 2 * halves, slot, at] = turned
        for h in range(halves):
            v_ref[h, slot, at] = made[:, (3 * halves + h) * HP : (3 * halves + h + 1) * HP].astype(bf16)

    work(0, 0, rows)
    spread.near.wait_recv()
    work(1, 0, rows)
    size = rows // PARTS
    for k in range(PARTS):
        spread.pass_on(k)
        work(2, k * size, size)
        spread.relay[k].wait_recv()
        work(3, k * size, size)
    out = pltpu.make_async_copy(rows_ref, all_ref, out_sem)
    out.start()
    out.wait()
    spread.end()
    background.finish()


def qkv_call(grid, plan, hidden, gain_row, weight, cosine, sine_part):
    rows, width = hidden.shape
    halves = grid.Z // 2
    shape = (halves, 4, rows, HP)
    return fused_call(
        grid, functools.partial(qkv_kernel, grid, halves), "qkv", plan,
        (hidden, gain_row, weight, cosine, sine_part), [VMEM] * 5,
        shaped(
            ((4, rows, width), bf16), ((2 * halves,) + shape[1:], bf16), (shape, bf16), (shape, bf16)
        ),
        (ANY, VMEM, VMEM, VMEM),
        [pltpu.VMEM((4, rows, width), bf16), Spread.sems, pltpu.SemaphoreType.DMA],
        28,
    )


def place_id(grid):
    x, _, c, _ = grid.me()
    return [2 * cc + xx for xx, cc in ((x, c), (x, 1 - c), (1 - x, c), (1 - x, 1 - c))]


def attend_kernel(
    grid, heads, background, cycle, h_ref, q_ref, k_ref, v_ref, tokk_ref, tokq_ref, from_ref, wo_ref,
    mid_ref, mixed_ref, lse_ref, top, total, acc, part, hold, sems,
):
    rows = h_ref.shape[0]
    scale = HD ** (-0.5)
    ids = place_id(grid)
    sib, over = greet(grid, True, cycle)
    background.advance()
    collect = Collect(hold, sems, sib, over)

    def attend(i):
        tok_q, begin = tokq_ref[i], from_ref[i]

        def block(j, first):
            tok_k = tokk_ref[j]
            allowed = (tok_k <= tok_q) & (tok_k >= begin)
            for h in range(heads):
                scores = dot_nt(q_ref[h, i], k_ref[h // 2, j])
                scores = jnp.where(allowed, scores * scale, NEVER)
                peak = jnp.max(scores, 1, keepdims=True)
                if not first:
                    before = top[h]
                    peak = jnp.maximum(peak, before)
                raised = jnp.exp(scores - peak)
                summed = jnp.sum(raised, 1, keepdims=True)
                got = jnp.dot(raised.astype(bf16), v_ref[h // 2, j], preferred_element_type=f32)
                if first:
                    total[h] = summed
                    acc[h] = got
                else:
                    shrink = jnp.exp(before - peak)
                    total[h] = total[h] * shrink + summed
                    acc[h] = acc[h] * shrink + got
                top[h] = peak

        block(i, True)
        for j in range(4):
            if j != i:
                pl.when((ids[j] < ids[i]) & (ids[j] >= ids[i] - 2))(functools.partial(block, j, False))
        for h in range(heads):
            mixed_ref[i, :, h * HP : (h + 1) * HP] = (acc[h] / total[h]).astype(bf16)
            log_total = top[h] + jnp.log(total[h])
            lse_ref[i, h] = jnp.transpose(jnp.broadcast_to(log_total, (rows, HP)))[:8]
        part[...] = dot_nt(mixed_ref[i], wo_ref[...])

    cuts = pieces_of(rows)
    attend(3)
    for k in range(PARTS):
        collect.give_side(k, part[cuts[k]])
    attend(2)
    for k in range(PARTS):
        collect.give_over(k, part[cuts[k]])
    attend(1)
    collect.give_near(part[...])
    attend(0)
    mid_ref[...] = collect.finish(part[...] + h_ref[...].astype(f32))
    collect.end()
    background.finish()


def attend_call(grid, plan, hidden, query, keys, values, facts, weight_o):
    rows, width = hidden.shape
    heads = query.shape[0]
    return fused_call(
        grid, functools.partial(attend_kernel, grid, heads), "attend", plan,
        (
            hidden, query, keys, values, facts["tok"][:, None, :], facts["tok"][:, :, None],
            facts["from"][:, :, None], weight_o,
        ),
        [VMEM] * 8,
        shaped(((rows, width), f32), ((4, rows, heads * HP), bf16), ((4, heads, 8, rows), f32)),
        (VMEM,) * 3,
        [
            pltpu.VMEM((heads, rows, 1), f32),
            pltpu.VMEM((heads, rows, 1), f32),
            pltpu.VMEM((heads, rows, HP), f32),
            pltpu.VMEM((rows, width), f32),
        ]
        + Collect.scratch(rows, width),
        32,
    )


def fetch_ffn(grid, offsets, pieces, held, sems):
    pos = grid.my_pos()
    _, tall, units = pieces[0].shape
    copies = []
    for i, offset in enumerate(offsets):
        yy, zz = grid.dyn_place(pos + offset)
        rows = pl.ds(pl.multiple_of(yy * tall, tall), tall)
        cols = pl.ds(pl.multiple_of(zz * units, units), units)
        copy = pltpu.make_async_copy(pieces[i], held.at[:, rows, cols], sems.at[i])
        copy.start()
        copies.append(copy)
    return copies


STEP = 512


def ffn_kernel(grid, offsets, background, cycle, mid_ref, gain_ref, *refs):
    count = len(offsets)
    pieces = refs[:count]
    (
        out_ref, all_ref, gate_ref, up_ref, hid_ref,
        held, w_sems, rows_ref, s_sems, part, hold, c_sems, out_sem,
    ) = refs[count:]
    rows, width = mid_ref.shape
    hidden = gate_ref.shape[2]
    fetched = fetch_ffn(grid, offsets, pieces, held, w_sems)
    sib, over = greet(grid, True, cycle)
    background.advance()
    rows_ref[0] = normed_rows(mid_ref[...], gain_ref[...]).astype(bf16)
    spread = Spread(rows_ref, s_sems, sib, over)
    collect = Collect(hold, c_sems, sib, over)
    spread.start()
    for copy in fetched:
        copy.wait()

    def work(slot, start, size):
        at = pl.ds(start, size)

        def tile(n, carry):
            cols = pl.ds(pl.multiple_of(n * STEP, STEP), STEP)
            some = rows_ref[slot, at]
            gate = jnp.dot(some, held[0, :, cols], preferred_element_type=f32)
            up = jnp.dot(some, held[1, :, cols], preferred_element_type=f32)
            gate_ref[slot, at, cols] = gate.astype(bf16)
            up_ref[slot, at, cols] = up.astype(bf16)
            hid_ref[slot, at, cols] = (gate * jax.nn.sigmoid(gate) * up).astype(bf16)
            return carry

        lax.fori_loop(0, hidden // STEP, tile, 0)

        def tile_down(n, carry):
            cols = pl.ds(pl.multiple_of(n * STEP, STEP), STEP)
            part[at, cols] = dot_nt(hid_ref[slot, at], held[2, cols])
            return carry

        lax.fori_loop(0, width // STEP, tile_down, 0)

    work(0, 0, rows)
    out_ref[...] = mid_ref[...] + part[...]
    spread.near.wait_recv()
    work(1, 0, rows)
    collect.give_near(part[...])
    cuts = pieces_of(rows)
    size = rows // PARTS
    for k in range(PARTS):
        spread.pass_on(k)
        spread.relay[k].wait_recv()
        work(3, k * size, size)
        collect.give_side(k, part[cuts[k]])
        work(2, k * size, size)
        collect.give_over(k, part[cuts[k]])
        background.advance()
    out = pltpu.make_async_copy(rows_ref, all_ref, out_sem)
    out.start()
    out_ref[...] = collect.finish(out_ref[...])
    out.wait()
    spread.end()
    collect.end()
    background.finish()


def ffn_call(grid, plan, middle, gain_row, found):
    rows, width = middle.shape
    offsets, blocks = [o for o, _ in found], [b for _, b in found]
    hidden = grid.Z * blocks[0].shape[2]
    return fused_call(
        grid, functools.partial(ffn_kernel, grid, offsets), "ffn", plan,
        (middle, gain_row, *blocks), [VMEM] * 2 + [ANY] * len(blocks),
        shaped(((rows, width), f32), ((4, rows, width), bf16), *[((4, rows, hidden), bf16)] * 3),
        (VMEM, ANY, VMEM, VMEM, VMEM),
        [
            pltpu.VMEM((3, width, hidden), bf16),
            pltpu.SemaphoreType.DMA((len(blocks),)),
            pltpu.VMEM((4, rows, width), bf16),
            Spread.sems,
            pltpu.VMEM((rows, width), f32),
        ]
        + Collect.scratch(rows, width)
        + [pltpu.SemaphoreType.DMA],
        44,
    )


def ffn_back_kernel(grid, offsets, background, cycle, g_ref, mid_ref, gain_ref, gate_ref, up_ref, *refs):
    count = len(offsets)
    pieces = refs[:count]
    (
        out_ref, gains_ref, all_ref, dgate_ref, dup_ref,
        held, w_sems, rows_ref, s_sems, part, own, hold, c_sems, out_sem,
    ) = refs[count:]
    rows, width = mid_ref.shape
    hidden = gate_ref.shape[2]
    fetched = fetch_ffn(grid, offsets, pieces, held, w_sems)
    sib, over = greet(grid, True, cycle)
    background.advance()
    rows_ref[0] = g_ref[...]
    spread = Spread(rows_ref, s_sems, sib, over)
    collect = Collect(hold, c_sems, sib, over)
    spread.start()
    for copy in fetched:
        copy.wait()

    def work(slot, start, size):
        at = pl.ds(start, size)

        def tile(n, carry):
            cols = pl.ds(pl.multiple_of(n * STEP, STEP), STEP)
            grad = jnp.dot(rows_ref[slot, at], held[2, :, cols], preferred_element_type=f32)
            gate = gate_ref[slot, at, cols].astype(f32)
            up = up_ref[slot, at, cols].astype(f32)
            sig = jax.nn.sigmoid(gate)
            dgate_ref[slot, at, cols] = (grad * up * sig * (1.0 + gate * (1.0 - sig))).astype(bf16)
            dup_ref[slot, at, cols] = (grad * gate * sig).astype(bf16)
            return carry

        lax.fori_loop(0, hidden // STEP, tile, 0)

        def tile_back(n, carry):
            cols = pl.ds(pl.multiple_of(n * STEP, STEP), STEP)
            part[at, cols] = dot_nt(dgate_ref[slot, at], held[0, cols]) + dot_nt(
                dup_ref[slot, at], held[1, cols]
            )
            return carry

        lax.fori_loop(0, width // STEP, tile_back, 0)

    work(0, 0, rows)
    own[...] = part[...]
    spread.near.wait_recv()
    work(1, 0, rows)
    collect.give_near(part[...])
    cuts = pieces_of(rows)
    size = rows // PARTS
    for k in range(PARTS):
        spread.pass_on(k)
        spread.relay[k].wait_recv()
        work(3, k * size, size)
        collect.give_side(k, part[cuts[k]])
        work(2, k * size, size)
        collect.give_over(k, part[cuts[k]])
    out = pltpu.make_async_copy(rows_ref, all_ref, out_sem)
    out.start()
    second = collect.finish(own[...])
    grad, gains = norm_back(mid_ref[...], gain_ref[...], second)
    out_ref[...] = g_ref[...].astype(f32) + grad
    gains_ref[...] = gains
    out.wait()
    spread.end()
    collect.end()
    background.finish()


def ffn_back_call(grid, plan, grad_out, middle, gain_row, gate, up, found):
    rows, width = middle.shape
    offsets, blocks = [o for o, _ in found], [b for _, b in found]
    hidden = gate.shape[2]
    return fused_call(
        grid, functools.partial(ffn_back_kernel, grid, offsets), "ffn_back", plan,
        (grad_out, middle, gain_row, gate, up, *blocks), [VMEM] * 5 + [ANY] * len(blocks),
        shaped(
            ((rows, width), f32), ((8, width), f32), ((4, rows, width), bf16),
            *[((4, rows, hidden), bf16)] * 2,
        ),
        (VMEM, VMEM, ANY, VMEM, VMEM),
        [
            pltpu.VMEM((3, width, hidden), bf16),
            pltpu.SemaphoreType.DMA((len(blocks),)),
            pltpu.VMEM((4, rows, width), bf16),
            Spread.sems,
            pltpu.VMEM((rows, width), f32),
            pltpu.VMEM((rows, width), f32),
        ]
        + Collect.scratch(rows, width)
        + [pltpu.SemaphoreType.DMA],
        44,
    )


def mixed_back_kernel(grid, background, cycle, g_ref, w_ref, all_ref, gm_ref, rows_ref, sems, out_sem):
    rows = g_ref.shape[0]
    sib, over = greet(grid, True, cycle)
    background.advance()
    rows_ref[0] = g_ref[...].astype(bf16)
    spread = Spread(rows_ref, sems, sib, over)
    spread.start()

    def work(slot, start, size):
        at = slice(start, start + size)
        made = jnp.dot(rows_ref[slot, at], w_ref[...], preferred_element_type=f32).astype(bf16)
        for h in range(gm_ref.shape[0]):
            gm_ref[h, slot, at] = made[:, h * HP : (h + 1) * HP]

    work(0, 0, rows)
    spread.near.wait_recv()
    work(1, 0, rows)
    size = rows // PARTS
    for k in range(PARTS):
        spread.pass_on(k)
        work(2, k * size, size)
        spread.relay[k].wait_recv()
        work(3, k * size, size)
    out = pltpu.make_async_copy(rows_ref, all_ref, out_sem)
    out.start()
    out.wait()
    spread.end()
    background.finish()


def mixed_back_call(grid, plan, grad_middle, weight_o):
    rows, width = grad_middle.shape
    heads = weight_o.shape[1] // HP
    return fused_call(
        grid, functools.partial(mixed_back_kernel, grid), "mixed_back", plan,
        (grad_middle, weight_o), [VMEM] * 2,
        shaped(((4, rows, width), bf16), ((heads, 4, rows, HP), bf16)), (ANY, VMEM),
        [pltpu.VMEM((4, rows, width), bf16), Spread.sems, pltpu.SemaphoreType.DMA],
        27,
    )


def normed_back_kernel(
    grid, background, cycle, dqkv_ref, w_ref, h_ref, gain_ref, gm_ref, out_ref, gains_ref, part, hold, sems
):
    rows = h_ref.shape[0]
    sib, over = greet(grid, True, cycle)
    background.advance()
    collect = Collect(hold, sems, sib, over)
    cuts = pieces_of(rows)

    def work(slot):
        part[...] = dot_nt(dqkv_ref[slot], w_ref[...])

    work(3)
    for k in range(PARTS):
        collect.give_side(k, part[cuts[k]])
    work(2)
    for k in range(PARTS):
        collect.give_over(k, part[cuts[k]])
    work(1)
    collect.give_near(part[...])
    work(0)
    grad, gains = norm_back(
        h_ref[...].astype(f32), gain_ref[...], collect.finish(part[...])
    )
    out_ref[...] = (gm_ref[...] + grad).astype(bf16)
    gains_ref[...] = gains
    collect.end()
    background.finish()


def normed_back_call(grid, plan, grad_qkv, weight, hidden, gain_row, grad_middle):
    rows, width = hidden.shape
    return fused_call(
        grid, functools.partial(normed_back_kernel, grid), "normed_back", plan,
        (grad_qkv, weight, hidden, gain_row, grad_middle), [VMEM] * 5,
        shaped(((rows, width), bf16), ((8, width), f32)), (VMEM, VMEM),
        [pltpu.VMEM((rows, width), f32)] + Collect.scratch(rows, width),
        27,
    )


def attend_back_kernel(
    grid, heads, background, cycle, q_ref, k_ref, v_ref, g_ref, m_ref, l_ref, tokc_ref, tokr_ref, from_ref,
    cos_ref, sin_ref, out_ref, key_sum, value_sum, query_sum, delta,
):
    rows = q_ref.shape[2]
    pairs = heads // 2
    scale = HD ** (-0.5)
    ids = place_id(grid)
    if cycle:
        greet(grid, False, True)
        background.advance()
    key_sum[...] = jnp.zeros_like(key_sum)
    value_sum[...] = jnp.zeros_like(value_sum)
    query_sum[...] = jnp.zeros_like(query_sum)

    def back(summed, at):
        one = summed * scale
        return (one * cos_ref[at] - swapped(one) * sin_ref[at]).astype(bf16)

    for i in range(4):
        for h in range(heads):
            product = g_ref[h, i].astype(f32) * m_ref[i, :, h * HP : (h + 1) * HP].astype(f32)
            summed = jnp.sum(product, 1, keepdims=True)
            delta[h] = jnp.transpose(jnp.broadcast_to(summed, (rows, HP)))[:8]

        def block(j):
            allowed = (tokc_ref[j] <= tokr_ref[i]) & (tokc_ref[j] >= from_ref[i])
            for h in range(heads):
                query, upstream = q_ref[h, i], g_ref[h, i]
                key, value = k_ref[h // 2, j], v_ref[h // 2, j]
                scores = jnp.where(allowed, dot_nt(key, query) * scale, NEVER)
                probs = jnp.exp(scores - l_ref[i, h, 0:1])
                value_sum[h // 2, j] += jnp.dot(
                    probs.astype(bf16), upstream, preferred_element_type=f32
                )
                grad_scores = (probs * (dot_nt(value, upstream) - delta[h, 0:1])).astype(bf16)
                key_sum[h // 2, j] += jnp.dot(grad_scores, query, preferred_element_type=f32)
                query_sum[h, i] += lax.dot_general(
                    grad_scores, key, (((0,), (0,)), ((), ())), preferred_element_type=f32
                )

        for j in range(4):
            if i == j:
                block(j)
            else:
                pl.when((ids[j] < ids[i]) & (ids[j] >= ids[i] - 2))(functools.partial(block, j))

    for i in range(4):
        for h in range(heads):
            out_ref[i, :, h * HP : (h + 1) * HP] = back(query_sum[h, i], i)
        for h in range(pairs):
            at = heads + h
            out_ref[i, :, at * HP : (at + 1) * HP] = back(key_sum[h, i], i)
            at = heads + pairs + h
            out_ref[i, :, at * HP : (at + 1) * HP] = value_sum[h, i].astype(bf16)
    if cycle:
        background.finish()


def attend_back_call(grid, plan, query, keys, values, upstream, mixed, lse, facts):
    heads, _, rows, _ = query.shape
    pairs = heads // 2
    return fused_call(
        grid, functools.partial(attend_back_kernel, grid, heads), "attend_back", plan,
        (
            query, keys, values, upstream, mixed, lse, facts["tok"][:, :, None],
            facts["tok"][:, None, :], facts["from"][:, None, :], facts["cos"], facts["sin"],
        ),
        [VMEM] * 11,
        shaped(((4, rows, 2 * heads * HP), bf16)), (VMEM,),
        [
            pltpu.VMEM((pairs, 4, rows, HP), f32),
            pltpu.VMEM((pairs, 4, rows, HP), f32),
            pltpu.VMEM((heads, 4, rows, HP), f32),
            pltpu.VMEM((heads, 8, rows), f32),
        ],
        19,
    )[0]


def left_t_times(a, b):
    return lax.dot_general(a, b, (((0,), (0,)), ((), ())), preferred_element_type=f32)


def turning(doc_row):
    places = jnp.arange(doc_row.shape[-1], dtype=jnp.int32)
    begins = jnp.concatenate([jnp.ones((1,), dtype=bool), doc_row[1:] != doc_row[:-1]], -1)
    starts = lax.cummax(jnp.where(begins, places, 0), axis=0)
    positions = (places - starts).astype(f32)
    ladder = jnp.arange(HD // 2, dtype=f32)
    frequency = rope_base ** (-2.0 * ladder / HD)
    angles = positions[..., None] * frequency
    cosine, sine_part = jnp.cos(angles), jnp.sin(angles)
    blank = jnp.zeros((doc_row.shape[0], HP - HD), f32)
    return (
        starts,
        jnp.concatenate([cosine, cosine, blank], -1),
        jnp.concatenate([-sine_part, sine_part, blank], -1),
    )


def layer_forward(grid, hidden_in, attn, ffn, next_attn, gain_pair, facts):
    weight_qkv, weight_o = attn
    plan = Plan()
    ffn.add(plan, 0, 1)
    whole, query, keys, values = qkv_call(
        grid, plan, hidden_in, gain_pair[0:1], weight_qkv, facts["cos"], facts["sin"]
    )
    plan = Plan()
    ffn.add(plan, 0, 1)
    middle, mixed, lse = attend_call(grid, plan, hidden_in, query, keys, values, facts, weight_o)
    plan = Plan()
    ffn.add(plan, 0)
    ring_call(grid, plan)
    plan = Plan()
    if next_attn is not None:
        next_attn.add(plan, 0)
    result, whole2, gate, up, hidden = ffn_call(grid, plan, middle, gain_pair[1:2], ffn.found)
    kept = (hidden_in, whole, query, keys, values, lse, mixed, middle, whole2, gate, up, hidden)
    return result.astype(bf16), kept


def flat(blocks):
    return blocks.reshape(-1, blocks.shape[-1])


def layer_backward(grid, grad_out, kept, attn, ffn, gain_pair, facts, running, sum_ffn, sum_attn):
    weight_qkv, weight_o = attn
    hidden_in, whole, query, keys, values, lse, mixed, middle, whole2, gate, up, hidden = kept

    def plan():
        made = Plan()
        for ring in running:
            ring.add(made, 0)
        return made

    grad_middle, gain_two, grad_whole, grad_gate, grad_up = ffn_back_call(
        grid, plan(), grad_out, middle, gain_pair[1:2], gate, up, ffn.found
    )
    down_term = left_t_times(flat(grad_whole), flat(hidden)).astype(bf16)
    gate_term = left_t_times(flat(whole2), flat(grad_gate)).astype(bf16)
    up_term = left_t_times(flat(whole2), flat(grad_up)).astype(bf16)
    running.append(sum_ffn(gate_term, up_term, down_term))
    grad_attn, grad_mixed = mixed_back_call(grid, plan(), grad_middle, weight_o)
    grad_qkv = attend_back_call(grid, plan(), query, keys, values, grad_mixed, mixed, lse, facts)
    grad_input, gain_one = normed_back_call(
        grid, plan(), grad_qkv, weight_qkv, hidden_in, gain_pair[0:1], grad_middle
    )
    out_term = left_t_times(flat(grad_attn), flat(mixed)).astype(bf16)
    qkv_term = left_t_times(flat(whole), flat(grad_qkv)).astype(bf16)
    running.append(sum_attn(qkv_term, out_term))
    gains = jnp.stack([jnp.sum(gain_one, 0), jnp.sum(gain_two, 0)])
    return grad_input, gains


def body(grid, inputs, doc_ids, cotangent, wq, wk, wv, wo, wg, wu, wd, gains):
    X, Y, C, Z = grid.X, grid.Y, grid.C, grid.Z
    x, y, c, z = grid.me()
    pos = grid.my_pos()
    micro, rows, width = inputs.shape
    depth = wq.shape[1]
    at_zero = x == 0

    def enter(block):
        def route(m):
            def go(x, y, c, z):
                if z % 2 != x:
                    return None
                return (x, y, z // 2, m * C + c)

            return go

        first, last = grid.send(block[0], route(0)), grid.send(block[1], route(1))
        return jnp.where(z // C == 0, first, last)

    def leave(block, section):
        def route(m):
            def go(x, y, c, z):
                if z // C != m:
                    return None
                return (section, y, z % C, 2 * c + x)

            return go

        return jnp.stack([grid.send(block, route(m)) for m in range(micro)])

    rows_in = enter(inputs)
    rows_cot = enter(cotangent)
    docs = grid.over_c(doc_ids)
    docs = jnp.where(c == z % C, doc_ids, docs)[:, 0]
    doc_row = lax.dynamic_index_in_dim(docs, z // C, 0, keepdims=False)
    length = doc_row.shape[0]
    starts, cosine, sine_part = turning(doc_row)
    ids = place_id(grid)

    def in_my_order(rows_of):
        return jnp.stack(
            [lax.dynamic_slice_in_dim(rows_of, ids[n] * rows, rows, 0) for n in range(4)]
        )

    facts = {
        "tok": in_my_order(jnp.arange(length, dtype=jnp.int32)),
        "from": in_my_order(starts),
        "cos": in_my_order(cosine),
        "sin": in_my_order(sine_part),
    }

    mine = (y * C + c) * Z + z
    table = lax.dynamic_update_slice(
        jnp.zeros((Y * C * Z,) + gains.shape[1:], bf16), gains, (mine, 0, 0)
    )
    for hop in grid.hops():
        table = table + grid.send(table, hop)
    gain_own = table.transpose(1, 0, 2).reshape(2, width)
    gain_other = grid.over_x(gain_own)
    gain_all = [
        jnp.where(at_zero, gain_own, gain_other).astype(f32),
        jnp.where(at_zero, gain_other, gain_own).astype(f32),
    ]

    def cut(block, index, count, axis):
        size = block.shape[axis] // count
        return lax.dynamic_slice_in_dim(block, index * size, size, axis)

    def pack_attn(side):
        qkv = jnp.concatenate([cut(wq[0], side, 2, 1), cut(wk[0], side, 2, 1), cut(wv[0], side, 2, 1)], 1)
        return jnp.concatenate([qkv, cut(wo[0], side, 2, 0).T], 1)

    def pack_ffn(side):
        return jnp.stack([cut(wg[0], side, 2, 1), cut(wu[0], side, 2, 1), cut(wd[0], side, 2, 0).T])

    def both_layers(pack):
        kept = pack(x)
        came = grid.over_x(pack(1 - x))
        return jnp.where(at_zero, kept, came), jnp.where(at_zero, came, kept)

    def sibling_join(mine, other, axis):
        came = grid.over_c(other)
        return jnp.where(
            c == 0,
            jnp.concatenate([mine, came], axis),
            jnp.concatenate([came, mine], axis),
        )

    halves = Z // 2
    tall = C * depth
    owner = lambda z: z // halves
    units = wg.shape[2] // 4
    attn_parts = both_layers(pack_attn)
    ffn_parts = both_layers(pack_ffn)

    def whole_attn(part):
        came = grid.send(part, lambda x, y, c, z: (x, y, 1 - c, z) if owner(z) != c else None)
        both = jnp.where(
            c == 0, jnp.concatenate([part, came], 0), jnp.concatenate([came, part], 0)
        )
        return Gather(grid, both, True)

    def whole_ffn(part):
        block = sibling_join(cut(part, c, 2, 2), cut(part, 1 - c, 2, 2), 1)
        return Gather(grid, block)

    attn = [whole_attn(attn_parts[s]) for s in range(2)]
    ffn = [whole_ffn(ffn_parts[s]) for s in range(2)]
    plan = Plan()
    attn[0].add(plan, 0)
    ring_call(grid, plan)

    hidden = rows_in
    kept, outs, joined = [], [], []
    for s in range(2):
        joined.append(attn_join(grid, attn[s].found, width))
        hidden, keep = layer_forward(
            grid, hidden, joined[s], ffn[s], attn[s + 1] if s == 0 else None, gain_all[s], facts
        )
        outs.append(leave(hidden, s))
        kept.append(keep)
    produced = jnp.where(at_zero, outs[0], outs[1])

    def spot(offset):
        yy, zz = grid.dyn_place(pos + offset)
        live = (zz // halves == c).astype(jnp.int32)
        return yy, zz, live

    def sum_ffn(*terms):
        def piece(offset, came):
            yy, zz, _ = spot(offset)
            at = jnp.stack([yy, zz]).astype(jnp.int32)
            return ffn_term(at, terms, came, tall, units)

        return Scatter(grid, piece, (3, tall, units))

    def sum_attn(qkv_term, out_term):
        def piece(offset, came):
            yy, zz, live = spot(offset)
            at = jnp.stack([yy, zz % halves, live]).astype(jnp.int32)
            return attn_term(at, qkv_term, out_term, came, tall, halves)

        return Scatter(grid, piece, (tall, 6 * HD), True)

    upstream = rows_cot
    grads_in, gain_terms, running = [None] * 2, [None] * 2, []
    for s in (1, 0):
        upstream, gain_terms[s] = layer_backward(
            grid, upstream, kept[s], joined[s], ffn[s], gain_all[s], facts, running, sum_ffn, sum_attn
        )
        grads_in[s] = leave(upstream, s)
    while any(ring.left() for ring in running):
        plan = Plan()
        for ring in running:
            ring.add(plan, 0)
        ring_call(grid, plan)
    ffn_sum = [running[2].result(), running[0].result()]
    attn_sum = [running[3].result(), running[1].result()]
    grads_in = jnp.where(at_zero, grads_in[0], grads_in[1]).astype(f32)

    def back_attn(total):
        mine = cut(total, c, 2, 0)
        came = grid.send(
            cut(total, 1 - c, 2, 0), lambda x, y, c, z: (x, y, 1 - c, z) if owner(z) == c else None
        )
        return jnp.where(z // halves == c, mine, came)

    def back_ffn(total):
        return sibling_join(cut(total, c, 2, 1), cut(total, 1 - c, 2, 1), 2)

    def home(terms):
        kept_part = jnp.where(at_zero, terms[0], terms[1])
        came = grid.over_x(jnp.where(at_zero, terms[1], terms[0]))
        return jnp.where(at_zero, kept_part, came).astype(f32), jnp.where(at_zero, came, kept_part).astype(f32)

    attn_back, ffn_back = [None] * 2, [None] * 2
    for s in (1, 0):
        ffn_back[s] = back_ffn(ffn_sum[s])
        attn_back[s] = back_attn(attn_sum[s])
    ffn_home = jnp.concatenate(home(ffn_back), 2)
    q_cols = wq.shape[2] // 2
    k_cols = wk.shape[2] // 2
    left, right = home(attn_back)
    cuts = [0, q_cols, q_cols + k_cols, q_cols + 2 * k_cols, q_cols * 2 + 2 * k_cols]
    query_home, key_home, value_home, out_home = [
        jnp.concatenate([left[:, a:b], right[:, a:b]], 1) for a, b in zip(cuts[:-1], cuts[1:])
    ]
    out_home = out_home.T

    gain_kept = jnp.where(at_zero, gain_terms[0], gain_terms[1])
    gain_sum = gain_kept + grid.over_x(jnp.where(at_zero, gain_terms[1], gain_terms[0]))
    for hop in grid.hops():
        gain_sum = gain_sum + grid.send(gain_sum, hop)
    share = width // (Y * C * Z)
    gain_share = lax.dynamic_slice_in_dim(gain_sum, mine * share, share, 1)[None]
    return (
        produced[None],
        grads_in[None],
        query_home[None],
        key_home[None],
        value_home[None],
        out_home[None],
        ffn_home[0][None],
        ffn_home[1][None],
        ffn_home[2].T[None],
        gain_share,
    )


def solution(mesh):
    grid = Grid(mesh)

    def run(*arguments):
        grid.calls = 0
        return body(grid, *arguments)

    return jax.shard_map(
        run,
        mesh=mesh,
        in_specs=(
            P(None, ("fsdp", "tensor"), None),
            P(None, "fsdp", None),
            P(None, ("fsdp", "tensor"), None),
            P("section", "fsdp", "tensor"),
            P("section", "fsdp", "tensor"),
            P("section", "fsdp", "tensor"),
            P("section", "tensor", "fsdp"),
            P("section", "fsdp", "tensor"),
            P("section", "fsdp", "tensor"),
            P("section", "tensor", "fsdp"),
            P("section", None, ("fsdp", "tensor")),
        ),
        out_specs=(
            P("section", None, ("fsdp", "tensor"), None),
            P("section", None, ("fsdp", "tensor"), None),
            P("section", "fsdp", "tensor"),
            P("section", "fsdp", "tensor"),
            P("section", "fsdp", "tensor"),
            P("section", "tensor", "fsdp"),
            P("section", "fsdp", "tensor"),
            P("section", "fsdp", "tensor"),
            P("section", "tensor", "fsdp"),
            P("section", None, ("fsdp", "tensor")),
        ),
        check_vma=False,
    )
```

```python
import functools

import jax
import jax.numpy as jnp
import jax.experimental.pallas as pl
import jax.experimental.pallas.tpu as pltpu
from jax import lax
from jax.sharding import PartitionSpec as P

HD = 96
HP = 128
NEVER = -1e30
epsilon = 1e-05
rope_base = 100000.0
AXES = ("section", "fsdp", "tensor")
bf16 = jnp.bfloat16
f32 = jnp.float32


class Grid:
    def __init__(self, mesh):
        self.calls = 0
        self.X = mesh.shape["section"]
        self.C = 2
        self.Y = mesh.shape["fsdp"] // self.C
        self.Z = mesh.shape["tensor"]
        self.R = self.Y * self.Z
        self.places = [
            (x, y, c, z)
            for x in range(self.X)
            for y in range(self.Y)
            for c in range(self.C)
            for z in range(self.Z)
        ]

    def rank(self, place):
        x, y, c, z = place
        return ((x * self.Y + y) * self.C + c) * self.Z + z

    def send(self, block, route):
        pairs = []
        for place in self.places:
            goal = route(*place)
            if goal is not None:
                pairs.append((self.rank(place), self.rank(goal)))
        return lax.ppermute(block, AXES, pairs)

    def over_x(self, block):
        return self.send(block, lambda x, y, c, z: (1 - x, y, c, z))

    def over_c(self, block):
        return self.send(block, lambda x, y, c, z: (x, y, 1 - c, z))

    def hops(self):
        routes = [lambda x, y, c, z: (x, y, 1 - c, z)]
        for bit in range((self.Y - 1).bit_length()):
            routes.append(lambda x, y, c, z, bit=bit: (x, y ^ (1 << bit), c, z))
        for bit in range((self.Z - 1).bit_length()):
            routes.append(lambda x, y, c, z, bit=bit: (x, y, c, z ^ (1 << bit)))
        return routes

    def place_of(self, p):
        p = p % self.R
        y, k = p // self.Z, p % self.Z
        return (y, k if y % 2 == 0 else self.Z - 1 - k)

    def pos_of(self, y, z):
        return y * self.Z + (z if y % 2 == 0 else self.Z - 1 - z)

    def neighbour(self, way):
        yy, zz = self.dyn_place(self.my_pos() + way)
        return {"fsdp": yy * self.C + lax.axis_index("fsdp") % self.C, "tensor": zz}

    def me(self):
        x = lax.axis_index("section")
        f = lax.axis_index("fsdp")
        z = lax.axis_index("tensor")
        return x, f // self.C, f % self.C, z

    def my_pos(self):
        x, y, c, z = self.me()
        return y * self.Z + jnp.where(y % 2 == 0, z, self.Z - 1 - z)

    def dyn_place(self, p):
        p = (p + 2 * self.R) % self.R
        y, k = p // self.Z, p % self.Z
        return y, jnp.where(y % 2 == 0, k, self.Z - 1 - k)

def params(limit=56):
    return pltpu.CompilerParams(vmem_limit_bytes=limit * 1024 * 1024)


def whole_vmem(count):
    return [pl.BlockSpec(memory_space=pltpu.VMEM)] * count


def cost(micros):
    return pl.CostEstimate(flops=int(micros * 1.0e9), bytes_accessed=1 << 20, transcendentals=0)


def swapped(values):
    lane = lax.broadcasted_iota(jnp.int32, values.shape, 1)
    half = HD // 2
    return jnp.where(lane < half, pltpu.roll(values, HP - half, 1), pltpu.roll(values, half, 1))


MESH = pl.DeviceIdType.MESH
NT = (((1,), (1,)), ((), ()))
PARTS = 2


def dot_nt(a, b):
    return lax.dot_general(a, b, NT, preferred_element_type=f32)


def partners(grid):
    x, y, c, _ = grid.me()
    return (
        {"fsdp": y * grid.C + 1 - c},
        {"section": 1 - x},
        {"section": 1 - x, "fsdp": y * grid.C + 1 - c},
    )


def greet(grid, sides, cycle):
    others = list(partners(grid)[:sides])
    if cycle:
        others += [grid.neighbour(1), grid.neighbour(-1)]
    barrier = pltpu.get_barrier_semaphore()
    for other in others:
        pl.semaphore_signal(barrier, inc=1, device_id=other, device_id_type=MESH)
    pl.semaphore_wait(barrier, len(others))
    return partners(grid)


def remote(src, dst, sems, n, device):
    return pltpu.make_async_remote_copy(
        src_ref=src, dst_ref=dst, send_sem=sems.at[0, n], recv_sem=sems.at[1, n],
        device_id=device, device_id_type=MESH,
    )


def pieces_of(rows):
    size = rows // PARTS
    return [pl.ds(k * size, size) for k in range(PARTS)]


def start_all(copies):
    for copy in copies:
        copy.start()


def wait_all(copies):
    for copy in copies:
        copy.wait()


class Plan:
    def __init__(self):
        self.inputs, self.outs, self.lands, self.stages, self.hooks = [], [], [], [], []
        self.slots, self.makes, self.totals, self.moves, self.copies = [], [], [], 0, 1

    def give(self, array):
        for n, known in enumerate(self.inputs):
            if known is array:
                return ("in", n)
        self.inputs.append(array)
        return ("in", len(self.inputs) - 1)

    def room(self, shape):
        self.outs.append(jax.ShapeDtypeStruct(shape, bf16))
        return ("out", len(self.outs) - 1)

    def land(self, shape):
        self.lands.append(shape)
        return ("land", len(self.lands) - 1)

    def slot(self, key, shape):
        if (key, shape) not in self.slots:
            self.slots.append((key, shape))
        return self.slots.index((key, shape))

    def make(self, stage, key, shape, parts, offset, owned):
        slot = self.slot(key, shape)
        made = []
        for places, came in parts:
            copies = [(self.give(array), src, dst) for array, src, dst in places]
            joins = [(h if isinstance(h, tuple) else self.give(h), at) for h, at in came]
            made.append((copies, joins))
        self.copies = max(self.copies, sum(len(c) + len(j) for c, j in made))
        self.makes.append((stage, slot, made, offset, owned))
        return ("make", len(self.makes) - 1)

    def move(self, stage, src, dst, way, offset, owned, cut, part=0, needs=None):
        while len(self.stages) <= stage:
            self.stages.append([])
        self.stages[stage].append((self.moves, src, dst, way, offset, owned, cut, part, needs))
        self.moves += 1
        return self.moves - 1

    def scratch(self):
        if not self.moves:
            return []
        held = [pltpu.VMEM(shape, bf16) for _, shape in self.slots for _ in range(2)]
        held += [pltpu.VMEM(shape, bf16) for shape in self.lands]
        sems = [pltpu.SemaphoreType.DMA((2, self.moves))]
        if self.slots:
            sems.append(pltpu.SemaphoreType.DMA((len(self.slots), self.copies)))
        return held + sems

    def settle(self, results):
        for hook in self.hooks:
            hook(lambda handle: self.inputs[handle[1]] if handle[0] == "in" else results[handle[1]])


class Background:
    def __init__(self, grid, plan, ins, outs, rest):
        self.stages, self.totals, self.now, self.sent = [], [], -1, 0
        if not plan.moves:
            return
        pos = grid.my_pos()
        core = lax.axis_index("fsdp") % grid.C
        count = 2 * len(plan.slots)
        held, lands = rest[:count], rest[count : count + len(plan.lands)]
        sems = rest[count + len(plan.lands)]
        local = rest[-1]
        self.refs = {"in": ins, "out": outs, "land": lands}

        def live(owned, offset):
            if not owned:
                return None
            return grid.dyn_place(pos + offset)[1] // (grid.Z // 2) == core

        def built(slot, made, offset, owned):
            term, more = held[2 * slot], held[2 * slot + 1]
            yy, zz = grid.dyn_place(pos + offset)
            n, parts = 0, []
            for copies, joins in made:
                fetches, adds = [], []
                for handle, src, dst in copies:
                    ref = self.refs[handle[0]][handle[1]].at[src(yy, zz)]
                    fetches.append(pltpu.make_async_copy(ref, term.at[dst], local.at[slot, n]))
                    n += 1
                for handle, at in joins:
                    ref = self.refs[handle[0]][handle[1]]
                    if handle[0] == "land":
                        adds.append((None, ref, at))
                    else:
                        copy = pltpu.make_async_copy(ref.at[at], more.at[at], local.at[slot, n])
                        adds.append((copy, more, at))
                    n += 1
                parts.append((fetches, adds, term, handle_early(joins)))
            return parts, live(owned, offset)

        def handle_early(joins):
            return all(handle[0] == "in" for handle, _ in joins)

        self.makes = [[] for _ in plan.stages]
        buffers = []
        for stage, slot, made, offset, owned in plan.makes:
            parts, alive = built(slot, made, offset, owned)
            self.makes[stage].append((parts, alive))
            buffers.append((held[2 * slot], parts, alive))
        for slot, made, owned in plan.totals:
            self.totals.append((held[2 * slot],) + built(slot, made, 0, owned))
        self.all = {}
        for stage in plan.stages:
            row = []
            for number, src, dst, way, offset, owned, cut, part, needs in stage:
                put = None
                if src[0] == "make":
                    src_ref, parts, alive = buffers[src[1]]
                    put = (parts[part], alive)
                else:
                    src_ref = self.refs[src[0]][src[1]]
                dst_ref = self.refs[dst[0]][dst[1]]
                copy = remote(src_ref.at[cut], dst_ref.at[cut], sems, number, grid.neighbour(way))
                self.all[number] = (copy, live(owned, offset), live(owned, offset - way))
                row.append((number, put, needs))
            self.stages.append(row)
        self.come, self.put_done = set(), set()

    @staticmethod
    def do(condition, action):
        if condition is None:
            action()
        else:
            pl.when(condition)(action)

    def fetch(self, stage):
        if stage < len(self.stages):
            for parts, alive in self.makes[stage]:
                for fetches, adds, _, early in parts:
                    copies = fetches + [copy for copy, _, _ in adds if copy is not None and early]
                    self.do(alive, functools.partial(start_all, copies))

    def begin(self):
        self.fetch(0)
        for _, parts, alive in self.totals:
            for fetches, _, _, _ in parts:
                self.do(alive, functools.partial(start_all, fetches))

    @staticmethod
    def put(part, started=True):
        fetches, adds, term, early = part
        wait_all(fetches)
        for copy, ref, at in adds:
            if copy is not None:
                if not (early and started):
                    copy.start()
                copy.wait()
            term[at] = (term[at].astype(f32) + ref[at].astype(f32)).astype(bf16)

    def arrive(self, number):
        if number is not None and number not in self.come:
            self.come.add(number)
            copy, _, come = self.all[number]
            self.do(come, copy.wait_recv)

    def advance(self):
        self.now += 1
        if self.now < len(self.stages):
            for number, put, needs in self.stages[self.now]:
                for need in needs or ():
                    self.arrive(need)
                if put is not None and id(put[0]) not in self.put_done:
                    self.put_done.add(id(put[0]))
                    self.do(put[1], functools.partial(self.put, put[0]))
                copy, go, _ = self.all[number]
                self.do(go, copy.start)
            if self.now + 1 < len(self.stages):
                self.wait_sends(self.now)
                self.fetch(self.now + 1)
        if self.now >= len(self.stages):
            for row in self.stages:
                for number, _, _ in row:
                    self.arrive(number)

    def arrived(self, stage):
        for row in self.stages[: stage + 1]:
            for number, _, _ in row:
                self.arrive(number)

    def wait_sends(self, stage):
        while self.sent < stage:
            for number, _, _ in self.stages[self.sent]:
                copy, go, _ = self.all[number]
                self.do(go, copy.wait_send)
            self.sent += 1

    def finish(self):
        while self.now < len(self.stages):
            self.advance()
        self.wait_sends(len(self.stages))


class Gather:
    def __init__(self, grid, shape, cuts, owned=False):
        self.grid, self.owned, self.shape, self.cuts = grid, owned, shape, cuts
        self.k, self.total = 0, grid.R // 2

    def begin(self, plan):
        room = plan.room(self.shape)
        self.up = self.down = room

        def hook(get):
            self.found = [(0, get(room))]
            if self.k == 0:
                self.up = self.down = get(room)

        plan.hooks.append(hook)
        return room

    def left(self):
        return self.total - self.k

    def add(self, plan, stage, hops=None):
        hops = self.left() if hops is None else min(hops, self.left())
        if hops == 0:
            return
        one = self.up is self.down
        up = self.up if isinstance(self.up, tuple) else plan.give(self.up)
        down = up if one else plan.give(self.down)
        new = []
        before = [(None, None)] * len(self.cuts)
        for n in range(hops):
            self.k += 1
            k = self.k
            last = k == self.total
            to_up = plan.room(self.shape)
            to_down = to_up if last else plan.room(self.shape)
            now = []
            for (cut, first, second), (need_up, need_down) in zip(self.cuts, before):
                pair = (first, second) if last else (cut, cut)
                moved = []
                for src, dst, way, part, need in (
                    (up, to_up, 1, pair[0], need_up), (down, to_down, -1, pair[1], need_down)
                ):
                    moved.append(
                        None
                        if part is None
                        else plan.move(
                            stage + n, src, dst, way, -way * (k - 1), self.owned, part,
                            needs=(need,),
                        )
                    )
                now.append(tuple(moved))
            before = now
            new.append((-k, to_up))
            if not last:
                new.append((k, to_down))
            up, down = to_up, to_down

        def hook(get):
            self.up, self.down = get(up), get(down)
            self.found += [(offset, get(handle)) for offset, handle in new]

        plan.hooks.append(hook)


class Scatter:
    def __init__(self, grid, parts, shape, owned=False):
        self.grid, self.parts, self.shape, self.owned = grid, parts, shape, owned
        self.k = grid.R // 2
        self.held = {1: None, -1: None}

    def left(self):
        return self.k

    def came(self, way, n):
        if self.held[way] is None:
            return []
        block, column = self.held[way]
        at = self.parts[n][0][column]
        return [] if at is None else [(block, at)]

    def add(self, plan, stage, steps=1, final=False):
        steps = min(steps, self.k)
        before = {way: [None] * len(self.parts) for way in (1, -1)}
        for n in range(steps):
            k = self.k
            self.k -= 1
            room = plan.land if n < steps - 1 or final else plan.room
            rooms = {way: room(self.shape) for way in (1, -1)}
            halves = k == self.grid.R // 2
            blocks = {}
            for way in (1, -1):
                if halves and way == -1:
                    blocks[way] = blocks[1]
                    continue
                parts = [(places, self.came(way, m)) for m, (_, places) in enumerate(self.parts)]
                blocks[way] = plan.make(
                    stage + n, (id(self), way, n % 2), self.shape, parts, way * k, self.owned
                )
            now = {1: [], -1: []}
            for m, (cuts, _) in enumerate(self.parts):
                for way in (1, -1):
                    column = (1 if way == 1 else 2) if halves else 0
                    moved = None
                    if cuts[column] is not None:
                        moved = plan.move(
                            stage + n, blocks[way], rooms[way], way, way * k, self.owned, cuts[column],
                            m, (before[way][m],),
                        )
                    now[way].append(moved)
            before = now
            self.held = {
                way: (rooms[way], (1 if way == 1 else 2) if halves else 0) for way in (1, -1)
            }

        def hook(get):
            self.held = {
                way: (get(block), column) if block[0] == "out" else (None, column)
                for way, (block, column) in self.held.items()
            }

        if steps:
            plan.hooks.append(hook)

    def total(self, plan):
        parts = [
            (places, self.came(1, m) + self.came(-1, m)) for m, (_, places) in enumerate(self.parts)
        ]
        slot = plan.slot(("total", id(self)), self.shape)
        made = []
        for places, came in parts:
            copies = [(plan.give(array), src, dst) for array, src, dst in places]
            joins = [(h if isinstance(h, tuple) else plan.give(h), at) for h, at in came]
            made.append((copies, joins))
        plan.copies = max(plan.copies, sum(len(c) + len(j) for c, j in made))
        plan.totals.append((slot, made, self.owned))


def fused_call(grid, kernel, name, plan, inputs, in_specs, outs, out_specs, scratch, micros):
    plan = Plan() if plan is None else plan
    a, b, c, d = len(inputs), len(plan.inputs), len(outs), len(plan.outs)
    moves = plan.moves

    def whole(*refs):
        fg_in, bg_in = refs[:a], refs[a : a + b]
        fg_out, bg_out = refs[a + b : a + b + c], refs[a + b + c : a + b + c + d]
        rest = refs[a + b + c + d :]
        own = len(scratch)
        background = Background(grid, plan, bg_in, bg_out, rest[own:])
        kernel(background, bool(moves), *fg_in, *fg_out, *rest[:own])

    number = grid.calls
    grid.calls += 1
    results = pl.pallas_call(
        whole,
        out_shape=tuple(outs) + tuple(plan.outs),
        in_specs=list(in_specs) + [ANY] * b,
        out_specs=tuple(out_specs) + (ANY,) * d,
        scratch_shapes=list(scratch) + plan.scratch(),
        compiler_params=remote_params(number),
        cost_estimate=cost(micros),
        name=name,
    )(*inputs, *plan.inputs)
    plan.settle(results[c:])
    return results[:c]


class Spread:
    sems = pltpu.SemaphoreType.DMA((2, 1 + 2 * PARTS))

    def __init__(self, rows_ref, sems, sib, over):
        cuts = pieces_of(rows_ref.shape[1])
        self.near = remote(rows_ref.at[0], rows_ref.at[1], sems, 0, sib)
        self.far = [
            remote(rows_ref.at[0, at], rows_ref.at[2, at], sems, 1 + k, over)
            for k, at in enumerate(cuts)
        ]
        self.relay = [
            remote(rows_ref.at[2, at], rows_ref.at[3, at], sems, 1 + PARTS + k, sib)
            for k, at in enumerate(cuts)
        ]

    def start(self):
        for copy in self.far:
            copy.start()
        self.near.start()

    def pass_on(self, k):
        self.far[k].wait_recv()
        self.relay[k].start()

    def end(self):
        self.near.wait_send()
        for copy in self.far + self.relay:
            copy.wait_send()


class Collect:
    sems = pltpu.SemaphoreType.DMA((2, 1 + 2 * PARTS))

    @staticmethod
    def scratch(rows, width):
        return [pltpu.VMEM((6, rows, width), bf16), Collect.sems]

    def __init__(self, hold, sems, sib, over):
        self.hold = hold
        self.cuts = pieces_of(hold.shape[1])
        self.near = remote(hold.at[0], hold.at[2], sems, 0, sib)
        self.side = [
            remote(hold.at[1, at], hold.at[3, at], sems, 1 + k, sib)
            for k, at in enumerate(self.cuts)
        ]
        self.over = [
            remote(hold.at[4, at], hold.at[5, at], sems, 1 + PARTS + k, over)
            for k, at in enumerate(self.cuts)
        ]

    def give_near(self, part):
        self.hold[0] = part.astype(bf16)
        self.near.start()

    def give_side(self, k, part):
        self.hold[1, self.cuts[k]] = part.astype(bf16)
        self.side[k].start()

    def give_over(self, k, part):
        self.side[k].wait_recv()
        self.hold[4, self.cuts[k]] = (part + self.hold[3, self.cuts[k]].astype(f32)).astype(bf16)
        self.over[k].start()

    def finish(self, part):
        self.near.wait_recv()
        part = part + self.hold[2].astype(f32)
        for copy in self.over:
            copy.wait_recv()
        return part + self.hold[5].astype(f32)

    def end(self):
        self.near.wait_send()
        for copy in self.side + self.over:
            copy.wait_send()


def normed_rows(values, gain_row):
    return values * lax.rsqrt(jnp.mean(values * values, -1, keepdims=True) + epsilon) * gain_row


def norm_back(values, gain_row, upstream):
    scale = lax.rsqrt(jnp.mean(values * values, -1, keepdims=True) + epsilon)
    unit = values * scale
    moved = upstream * gain_row
    grad = scale * (moved - unit * jnp.mean(moved * unit, -1, keepdims=True))
    gains = upstream * unit
    return grad, jnp.sum(gains.reshape(-1, 8, gains.shape[-1]), 0)


def remote_params(number, limit=58):
    return pltpu.CompilerParams(
        vmem_limit_bytes=limit * 1024 * 1024, collective_id=number, has_side_effects=True
    )


def shaped(*pairs):
    return tuple(jax.ShapeDtypeStruct(shape, dtype) for shape, dtype in pairs)


ANY = pl.BlockSpec(memory_space=pl.ANY)
VMEM = pl.BlockSpec(memory_space=pltpu.VMEM)


def attn_kernel(
    grid, heads, offsets, background, cycle, h_ref, gain_ref, cos_ref, sin_ref, tokk_ref, tokq_ref,
    from_ref, *refs,
):
    pieces = refs[: len(offsets)]
    (
        all_ref, q_ref, k_ref, v_ref, mid_ref, mixed_ref, lse_ref,
        held, w_sems, wo_ref, wo_sems, rows_ref, s_sems, out_sem, top, total, acc, part, hold, c_sems,
    ) = refs[len(offsets) :]
    rows = h_ref.shape[0]
    halves = heads // 2
    scale = HD ** (-0.5)
    ids = place_id(grid)
    background.begin()
    fetched = fetch_attn(grid, offsets, pieces, held, None, w_sems)
    fetched_out = fetch_attn(grid, offsets, pieces, None, wo_ref, wo_sems)
    sib, over, _ = greet(grid, 2, cycle)
    rows_ref[0] = normed_rows(h_ref[...].astype(f32), gain_ref[...]).astype(bf16)
    spread = Spread(rows_ref, s_sems, sib, over)
    spread.start()
    background.advance()
    end_fetch(fetched)

    def work(slot, start, size):
        cosine, sine_part = cos_ref[slot, start : start + size], sin_ref[slot, start : start + size]
        at = slice(start, start + size)
        made = jnp.dot(rows_ref[slot, at], held[...], preferred_element_type=f32)
        for h in range(3 * halves):
            one = made[:, h * HP : (h + 1) * HP]
            turned = (one * cosine + swapped(one) * sine_part).astype(bf16)
            if h < 2 * halves:
                q_ref[h, slot, at] = turned
            else:
                k_ref[h - 2 * halves, slot, at] = turned
        for h in range(halves):
            v_ref[h, slot, at] = made[:, (3 * halves + h) * HP : (3 * halves + h + 1) * HP].astype(bf16)

    work(0, 0, rows)
    spread.near.wait_recv()
    work(1, 0, rows)
    size = rows // PARTS
    for k in range(PARTS):
        spread.pass_on(k)
        work(2, k * size, size)
        spread.relay[k].wait_recv()
        work(3, k * size, size)
    out = pltpu.make_async_copy(rows_ref, all_ref, out_sem)
    out.start()
    end_fetch(fetched_out)
    collect = Collect(hold, c_sems, sib, over)

    def attend(i):
        tok_q, begin = tokq_ref[i], from_ref[i]

        def block(j, first):
            tok_k = tokk_ref[j]
            allowed = (tok_k <= tok_q) & (tok_k >= begin)
            for h in range(heads):
                scores = dot_nt(q_ref[h, i], k_ref[h // 2, j])
                scores = jnp.where(allowed, scores * scale, NEVER)
                peak = jnp.max(scores, 1, keepdims=True)
                if not first:
                    before = top[h]
                    peak = jnp.maximum(peak, before)
                raised = jnp.exp(scores - peak)
                summed = jnp.sum(raised, 1, keepdims=True)
                got = jnp.dot(raised.astype(bf16), v_ref[h // 2, j], preferred_element_type=f32)
                if first:
                    total[h] = summed
                    acc[h] = got
                else:
                    shrink = jnp.exp(before - peak)
                    total[h] = total[h] * shrink + summed
                    acc[h] = acc[h] * shrink + got
                top[h] = peak

        block(i, True)
        for j in range(4):
            if j != i:
                pl.when((ids[j] < ids[i]) & (ids[j] >= ids[i] - 2))(functools.partial(block, j, False))
        for h in range(heads):
            mixed_ref[i, :, h * HP : (h + 1) * HP] = (acc[h] / total[h]).astype(bf16)
            log_total = top[h] + jnp.log(total[h])
            lse_ref[i, h] = jnp.transpose(jnp.broadcast_to(log_total, (rows, HP)))[:8]
        part[...] = dot_nt(mixed_ref[i], wo_ref[...])

    cuts = pieces_of(rows)
    attend(3)
    for k in range(PARTS):
        collect.give_side(k, part[cuts[k]])
    background.advance()
    attend(2)
    for k in range(PARTS):
        collect.give_over(k, part[cuts[k]])
    attend(1)
    collect.give_near(part[...])
    attend(0)
    mid_ref[...] = collect.finish(part[...] + h_ref[...].astype(f32))
    background.advance()
    out.wait()
    spread.end()
    collect.end()
    background.finish()


def attn_call(grid, plan, hidden, gain_row, facts, found):
    rows, width = hidden.shape
    halves = grid.Z // 2
    heads = 2 * halves
    offsets, blocks = apart(found)
    shape = (halves, 4, rows, HP)
    return fused_call(
        grid, functools.partial(attn_kernel, grid, heads, offsets), "attn", plan,
        (
            hidden, gain_row, facts["cos"], facts["sin"], facts["tok"][:, None, :],
            facts["tok"][:, :, None], facts["from"][:, :, None], *blocks,
        ),
        [VMEM] * 7 + [ANY] * len(blocks),
        shaped(
            ((4, rows, width), bf16), ((heads,) + shape[1:], bf16), (shape, bf16), (shape, bf16),
            ((rows, width), f32), ((4, rows, heads * HP), bf16), ((4, heads, 8, rows), f32),
        ),
        (ANY,) + (VMEM,) * 6,
        [
            pltpu.VMEM((width, 4 * halves * HP), bf16), fetch_sems(found),
            pltpu.VMEM((width, heads * HP), bf16), fetch_sems(found),
            pltpu.VMEM((4, rows, width), bf16), Spread.sems, pltpu.SemaphoreType.DMA,
            pltpu.VMEM((heads, rows, 1), f32),
            pltpu.VMEM((heads, rows, 1), f32),
            pltpu.VMEM((heads, rows, HP), f32),
            pltpu.VMEM((rows, width), f32),
        ]
        + Collect.scratch(rows, width),
        60,
    )


def fetch_attn(grid, offsets, pieces, qkv, out, sems):
    pos = grid.my_pos()
    core = lax.axis_index("fsdp") % grid.C
    halves = grid.Z // 2
    tall = pieces[0].shape[0]
    fetched = []
    for i, offset in enumerate(offsets):
        yy, zz = grid.dyn_place(pos + offset)
        j = zz % halves
        rows = pl.ds(pl.multiple_of(yy * tall, tall), tall)

        def copy(n, first, width, ref, at):
            return pltpu.make_async_copy(
                pieces[i].at[:, pl.ds(first * HP, width * HP)],
                ref.at[rows, pl.ds(pl.multiple_of(at * HP, HP), width * HP)],
                sems.at[i, n],
            )

        if out is None:
            copies = [
                copy(0, 0, 2, qkv, 2 * j),
                copy(1, 2, 1, qkv, 2 * halves + j),
                copy(2, 3, 1, qkv, 3 * halves + j),
            ]
        else:
            copies = [copy(0, 4, 2, out, 2 * j)]
        live = zz // halves == core
        pl.when(live)(functools.partial(start_all, copies))
        fetched.append((live, copies))
    return fetched


def end_fetch(fetched):
    for live, copies in fetched:
        pl.when(live)(functools.partial(wait_all, copies))


def fetch_sems(found):
    return pltpu.SemaphoreType.DMA((len(found), 3))


def apart(found):
    return [offset for offset, _ in found], [block for _, block in found]


def place_id(grid):
    x, _, c, z = grid.me()
    return [2 * cc + (xx + z) % 2 for xx, cc in ((x, c), (x, 1 - c), (1 - x, c), (1 - x, 1 - c))]


def fetch_ffn(grid, offsets, pieces, held, sems):
    pos = grid.my_pos()
    _, tall, units = pieces[0].shape
    copies = []
    for i, offset in enumerate(offsets):
        yy, zz = grid.dyn_place(pos + offset)
        rows = pl.ds(pl.multiple_of(yy * tall, tall), tall)
        cols = pl.ds(pl.multiple_of(zz * units, units), units)
        copy = pltpu.make_async_copy(pieces[i], held.at[:, rows, cols], sems.at[i])
        copy.start()
        copies.append(copy)
    return copies


STEP = 512


def ffn_kernel(grid, offsets, background, cycle, mid_ref, gain_ref, *refs):
    count = len(offsets)
    pieces = refs[:count]
    (
        out_ref, all_ref, gate_ref, up_ref, hid_ref,
        held, w_sems, rows_ref, s_sems, part, own, hold, c_sems, out_sem,
    ) = refs[count:]
    rows, width = mid_ref.shape
    hidden = gate_ref.shape[2]
    background.begin()
    fetched = fetch_ffn(grid, offsets, pieces, held, w_sems)
    sib, over, _ = greet(grid, 2, cycle)
    rows_ref[0] = normed_rows(mid_ref[...], gain_ref[...]).astype(bf16)
    spread = Spread(rows_ref, s_sems, sib, over)
    collect = Collect(hold, c_sems, sib, over)
    spread.start()
    background.advance()
    for copy in fetched:
        copy.wait()

    def work(slot, start, size):
        at = pl.ds(start, size)

        def tile(n, carry):
            cols = pl.ds(pl.multiple_of(n * STEP, STEP), STEP)
            some = rows_ref[slot, at]
            gate = jnp.dot(some, held[0, :, cols], preferred_element_type=f32)
            up = jnp.dot(some, held[1, :, cols], preferred_element_type=f32)
            gate_ref[slot, at, cols] = gate.astype(bf16)
            up_ref[slot, at, cols] = up.astype(bf16)
            hid_ref[slot, at, cols] = (gate * jax.nn.sigmoid(gate) * up).astype(bf16)
            return carry

        lax.fori_loop(0, hidden // STEP, tile, 0)

        def tile_down(n, carry):
            cols = pl.ds(pl.multiple_of(n * STEP, STEP), STEP)
            part[at, cols] = dot_nt(hid_ref[slot, at], held[2, cols])
            return carry

        lax.fori_loop(0, width // STEP, tile_down, 0)

    work(0, 0, rows)
    own[...] = mid_ref[...] + part[...]
    spread.near.wait_recv()
    work(1, 0, rows)
    collect.give_near(part[...])
    cuts = pieces_of(rows)
    size = rows // PARTS
    for k in range(PARTS):
        spread.pass_on(k)
        if k:
            background.advance()
        spread.relay[k].wait_recv()
        work(3, k * size, size)
        collect.give_side(k, part[cuts[k]])
        work(2, k * size, size)
        collect.give_over(k, part[cuts[k]])
    background.advance()
    out = pltpu.make_async_copy(rows_ref, all_ref, out_sem)
    out.start()
    out_ref[...] = collect.finish(own[...]).astype(bf16)
    out.wait()
    spread.end()
    collect.end()
    background.finish()


def ffn_call(grid, plan, middle, gain_row, found):
    rows, width = middle.shape
    offsets, blocks = [o for o, _ in found], [b for _, b in found]
    hidden = grid.Z * blocks[0].shape[2]
    return fused_call(
        grid, functools.partial(ffn_kernel, grid, offsets), "ffn", plan,
        (middle, gain_row, *blocks), [VMEM] * 2 + [ANY] * len(blocks),
        shaped(((rows, width), bf16), ((4, rows, width), bf16), *[((4, rows, hidden), bf16)] * 3),
        (VMEM, ANY, VMEM, VMEM, VMEM),
        [
            pltpu.VMEM((3, width, hidden), bf16),
            pltpu.SemaphoreType.DMA((len(blocks),)),
            pltpu.VMEM((4, rows, width), bf16),
            Spread.sems,
            pltpu.VMEM((rows, width), f32),
            pltpu.VMEM((rows, width), f32),
        ]
        + Collect.scratch(rows, width)
        + [pltpu.SemaphoreType.DMA],
        44,
    )


TN = (((0,), (0,)), ((), ()))


def weight_terms(out, left, right, step=512):
    whole = right[...].reshape(-1, right.shape[-1])

    def tile(n, carry):
        cols = pl.ds(pl.multiple_of(n * step, step), step)
        some = left[:, :, cols].reshape(-1, step)
        out[cols, :] = lax.dot_general(some, whole, TN, preferred_element_type=f32).astype(bf16)
        return carry

    lax.fori_loop(0, left.shape[-1] // step, tile, 0)


def ffn_back_kernel(
    grid, offsets, background, cycle, g_ref, mid_ref, gain_ref, gate_ref, up_ref, hid_ref, whole_ref, *refs
):
    count = len(offsets)
    pieces = refs[:count]
    (
        out_ref, gains_ref, terms_ref,
        held, w_sems, rows_ref, s_sems, dgate_ref, dup_ref, part, own, hold, c_sems, out_sems,
    ) = refs[count:]
    rows, width = mid_ref.shape
    hidden = gate_ref.shape[2]
    background.begin()
    fetched = fetch_ffn(grid, offsets, pieces, held, w_sems)
    sib, over, _ = greet(grid, 2, cycle)
    rows_ref[0] = g_ref[...]
    spread = Spread(rows_ref, s_sems, sib, over)
    collect = Collect(hold, c_sems, sib, over)
    spread.start()
    background.advance()
    wait_all(fetched)

    def work(slot, start, size):
        at = pl.ds(start, size)

        def tile(n, carry):
            cols = pl.ds(pl.multiple_of(n * STEP, STEP), STEP)
            grad = jnp.dot(rows_ref[slot, at], held[2, :, cols], preferred_element_type=f32)
            gate = gate_ref[slot, at, cols].astype(f32)
            up = up_ref[slot, at, cols].astype(f32)
            sig = jax.nn.sigmoid(gate)
            dgate_ref[slot, at, cols] = (grad * up * sig * (1.0 + gate * (1.0 - sig))).astype(bf16)
            dup_ref[slot, at, cols] = (grad * gate * sig).astype(bf16)
            return carry

        lax.fori_loop(0, hidden // STEP, tile, 0)

        def tile_back(n, carry):
            cols = pl.ds(pl.multiple_of(n * STEP, STEP), STEP)
            part[at, cols] = dot_nt(dgate_ref[slot, at], held[0, cols]) + dot_nt(
                dup_ref[slot, at], held[1, cols]
            )
            return carry

        lax.fori_loop(0, width // STEP, tile_back, 0)

    work(0, 0, rows)
    own[...] = part[...]
    spread.near.wait_recv()
    work(1, 0, rows)
    collect.give_near(part[...])
    cuts = pieces_of(rows)
    size = rows // PARTS
    for k in range(PARTS):
        spread.pass_on(k)
        if k:
            background.advance()
        spread.relay[k].wait_recv()
        work(3, k * size, size)
        collect.give_side(k, part[cuts[k]])
        work(2, k * size, size)
        collect.give_over(k, part[cuts[k]])
    outs = []
    for m, (left, right) in enumerate(
        ((rows_ref, hid_ref), (whole_ref, dgate_ref), (whole_ref, dup_ref))
    ):
        n = (m + 2) % 3
        weight_terms(held.at[n], left, right)
        outs.append(pltpu.make_async_copy(held.at[n], terms_ref.at[n], out_sems.at[n]))
        outs[-1].start()
        if m == 0:
            background.advance()
    second = collect.finish(own[...])
    grad, gains = norm_back(mid_ref[...], gain_ref[...], second)
    out_ref[...] = g_ref[...].astype(f32) + grad
    gains_ref[...] = gains
    background.advance()
    wait_all(outs)
    spread.end()
    collect.end()
    background.finish()


def ffn_back_call(grid, plan, grad_out, middle, gain_row, gate, up, hidden_low, whole, found):
    rows, width = middle.shape
    offsets, blocks = apart(found)
    hidden = gate.shape[2]
    return fused_call(
        grid, functools.partial(ffn_back_kernel, grid, offsets), "ffn_back", plan,
        (grad_out, middle, gain_row, gate, up, hidden_low, whole, *blocks),
        [VMEM] * 7 + [ANY] * len(blocks),
        shaped(((rows, width), f32), ((8, width), f32), ((3, width, hidden), bf16)),
        (VMEM, VMEM, ANY),
        [
            pltpu.VMEM((3, width, hidden), bf16),
            pltpu.SemaphoreType.DMA((len(blocks),)),
            pltpu.VMEM((4, rows, width), bf16),
            Spread.sems,
            pltpu.VMEM((4, rows, hidden), bf16),
            pltpu.VMEM((4, rows, hidden), bf16),
            pltpu.VMEM((rows, width), f32),
            pltpu.VMEM((rows, width), f32),
        ]
        + Collect.scratch(rows, width)
        + [pltpu.SemaphoreType.DMA((3,))],
        60,
    )


def attn_back_kernel(
    grid, heads, offsets, background, cycle, g_ref, h_ref, gain_ref, cos_ref, sin_ref, q_ref, k_ref,
    v_ref, m_ref, l_ref, tokc_ref, tokr_ref, from_ref, whole_ref, *refs,
):
    pieces = refs[: len(offsets)]
    (
        out_ref, gains_ref, qkv_term, out_term,
        held, w_sems, wo_ref, wo_sems, rows_ref, s_sems, gm_ref, dqkv_ref,
        key_sum, value_sum, query_sum, delta, part, hold, c_sems,
    ) = refs[len(offsets) :]
    rows = g_ref.shape[0]
    pairs = heads // 2
    scale = HD ** (-0.5)
    ids = place_id(grid)
    background.begin()
    fetched_out = fetch_attn(grid, offsets, pieces, None, wo_ref, wo_sems)
    fetched = fetch_attn(grid, offsets, pieces, held, None, w_sems)
    sib, over, _ = greet(grid, 2, cycle)
    rows_ref[0] = g_ref[...].astype(bf16)
    spread = Spread(rows_ref, s_sems, sib, over)
    spread.start()
    background.advance()
    end_fetch(fetched_out)

    def work(slot, start, size):
        at = slice(start, start + size)
        made = jnp.dot(rows_ref[slot, at], wo_ref[...], preferred_element_type=f32).astype(bf16)
        for h in range(heads):
            gm_ref[h, slot, at] = made[:, h * HP : (h + 1) * HP]

    key_sum[...] = jnp.zeros_like(key_sum)
    value_sum[...] = jnp.zeros_like(value_sum)
    query_sum[...] = jnp.zeros_like(query_sum)

    def attend_back(i):
        for h in range(heads):
            product = gm_ref[h, i].astype(f32) * m_ref[i, :, h * HP : (h + 1) * HP].astype(f32)
            summed = jnp.sum(product, 1, keepdims=True)
            delta[h] = jnp.transpose(jnp.broadcast_to(summed, (rows, HP)))[:8]

        def block(j):
            allowed = (tokc_ref[j] <= tokr_ref[i]) & (tokc_ref[j] >= from_ref[i])
            for h in range(heads):
                query, upstream = q_ref[h, i], gm_ref[h, i]
                key, value = k_ref[h // 2, j], v_ref[h // 2, j]
                scores = jnp.where(allowed, dot_nt(key, query) * scale, NEVER)
                probs = jnp.exp(scores - l_ref[i, h, 0:1])
                value_sum[h // 2, j] += jnp.dot(
                    probs.astype(bf16), upstream, preferred_element_type=f32
                )
                grad_scores = (probs * (dot_nt(value, upstream) - delta[h, 0:1])).astype(bf16)
                key_sum[h // 2, j] += jnp.dot(grad_scores, query, preferred_element_type=f32)
                query_sum[h, i] += lax.dot_general(
                    grad_scores, key, TN, preferred_element_type=f32
                )

        for j in range(4):
            if i == j:
                block(j)
            else:
                pl.when((ids[j] < ids[i]) & (ids[j] >= ids[i] - 2))(functools.partial(block, j))

    work(0, 0, rows)
    spread.near.wait_recv()
    work(1, 0, rows)
    attend_back(0)
    attend_back(1)
    size = rows // PARTS
    for k in range(PARTS):
        spread.pass_on(k)
        work(2, k * size, size)
        spread.relay[k].wait_recv()
        work(3, k * size, size)
    background.advance()
    attend_back(2)
    attend_back(3)

    def back(summed, at):
        one = summed * scale
        return (one * cos_ref[at] - swapped(one) * sin_ref[at]).astype(bf16)

    collect = Collect(hold, c_sems, sib, over)
    cuts = pieces_of(rows)
    end_fetch(fetched)

    def work_back(i):
        for h in range(heads):
            dqkv_ref[i, :, h * HP : (h + 1) * HP] = back(query_sum[h, i], i)
        for h in range(pairs):
            at = heads + h
            dqkv_ref[i, :, at * HP : (at + 1) * HP] = back(key_sum[h, i], i)
            at = heads + pairs + h
            dqkv_ref[i, :, at * HP : (at + 1) * HP] = value_sum[h, i].astype(bf16)
        part[...] = dot_nt(dqkv_ref[i], held[...])

    work_back(3)
    for k in range(PARTS):
        collect.give_side(k, part[cuts[k]])
    work_back(2)
    for k in range(PARTS):
        collect.give_over(k, part[cuts[k]])
    background.advance()
    work_back(1)
    collect.give_near(part[...])
    work_back(0)
    weight_terms(out_term, rows_ref, m_ref)
    weight_terms(qkv_term, whole_ref, dqkv_ref)
    grad, gains = norm_back(h_ref[...].astype(f32), gain_ref[...], collect.finish(part[...]))
    out_ref[...] = (g_ref[...] + grad).astype(bf16)
    gains_ref[...] = gains
    background.advance()
    spread.end()
    collect.end()
    background.finish()


def attn_back_call(grid, plan, grad_middle, hidden, gain_row, facts, kept, found):
    whole, query, keys, values, mixed, lse = kept
    rows, width = hidden.shape
    heads = query.shape[0]
    pairs = heads // 2
    offsets, blocks = apart(found)
    return fused_call(
        grid, functools.partial(attn_back_kernel, grid, heads, offsets), "attn_back", plan,
        (
            grad_middle, hidden, gain_row, facts["cos"], facts["sin"], query, keys, values, mixed, lse,
            facts["tok"][:, :, None], facts["tok"][:, None, :], facts["from"][:, None, :], whole,
            *blocks,
        ),
        [VMEM] * 14 + [ANY] * len(blocks),
        shaped(
            ((rows, width), bf16), ((8, width), f32), ((width, 2 * heads * HP), bf16),
            ((width, heads * HP), bf16),
        ),
        (VMEM,) * 4,
        [
            pltpu.VMEM((width, 2 * heads * HP), bf16), fetch_sems(found),
            pltpu.VMEM((width, heads * HP), bf16), fetch_sems(found),
            pltpu.VMEM((4, rows, width), bf16), Spread.sems,
            pltpu.VMEM((heads, 4, rows, HP), bf16),
            pltpu.VMEM((4, rows, 2 * heads * HP), bf16),
            pltpu.VMEM((pairs, 4, rows, HP), f32),
            pltpu.VMEM((pairs, 4, rows, HP), f32),
            pltpu.VMEM((heads, 4, rows, HP), f32),
            pltpu.VMEM((heads, 8, rows), f32),
            pltpu.VMEM((rows, width), f32),
        ]
        + Collect.scratch(rows, width),
        80,
    )


def start_kernel(grid, joins, early, background, cycle, attn_ref, ffn_ref, sems, local):
    x, _, c, z = grid.me()
    mine = z // (grid.Z // 2) == c
    attn_to = [background.refs[h[0]][h[1]] for h in joins[0]]
    ffn_to = [background.refs[h[0]][h[1]] for h in joins[1]]
    depth = attn_ref.shape[1]
    rows = pl.ds(pl.multiple_of(c * depth, depth), depth)
    sib, over, diag = greet(grid, 3, cycle)
    everything = []
    for layer in range(2):
        to = attn_to[layer].at[rows]
        moves = [
            (mine, pltpu.make_async_copy(attn_ref.at[layer], to, local.at[0])),
            (~mine, remote(attn_ref.at[layer], to, sems, 0, sib)),
            (mine, remote(attn_ref.at[1 - layer], to, sems, 1, over)),
            (~mine, remote(attn_ref.at[1 - layer], to, sems, 2, diag)),
        ]
        into = ffn_to[layer].at[:, rows]
        quarter = lambda side, core: ffn_ref.at[2 * side + core]
        parts = [
            remote(quarter(1 - layer, c), into, sems, 4, over),
            remote(quarter(1 - layer, 1 - c), into, sems, 5, diag),
            remote(quarter(layer, 1 - c), into, sems, 3, sib),
            pltpu.make_async_copy(quarter(layer, c), into, local.at[1]),
        ]
        everything.append((moves, parts))

        @pl.when(x == layer)
        def _():
            for condition, copy in moves:
                pl.when(condition)(copy.start)

    (own, to_sib, to_over, to_diag), parts = [copy for _, copy in moves], parts

    @pl.when(mine)
    def _():
        own.wait()
        to_over.wait_send()
        for copy in (to_sib, to_over, to_diag):
            copy.wait_recv()

    @pl.when(~mine)
    def _():
        to_sib.wait_send()
        to_diag.wait_send()

    background.advance()
    for layer in range(2):
        pl.when(x == layer)(functools.partial(start_all, everything[layer][1]))
    for n in range(early):
        background.advance()
    wait_all(parts)
    background.finish()


def start_call(grid, plan, joins, early, attn_pack, ffn_pack):
    fused_call(
        grid, functools.partial(start_kernel, grid, joins, early), "start", plan,
        (attn_pack, ffn_pack), [ANY] * 2, (), (),
        [pltpu.SemaphoreType.DMA((2, 6)), pltpu.SemaphoreType.DMA((2,))], 70,
    )


def tail_kernel(
    grid, ready, background, cycle, ffn_own, ffn_came, attn_own, attn_came, sems, local
):
    x, _, c, z = grid.me()
    mine = z // (grid.Z // 2) == c
    depth = attn_own.shape[0]
    rows = pl.ds(pl.multiple_of(c * depth, depth), depth)
    other = pl.ds(pl.multiple_of((1 - c) * depth, depth), depth)
    background.begin()
    sib, over, diag = greet(grid, 3, cycle)
    background.advance()

    def home(n, layer, heads):
        term, parts, alive = background.totals[n]
        for part in parts:
            background.do(alive, functools.partial(background.put, part, False))
        if heads:
            keep = (term.at[rows], attn_own)
            moves = [
                remote(term.at[other], attn_own, sems, 3, sib),
                remote(term.at[rows], attn_came, sems, 4, over),
                remote(term.at[other], attn_came, sems, 5, diag),
            ]
        else:
            keep = (term.at[:, rows], ffn_own.at[c])
            moves = [
                remote(term.at[:, other], ffn_own.at[c], sems, 0, sib),
                remote(term.at[:, rows], ffn_came.at[c], sems, 1, over),
                remote(term.at[:, other], ffn_came.at[c], sems, 2, diag),
            ]
        stay = pltpu.make_async_copy(*keep, local.at[1 if heads else 0])
        here = x == layer
        there = x != layer
        if heads:
            here, there = here & mine, there & mine

        @pl.when(here)
        def _():
            stay.start()
            moves[0].start()

        @pl.when(there)
        def _():
            moves[1].start()
            moves[2].start()

        return stay, moves

    done = {}
    waiting = list(enumerate(ready))
    while waiting or background.now < len(background.stages):
        for n, (layer, heads, stage) in list(waiting):
            if stage < background.now:
                background.arrived(stage)
                done[heads] = home(n, layer, heads)
                waiting.remove((n, (layer, heads, stage)))
        if background.now < len(background.stages):
            background.advance()
    background.finish()
    stay, moves = done[False]
    stay.wait()
    for copy in moves:
        copy.wait()
    stay, moves = done[True]

    @pl.when(mine)
    def _():
        stay.wait()
        for copy in moves:
            copy.wait_send()
        moves[1].wait_recv()

    @pl.when(~mine)
    def _():
        moves[0].wait_recv()
        moves[2].wait_recv()


def tail_call(grid, plan, ready, depth, units):
    return fused_call(
        grid, functools.partial(tail_kernel, grid, ready), "tail", plan, (), (),
        shaped(*[((2, 3, depth, units), bf16)] * 2, *[((depth, 6 * HP), bf16)] * 2), (ANY,) * 4,
        [pltpu.SemaphoreType.DMA((2, 6)), pltpu.SemaphoreType.DMA((2,))], 60,
    )


def turning(doc_row):
    places = jnp.arange(doc_row.shape[-1], dtype=jnp.int32)
    begins = jnp.concatenate([jnp.ones((1,), dtype=bool), doc_row[1:] != doc_row[:-1]], -1)
    starts = lax.cummax(jnp.where(begins, places, 0), axis=0)
    positions = (places - starts).astype(f32)
    ladder = jnp.arange(HD // 2, dtype=f32)
    frequency = rope_base ** (-2.0 * ladder / HD)
    angles = positions[..., None] * frequency
    cosine, sine_part = jnp.cos(angles), jnp.sin(angles)
    blank = jnp.zeros((doc_row.shape[0], HP - HD), f32)
    return (
        starts,
        jnp.concatenate([cosine, cosine, blank], -1),
        jnp.concatenate([-sine_part, sine_part, blank], -1),
    )


def after(value, *others):
    return lax.optimization_barrier((value,) + others)[0]


def layer_forward(grid, hidden_in, attn, ffn, nexts, gain_pair, facts, before_ffn):
    plan = Plan()
    ffn.add(plan, 0)
    whole, query, keys, values, middle, mixed, lse = attn_call(
        grid, plan, hidden_in, gain_pair[0:1], facts, attn.found
    )
    plan = Plan()
    if nexts:
        nexts[0].add(plan, 0)
        nexts[1].add(plan, max(0, len(plan.stages) - 2), 1)
    result, whole2, gate, up, hidden = ffn_call(
        grid, plan, middle, after(gain_pair[1:2], *before_ffn), ffn.found
    )
    kept = (hidden_in, (whole, query, keys, values, mixed, lse), middle, whole2, gate, up, hidden)
    return result, kept


def layer_backward(grid, grad_out, kept, attn, ffn, gain_pair, facts, running, sum_ffn, sum_attn, leaving):
    hidden_in, kept_attn, middle, whole2, gate, up, hidden = kept
    plan = Plan()
    for ring in running:
        ring.add(plan, 0, min(4, ring.left()))
    grad_middle, gain_two, terms = ffn_back_call(
        grid, plan, grad_out, middle, gain_pair[1:2], gate, up, hidden, whole2, ffn.found
    )
    sums = sum_ffn(terms)
    running.append(sums)
    plan = Plan()
    sums.add(plan, 0, 3)
    grad_input, gain_one, qkv_term, out_term = attn_back_call(
        grid, plan, grad_middle, hidden_in, after(gain_pair[0:1], *leaving), facts, kept_attn, attn.found
    )
    running.append(sum_attn(qkv_term, out_term))
    gains = jnp.stack([jnp.sum(gain_one, 0), jnp.sum(gain_two, 0)])
    return grad_input, gains


def body(grid, inputs, doc_ids, cotangent, wq, wk, wv, wo, wg, wu, wd, gains):
    X, Y, C, Z = grid.X, grid.Y, grid.C, grid.Z
    x, y, c, z = grid.me()
    pos = grid.my_pos()
    micro, rows, width = inputs.shape
    depth = wq.shape[1]
    at_zero = x == 0

    def enter(block):
        def route(m):
            def go(x, y, c, z):
                if z % 2 != (x + m * C + c) % 2:
                    return None
                return (x, y, z // 2, m * C + c)

            return go

        first, last = grid.send(block[0], route(0)), grid.send(block[1], route(1))
        return jnp.where(z // C == 0, first, last)

    def leave(block, section):
        def route(m):
            def go(x, y, c, z):
                if z // C != m:
                    return None
                return (section, y, z % C, 2 * c + (x + z) % 2)

            return go

        return [grid.send(block, route(m)) for m in range(micro)]

    rows_in = enter(inputs)
    docs = grid.over_c(doc_ids)
    docs = jnp.where(c == z % C, doc_ids, docs)[:, 0]
    doc_row = lax.dynamic_index_in_dim(docs, z // C, 0, keepdims=False)
    length = doc_row.shape[0]
    starts, cosine, sine_part = turning(doc_row)
    ids = place_id(grid)

    def in_my_order(rows_of):
        return jnp.stack(
            [lax.dynamic_slice_in_dim(rows_of, ids[n] * rows, rows, 0) for n in range(4)]
        )

    facts = {
        "tok": in_my_order(jnp.arange(length, dtype=jnp.int32)),
        "from": in_my_order(starts),
        "cos": in_my_order(cosine),
        "sin": in_my_order(sine_part),
    }

    mine = (y * C + c) * Z + z
    table = lax.dynamic_update_slice(
        jnp.zeros((Y * C * Z,) + gains.shape[1:], bf16), gains, (mine, 0, 0)
    )
    for hop in grid.hops():
        table = table + grid.send(table, hop)
    gain_own = table.transpose(1, 0, 2).reshape(2, width)
    gain_other = grid.over_x(gain_own)
    gain_all = [
        jnp.where(at_zero, gain_own, gain_other).astype(f32),
        jnp.where(at_zero, gain_other, gain_own).astype(f32),
    ]

    def cut(block, index, count, axis):
        size = block.shape[axis] // count
        return lax.dynamic_slice_in_dim(block, index * size, size, axis)

    def heads_of(block):
        split = block.reshape(block.shape[0], -1, HD)
        return jnp.pad(split, ((0, 0), (0, 0), (0, HP - HD))).reshape(block.shape[0], -1)

    def pack_attn(side):
        parts = [cut(wq[0], side, 2, 1), cut(wk[0], side, 2, 1), cut(wv[0], side, 2, 1)]
        return heads_of(jnp.concatenate(parts + [cut(wo[0], side, 2, 0).T], 1))

    def pack_ffn(quarter):
        return jnp.stack(
            [cut(wg[0], quarter, 4, 1), cut(wu[0], quarter, 4, 1), cut(wd[0], quarter, 4, 0).T]
        )

    halves = Z // 2
    tall = C * depth
    units = wg.shape[2] // 4
    upper, lower = pl.ds(0, tall // 2), pl.ds(tall // 2, tall // 2)
    attn_cuts = [((upper,), (upper,), None), ((lower,), None, (lower,))]
    ffn_cuts = [((m,), (m, upper), (m, lower)) for m in range(3)]
    attn = [Gather(grid, (tall, 6 * HP), attn_cuts, True) for _ in range(2)]
    ffn = [Gather(grid, (3, tall, units), ffn_cuts) for _ in range(2)]
    plan = Plan()
    joins = [[ring.begin(plan) for ring in rings] for rings in (attn, ffn)]
    attn[0].add(plan, 0)
    ffn[0].add(plan, max(0, len(plan.stages) - 2), 1)
    start_call(
        grid, plan, joins, max(0, len(plan.stages) - 3), jnp.stack([pack_attn(0), pack_attn(1)]),
        jnp.stack([pack_ffn(quarter) for quarter in range(4)]),
    )

    hidden = rows_in
    kept = []
    for s in range(2):
        nexts = (attn[1], ffn[1]) if s == 0 else None
        if s == 1:
            rows_cot = enter(after(cotangent, hidden))
        hidden, keep = layer_forward(
            grid, hidden, attn[s], ffn[s], nexts, gain_all[s], facts, (rows_cot,) if s == 1 else ()
        )
        kept.append(keep)
    outs = [leave(after(kept[1][0], hidden), 0), leave(hidden, 1)]

    def sum_ffn(terms):
        def block(m):
            return lambda yy, zz: (
                m,
                pl.ds(pl.multiple_of(yy * tall, tall), tall),
                pl.ds(pl.multiple_of(zz * units, units), units),
            )

        parts = [(cuts, [(terms, block(m), (m,))]) for m, cuts in enumerate(ffn_cuts)]
        return Scatter(grid, parts, (3, tall, units))

    def sum_attn(qkv_term, out_term):
        size = tall // 2

        def block(row, first, count):
            def at(yy, zz):
                here = (first + count * (zz % halves)) * HP
                return (
                    pl.ds(pl.multiple_of(yy * tall + row, size), size),
                    pl.ds(pl.multiple_of(here, HP), count * HP),
                )

            return at

        parts = []
        for cuts, rows_at, row in ((attn_cuts[0], upper, 0), (attn_cuts[1], lower, size)):
            parts.append(
                (
                    cuts,
                    [
                        (qkv_term, block(row, 0, 2), (rows_at, pl.ds(0, 2 * HP))),
                        (qkv_term, block(row, 2 * halves, 1), (rows_at, pl.ds(2 * HP, HP))),
                        (qkv_term, block(row, 3 * halves, 1), (rows_at, pl.ds(3 * HP, HP))),
                        (out_term, block(row, 0, 2), (rows_at, pl.ds(4 * HP, 2 * HP))),
                    ],
                )
            )
        return Scatter(grid, parts, (tall, 6 * HP), True)

    upstream = rows_cot
    gain_terms, running = [None] * 2, []
    leaving = outs[0] + outs[1]
    for s in (1, 0):
        upstream, gain_terms[s] = layer_backward(
            grid, upstream, kept[s], attn[s], ffn[s], gain_all[s], facts, running, sum_ffn, sum_attn, leaving
        )
        leaving = leave(upstream, s)
        if s == 1:
            upper_grads = leaving
    grads_in = [leaving, upper_grads]
    produced = jnp.where(at_zero, jnp.stack(outs[0]), jnp.stack(outs[1]))
    plan = Plan()
    ready = []
    for n, ring in enumerate(running):
        left = ring.left()
        ring.add(plan, 0, left, True)
        ready.append((1 - n // 2, n % 2 == 1, left - 1))
    for ring in running:
        ring.total(plan)
    ffn_own, ffn_came, attn_own, attn_came = tail_call(grid, plan, ready, depth, units)
    grads_in = jnp.where(at_zero, jnp.stack(grads_in[0]), jnp.stack(grads_in[1])).astype(f32)

    def in_order(own, came):
        return jnp.where(at_zero, own, came), jnp.where(at_zero, came, own)

    ffn_home = jnp.concatenate([half[core] for half in in_order(ffn_own, ffn_came) for core in range(C)], 2)
    ffn_home = ffn_home.astype(f32)
    sides = in_order(attn_own, attn_came)
    query_home, key_home, value_home, out_home = [
        jnp.concatenate(
            [side[:, h * HP : h * HP + HD] for side in sides for h in some], 1
        ).astype(f32)
        for some in ((0, 1), (2,), (3,), (4, 5))
    ]
    out_home = out_home.T

    gain_kept = jnp.where(at_zero, gain_terms[0], gain_terms[1])
    gain_sum = gain_kept + grid.over_x(jnp.where(at_zero, gain_terms[1], gain_terms[0]))
    for hop in grid.hops():
        gain_sum = gain_sum + grid.send(gain_sum, hop)
    share = width // (Y * C * Z)
    gain_share = lax.dynamic_slice_in_dim(gain_sum, mine * share, share, 1)[None]
    return (
        produced[None],
        grads_in[None],
        query_home[None],
        key_home[None],
        value_home[None],
        out_home[None],
        ffn_home[0][None],
        ffn_home[1][None],
        ffn_home[2].T[None],
        gain_share,
    )


def solution(mesh):
    grid = Grid(mesh)

    def run(*arguments):
        grid.calls = 0
        return body(grid, *arguments)

    return jax.shard_map(
        run,
        mesh=mesh,
        in_specs=(
            P(None, ("fsdp", "tensor"), None),
            P(None, "fsdp", None),
            P(None, ("fsdp", "tensor"), None),
            P("section", "fsdp", "tensor"),
            P("section", "fsdp", "tensor"),
            P("section", "fsdp", "tensor"),
            P("section", "tensor", "fsdp"),
            P("section", "fsdp", "tensor"),
            P("section", "fsdp", "tensor"),
            P("section", "tensor", "fsdp"),
            P("section", None, ("fsdp", "tensor")),
        ),
        out_specs=(
            P("section", None, ("fsdp", "tensor"), None),
            P("section", None, ("fsdp", "tensor"), None),
            P("section", "fsdp", "tensor"),
            P("section", "fsdp", "tensor"),
            P("section", "fsdp", "tensor"),
            P("section", "tensor", "fsdp"),
            P("section", "fsdp", "tensor"),
            P("section", "fsdp", "tensor"),
            P("section", "tensor", "fsdp"),
            P("section", None, ("fsdp", "tensor")),
        ),
        check_vma=False,
    )
```

```python
import functools

import jax
import jax.numpy as jnp
import jax.experimental.pallas as pl
import jax.experimental.pallas.tpu as pltpu
from jax import lax
from jax.sharding import PartitionSpec as P

HD = 96
HP = 128
NEVER = -1e30
BLOCK = 4 * HD + 2 * HP
epsilon = 1e-05
rope_base = 100000.0
AXES = ("section", "fsdp", "tensor")
bf16 = jnp.bfloat16
f32 = jnp.float32


class Grid:
    def __init__(self, mesh):
        self.calls = 0
        self.X = mesh.shape["section"]
        self.C = 2
        self.Y = mesh.shape["fsdp"] // self.C
        self.Z = mesh.shape["tensor"]
        self.R = self.Y * self.Z
        self.places = [
            (x, y, c, z)
            for x in range(self.X)
            for y in range(self.Y)
            for c in range(self.C)
            for z in range(self.Z)
        ]

    def rank(self, place):
        x, y, c, z = place
        return ((x * self.Y + y) * self.C + c) * self.Z + z

    def send(self, block, route):
        pairs = []
        for place in self.places:
            goal = route(*place)
            if goal is not None:
                pairs.append((self.rank(place), self.rank(goal)))
        return lax.ppermute(block, AXES, pairs)

    def over_x(self, block):
        return self.send(block, lambda x, y, c, z: (1 - x, y, c, z))

    def over_c(self, block):
        return self.send(block, lambda x, y, c, z: (x, y, 1 - c, z))

    def place_of(self, p):
        p = p % self.R
        y, k = p // self.Z, p % self.Z
        return (y, k if y % 2 == 0 else self.Z - 1 - k)

    def pos_of(self, y, z):
        return y * self.Z + (z if y % 2 == 0 else self.Z - 1 - z)

    def neighbour(self, way):
        yy, zz = self.dyn_place(self.my_pos() + way)
        return {"fsdp": yy * self.C + lax.axis_index("fsdp") % self.C, "tensor": zz}

    def me(self):
        x = lax.axis_index("section")
        f = lax.axis_index("fsdp")
        z = lax.axis_index("tensor")
        return x, f // self.C, f % self.C, z

    def my_pos(self):
        x, y, c, z = self.me()
        return y * self.Z + jnp.where(y % 2 == 0, z, self.Z - 1 - z)

    def dyn_place(self, p):
        p = (p + 2 * self.R) % self.R
        y, k = p // self.Z, p % self.Z
        return y, jnp.where(y % 2 == 0, k, self.Z - 1 - k)

def params(limit=56):
    return pltpu.CompilerParams(vmem_limit_bytes=limit * 1024 * 1024)


def whole_vmem(count):
    return [pl.BlockSpec(memory_space=pltpu.VMEM)] * count


def cost(micros):
    return pl.CostEstimate(flops=int(micros * 1.0e9), bytes_accessed=1 << 20, transcendentals=0)


def swapped(values):
    lane = lax.broadcasted_iota(jnp.int32, values.shape, 1)
    half = HD // 2
    return jnp.where(lane < half, pltpu.roll(values, HP - half, 1), pltpu.roll(values, half, 1))


MESH = pl.DeviceIdType.MESH
NT = (((1,), (1,)), ((), ()))
PARTS = 2


def dot_nt(a, b):
    return lax.dot_general(a, b, NT, preferred_element_type=f32)


def partners(grid):
    x, y, c, _ = grid.me()
    return (
        {"fsdp": y * grid.C + 1 - c},
        {"section": 1 - x},
        {"section": 1 - x, "fsdp": y * grid.C + 1 - c},
    )


def doubling(grid):
    _, y, c, z = grid.me()
    found = []
    for bit in range((grid.Y - 1).bit_length()):
        step = 1 << bit
        found.append({"fsdp": (y + step * (1 - 2 * ((y // step) % 2))) * grid.C + c})
    for bit in range((grid.Z - 1).bit_length()):
        step = 1 << bit
        found.append({"tensor": z + step * (1 - 2 * ((z // step) % 2))})
    return found


def greet(grid, sides, cycle, more=(), meanwhile=lambda: None):
    others = list(partners(grid)[:sides]) + list(more)
    if cycle:
        others += [grid.neighbour(1), grid.neighbour(-1)]
    barrier = pltpu.get_barrier_semaphore()
    for other in others:
        pl.semaphore_signal(barrier, inc=1, device_id=other, device_id_type=MESH)
    meanwhile()
    pl.semaphore_wait(barrier, len(others))
    return partners(grid)


def sum_over(table, land, sems, others):
    for n, other in enumerate(others):
        copy = remote(table.at[n], land.at[n], sems, n, other)
        copy.start()
        copy.wait()
        table[n + 1] = table[n] + land[n]
        yield n


def remote(src, dst, sems, n, device):
    return pltpu.make_async_remote_copy(
        src_ref=src, dst_ref=dst, send_sem=sems.at[0, n], recv_sem=sems.at[1, n],
        device_id=device, device_id_type=MESH,
    )


def pieces_of(rows):
    size = rows // PARTS
    return [pl.ds(k * size, size) for k in range(PARTS)]


def start_all(copies):
    for copy in copies:
        copy.start()


def wait_all(copies):
    for copy in copies:
        copy.wait()


class Plan:
    def __init__(self):
        self.inputs, self.outs, self.lands, self.stages, self.hooks = [], [], [], [], []
        self.slots, self.makes, self.totals, self.moves, self.copies = [], [], [], 0, 1

    def give(self, array):
        for n, known in enumerate(self.inputs):
            if known is array:
                return ("in", n)
        self.inputs.append(array)
        return ("in", len(self.inputs) - 1)

    def room(self, shape):
        self.outs.append(jax.ShapeDtypeStruct(shape, bf16))
        return ("out", len(self.outs) - 1)

    def land(self, shape):
        self.lands.append(shape)
        return ("land", len(self.lands) - 1)

    def slot(self, key, shape):
        if (key, shape) not in self.slots:
            self.slots.append((key, shape))
        return self.slots.index((key, shape))

    def make(self, stage, key, shape, parts, offset, owned):
        slot = self.slot(key, shape)
        made = []
        for places, came in parts:
            copies = [(self.give(array), src, dst) for array, src, dst in places]
            joins = [(h if isinstance(h, tuple) else self.give(h), at) for h, at in came]
            made.append((copies, joins))
        self.copies = max(self.copies, sum(len(c) + len(j) for c, j in made))
        self.makes.append((stage, slot, made, offset, owned))
        return ("make", len(self.makes) - 1)

    def move(self, stage, src, dst, way, offset, owned, cut, part=0, needs=None):
        while len(self.stages) <= stage:
            self.stages.append([])
        self.stages[stage].append((self.moves, src, dst, way, offset, owned, cut, part, needs))
        self.moves += 1
        return self.moves - 1

    def scratch(self):
        if not self.moves:
            return []
        held = [pltpu.VMEM(shape, bf16) for _, shape in self.slots for _ in range(2)]
        held += [pltpu.VMEM(shape, bf16) for shape in self.lands]
        sems = [pltpu.SemaphoreType.DMA((2, self.moves))]
        if self.slots:
            sems.append(pltpu.SemaphoreType.DMA((len(self.slots), self.copies)))
        return held + sems

    def settle(self, results):
        for hook in self.hooks:
            hook(lambda handle: self.inputs[handle[1]] if handle[0] == "in" else results[handle[1]])


class Background:
    def __init__(self, grid, plan, ins, outs, rest):
        self.stages, self.totals, self.now, self.sent = [], [], -1, 0
        if not plan.moves:
            return
        pos = grid.my_pos()
        core = lax.axis_index("fsdp") % grid.C
        count = 2 * len(plan.slots)
        held, lands = rest[:count], rest[count : count + len(plan.lands)]
        sems = rest[count + len(plan.lands)]
        local = rest[-1]
        self.refs = {"in": ins, "out": outs, "land": lands}

        def live(owned, offset):
            if not owned:
                return None
            return grid.dyn_place(pos + offset)[1] // (grid.Z // 2) == core

        def built(slot, made, offset, owned):
            term, more = held[2 * slot], held[2 * slot + 1]
            yy, zz = grid.dyn_place(pos + offset)
            n, parts = 0, []
            for copies, joins in made:
                fetches, adds = [], []
                for handle, src, dst in copies:
                    ref = self.refs[handle[0]][handle[1]].at[src(yy, zz)]
                    fetches.append(pltpu.make_async_copy(ref, term.at[dst], local.at[slot, n]))
                    n += 1
                for handle, at in joins:
                    ref = self.refs[handle[0]][handle[1]]
                    if handle[0] == "land":
                        adds.append((None, ref, at))
                    else:
                        copy = pltpu.make_async_copy(ref.at[at], more.at[at], local.at[slot, n])
                        adds.append((copy, more, at))
                    n += 1
                parts.append((fetches, adds, term, handle_early(joins)))
            return parts, live(owned, offset)

        def handle_early(joins):
            return all(handle[0] == "in" for handle, _ in joins)

        self.makes = [[] for _ in plan.stages]
        buffers = []
        for stage, slot, made, offset, owned in plan.makes:
            parts, alive = built(slot, made, offset, owned)
            self.makes[stage].append((parts, alive))
            buffers.append((held[2 * slot], parts, alive))
        for slot, made, owned in plan.totals:
            self.totals.append((held[2 * slot],) + built(slot, made, 0, owned))
        self.all = {}
        for stage in plan.stages:
            row = []
            for number, src, dst, way, offset, owned, cut, part, needs in stage:
                put = None
                if src[0] == "make":
                    src_ref, parts, alive = buffers[src[1]]
                    put = (parts[part], alive)
                else:
                    src_ref = self.refs[src[0]][src[1]]
                dst_ref = self.refs[dst[0]][dst[1]]
                copy = remote(src_ref.at[cut], dst_ref.at[cut], sems, number, grid.neighbour(way))
                self.all[number] = (copy, live(owned, offset), live(owned, offset - way))
                row.append((number, put, needs))
            self.stages.append(row)
        self.come, self.put_done = set(), set()

    @staticmethod
    def do(condition, action):
        if condition is None:
            action()
        else:
            pl.when(condition)(action)

    def fetch(self, stage):
        if stage < len(self.stages):
            for parts, alive in self.makes[stage]:
                for fetches, adds, _, early in parts:
                    copies = fetches + [copy for copy, _, _ in adds if copy is not None and early]
                    self.do(alive, functools.partial(start_all, copies))

    def begin(self):
        self.fetch(0)
        for _, parts, alive in self.totals:
            for fetches, _, _, _ in parts:
                self.do(alive, functools.partial(start_all, fetches))

    @staticmethod
    def put(part, started=True):
        fetches, adds, term, early = part
        wait_all(fetches)
        for copy, ref, at in adds:
            if copy is not None:
                if not (early and started):
                    copy.start()
                copy.wait()
            term[at] = (term[at].astype(f32) + ref[at].astype(f32)).astype(bf16)

    def arrive(self, number):
        if number is not None and number not in self.come:
            self.come.add(number)
            copy, _, come = self.all[number]
            self.do(come, copy.wait_recv)

    def advance(self):
        self.now += 1
        if self.now < len(self.stages):
            for number, put, needs in self.stages[self.now]:
                for need in needs or ():
                    self.arrive(need)
                if put is not None and id(put[0]) not in self.put_done:
                    self.put_done.add(id(put[0]))
                    self.do(put[1], functools.partial(self.put, put[0]))
                copy, go, _ = self.all[number]
                self.do(go, copy.start)
            if self.now + 1 < len(self.stages):
                self.wait_sends(self.now)
                self.fetch(self.now + 1)
        if self.now >= len(self.stages):
            for row in self.stages:
                for number, _, _ in row:
                    self.arrive(number)

    def arrived(self, stage):
        for row in self.stages[: stage + 1]:
            for number, _, _ in row:
                self.arrive(number)

    def wait_sends(self, stage):
        while self.sent < stage:
            for number, _, _ in self.stages[self.sent]:
                copy, go, _ = self.all[number]
                self.do(go, copy.wait_send)
            self.sent += 1

    def finish(self):
        while self.now < len(self.stages):
            self.advance()
        self.wait_sends(len(self.stages))


class Gather:
    def __init__(self, grid, shape, cuts, owned=False):
        self.grid, self.owned, self.shape, self.cuts = grid, owned, shape, cuts
        self.k, self.total = 0, grid.R // 2

    def begin(self, plan):
        room = plan.room(self.shape)
        self.up = self.down = room

        def hook(get):
            self.found = [(0, get(room))]
            if self.k == 0:
                self.up = self.down = get(room)

        plan.hooks.append(hook)
        return room

    def left(self):
        return self.total - self.k

    def add(self, plan, stage, hops=None):
        hops = self.left() if hops is None else min(hops, self.left())
        if hops == 0:
            return
        one = self.up is self.down
        up = self.up if isinstance(self.up, tuple) else plan.give(self.up)
        down = up if one else plan.give(self.down)
        new = []
        before = [(None, None)] * len(self.cuts)
        for n in range(hops):
            self.k += 1
            k = self.k
            last = k == self.total
            to_up = plan.room(self.shape)
            to_down = to_up if last else plan.room(self.shape)
            now = []
            for (cut, first, second), (need_up, need_down) in zip(self.cuts, before):
                pair = (first, second) if last else (cut, cut)
                moved = []
                for src, dst, way, part, need in (
                    (up, to_up, 1, pair[0], need_up), (down, to_down, -1, pair[1], need_down)
                ):
                    moved.append(
                        None
                        if part is None
                        else plan.move(
                            stage + n, src, dst, way, -way * (k - 1), self.owned, part,
                            needs=(need,),
                        )
                    )
                now.append(tuple(moved))
            before = now
            new.append((-k, to_up))
            if not last:
                new.append((k, to_down))
            up, down = to_up, to_down

        def hook(get):
            self.up, self.down = get(up), get(down)
            self.found += [(offset, get(handle)) for offset, handle in new]

        plan.hooks.append(hook)


class Scatter:
    def __init__(self, grid, parts, shape, owned=False):
        self.grid, self.parts, self.shape, self.owned = grid, parts, shape, owned
        self.k = grid.R // 2
        self.held = {1: None, -1: None}

    def left(self):
        return self.k

    def came(self, way, n):
        if self.held[way] is None:
            return []
        block, column = self.held[way]
        at = self.parts[n][0][column]
        return [] if at is None else [(block, at)]

    def add(self, plan, stage, steps=1, final=False):
        steps = min(steps, self.k)
        before = {way: [None] * len(self.parts) for way in (1, -1)}
        for n in range(steps):
            k = self.k
            self.k -= 1
            room = plan.land if n < steps - 1 or final else plan.room
            rooms = {way: room(self.shape) for way in (1, -1)}
            halves = k == self.grid.R // 2
            blocks = {}
            for way in (1, -1):
                if halves and way == -1:
                    blocks[way] = blocks[1]
                    continue
                parts = [(places, self.came(way, m)) for m, (_, places) in enumerate(self.parts)]
                blocks[way] = plan.make(
                    stage + n, (id(self), way, n % 2), self.shape, parts, way * k, self.owned
                )
            now = {1: [], -1: []}
            for m, (cuts, _) in enumerate(self.parts):
                for way in (1, -1):
                    column = (1 if way == 1 else 2) if halves else 0
                    moved = None
                    if cuts[column] is not None:
                        moved = plan.move(
                            stage + n, blocks[way], rooms[way], way, way * k, self.owned, cuts[column],
                            m, (before[way][m],),
                        )
                    now[way].append(moved)
            before = now
            self.held = {
                way: (rooms[way], (1 if way == 1 else 2) if halves else 0) for way in (1, -1)
            }

        def hook(get):
            self.held = {
                way: (get(block), column) if block[0] == "out" else (None, column)
                for way, (block, column) in self.held.items()
            }

        if steps:
            plan.hooks.append(hook)

    def total(self, plan):
        parts = [
            (places, self.came(1, m) + self.came(-1, m)) for m, (_, places) in enumerate(self.parts)
        ]
        slot = plan.slot(("total", id(self)), self.shape)
        made = []
        for places, came in parts:
            copies = [(plan.give(array), src, dst) for array, src, dst in places]
            joins = [(h if isinstance(h, tuple) else plan.give(h), at) for h, at in came]
            made.append((copies, joins))
        plan.copies = max(plan.copies, sum(len(c) + len(j) for c, j in made))
        plan.totals.append((slot, made, self.owned))


def fused_call(grid, kernel, name, plan, inputs, in_specs, outs, out_specs, scratch, micros):
    plan = Plan() if plan is None else plan
    a, b, c, d = len(inputs), len(plan.inputs), len(outs), len(plan.outs)
    moves = plan.moves

    def whole(*refs):
        fg_in, bg_in = refs[:a], refs[a : a + b]
        fg_out, bg_out = refs[a + b : a + b + c], refs[a + b + c : a + b + c + d]
        rest = refs[a + b + c + d :]
        own = len(scratch)
        background = Background(grid, plan, bg_in, bg_out, rest[own:])
        kernel(background, bool(moves), *fg_in, *fg_out, *rest[:own])

    number = grid.calls
    grid.calls += 1
    results = pl.pallas_call(
        whole,
        out_shape=tuple(outs) + tuple(plan.outs),
        in_specs=list(in_specs) + [ANY] * b,
        out_specs=tuple(out_specs) + (ANY,) * d,
        scratch_shapes=list(scratch) + plan.scratch(),
        compiler_params=remote_params(number),
        cost_estimate=cost(micros),
        name=name,
    )(*inputs, *plan.inputs)
    plan.settle(results[c:])
    return results[:c]


def load(sources, places, sems):
    copies = [
        pltpu.make_async_copy(src, dst, sems.at[n]) for n, (src, dst) in enumerate(zip(sources, places))
    ]
    start_all(copies)
    return copies


class Spread:
    sems = pltpu.SemaphoreType.DMA((2, 1 + 2 * PARTS))

    def __init__(self, rows_ref, sems, sib, over):
        cuts = pieces_of(rows_ref.shape[1])
        self.near = remote(rows_ref.at[0], rows_ref.at[1], sems, 0, sib)
        self.far = [
            remote(rows_ref.at[0, at], rows_ref.at[2, at], sems, 1 + k, over)
            for k, at in enumerate(cuts)
        ]
        self.relay = [
            remote(rows_ref.at[2, at], rows_ref.at[3, at], sems, 1 + PARTS + k, sib)
            for k, at in enumerate(cuts)
        ]

    def start(self):
        for copy in self.far:
            copy.start()
        self.near.start()

    def pass_on(self, k):
        self.far[k].wait_recv()
        self.relay[k].start()

    def end(self):
        self.near.wait_send()
        for copy in self.far + self.relay:
            copy.wait_send()


class Collect:
    sems = pltpu.SemaphoreType.DMA((2, 1 + 2 * PARTS))

    @staticmethod
    def scratch(rows, width):
        return [pltpu.VMEM((6, rows, width), bf16), Collect.sems]

    def __init__(self, hold, sems, sib, over):
        self.hold = hold
        self.cuts = pieces_of(hold.shape[1])
        self.near = remote(hold.at[0], hold.at[2], sems, 0, sib)
        self.side = [
            remote(hold.at[1, at], hold.at[3, at], sems, 1 + k, sib)
            for k, at in enumerate(self.cuts)
        ]
        self.over = [
            remote(hold.at[4, at], hold.at[5, at], sems, 1 + PARTS + k, over)
            for k, at in enumerate(self.cuts)
        ]

    def give_near(self, part):
        self.hold[0] = part.astype(bf16)
        self.near.start()

    def give_side(self, k, part):
        self.hold[1, self.cuts[k]] = part.astype(bf16)
        self.side[k].start()

    def give_over(self, k, part):
        self.side[k].wait_recv()
        self.hold[4, self.cuts[k]] = (part + self.hold[3, self.cuts[k]].astype(f32)).astype(bf16)
        self.over[k].start()

    def finish(self, part):
        self.near.wait_recv()
        part = part + self.hold[2].astype(f32)
        for copy in self.over:
            copy.wait_recv()
        return part + self.hold[5].astype(f32)

    def end(self):
        self.near.wait_send()
        for copy in self.side + self.over:
            copy.wait_send()


def normed_rows(values, gain_row):
    return values * lax.rsqrt(jnp.mean(values * values, -1, keepdims=True) + epsilon) * gain_row


def norm_back(values, gain_row, upstream):
    scale = lax.rsqrt(jnp.mean(values * values, -1, keepdims=True) + epsilon)
    unit = values * scale
    moved = upstream * gain_row
    grad = scale * (moved - unit * jnp.mean(moved * unit, -1, keepdims=True))
    gains = upstream * unit
    return grad, jnp.sum(gains.reshape(-1, 8, gains.shape[-1]), 0)


def remote_params(number, limit=58):
    return pltpu.CompilerParams(
        vmem_limit_bytes=limit * 1024 * 1024, collective_id=number, has_side_effects=True
    )


def shaped(*pairs):
    return tuple(jax.ShapeDtypeStruct(shape, dtype) for shape, dtype in pairs)


ANY = pl.BlockSpec(memory_space=pl.ANY)
VMEM = pl.BlockSpec(memory_space=pltpu.VMEM)


def attn_kernel(
    grid, heads, offsets, background, cycle, h_ref, gain_ref, cos_ref, sin_ref, tokk_ref, tokq_ref,
    from_ref, *refs,
):
    pieces = refs[: len(offsets)]
    (
        all_ref, q_ref, k_ref, v_ref, mid_ref, mixed_ref, lse_ref,
        stage, w_sems, held, wo_ref, rows_ref, s_sems, out_sem, top, total, acc, part, hold, c_sems,
    ) = refs[len(offsets) :]
    rows = h_ref.shape[0]
    halves = heads // 2
    scale = HD ** (-0.5)
    ids = place_id(grid)
    background.begin()
    fetched = fetch_attn(grid, offsets, pieces, stage, w_sems)
    sib, over, _ = greet(grid, 2, cycle)
    rows_ref[0] = normed_rows(h_ref[...].astype(f32), gain_ref[...]).astype(bf16)
    spread = Spread(rows_ref, s_sems, sib, over)
    spread.start()
    background.advance()
    end_fetch(grid, fetched, stage, held, wo_ref)

    def work(slot, start, size):
        cosine, sine_part = cos_ref[slot, start : start + size], sin_ref[slot, start : start + size]
        at = slice(start, start + size)
        made = jnp.dot(rows_ref[slot, at], held[...], preferred_element_type=f32)
        for h in range(3 * halves):
            one = made[:, h * HP : (h + 1) * HP]
            turned = (one * cosine + swapped(one) * sine_part).astype(bf16)
            if h < 2 * halves:
                q_ref[h, slot, at] = turned
            else:
                k_ref[h - 2 * halves, slot, at] = turned
        for h in range(halves):
            v_ref[h, slot, at] = made[:, (3 * halves + h) * HP : (3 * halves + h + 1) * HP].astype(bf16)

    work(0, 0, rows)
    spread.near.wait_recv()
    work(1, 0, rows)
    size = rows // PARTS
    for k in range(PARTS):
        spread.pass_on(k)
        work(2, k * size, size)
        spread.relay[k].wait_recv()
        work(3, k * size, size)
    out = pltpu.make_async_copy(rows_ref, all_ref, out_sem)
    out.start()
    collect = Collect(hold, c_sems, sib, over)

    def attend(i):
        tok_q, begin = tokq_ref[i], from_ref[i]

        def block(j, first):
            tok_k = tokk_ref[j]
            allowed = (tok_k <= tok_q) & (tok_k >= begin)
            for h in range(heads):
                scores = dot_nt(q_ref[h, i], k_ref[h // 2, j])
                scores = jnp.where(allowed, scores * scale, NEVER)
                peak = jnp.max(scores, 1, keepdims=True)
                if not first:
                    before = top[h]
                    peak = jnp.maximum(peak, before)
                raised = jnp.exp(scores - peak)
                summed = jnp.sum(raised, 1, keepdims=True)
                got = jnp.dot(raised.astype(bf16), v_ref[h // 2, j], preferred_element_type=f32)
                if first:
                    total[h] = summed
                    acc[h] = got
                else:
                    shrink = jnp.exp(before - peak)
                    total[h] = total[h] * shrink + summed
                    acc[h] = acc[h] * shrink + got
                top[h] = peak

        block(i, True)
        for j in range(4):
            if j != i:
                pl.when((ids[j] < ids[i]) & (ids[j] >= ids[i] - 2))(functools.partial(block, j, False))
        for h in range(heads):
            mixed_ref[i, :, h * HP : (h + 1) * HP] = (acc[h] / total[h]).astype(bf16)
            log_total = top[h] + jnp.log(total[h])
            lse_ref[i, h] = jnp.transpose(jnp.broadcast_to(log_total, (rows, HP)))[:8]
        part[...] = dot_nt(mixed_ref[i], wo_ref[...])

    cuts = pieces_of(rows)
    attend(3)
    for k in range(PARTS):
        collect.give_side(k, part[cuts[k]])
    background.advance()
    attend(2)
    for k in range(PARTS):
        collect.give_over(k, part[cuts[k]])
    attend(1)
    collect.give_near(part[...])
    attend(0)
    mid_ref[...] = collect.finish(part[...] + h_ref[...].astype(f32))
    background.advance()
    out.wait()
    spread.end()
    collect.end()
    background.finish()


def attn_call(grid, plan, hidden, gain_row, facts, found):
    rows, width = hidden.shape
    halves = grid.Z // 2
    heads = 2 * halves
    offsets, blocks = apart(found)
    shape = (halves, 4, rows, HP)
    return fused_call(
        grid, functools.partial(attn_kernel, grid, heads, offsets), "attn", plan,
        (
            hidden, gain_row, facts["cos"], facts["sin"], facts["tok"][:, None, :],
            facts["tok"][:, :, None], facts["from"][:, :, None], *blocks,
        ),
        [VMEM] * 7 + [ANY] * len(blocks),
        shaped(
            ((4, rows, width), bf16), ((heads,) + shape[1:], bf16), (shape, bf16), (shape, bf16),
            ((rows, width), f32), ((4, rows, heads * HP), bf16), ((4, heads, 8, rows), f32),
        ),
        (ANY,) + (VMEM,) * 6,
        [
            *attn_weights(grid, found, width),
            pltpu.VMEM((4, rows, width), bf16), Spread.sems, pltpu.SemaphoreType.DMA,
            pltpu.VMEM((heads, rows, 1), f32),
            pltpu.VMEM((heads, rows, 1), f32),
            pltpu.VMEM((heads, rows, HP), f32),
            pltpu.VMEM((rows, width), f32),
        ]
        + Collect.scratch(rows, width),
        60,
    )


def fetch_attn(grid, offsets, pieces, stage, sems):
    pos = grid.my_pos()
    core = lax.axis_index("fsdp") % grid.C
    halves = grid.Z // 2
    fetched = []
    for i, offset in enumerate(offsets):
        yy, zz = grid.dyn_place(pos + offset)
        copy = pltpu.make_async_copy(pieces[i], stage.at[yy * halves + zz % halves], sems.at[i])
        live = zz // halves == core
        pl.when(live)(copy.start)
        fetched.append((live, copy))
    return fetched


def end_fetch(grid, fetched, stage, qkv, out):
    for live, copy in fetched:
        pl.when(live)(copy.wait)
    halves = grid.Z // 2
    tall = stage.shape[1]
    blank = jnp.zeros((tall, HP - HD), bf16)
    for yy in range(grid.Y):
        rows = slice(yy * tall, (yy + 1) * tall)
        for j in range(halves):
            block = stage.at[yy * halves + j]
            places = [(qkv, 2 * j), (qkv, 2 * j + 1), (qkv, 2 * halves + j), (qkv, 3 * halves + j)]
            places += [(out, 2 * j), (out, 2 * j + 1)]
            for n, (ref, at) in enumerate(places):
                head = block[:, n * HD : (n + 1) * HD]
                ref[rows, at * HP : (at + 1) * HP] = jnp.concatenate([head, blank], 1)


def attn_weights(grid, found, width):
    tall, halves = found[0][1].shape[0], grid.Z // 2
    return [
        pltpu.VMEM((grid.Y * halves, tall, BLOCK), bf16),
        pltpu.SemaphoreType.DMA((len(found),)),
        pltpu.VMEM((width, 4 * halves * HP), bf16),
        pltpu.VMEM((width, 2 * halves * HP), bf16),
    ]


def apart(found):
    return [offset for offset, _ in found], [block for _, block in found]


def place_id(grid):
    x, _, c, z = grid.me()
    return [2 * cc + (xx + z) % 2 for xx, cc in ((x, c), (x, 1 - c), (1 - x, c), (1 - x, 1 - c))]


def fetch_ffn(grid, offsets, pieces, held, sems):
    pos = grid.my_pos()
    _, tall, units = pieces[0].shape
    copies = []
    for i, offset in enumerate(offsets):
        yy, zz = grid.dyn_place(pos + offset)
        rows = pl.ds(pl.multiple_of(yy * tall, tall), tall)
        cols = pl.ds(pl.multiple_of(zz * units, units), units)
        copy = pltpu.make_async_copy(pieces[i], held.at[:, rows, cols], sems.at[i])
        copy.start()
        copies.append(copy)
    return copies


STEP = 512


def ffn_kernel(grid, offsets, background, cycle, mid_ref, gain_ref, *refs):
    count = len(offsets)
    pieces = refs[:count]
    (
        out_ref, all_ref, *stored,
        held, w_sems, rows_ref, s_sems, part, own, hold, c_sems, out_sem,
        gate_ref, up_ref, hid_ref, g_sems,
    ) = refs[count:]
    rows, width = mid_ref.shape
    hidden = gate_ref.shape[2]
    writes = []

    def store(slot):
        for n, (src, dst) in enumerate(zip((gate_ref, up_ref, hid_ref), stored)):
            writes.append(pltpu.make_async_copy(src.at[slot], dst.at[slot], g_sems.at[n, slot]))
            writes[-1].start()

    background.begin()
    fetched = fetch_ffn(grid, offsets, pieces, held, w_sems)
    sib, over, _ = greet(grid, 2, cycle)
    rows_ref[0] = normed_rows(mid_ref[...], gain_ref[...]).astype(bf16)
    spread = Spread(rows_ref, s_sems, sib, over)
    collect = Collect(hold, c_sems, sib, over)
    spread.start()
    background.advance()
    for copy in fetched:
        copy.wait()

    def work(slot, start, size):
        at = pl.ds(start, size)

        def tile(n, carry):
            cols = pl.ds(pl.multiple_of(n * STEP, STEP), STEP)
            some = rows_ref[slot, at]
            gate = jnp.dot(some, held[0, :, cols], preferred_element_type=f32)
            up = jnp.dot(some, held[1, :, cols], preferred_element_type=f32)
            gate_ref[slot, at, cols] = gate.astype(bf16)
            up_ref[slot, at, cols] = up.astype(bf16)
            hid_ref[slot, at, cols] = (gate * jax.nn.sigmoid(gate) * up).astype(bf16)
            return carry

        lax.fori_loop(0, hidden // STEP, tile, 0)

        def tile_down(n, carry):
            cols = pl.ds(pl.multiple_of(n * STEP, STEP), STEP)
            part[at, cols] = dot_nt(hid_ref[slot, at], held[2, cols])
            return carry

        lax.fori_loop(0, width // STEP, tile_down, 0)

    work(0, 0, rows)
    store(0)
    own[...] = mid_ref[...] + part[...]
    spread.near.wait_recv()
    work(1, 0, rows)
    store(1)
    collect.give_near(part[...])
    cuts = pieces_of(rows)
    size = rows // PARTS
    for k in range(PARTS):
        spread.pass_on(k)
        if k:
            background.advance()
        spread.relay[k].wait_recv()
        work(3, k * size, size)
        collect.give_side(k, part[cuts[k]])
        work(2, k * size, size)
        collect.give_over(k, part[cuts[k]])
    store(2)
    store(3)
    background.advance()
    out = pltpu.make_async_copy(rows_ref, all_ref, out_sem)
    out.start()
    out_ref[...] = collect.finish(own[...]).astype(bf16)
    out.wait()
    wait_all(writes)
    spread.end()
    collect.end()
    background.finish()


def ffn_call(grid, plan, middle, gain_row, found):
    rows, width = middle.shape
    offsets, blocks = [o for o, _ in found], [b for _, b in found]
    hidden = grid.Z * blocks[0].shape[2]
    return fused_call(
        grid, functools.partial(ffn_kernel, grid, offsets), "ffn", plan,
        (middle, gain_row, *blocks), [VMEM] * 2 + [ANY] * len(blocks),
        shaped(((rows, width), bf16), ((4, rows, width), bf16), *[((4, rows, hidden), bf16)] * 3),
        (VMEM,) + (ANY,) * 4,
        [
            pltpu.VMEM((3, width, hidden), bf16),
            pltpu.SemaphoreType.DMA((len(blocks),)),
            pltpu.VMEM((4, rows, width), bf16),
            Spread.sems,
            pltpu.VMEM((rows, width), f32),
            pltpu.VMEM((rows, width), f32),
        ]
        + Collect.scratch(rows, width)
        + [pltpu.SemaphoreType.DMA]
        + [pltpu.VMEM((4, rows, hidden), bf16)] * 3
        + [pltpu.SemaphoreType.DMA((3, 4))],
        44,
    )


TN = (((0,), (0,)), ((), ()))


def weight_terms(out, left, right, step=512):
    whole = right[...].reshape(-1, right.shape[-1])

    def tile(n, carry):
        cols = pl.ds(pl.multiple_of(n * step, step), step)
        some = left[:, :, cols].reshape(-1, step)
        out[cols, :] = lax.dot_general(some, whole, TN, preferred_element_type=f32).astype(bf16)
        return carry

    lax.fori_loop(0, left.shape[-1] // step, tile, 0)


def ffn_back_kernel(
    grid, offsets, background, cycle, g_ref, mid_ref, gain_ref, *refs
):
    count = len(offsets)
    sources, pieces = refs[:4], refs[4 : 4 + count]
    (
        out_ref, gains_ref, terms_ref,
        held, w_sems, rows_ref, s_sems, dgate_ref, dup_ref, part, own, hold, c_sems, out_sems,
        gate_ref, up_ref, hid_ref, whole_ref, in_sems,
    ) = refs[4 + count :]
    rows, width = mid_ref.shape
    hidden = gate_ref.shape[2]
    loads = load(sources, (gate_ref, up_ref, hid_ref, whole_ref), in_sems)
    background.begin()
    fetched = fetch_ffn(grid, offsets, pieces, held, w_sems)
    sib, over, _ = greet(grid, 2, cycle)
    rows_ref[0] = g_ref[...]
    spread = Spread(rows_ref, s_sems, sib, over)
    collect = Collect(hold, c_sems, sib, over)
    spread.start()
    background.advance()
    wait_all(fetched + loads[:2])

    def work(slot, start, size):
        at = pl.ds(start, size)

        def tile(n, carry):
            cols = pl.ds(pl.multiple_of(n * STEP, STEP), STEP)
            grad = jnp.dot(rows_ref[slot, at], held[2, :, cols], preferred_element_type=f32)
            gate = gate_ref[slot, at, cols].astype(f32)
            up = up_ref[slot, at, cols].astype(f32)
            sig = jax.nn.sigmoid(gate)
            dgate_ref[slot, at, cols] = (grad * up * sig * (1.0 + gate * (1.0 - sig))).astype(bf16)
            dup_ref[slot, at, cols] = (grad * gate * sig).astype(bf16)
            return carry

        lax.fori_loop(0, hidden // STEP, tile, 0)

        def tile_back(n, carry):
            cols = pl.ds(pl.multiple_of(n * STEP, STEP), STEP)
            part[at, cols] = dot_nt(dgate_ref[slot, at], held[0, cols]) + dot_nt(
                dup_ref[slot, at], held[1, cols]
            )
            return carry

        lax.fori_loop(0, width // STEP, tile_back, 0)

    work(0, 0, rows)
    own[...] = part[...]
    spread.near.wait_recv()
    work(1, 0, rows)
    collect.give_near(part[...])
    cuts = pieces_of(rows)
    size = rows // PARTS
    for k in range(PARTS):
        spread.pass_on(k)
        if k:
            background.advance()
        spread.relay[k].wait_recv()
        work(3, k * size, size)
        collect.give_side(k, part[cuts[k]])
        work(2, k * size, size)
        collect.give_over(k, part[cuts[k]])
    wait_all(loads[2:])
    outs = []
    for m, (left, right) in enumerate(
        ((rows_ref, hid_ref), (whole_ref, dgate_ref), (whole_ref, dup_ref))
    ):
        n = (m + 2) % 3
        weight_terms(held.at[n], left, right)
        outs.append(pltpu.make_async_copy(held.at[n], terms_ref.at[n], out_sems.at[n]))
        outs[-1].start()
        if m == 0:
            background.advance()
    second = collect.finish(own[...])
    grad, gains = norm_back(mid_ref[...], gain_ref[...], second)
    out_ref[...] = g_ref[...].astype(f32) + grad
    gains_ref[...] = gains
    background.advance()
    wait_all(outs)
    spread.end()
    collect.end()
    background.finish()


def ffn_back_call(grid, plan, grad_out, middle, gain_row, gate, up, hidden_low, whole, found):
    rows, width = middle.shape
    offsets, blocks = apart(found)
    hidden = gate.shape[2]
    return fused_call(
        grid, functools.partial(ffn_back_kernel, grid, offsets), "ffn_back", plan,
        (grad_out, middle, gain_row, gate, up, hidden_low, whole, *blocks),
        [VMEM] * 3 + [ANY] * (4 + len(blocks)),
        shaped(((rows, width), f32), ((8, width), f32), ((3, width, hidden), bf16)),
        (VMEM, VMEM, ANY),
        [
            pltpu.VMEM((3, width, hidden), bf16),
            pltpu.SemaphoreType.DMA((len(blocks),)),
            pltpu.VMEM((4, rows, width), bf16),
            Spread.sems,
            pltpu.VMEM((4, rows, hidden), bf16),
            pltpu.VMEM((4, rows, hidden), bf16),
            pltpu.VMEM((rows, width), f32),
            pltpu.VMEM((rows, width), f32),
        ]
        + Collect.scratch(rows, width)
        + [pltpu.SemaphoreType.DMA((3,))]
        + [pltpu.VMEM((4, rows, hidden), bf16)] * 3
        + [pltpu.VMEM((4, rows, width), bf16), pltpu.SemaphoreType.DMA((4,))],
        60,
    )


def attn_back_kernel(
    grid, heads, offsets, background, cycle, g_ref, h_ref, gain_ref, l_ref, tokc_ref, tokr_ref,
    from_ref, *refs,
):
    sources, pieces = refs[:7], refs[7 : 7 + len(offsets)]
    (
        out_ref, gains_ref, qkv_term, out_term,
        stage, w_sems, held, wo_ref, rows_ref, s_sems, gm_ref, dqkv_ref, low_ref, low_m,
        key_sum, value_sum, query_sum, delta, part, hold, c_sems,
        q_ref, k_ref, v_ref, m_ref, cos_ref, sin_ref, whole_ref, in_sems,
    ) = refs[7 + len(offsets) :]
    rows = g_ref.shape[0]
    pairs = heads // 2
    scale = HD ** (-0.5)
    ids = place_id(grid)
    background.begin()
    fetched = fetch_attn(grid, offsets, pieces, stage, w_sems)
    loads = load(sources, (q_ref, k_ref, v_ref, m_ref, cos_ref, sin_ref, whole_ref), in_sems)
    sib, over, _ = greet(grid, 2, cycle)
    rows_ref[0] = g_ref[...].astype(bf16)
    spread = Spread(rows_ref, s_sems, sib, over)
    spread.start()
    background.advance()
    end_fetch(grid, fetched, stage, held, wo_ref)

    def work(slot, start, size):
        at = slice(start, start + size)
        made = jnp.dot(rows_ref[slot, at], wo_ref[...], preferred_element_type=f32).astype(bf16)
        for h in range(heads):
            gm_ref[h, slot, at] = made[:, h * HP : (h + 1) * HP]

    key_sum[...] = jnp.zeros_like(key_sum)
    value_sum[...] = jnp.zeros_like(value_sum)
    query_sum[...] = jnp.zeros_like(query_sum)

    def attend_back(i):
        for h in range(heads):
            product = gm_ref[h, i].astype(f32) * m_ref[i, :, h * HP : (h + 1) * HP].astype(f32)
            summed = jnp.sum(product, 1, keepdims=True)
            delta[h] = jnp.transpose(jnp.broadcast_to(summed, (rows, HP)))[:8]

        def block(j):
            allowed = (tokc_ref[j] <= tokr_ref[i]) & (tokc_ref[j] >= from_ref[i])
            for h in range(heads):
                query, upstream = q_ref[h, i], gm_ref[h, i]
                key, value = k_ref[h // 2, j], v_ref[h // 2, j]
                scores = jnp.where(allowed, dot_nt(key, query) * scale, NEVER)
                probs = jnp.exp(scores - l_ref[i, h, 0:1])
                value_sum[h // 2, j] += jnp.dot(
                    probs.astype(bf16), upstream, preferred_element_type=f32
                )
                grad_scores = (probs * (dot_nt(value, upstream) - delta[h, 0:1])).astype(bf16)
                key_sum[h // 2, j] += jnp.dot(grad_scores, query, preferred_element_type=f32)
                query_sum[h, i] += lax.dot_general(
                    grad_scores, key, TN, preferred_element_type=f32
                )

        for j in range(4):
            if i == j:
                block(j)
            else:
                pl.when((ids[j] < ids[i]) & (ids[j] >= ids[i] - 2))(functools.partial(block, j))

    work(0, 0, rows)
    spread.near.wait_recv()
    work(1, 0, rows)
    wait_all(loads[:4])
    attend_back(0)
    attend_back(1)
    size = rows // PARTS
    for k in range(PARTS):
        spread.pass_on(k)
        work(2, k * size, size)
        spread.relay[k].wait_recv()
        work(3, k * size, size)
    background.advance()
    attend_back(2)
    attend_back(3)

    def back(summed, at):
        one = summed * scale
        return (one * cos_ref[at] - swapped(one) * sin_ref[at]).astype(bf16)

    collect = Collect(hold, c_sems, sib, over)
    cuts = pieces_of(rows)
    wait_all(loads[4:])

    def work_back(i):
        for at in range(2 * heads):
            if at < heads:
                made, low = back(query_sum[at, i], i), at // 2 * 4 + at % 2
            elif at < heads + pairs:
                made, low = back(key_sum[at - heads, i], i), (at - heads) * 4 + 2
            else:
                h = at - heads - pairs
                made, low = value_sum[h, i].astype(bf16), h * 4 + 3
            dqkv_ref[i, :, at * HP : (at + 1) * HP] = made
            low_ref[i, :, low * HD : (low + 1) * HD] = made[:, :HD]
        part[...] = dot_nt(dqkv_ref[i], held[...])

    work_back(3)
    for k in range(PARTS):
        collect.give_side(k, part[cuts[k]])
    work_back(2)
    for k in range(PARTS):
        collect.give_over(k, part[cuts[k]])
    background.advance()
    work_back(1)
    collect.give_near(part[...])
    work_back(0)
    low_m[...] = jnp.zeros_like(low_m)
    for i in range(4):
        for h in range(heads):
            at = h // 2 * 2 * HP + h % 2 * HD
            low_m[i, :, at : at + HD] = m_ref[i, :, h * HP : h * HP + HD]
    weight_terms(out_term, rows_ref, low_m)
    weight_terms(qkv_term, whole_ref, low_ref)
    grad, gains = norm_back(h_ref[...].astype(f32), gain_ref[...], collect.finish(part[...]))
    out_ref[...] = (g_ref[...] + grad).astype(bf16)
    gains_ref[...] = gains
    background.advance()
    spread.end()
    collect.end()
    background.finish()


def attn_back_call(grid, plan, grad_middle, hidden, gain_row, facts, kept, found):
    whole, query, keys, values, mixed, lse = kept
    rows, width = hidden.shape
    heads = query.shape[0]
    pairs = heads // 2
    offsets, blocks = apart(found)
    return fused_call(
        grid, functools.partial(attn_back_kernel, grid, heads, offsets), "attn_back", plan,
        (
            grad_middle, hidden, gain_row, lse, facts["tok"][:, :, None], facts["tok"][:, None, :],
            facts["from"][:, None, :], query, keys, values, mixed, facts["cos"], facts["sin"], whole,
            *blocks,
        ),
        [VMEM] * 7 + [ANY] * (7 + len(blocks)),
        shaped(
            ((rows, width), bf16), ((8, width), f32), ((width, 2 * heads * HD), bf16),
            ((width, heads * HP), bf16),
        ),
        (VMEM,) * 4,
        [
            *attn_weights(grid, found, width),
            pltpu.VMEM((4, rows, width), bf16), Spread.sems,
            pltpu.VMEM((heads, 4, rows, HP), bf16),
            pltpu.VMEM((4, rows, 2 * heads * HP), bf16),
            pltpu.VMEM((4, rows, 2 * heads * HD), bf16),
            pltpu.VMEM((4, rows, heads * HP), bf16),
            pltpu.VMEM((pairs, 4, rows, HP), f32),
            pltpu.VMEM((pairs, 4, rows, HP), f32),
            pltpu.VMEM((heads, 4, rows, HP), f32),
            pltpu.VMEM((heads, 8, rows), f32),
            pltpu.VMEM((rows, width), f32),
        ]
        + Collect.scratch(rows, width)
        + [
            pltpu.VMEM((heads, 4, rows, HP), bf16),
            pltpu.VMEM((pairs, 4, rows, HP), bf16),
            pltpu.VMEM((pairs, 4, rows, HP), bf16),
            pltpu.VMEM((4, rows, heads * HP), bf16),
            pltpu.VMEM((4, rows, HP), f32),
            pltpu.VMEM((4, rows, HP), f32),
            pltpu.VMEM((4, rows, width), bf16),
            pltpu.SemaphoreType.DMA((7,)),
        ],
        80,
    )


def start_kernel(
    grid, joins, early, background, cycle, wq, wk, wv, wo, wg, wu, wd, gains_ref, all_gains,
    attn_ref, ffn_ref, sems, local, table, land, t_sems,
):
    x, y, c, z = grid.me()
    mine = z // (grid.Z // 2) == c
    attn_to = [background.refs[h[0]][h[1]] for h in joins[0]]
    ffn_to = [background.refs[h[0]][h[1]] for h in joins[1]]
    depth = attn_ref.shape[1]
    units = ffn_ref.shape[3]
    rows = pl.ds(pl.multiple_of(c * depth, depth), depth)

    def pack():
        for side in range(2):
            heads = [wq[0, :, 2 * side * HD : 2 * (side + 1) * HD]]
            heads += [ref[0, :, side * HD : (side + 1) * HD] for ref in (wk, wv)]
            heads.append(
                jnp.transpose(wo[0, 2 * side * HD : 2 * (side + 1) * HD].astype(f32)).astype(bf16)
            )
            heads.append(jnp.zeros((depth, BLOCK - 6 * HD), bf16))
            attn_ref[side] = jnp.concatenate(heads, 1)

    others = doubling(grid)
    sib, over, diag = greet(grid, 3, cycle, others, pack)
    everything = []
    for layer in range(2):
        to = attn_to[layer].at[rows]
        moves = [
            (mine, pltpu.make_async_copy(attn_ref.at[layer], to, local.at[0])),
            (~mine, remote(attn_ref.at[layer], to, sems, 0, sib)),
            (mine, remote(attn_ref.at[1 - layer], to, sems, 1, over)),
            (~mine, remote(attn_ref.at[1 - layer], to, sems, 2, diag)),
        ]
        into = ffn_to[layer].at[:, rows]
        quarter = lambda side, core: ffn_ref.at[2 * side + core]
        parts = [
            remote(quarter(1 - layer, c), into, sems, 4, over),
            remote(quarter(1 - layer, 1 - c), into, sems, 5, diag),
            remote(quarter(layer, 1 - c), into, sems, 3, sib),
            pltpu.make_async_copy(quarter(layer, c), into, local.at[1]),
        ]
        everything.append((moves, parts))

        @pl.when(x == layer)
        def _():
            for condition, copy in moves:
                pl.when(condition)(copy.start)

    for q in range(4):
        cols = slice(q * units, (q + 1) * units)
        ffn_ref[q, 0] = wg[0, :, cols]
        ffn_ref[q, 1] = wu[0, :, cols]
        ffn_ref[q, 2] = jnp.transpose(wd[0, cols].astype(f32)).astype(bf16)

    (own, to_sib, to_over, to_diag), parts = [copy for _, copy in moves], parts

    @pl.when(mine)
    def _():
        for copy in (to_sib, to_over, to_diag):
            copy.wait_recv()
        own.wait()
        to_over.wait_send()

    @pl.when(~mine)
    def _():
        to_sib.wait_send()
        to_diag.wait_send()

    background.advance()
    for layer in range(2):
        pl.when(x == layer)(functools.partial(start_all, everything[layer][1]))
    shares = grid.Y * grid.C * grid.Z
    share = gains_ref.shape[2]
    table[0] = jnp.zeros_like(table[0])
    padded = jnp.concatenate([gains_ref[0].astype(f32), jnp.zeros((2, HP - share), f32)], 1)
    table[0, (y * grid.C + c) * grid.Z + z, :2, :] = padded
    for n in sum_over(table, land, t_sems, [sib] + others):
        if n % 2 == 1 and early:
            background.advance()
            early -= 1
    last = len(others) + 1
    copy = remote(table.at[last], land.at[last], t_sems, last, over)
    copy.start()
    copy.wait()
    for p in range(shares):
        own, other = table[last, p, :2, :share], land[last, p, :2, :share]
        at = slice(p * share, (p + 1) * share)
        all_gains[0, :, at] = jnp.where(x == 0, own, other)
        all_gains[1, :, at] = jnp.where(x == 0, other, own)
    for n in range(early):
        background.advance()
    wait_all(parts)
    background.finish()


def start_call(grid, plan, joins, early, shards, gains):
    depth, width = shards[0].shape[1], grid.Y * grid.C * shards[0].shape[1]
    units = shards[4].shape[2] // 4
    hops = len(doubling(grid)) + 1
    table = (hops + 1, grid.Y * grid.C * grid.Z, 8, HP)
    return fused_call(
        grid, functools.partial(start_kernel, grid, joins, early), "start", plan,
        (*shards, gains), [VMEM] * 8, shaped(((2, 2, width), f32)), (VMEM,),
        [
            pltpu.VMEM((2, depth, BLOCK), bf16),
            pltpu.VMEM((4, 3, depth, units), bf16),
            pltpu.SemaphoreType.DMA((2, 6)),
            pltpu.SemaphoreType.DMA((2,)),
            pltpu.VMEM(table, f32),
            pltpu.VMEM(table, f32),
            pltpu.SemaphoreType.DMA((2, hops + 1)),
        ],
        70,
    )[0]


def tail_kernel(
    grid, ready, background, cycle, one_0, two_0, one_1, two_1, ffn_own, ffn_came, attn_own, attn_came,
    gain_out, sems, local, table, land, t_sems,
):
    x, _, c, z = grid.me()
    mine = z // (grid.Z // 2) == c
    depth = attn_own.shape[0]
    rows = pl.ds(pl.multiple_of(c * depth, depth), depth)
    other = pl.ds(pl.multiple_of((1 - c) * depth, depth), depth)
    background.begin()
    others = doubling(grid)
    sib, over, diag = greet(grid, 3, cycle, others)
    background.advance()
    table[0] = jnp.concatenate(
        [jnp.sum(ref[...], 0, keepdims=True) for ref in (one_0, two_0, one_1, two_1)]
        + [jnp.zeros((4, table.shape[2]), f32)],
        0,
    )

    def home(n, layer, heads):
        term, parts, alive = background.totals[n]
        for part in parts:
            background.do(alive, functools.partial(background.put, part, False))
        if heads:
            keep = (term.at[rows], attn_own)
            moves = [
                remote(term.at[other], attn_own, sems, 3, sib),
                remote(term.at[rows], attn_came, sems, 4, over),
                remote(term.at[other], attn_came, sems, 5, diag),
            ]
        else:
            keep = (term.at[:, rows], ffn_own.at[c])
            moves = [
                remote(term.at[:, other], ffn_own.at[c], sems, 0, sib),
                remote(term.at[:, rows], ffn_came.at[c], sems, 1, over),
                remote(term.at[:, other], ffn_came.at[c], sems, 2, diag),
            ]
        stay = pltpu.make_async_copy(*keep, local.at[1 if heads else 0])
        here = x == layer
        there = x != layer
        if heads:
            here, there = here & mine, there & mine

        @pl.when(here)
        def _():
            stay.start()
            moves[0].start()

        @pl.when(there)
        def _():
            moves[1].start()
            moves[2].start()

        return stay, moves

    done = {}
    waiting = list(enumerate(ready))
    hops = sum_over(table, land, t_sems, [over, sib] + others)
    while waiting or background.now < len(background.stages):
        for n, (layer, heads, stage) in list(waiting):
            if stage < background.now:
                background.arrived(stage)
                done[heads] = home(n, layer, heads)
                waiting.remove((n, (layer, heads, stage)))
        next(hops, None)
        next(hops, None)
        if background.now < len(background.stages):
            background.advance()
    for _ in hops:
        pass
    gain_out[...] = table[len(others) + 2]
    background.finish()
    stay, moves = done[False]
    stay.wait()
    for copy in moves:
        copy.wait()
    stay, moves = done[True]

    @pl.when(mine)
    def _():
        stay.wait()
        for copy in moves:
            copy.wait_send()
        moves[1].wait_recv()

    @pl.when(~mine)
    def _():
        moves[0].wait_recv()
        moves[2].wait_recv()


def tail_call(grid, plan, ready, gain_rows, depth, units):
    width = gain_rows[0].shape[1]
    hops = len(doubling(grid)) + 2
    table = (hops + 1, 8, width)
    return fused_call(
        grid, functools.partial(tail_kernel, grid, ready), "tail", plan, gain_rows, [VMEM] * 4,
        shaped(
            *[((2, 3, depth, units), bf16)] * 2, *[((depth, BLOCK), bf16)] * 2, ((8, width), f32)
        ),
        (ANY,) * 4 + (VMEM,),
        [
            pltpu.SemaphoreType.DMA((2, 6)),
            pltpu.SemaphoreType.DMA((2,)),
            pltpu.VMEM(table, f32),
            pltpu.VMEM(table, f32),
            pltpu.SemaphoreType.DMA((2, hops)),
        ],
        60,
    )


def finish_kernel(
    ffn_own, ffn_came, attn_own, attn_came, query, key, value, out, gate, up, down
):
    x = lax.axis_index("section")
    units = ffn_own.shape[3]

    def put(side, ffn_ref, attn_ref):
        for core in range(2):
            at = slice((2 * side + core) * units, (2 * side + core + 1) * units)
            gate[:, at] = ffn_ref[core, 0].astype(f32)
            up[:, at] = ffn_ref[core, 1].astype(f32)
            down[at] = jnp.transpose(ffn_ref[core, 2].astype(f32))

        def head(n):
            return attn_ref[:, n * HD : (n + 1) * HD].astype(f32)

        for h in range(2):
            at = slice((2 * side + h) * HD, (2 * side + h + 1) * HD)
            query[:, at] = head(h)
            out[at] = jnp.transpose(head(4 + h))
        key[:, side * HD : (side + 1) * HD] = head(2)
        value[:, side * HD : (side + 1) * HD] = head(3)

    for layer in range(2):

        @pl.when(x == layer)
        def _():
            put(layer, ffn_own, attn_own)
            put(1 - layer, ffn_came, attn_came)


def finish_call(blocks, shards):
    return pl.pallas_call(
        finish_kernel,
        out_shape=tuple(jax.ShapeDtypeStruct(shard.shape[1:], f32) for shard in shards),
        in_specs=[VMEM] * 4,
        out_specs=(VMEM,) * 7,
        compiler_params=params(),
        cost_estimate=cost(6),
        name="finish",
    )(*blocks)


def turning(doc_row):
    places = jnp.arange(doc_row.shape[-1], dtype=jnp.int32)
    begins = jnp.concatenate([jnp.ones((1,), dtype=bool), doc_row[1:] != doc_row[:-1]], -1)
    starts = lax.cummax(jnp.where(begins, places, 0), axis=0)
    positions = (places - starts).astype(f32)
    ladder = jnp.arange(HD // 2, dtype=f32)
    frequency = rope_base ** (-2.0 * ladder / HD)
    angles = positions[..., None] * frequency
    cosine, sine_part = jnp.cos(angles), jnp.sin(angles)
    blank = jnp.zeros((doc_row.shape[0], HP - HD), f32)
    return (
        starts,
        jnp.concatenate([cosine, cosine, blank], -1),
        jnp.concatenate([-sine_part, sine_part, blank], -1),
    )


def after(value, *others):
    return lax.optimization_barrier((value,) + others)[0]


def layer_forward(grid, hidden_in, attn, ffn, nexts, gain_pair, facts):
    plan = Plan()
    ffn.add(plan, 0)
    whole, query, keys, values, middle, mixed, lse = attn_call(
        grid, plan, hidden_in, gain_pair[0:1], facts, attn.found
    )
    plan = Plan()
    if nexts:
        nexts[0].add(plan, 0)
        nexts[1].add(plan, max(0, len(plan.stages) - 2), 1)
    result, whole2, gate, up, hidden = ffn_call(grid, plan, middle, gain_pair[1:2], ffn.found)
    kept = (hidden_in, (whole, query, keys, values, mixed, lse), middle, whole2, gate, up, hidden)
    return result, kept


def layer_backward(grid, grad_out, kept, attn, ffn, gain_pair, facts, running, sum_ffn, sum_attn, leaving):
    hidden_in, kept_attn, middle, whole2, gate, up, hidden = kept
    plan = Plan()
    for ring in running:
        ring.add(plan, 0, min(4, ring.left()))
    grad_middle, gain_two, terms = ffn_back_call(
        grid, plan, grad_out, middle, gain_pair[1:2], gate, up, hidden, whole2, ffn.found
    )
    sums = sum_ffn(terms)
    running.append(sums)
    plan = Plan()
    sums.add(plan, 0, 3)
    grad_input, gain_one, qkv_term, out_term = attn_back_call(
        grid, plan, grad_middle, hidden_in, after(gain_pair[0:1], *leaving), facts, kept_attn, attn.found
    )
    running.append(sum_attn(qkv_term, out_term))
    return grad_input, (gain_one, gain_two)


def body(grid, inputs, doc_ids, cotangent, wq, wk, wv, wo, wg, wu, wd, gains):
    X, Y, C, Z = grid.X, grid.Y, grid.C, grid.Z
    x, y, c, z = grid.me()
    pos = grid.my_pos()
    micro, rows, width = inputs.shape
    depth = wq.shape[1]
    at_zero = x == 0

    def enter(block):
        def route(m):
            def go(x, y, c, z):
                if z % 2 != (x + m * C + c) % 2:
                    return None
                return (x, y, z // 2, m * C + c)

            return go

        first, last = grid.send(block[0], route(0)), grid.send(block[1], route(1))
        return jnp.where(z // C == 0, first, last)

    def leave(block, section):
        def route(m):
            def go(x, y, c, z):
                if z // C != m:
                    return None
                return (section, y, z % C, 2 * c + (x + z) % 2)

            return go

        return [grid.send(block, route(m)) for m in range(micro)]

    rows_in = enter(inputs)
    docs = grid.over_c(doc_ids)
    docs = jnp.where(c == z % C, doc_ids, docs)[:, 0]
    doc_row = lax.dynamic_index_in_dim(docs, z // C, 0, keepdims=False)
    length = doc_row.shape[0]
    starts, cosine, sine_part = turning(doc_row)
    ids = place_id(grid)

    def in_my_order(rows_of):
        return jnp.stack(
            [lax.dynamic_slice_in_dim(rows_of, ids[n] * rows, rows, 0) for n in range(4)]
        )

    facts = {
        "tok": in_my_order(jnp.arange(length, dtype=jnp.int32)),
        "from": in_my_order(starts),
        "cos": in_my_order(cosine),
        "sin": in_my_order(sine_part),
    }

    halves = Z // 2
    tall = C * depth
    units = wg.shape[2] // 4
    upper, lower = pl.ds(0, tall // 2), pl.ds(tall // 2, tall // 2)
    attn_cuts = [((upper,), (upper,), None), ((lower,), None, (lower,))]
    ffn_cuts = [((m,), (m, upper), (m, lower)) for m in range(3)]
    attn = [Gather(grid, (tall, BLOCK), attn_cuts, True) for _ in range(2)]
    ffn = [Gather(grid, (3, tall, units), ffn_cuts) for _ in range(2)]
    plan = Plan()
    joins = [[ring.begin(plan) for ring in rings] for rings in (attn, ffn)]
    attn[0].add(plan, 0)
    ffn[0].add(plan, max(0, len(plan.stages) - 2), 1)
    shards = (wq, wk, wv, wo, wg, wu, wd)
    gain_all = start_call(grid, plan, joins, max(0, len(plan.stages) - 3), shards, gains)

    hidden = rows_in
    kept = []
    for s in range(2):
        nexts = (attn[1], ffn[1]) if s == 0 else None
        hidden, keep = layer_forward(grid, hidden, attn[s], ffn[s], nexts, gain_all[s], facts)
        kept.append(keep)
    rows_cot = enter(after(cotangent, kept[1][2]))
    outs = [leave(after(kept[1][0], hidden, rows_cot), 0), leave(after(hidden, rows_cot), 1)]

    def sum_ffn(terms):
        def block(m):
            return lambda yy, zz: (
                m,
                pl.ds(pl.multiple_of(yy * tall, tall), tall),
                pl.ds(pl.multiple_of(zz * units, units), units),
            )

        parts = [(cuts, [(terms, block(m), (m,))]) for m, cuts in enumerate(ffn_cuts)]
        return Scatter(grid, parts, (3, tall, units))

    def sum_attn(qkv_term, out_term):
        size = tall // 2

        def block(row, count):
            return lambda yy, zz: (
                pl.ds(pl.multiple_of(yy * tall + row, size), size),
                pl.ds(pl.multiple_of(zz % halves * count, HP), count),
            )

        parts = []
        for cuts, rows_at, row in ((attn_cuts[0], upper, 0), (attn_cuts[1], lower, size)):
            parts.append(
                (
                    cuts,
                    [
                        (qkv_term, block(row, 4 * HD), (rows_at, pl.ds(0, 4 * HD))),
                        (out_term, block(row, 2 * HP), (rows_at, pl.ds(4 * HD, 2 * HP))),
                    ],
                )
            )
        return Scatter(grid, parts, (tall, BLOCK), True)

    upstream = rows_cot
    gain_terms, running = [None] * 2, []
    leaving = outs[0] + outs[1]
    for s in (1, 0):
        upstream, gain_terms[s] = layer_backward(
            grid, upstream, kept[s], attn[s], ffn[s], gain_all[s], facts, running, sum_ffn, sum_attn, leaving
        )
        leaving = leave(upstream, s)
        if s == 1:
            upper_grads = leaving
    grads_in = [leaving, upper_grads]
    produced = jnp.where(at_zero, jnp.stack(outs[0]), jnp.stack(outs[1]))
    plan = Plan()
    ready = []
    for n in (1, 3, 0, 2):
        left = running[n].left()
        running[n].add(plan, 0, left, True)
        ready.append((1 - n // 2, n % 2 == 1, left - 1))
        running[n].total(plan)
    *blocks, gain_sum = tail_call(grid, plan, ready, gain_terms[0] + gain_terms[1], depth, units)
    grads_in = jnp.where(at_zero, jnp.stack(grads_in[0]), jnp.stack(grads_in[1])).astype(f32)

    terms = finish_call(blocks, shards)
    share = gains.shape[2]
    mine = (y * C + c) * Z + z
    gain_share = lax.dynamic_slice(gain_sum, (2 * x, mine * share), (2, share))[None]
    return (
        produced[None],
        grads_in[None],
        *[term[None] for term in terms],
        gain_share,
    )


def solution(mesh):
    grid = Grid(mesh)

    def run(*arguments):
        grid.calls = 0
        return body(grid, *arguments)

    return jax.shard_map(
        run,
        mesh=mesh,
        in_specs=(
            P(None, ("fsdp", "tensor"), None),
            P(None, "fsdp", None),
            P(None, ("fsdp", "tensor"), None),
            P("section", "fsdp", "tensor"),
            P("section", "fsdp", "tensor"),
            P("section", "fsdp", "tensor"),
            P("section", "tensor", "fsdp"),
            P("section", "fsdp", "tensor"),
            P("section", "fsdp", "tensor"),
            P("section", "tensor", "fsdp"),
            P("section", None, ("fsdp", "tensor")),
        ),
        out_specs=(
            P("section", None, ("fsdp", "tensor"), None),
            P("section", None, ("fsdp", "tensor"), None),
            P("section", "fsdp", "tensor"),
            P("section", "fsdp", "tensor"),
            P("section", "fsdp", "tensor"),
            P("section", "tensor", "fsdp"),
            P("section", "fsdp", "tensor"),
            P("section", "fsdp", "tensor"),
            P("section", "tensor", "fsdp"),
            P("section", None, ("fsdp", "tensor")),
        ),
        check_vma=False,
    )
```

```python
import functools

import jax
import jax.numpy as jnp
import numpy as np
import jax.experimental.pallas as pl
import jax.experimental.pallas.tpu as pltpu
from jax import lax
from jax.sharding import PartitionSpec as P

HD = 96
DOCS = 4
HP = 128
NEVER = -1e30
BLOCK = 4 * HD
epsilon = 1e-05
rope_base = 100000.0
AXES = ("section", "fsdp", "tensor")
bf16 = jnp.bfloat16
f32 = jnp.float32


class Grid:
    def __init__(self, mesh):
        self.calls = 0
        self.X = mesh.shape["section"]
        self.C = 2
        self.Y = mesh.shape["fsdp"] // self.C
        self.Z = mesh.shape["tensor"]
        self.R = self.Y * self.Z
        self.places = [
            (x, y, c, z)
            for x in range(self.X)
            for y in range(self.Y)
            for c in range(self.C)
            for z in range(self.Z)
        ]

    def rank(self, place):
        x, y, c, z = place
        return ((x * self.Y + y) * self.C + c) * self.Z + z

    def send(self, block, route):
        pairs = []
        for place in self.places:
            goal = route(*place)
            if goal is not None:
                pairs.append((self.rank(place), self.rank(goal)))
        return lax.ppermute(block, AXES, pairs)

    def over_x(self, block):
        return self.send(block, lambda x, y, c, z: (1 - x, y, c, z))

    def over_c(self, block):
        return self.send(block, lambda x, y, c, z: (x, y, 1 - c, z))

    def place_of(self, p):
        p = p % self.R
        y, k = p // self.Z, p % self.Z
        return (y, k if y % 2 == 0 else self.Z - 1 - k)

    def pos_of(self, y, z):
        return y * self.Z + (z if y % 2 == 0 else self.Z - 1 - z)

    def neighbour(self, way):
        yy, zz = self.dyn_place(self.my_pos() + way)
        return {"fsdp": yy * self.C + lax.axis_index("fsdp") % self.C, "tensor": zz}

    def me(self):
        x = lax.axis_index("section")
        f = lax.axis_index("fsdp")
        z = lax.axis_index("tensor")
        return x, f // self.C, f % self.C, z

    def my_pos(self):
        x, y, c, z = self.me()
        return y * self.Z + jnp.where(y % 2 == 0, z, self.Z - 1 - z)

    def dyn_place(self, p):
        p = (p + 2 * self.R) % self.R
        y, k = p // self.Z, p % self.Z
        return y, jnp.where(y % 2 == 0, k, self.Z - 1 - k)

def params(limit=56):
    return pltpu.CompilerParams(vmem_limit_bytes=limit * 1024 * 1024)


def whole_vmem(count):
    return [pl.BlockSpec(memory_space=pltpu.VMEM)] * count


def cost(micros):
    return pl.CostEstimate(flops=int(micros * 1.0e9), bytes_accessed=1 << 20, transcendentals=0)


def swapped(values):
    lane = lax.broadcasted_iota(jnp.int32, values.shape, 1)
    half = HD // 2
    return jnp.where(lane < half, pltpu.roll(values, HP - half, 1), pltpu.roll(values, half, 1))


MESH = pl.DeviceIdType.MESH
NT = (((1,), (1,)), ((), ()))
PARTS = 2


def dot_nt(a, b):
    return lax.dot_general(a, b, NT, preferred_element_type=f32)


def partners(grid):
    x, y, c, _ = grid.me()
    return (
        {"fsdp": y * grid.C + 1 - c},
        {"section": 1 - x},
        {"section": 1 - x, "fsdp": y * grid.C + 1 - c},
    )


def doubling(grid):
    _, y, c, z = grid.me()
    found = []
    for bit in range((grid.Y - 1).bit_length()):
        step = 1 << bit
        found.append({"fsdp": (y + step * (1 - 2 * ((y // step) % 2))) * grid.C + c})
    for bit in range((grid.Z - 1).bit_length()):
        step = 1 << bit
        found.append({"tensor": z + step * (1 - 2 * ((z // step) % 2))})
    return found


def greet(grid, sides, cycle, more=(), meanwhile=lambda: None):
    others = list(partners(grid)[:sides]) + list(more)
    if cycle:
        others += [grid.neighbour(1), grid.neighbour(-1)]
    barrier = pltpu.get_barrier_semaphore()
    for other in others:
        pl.semaphore_signal(barrier, inc=1, device_id=other, device_id_type=MESH)
    meanwhile()
    pl.semaphore_wait(barrier, len(others))
    return partners(grid)


def sum_over(table, land, sems, others):
    for n, other in enumerate(others):
        copy = remote(table.at[n], land.at[n], sems, n, other)
        copy.start()
        copy.wait()
        table[n + 1] = table[n] + land[n]
        yield n


def remote(src, dst, sems, n, device):
    return pltpu.make_async_remote_copy(
        src_ref=src, dst_ref=dst, send_sem=sems.at[0, n], recv_sem=sems.at[1, n],
        device_id=device, device_id_type=MESH,
    )


def pieces_of(rows):
    size = rows // PARTS
    return [pl.ds(k * size, size) for k in range(PARTS)]


def start_all(copies):
    for copy in copies:
        copy.start()


def wait_all(copies):
    for copy in copies:
        copy.wait()


class Plan:
    def __init__(self):
        self.inputs, self.outs, self.lands, self.stages, self.hooks = [], [], [], [], []
        self.slots, self.makes, self.totals, self.moves, self.copies = [], [], [], 0, 1

    def give(self, array):
        for n, known in enumerate(self.inputs):
            if known is array:
                return ("in", n)
        self.inputs.append(array)
        return ("in", len(self.inputs) - 1)

    def room(self, shape):
        self.outs.append(jax.ShapeDtypeStruct(shape, bf16))
        return ("out", len(self.outs) - 1)

    def land(self, shape):
        self.lands.append(shape)
        return ("land", len(self.lands) - 1)

    def slot(self, key, shape):
        if (key, shape) not in self.slots:
            self.slots.append((key, shape))
        return self.slots.index((key, shape))

    def make(self, stage, key, shape, parts, offset, owned):
        slot = self.slot(key, shape)
        made = []
        for places, came in parts:
            copies = [(self.give(array), src, dst) for array, src, dst in places]
            joins = [(h if isinstance(h, tuple) else self.give(h), at) for h, at in came]
            made.append((copies, joins))
        self.copies = max(self.copies, sum(len(c) + len(j) for c, j in made))
        self.makes.append((stage, slot, made, offset, owned))
        return ("make", len(self.makes) - 1)

    def move(self, stage, src, dst, way, offset, owned, cut, part=0, needs=None):
        while len(self.stages) <= stage:
            self.stages.append([])
        self.stages[stage].append((self.moves, src, dst, way, offset, owned, cut, part, needs))
        self.moves += 1
        return self.moves - 1

    def scratch(self):
        if not self.moves:
            return []
        held = [pltpu.VMEM(shape, bf16) for _, shape in self.slots for _ in range(2)]
        held += [pltpu.VMEM(shape, bf16) for shape in self.lands]
        sems = [pltpu.SemaphoreType.DMA((2, self.moves))]
        if self.slots:
            sems.append(pltpu.SemaphoreType.DMA((len(self.slots), self.copies)))
        return held + sems

    def settle(self, results):
        for hook in self.hooks:
            hook(lambda handle: self.inputs[handle[1]] if handle[0] == "in" else results[handle[1]])


class Background:
    def __init__(self, grid, plan, ins, outs, rest):
        self.stages, self.totals, self.now, self.sent = [], [], -1, 0
        if not plan.moves:
            return
        pos = grid.my_pos()
        core = lax.axis_index("fsdp") % grid.C
        count = 2 * len(plan.slots)
        held, lands = rest[:count], rest[count : count + len(plan.lands)]
        sems = rest[count + len(plan.lands)]
        local = rest[-1]
        self.refs = {"in": ins, "out": outs, "land": lands}

        def live(owned, offset):
            if not owned:
                return None
            return grid.dyn_place(pos + offset)[1] // (grid.Z // 2) == core

        def built(slot, made, offset, owned):
            term, more = held[2 * slot], held[2 * slot + 1]
            yy, zz = grid.dyn_place(pos + offset)
            n, parts = 0, []
            for copies, joins in made:
                fetches, adds = [], []
                for handle, src, dst in copies:
                    ref = self.refs[handle[0]][handle[1]].at[src(yy, zz)]
                    fetches.append(pltpu.make_async_copy(ref, term.at[dst], local.at[slot, n]))
                    n += 1
                for handle, at in joins:
                    ref = self.refs[handle[0]][handle[1]]
                    if handle[0] == "land":
                        adds.append((None, ref, at))
                    else:
                        copy = pltpu.make_async_copy(ref.at[at], more.at[at], local.at[slot, n])
                        adds.append((copy, more, at))
                    n += 1
                parts.append((fetches, adds, term, handle_early(joins)))
            return parts, live(owned, offset)

        def handle_early(joins):
            return all(handle[0] == "in" for handle, _ in joins)

        self.makes = [[] for _ in plan.stages]
        buffers = []
        for stage, slot, made, offset, owned in plan.makes:
            parts, alive = built(slot, made, offset, owned)
            self.makes[stage].append((parts, alive))
            buffers.append((held[2 * slot], parts, alive))
        for slot, made, owned in plan.totals:
            self.totals.append((held[2 * slot],) + built(slot, made, 0, owned))
        self.all = {}
        for stage in plan.stages:
            row = []
            for number, src, dst, way, offset, owned, cut, part, needs in stage:
                put = None
                if src[0] == "make":
                    src_ref, parts, alive = buffers[src[1]]
                    put = (parts[part], alive)
                else:
                    src_ref = self.refs[src[0]][src[1]]
                dst_ref = self.refs[dst[0]][dst[1]]
                copy = remote(src_ref.at[cut], dst_ref.at[cut], sems, number, grid.neighbour(way))
                self.all[number] = (copy, live(owned, offset), live(owned, offset - way))
                row.append((number, put, needs))
            self.stages.append(row)
        self.come, self.put_done = set(), set()

    @staticmethod
    def do(condition, action):
        if condition is None:
            action()
        else:
            pl.when(condition)(action)

    def fetch(self, stage):
        if stage < len(self.stages):
            for parts, alive in self.makes[stage]:
                for fetches, adds, _, early in parts:
                    copies = fetches + [copy for copy, _, _ in adds if copy is not None and early]
                    self.do(alive, functools.partial(start_all, copies))

    def begin(self):
        self.fetch(0)
        for _, parts, alive in self.totals:
            for fetches, _, _, _ in parts:
                self.do(alive, functools.partial(start_all, fetches))

    @staticmethod
    def put(part, started=True):
        fetches, adds, term, early = part
        wait_all(fetches)
        for copy, ref, at in adds:
            if copy is not None:
                if not (early and started):
                    copy.start()
                copy.wait()
            term[at] = (term[at].astype(f32) + ref[at].astype(f32)).astype(bf16)

    def arrive(self, number):
        if number is not None and number not in self.come:
            self.come.add(number)
            copy, _, come = self.all[number]
            self.do(come, copy.wait_recv)

    def advance(self):
        self.now += 1
        if self.now < len(self.stages):
            for number, put, needs in self.stages[self.now]:
                for need in needs or ():
                    self.arrive(need)
                if put is not None and id(put[0]) not in self.put_done:
                    self.put_done.add(id(put[0]))
                    self.do(put[1], functools.partial(self.put, put[0]))
                copy, go, _ = self.all[number]
                self.do(go, copy.start)
            if self.now + 1 < len(self.stages):
                self.wait_sends(self.now)
                self.fetch(self.now + 1)
        if self.now >= len(self.stages):
            for row in self.stages:
                for number, _, _ in row:
                    self.arrive(number)

    def arrived(self, stage):
        for row in self.stages[: stage + 1]:
            for number, _, _ in row:
                self.arrive(number)

    def wait_sends(self, stage):
        while self.sent < stage:
            for number, _, _ in self.stages[self.sent]:
                copy, go, _ = self.all[number]
                self.do(go, copy.wait_send)
            self.sent += 1

    def finish(self):
        while self.now < len(self.stages):
            self.advance()
        self.wait_sends(len(self.stages))


class Gather:
    def __init__(self, grid, shape, cuts, owned=False):
        self.grid, self.owned, self.shape, self.cuts = grid, owned, shape, cuts
        self.k, self.total = 0, grid.R // 2

    def begin(self, plan):
        room = plan.room(self.shape)
        self.up = self.down = room

        def hook(get):
            self.found = [(0, get(room))]
            if self.k == 0:
                self.up = self.down = get(room)

        plan.hooks.append(hook)
        return room

    def left(self):
        return self.total - self.k

    def add(self, plan, stage, hops=None):
        hops = self.left() if hops is None else min(hops, self.left())
        if hops == 0:
            return
        one = self.up is self.down
        up = self.up if isinstance(self.up, tuple) else plan.give(self.up)
        down = up if one else plan.give(self.down)
        new = []
        before = [(None, None)] * len(self.cuts)
        for n in range(hops):
            self.k += 1
            k = self.k
            last = k == self.total
            to_up = plan.room(self.shape)
            to_down = to_up if last else plan.room(self.shape)
            now = []
            for (cut, first, second), (need_up, need_down) in zip(self.cuts, before):
                pair = (first, second) if last else (cut, cut)
                moved = []
                for src, dst, way, part, need in (
                    (up, to_up, 1, pair[0], need_up), (down, to_down, -1, pair[1], need_down)
                ):
                    moved.append(
                        None
                        if part is None
                        else plan.move(
                            stage + n, src, dst, way, -way * (k - 1), self.owned, part,
                            needs=(need,),
                        )
                    )
                now.append(tuple(moved))
            before = now
            new.append((-k, to_up))
            if not last:
                new.append((k, to_down))
            up, down = to_up, to_down

        def hook(get):
            self.up, self.down = get(up), get(down)
            self.found += [(offset, get(handle)) for offset, handle in new]

        plan.hooks.append(hook)


class Scatter:
    def __init__(self, grid, parts, shape, owned=False):
        self.grid, self.parts, self.shape, self.owned = grid, parts, shape, owned
        self.k = grid.R // 2
        self.held = {1: None, -1: None}

    def left(self):
        return self.k

    def came(self, way, n):
        if self.held[way] is None:
            return []
        block, column = self.held[way]
        at = self.parts[n][0][column]
        return [] if at is None else [(block, at)]

    def add(self, plan, stage, steps=1, final=False):
        steps = min(steps, self.k)
        before = {way: [None] * len(self.parts) for way in (1, -1)}
        for n in range(steps):
            k = self.k
            self.k -= 1
            room = plan.land if n < steps - 1 or final else plan.room
            rooms = {way: room(self.shape) for way in (1, -1)}
            halves = k == self.grid.R // 2
            blocks = {}
            for way in (1, -1):
                if halves and way == -1:
                    blocks[way] = blocks[1]
                    continue
                parts = [(places, self.came(way, m)) for m, (_, places) in enumerate(self.parts)]
                blocks[way] = plan.make(
                    stage + n, (id(self), way, n % 2), self.shape, parts, way * k, self.owned
                )
            now = {1: [], -1: []}
            for m, (cuts, _) in enumerate(self.parts):
                for way in (1, -1):
                    column = (1 if way == 1 else 2) if halves else 0
                    moved = None
                    if cuts[column] is not None:
                        moved = plan.move(
                            stage + n, blocks[way], rooms[way], way, way * k, self.owned, cuts[column],
                            m, (before[way][m],),
                        )
                    now[way].append(moved)
            before = now
            self.held = {
                way: (rooms[way], (1 if way == 1 else 2) if halves else 0) for way in (1, -1)
            }

        def hook(get):
            self.held = {
                way: (get(block), column) if block[0] == "out" else (None, column)
                for way, (block, column) in self.held.items()
            }

        if steps:
            plan.hooks.append(hook)

    def total(self, plan):
        parts = [
            (places, self.came(1, m) + self.came(-1, m)) for m, (_, places) in enumerate(self.parts)
        ]
        slot = plan.slot(("total", id(self)), self.shape)
        made = []
        for places, came in parts:
            copies = [(plan.give(array), src, dst) for array, src, dst in places]
            joins = [(h if isinstance(h, tuple) else plan.give(h), at) for h, at in came]
            made.append((copies, joins))
        plan.copies = max(plan.copies, sum(len(c) + len(j) for c, j in made))
        plan.totals.append((slot, made, self.owned))


def fused_call(grid, kernel, name, plan, inputs, in_specs, outs, out_specs, scratch, micros):
    plan = Plan() if plan is None else plan
    a, b, c, d = len(inputs), len(plan.inputs), len(outs), len(plan.outs)
    moves = plan.moves

    def whole(*refs):
        fg_in, bg_in = refs[:a], refs[a : a + b]
        fg_out, bg_out = refs[a + b : a + b + c], refs[a + b + c : a + b + c + d]
        rest = refs[a + b + c + d :]
        own = len(scratch)
        background = Background(grid, plan, bg_in, bg_out, rest[own:])
        kernel(background, bool(moves), *fg_in, *fg_out, *rest[:own])

    number = grid.calls
    grid.calls += 1
    results = pl.pallas_call(
        whole,
        out_shape=tuple(outs) + tuple(plan.outs),
        in_specs=list(in_specs) + [ANY] * b,
        out_specs=tuple(out_specs) + (ANY,) * d,
        scratch_shapes=list(scratch) + plan.scratch(),
        compiler_params=remote_params(number),
        cost_estimate=cost(micros),
        name=name,
    )(*inputs, *plan.inputs)
    plan.settle(results[c:])
    return results[:c]


def load(sources, places, sems):
    copies = [
        pltpu.make_async_copy(src, dst, sems.at[n]) for n, (src, dst) in enumerate(zip(sources, places))
    ]
    start_all(copies)
    return copies


class Spread:
    sems = pltpu.SemaphoreType.DMA((2, 1 + 2 * PARTS))

    def __init__(self, rows_ref, sems, sib, over):
        cuts = pieces_of(rows_ref.shape[1])
        self.near = remote(rows_ref.at[0], rows_ref.at[1], sems, 0, sib)
        self.far = [
            remote(rows_ref.at[0, at], rows_ref.at[2, at], sems, 1 + k, over)
            for k, at in enumerate(cuts)
        ]
        self.relay = [
            remote(rows_ref.at[2, at], rows_ref.at[3, at], sems, 1 + PARTS + k, sib)
            for k, at in enumerate(cuts)
        ]

    def start(self):
        for copy in self.far:
            copy.start()
        self.near.start()

    def pass_on(self, k):
        self.far[k].wait_recv()
        self.relay[k].start()

    def end(self):
        self.near.wait_send()
        for copy in self.far + self.relay:
            copy.wait_send()


class Collect:
    sems = pltpu.SemaphoreType.DMA((2, 1 + 2 * PARTS))

    @staticmethod
    def scratch(rows, width):
        return [pltpu.VMEM((6, rows, width), bf16), Collect.sems]

    def __init__(self, hold, sems, sib, over):
        self.hold = hold
        self.cuts = pieces_of(hold.shape[1])
        self.near = remote(hold.at[0], hold.at[2], sems, 0, sib)
        self.side = [
            remote(hold.at[1, at], hold.at[3, at], sems, 1 + k, sib)
            for k, at in enumerate(self.cuts)
        ]
        self.over = [
            remote(hold.at[4, at], hold.at[5, at], sems, 1 + PARTS + k, over)
            for k, at in enumerate(self.cuts)
        ]

    def give_near(self, part):
        self.hold[0] = part.astype(bf16)
        self.near.start()

    def give_side(self, k, part):
        self.hold[1, self.cuts[k]] = part.astype(bf16)
        self.side[k].start()

    def give_over(self, k, part):
        self.side[k].wait_recv()
        self.hold[4, self.cuts[k]] = (part + self.hold[3, self.cuts[k]].astype(f32)).astype(bf16)
        self.over[k].start()

    def finish(self, part):
        self.near.wait_recv()
        part = part + self.hold[2].astype(f32)
        for copy in self.over:
            copy.wait_recv()
        return part + self.hold[5].astype(f32)

    def end(self):
        self.near.wait_send()
        for copy in self.side + self.over:
            copy.wait_send()


def normed_rows(values, gain_row):
    return values * lax.rsqrt(jnp.mean(values * values, -1, keepdims=True) + epsilon) * gain_row


def norm_back(values, gain_row, upstream):
    scale = lax.rsqrt(jnp.mean(values * values, -1, keepdims=True) + epsilon)
    unit = values * scale
    moved = upstream * gain_row
    grad = scale * (moved - unit * jnp.mean(moved * unit, -1, keepdims=True))
    gains = upstream * unit
    return grad, jnp.sum(gains.reshape(-1, 8, gains.shape[-1]), 0)


def remote_params(number, limit=58):
    return pltpu.CompilerParams(
        vmem_limit_bytes=limit * 1024 * 1024, collective_id=number, has_side_effects=True
    )


def shaped(*pairs):
    return tuple(jax.ShapeDtypeStruct(shape, dtype) for shape, dtype in pairs)


ANY = pl.BlockSpec(memory_space=pl.ANY)
VMEM = pl.BlockSpec(memory_space=pltpu.VMEM)


def attn_kernel(
    grid, heads, offsets, background, cycle, h_ref, gain_ref, cos_ref, sin_ref, tokk_ref, tokq_ref,
    from_ref, *refs,
):
    pieces = refs[: len(offsets)]
    (
        all_ref, q_ref, k_ref, v_ref, mid_ref, mixed_ref, lse_ref,
        stage, w_sems, held, wo_ref, rows_ref, s_sems, out_sem, top, total, acc, part, hold, c_sems,
    ) = refs[len(offsets) :]
    rows = h_ref.shape[0]
    halves = heads // 2
    scale = HD ** (-0.5)
    ids = place_id(grid)
    background.begin()
    fetched = fetch_attn(grid, offsets, pieces, stage, w_sems)
    sib, over, _ = greet(grid, 2, cycle)
    rows_ref[0] = normed_rows(h_ref[...].astype(f32), gain_ref[...]).astype(bf16)
    spread = Spread(rows_ref, s_sems, sib, over)
    spread.start()
    background.advance()
    end_fetch(grid, fetched, stage, held, wo_ref)

    def work(slot, start, size):
        cosine, sine_part = cos_ref[slot, start : start + size], sin_ref[slot, start : start + size]
        at = slice(start, start + size)
        made = jnp.dot(rows_ref[slot, at], held[...], preferred_element_type=f32)
        for h in range(3 * halves):
            one = made[:, h * HP : (h + 1) * HP]
            turned = (one * cosine + swapped(one) * sine_part).astype(bf16)
            if h < 2 * halves:
                q_ref[h, slot, at] = turned
            else:
                k_ref[h - 2 * halves, slot, at] = turned
        for h in range(halves):
            v_ref[h, slot, at] = made[:, (3 * halves + h) * HP : (3 * halves + h + 1) * HP].astype(bf16)

    work(0, 0, rows)
    spread.near.wait_recv()
    work(1, 0, rows)
    size = rows // PARTS
    for k in range(PARTS):
        spread.pass_on(k)
        work(2, k * size, size)
        spread.relay[k].wait_recv()
        work(3, k * size, size)
    out = pltpu.make_async_copy(rows_ref, all_ref, out_sem)
    out.start()
    collect = Collect(hold, c_sems, sib, over)

    def attend(i):
        tok_q, begin = tokq_ref[i], from_ref[i]

        def block(j, first):
            tok_k = tokk_ref[j]
            allowed = (tok_k <= tok_q) & (tok_k >= begin)
            for h in range(heads):
                scores = dot_nt(q_ref[h, i], k_ref[h // 2, j])
                scores = jnp.where(allowed, scores * scale, NEVER)
                peak = jnp.max(scores, 1, keepdims=True)
                if not first:
                    before = top[h]
                    peak = jnp.maximum(peak, before)
                raised = jnp.exp(scores - peak)
                summed = jnp.sum(raised, 1, keepdims=True)
                got = jnp.dot(raised.astype(bf16), v_ref[h // 2, j], preferred_element_type=f32)
                if first:
                    total[h] = summed
                    acc[h] = got
                else:
                    shrink = jnp.exp(before - peak)
                    total[h] = total[h] * shrink + summed
                    acc[h] = acc[h] * shrink + got
                top[h] = peak

        block(i, True)
        for j in range(4):
            if j != i:
                pl.when((ids[j] < ids[i]) & (ids[j] >= ids[i] - 2))(functools.partial(block, j, False))
        for h in range(heads):
            mixed_ref[i, :, h * HP : (h + 1) * HP] = (acc[h] / total[h]).astype(bf16)
            log_total = top[h] + jnp.log(total[h])
            lse_ref[i, h] = jnp.transpose(jnp.broadcast_to(log_total, (rows, HP)))[:8]
        part[...] = dot_nt(mixed_ref[i], wo_ref[...])

    cuts = pieces_of(rows)
    attend(3)
    for k in range(PARTS):
        collect.give_side(k, part[cuts[k]])
    background.advance()
    attend(2)
    for k in range(PARTS):
        collect.give_over(k, part[cuts[k]])
    attend(1)
    collect.give_near(part[...])
    attend(0)
    mid_ref[...] = collect.finish(part[...] + h_ref[...].astype(f32))
    background.advance()
    out.wait()
    spread.end()
    collect.end()
    background.finish()


def attn_call(grid, plan, hidden, gain_row, facts, found):
    rows, width = hidden.shape
    halves = grid.Z // 2
    heads = 2 * halves
    offsets, blocks = apart(found)
    shape = (halves, 4, rows, HP)
    return fused_call(
        grid, functools.partial(attn_kernel, grid, heads, offsets), "attn", plan,
        (
            hidden, gain_row, facts["cos"], facts["sin"], facts["tok_row"], facts["tok_col"],
            facts["from_col"], *blocks,
        ),
        [VMEM] * 7 + [ANY] * len(blocks),
        shaped(
            ((4, rows, width), bf16), ((heads,) + shape[1:], bf16), (shape, bf16), (shape, bf16),
            ((rows, width), f32), ((4, rows, heads * HP), bf16), ((4, heads, 8, rows), f32),
        ),
        (ANY,) + (VMEM,) * 6,
        [
            *attn_weights(grid, found, width),
            pltpu.VMEM((4, rows, width), bf16), Spread.sems, pltpu.SemaphoreType.DMA,
            pltpu.VMEM((heads, rows, 1), f32),
            pltpu.VMEM((heads, rows, 1), f32),
            pltpu.VMEM((heads, rows, HP), f32),
            pltpu.VMEM((rows, width), f32),
        ]
        + Collect.scratch(rows, width),
        60,
    )


def fetch_attn(grid, offsets, pieces, stage, sems):
    pos = grid.my_pos()
    core = lax.axis_index("fsdp") % grid.C
    halves = grid.Z // 2
    fetched = []
    for i, offset in enumerate(offsets):
        yy, zz = grid.dyn_place(pos + offset)
        copy = pltpu.make_async_copy(pieces[i], stage.at[yy * halves + zz % halves], sems.at[i])
        live = zz // halves == core
        pl.when(live)(copy.start)
        fetched.append((live, copy))
    return fetched


def end_fetch(grid, fetched, stage, qkv, out):
    for live, copy in fetched:
        pl.when(live)(copy.wait)
    halves = grid.Z // 2
    share_rows = stage.shape[1] // grid.C
    depth = share_rows * 2 // 3
    half = depth // 2

    def put(ref, first, count, at, head):
        blank = jnp.zeros((count, HP - HD), bf16)
        ref[first : first + count, at * HP : (at + 1) * HP] = jnp.concatenate([head, blank], 1)

    for yy in range(grid.Y):
        for j in range(halves):
            block = stage.at[yy * halves + j]
            for core in range(grid.C):
                first, base = (yy * grid.C + core) * depth, core * share_rows
                for n, at in enumerate((2 * j, 2 * j + 1, 2 * halves + j, 3 * halves + j)):
                    put(qkv, first, depth, at, block[base : base + depth, n * HD : (n + 1) * HD])
                for n in range(4):
                    head = block[base + depth : base + share_rows, n * HD : (n + 1) * HD]
                    put(out, first + n // 2 * half, half, 2 * j + n % 2, head)


def attn_weights(grid, found, width):
    tall, halves = found[0][1].shape[0], grid.Z // 2
    return [
        pltpu.VMEM((grid.Y * halves, tall, BLOCK), bf16),
        pltpu.SemaphoreType.DMA((len(found),)),
        pltpu.VMEM((width, 4 * halves * HP), bf16),
        pltpu.VMEM((width, 2 * halves * HP), bf16),
    ]


def apart(found):
    return [offset for offset, _ in found], [block for _, block in found]


def place_id(grid):
    x, _, c, z = grid.me()
    return [2 * cc + (xx + z) % 2 for xx, cc in ((x, c), (x, 1 - c), (1 - x, c), (1 - x, 1 - c))]


def fetch_ffn(grid, offsets, pieces, held, sems):
    pos = grid.my_pos()
    _, tall, units = pieces[0].shape
    copies = []
    for i, offset in enumerate(offsets):
        yy, zz = grid.dyn_place(pos + offset)
        rows = pl.ds(pl.multiple_of(yy * tall, tall), tall)
        cols = pl.ds(pl.multiple_of(zz * units, units), units)
        copy = pltpu.make_async_copy(pieces[i], held.at[:, rows, cols], sems.at[i])
        copy.start()
        copies.append(copy)
    return copies


STEP = 512


def ffn_kernel(grid, offsets, background, cycle, mid_ref, gain_ref, *refs):
    count = len(offsets)
    pieces = refs[:count]
    (
        out_ref, all_ref, *stored,
        held, w_sems, rows_ref, s_sems, part, own, hold, c_sems, out_sem,
        gate_ref, up_ref, hid_ref, g_sems,
    ) = refs[count:]
    rows, width = mid_ref.shape
    hidden = gate_ref.shape[2]
    writes = []

    def store(slot):
        for n, (src, dst) in enumerate(zip((gate_ref, up_ref, hid_ref), stored)):
            writes.append(pltpu.make_async_copy(src.at[slot], dst.at[slot], g_sems.at[n, slot]))
            writes[-1].start()

    background.begin()
    fetched = fetch_ffn(grid, offsets, pieces, held, w_sems)
    sib, over, _ = greet(grid, 2, cycle)
    rows_ref[0] = normed_rows(mid_ref[...], gain_ref[...]).astype(bf16)
    spread = Spread(rows_ref, s_sems, sib, over)
    collect = Collect(hold, c_sems, sib, over)
    spread.start()
    background.advance()
    for copy in fetched:
        copy.wait()

    def work(slot, start, size):
        at = pl.ds(start, size)

        def tile(n, carry):
            cols = pl.ds(pl.multiple_of(n * STEP, STEP), STEP)
            some = rows_ref[slot, at]
            gate = jnp.dot(some, held[0, :, cols], preferred_element_type=f32)
            up = jnp.dot(some, held[1, :, cols], preferred_element_type=f32)
            gate_ref[slot, at, cols] = gate.astype(bf16)
            up_ref[slot, at, cols] = up.astype(bf16)
            hid_ref[slot, at, cols] = (gate * jax.nn.sigmoid(gate) * up).astype(bf16)
            return carry

        lax.fori_loop(0, hidden // STEP, tile, 0)

        def tile_down(n, carry):
            cols = pl.ds(pl.multiple_of(n * STEP, STEP), STEP)
            part[at, cols] = dot_nt(hid_ref[slot, at], held[2, cols])
            return carry

        lax.fori_loop(0, width // STEP, tile_down, 0)

    work(0, 0, rows)
    store(0)
    own[...] = mid_ref[...] + part[...]
    spread.near.wait_recv()
    work(1, 0, rows)
    store(1)
    collect.give_near(part[...])
    background.advance()
    cuts = pieces_of(rows)
    size = rows // PARTS
    for k in range(PARTS):
        spread.pass_on(k)
        if k:
            background.advance()
        spread.relay[k].wait_recv()
        work(3, k * size, size)
        collect.give_side(k, part[cuts[k]])
        work(2, k * size, size)
        collect.give_over(k, part[cuts[k]])
    store(2)
    store(3)
    background.advance()
    out = pltpu.make_async_copy(rows_ref, all_ref, out_sem)
    out.start()
    out_ref[...] = collect.finish(own[...]).astype(bf16)
    out.wait()
    wait_all(writes)
    spread.end()
    collect.end()
    background.finish()


def ffn_call(grid, plan, middle, gain_row, found):
    rows, width = middle.shape
    offsets, blocks = [o for o, _ in found], [b for _, b in found]
    hidden = grid.Z * blocks[0].shape[2]
    return fused_call(
        grid, functools.partial(ffn_kernel, grid, offsets), "ffn", plan,
        (middle, gain_row, *blocks), [VMEM] * 2 + [ANY] * len(blocks),
        shaped(((rows, width), bf16), ((4, rows, width), bf16), *[((4, rows, hidden), bf16)] * 3),
        (VMEM,) + (ANY,) * 4,
        [
            pltpu.VMEM((3, width, hidden), bf16),
            pltpu.SemaphoreType.DMA((len(blocks),)),
            pltpu.VMEM((4, rows, width), bf16),
            Spread.sems,
            pltpu.VMEM((rows, width), f32),
            pltpu.VMEM((rows, width), f32),
        ]
        + Collect.scratch(rows, width)
        + [pltpu.SemaphoreType.DMA]
        + [pltpu.VMEM((4, rows, hidden), bf16)] * 3
        + [pltpu.SemaphoreType.DMA((3, 4))],
        44,
    )


TN = (((0,), (0,)), ((), ()))


def weight_terms(out, left, right, step=512):
    whole = right[...].reshape(-1, right.shape[-1])

    def tile(n, carry):
        cols = pl.ds(pl.multiple_of(n * step, step), step)
        some = left[:, :, cols].reshape(-1, step)
        out[cols, :] = lax.dot_general(some, whole, TN, preferred_element_type=f32).astype(bf16)
        return carry

    lax.fori_loop(0, left.shape[-1] // step, tile, 0)


def ffn_back_kernel(
    grid, offsets, background, cycle, g_ref, mid_ref, gain_ref, *refs
):
    count = len(offsets)
    sources, pieces = refs[:4], refs[4 : 4 + count]
    (
        out_ref, gains_ref, terms_ref,
        held, w_sems, rows_ref, s_sems, dgate_ref, dup_ref, part, own, hold, c_sems, out_sems,
        gate_ref, up_ref, hid_ref, whole_ref, in_sems,
    ) = refs[4 + count :]
    rows, width = mid_ref.shape
    hidden = gate_ref.shape[2]
    loads = load(sources, (gate_ref, up_ref, hid_ref, whole_ref), in_sems)
    background.begin()
    fetched = fetch_ffn(grid, offsets, pieces, held, w_sems)
    sib, over, _ = greet(grid, 2, cycle)
    rows_ref[0] = g_ref[...]
    spread = Spread(rows_ref, s_sems, sib, over)
    collect = Collect(hold, c_sems, sib, over)
    spread.start()
    background.advance()
    wait_all(fetched + loads[:2])

    def work(slot, start, size):
        at = pl.ds(start, size)

        def tile(n, carry):
            cols = pl.ds(pl.multiple_of(n * STEP, STEP), STEP)
            grad = jnp.dot(rows_ref[slot, at], held[2, :, cols], preferred_element_type=f32)
            gate = gate_ref[slot, at, cols].astype(f32)
            up = up_ref[slot, at, cols].astype(f32)
            sig = jax.nn.sigmoid(gate)
            dgate_ref[slot, at, cols] = (grad * up * sig * (1.0 + gate * (1.0 - sig))).astype(bf16)
            dup_ref[slot, at, cols] = (grad * gate * sig).astype(bf16)
            return carry

        lax.fori_loop(0, hidden // STEP, tile, 0)

        def tile_back(n, carry):
            cols = pl.ds(pl.multiple_of(n * STEP, STEP), STEP)
            part[at, cols] = dot_nt(dgate_ref[slot, at], held[0, cols]) + dot_nt(
                dup_ref[slot, at], held[1, cols]
            )
            return carry

        lax.fori_loop(0, width // STEP, tile_back, 0)

    work(0, 0, rows)
    own[...] = part[...]
    spread.near.wait_recv()
    work(1, 0, rows)
    collect.give_near(part[...])
    background.advance()
    cuts = pieces_of(rows)
    size = rows // PARTS
    for k in range(PARTS):
        spread.pass_on(k)
        if k:
            background.advance()
        spread.relay[k].wait_recv()
        work(3, k * size, size)
        collect.give_side(k, part[cuts[k]])
        work(2, k * size, size)
        collect.give_over(k, part[cuts[k]])
    background.advance()
    wait_all(loads[2:])
    outs = []
    for m, (left, right) in enumerate(
        ((rows_ref, hid_ref), (whole_ref, dgate_ref), (whole_ref, dup_ref))
    ):
        n = (m + 2) % 3
        weight_terms(held.at[n], left, right)
        outs.append(pltpu.make_async_copy(held.at[n], terms_ref.at[n], out_sems.at[n]))
        outs[-1].start()
    second = collect.finish(own[...])
    grad, gains = norm_back(mid_ref[...], gain_ref[...], second)
    out_ref[...] = g_ref[...].astype(f32) + grad
    gains_ref[...] = gains
    background.advance()
    wait_all(outs)
    spread.end()
    collect.end()
    background.finish()


def ffn_back_call(grid, plan, grad_out, middle, gain_row, gate, up, hidden_low, whole, found):
    rows, width = middle.shape
    offsets, blocks = apart(found)
    hidden = gate.shape[2]
    return fused_call(
        grid, functools.partial(ffn_back_kernel, grid, offsets), "ffn_back", plan,
        (grad_out, middle, gain_row, gate, up, hidden_low, whole, *blocks),
        [VMEM] * 3 + [ANY] * (4 + len(blocks)),
        shaped(((rows, width), f32), ((8, width), f32), ((3, width, hidden), bf16)),
        (VMEM, VMEM, ANY),
        [
            pltpu.VMEM((3, width, hidden), bf16),
            pltpu.SemaphoreType.DMA((len(blocks),)),
            pltpu.VMEM((4, rows, width), bf16),
            Spread.sems,
            pltpu.VMEM((4, rows, hidden), bf16),
            pltpu.VMEM((4, rows, hidden), bf16),
            pltpu.VMEM((rows, width), f32),
            pltpu.VMEM((rows, width), f32),
        ]
        + Collect.scratch(rows, width)
        + [pltpu.SemaphoreType.DMA((3,))]
        + [pltpu.VMEM((4, rows, hidden), bf16)] * 3
        + [pltpu.VMEM((4, rows, width), bf16), pltpu.SemaphoreType.DMA((4,))],
        60,
    )


def attn_back_kernel(
    grid, heads, offsets, background, cycle, g_ref, h_ref, gain_ref, l_ref, tokc_ref, tokr_ref,
    from_ref, *refs,
):
    sources, pieces = refs[:7], refs[7 : 7 + len(offsets)]
    (
        out_ref, gains_ref, qkv_term, out_term,
        stage, w_sems, held, wo_ref, rows_ref, s_sems, gm_ref, dqkv_ref, low_ref, low_m, whole_out,
        key_sum, value_sum, query_sum, delta, part, hold, c_sems,
        q_ref, k_ref, v_ref, m_ref, cos_ref, sin_ref, whole_ref, in_sems,
    ) = refs[7 + len(offsets) :]
    rows = g_ref.shape[0]
    pairs = heads // 2
    scale = HD ** (-0.5)
    ids = place_id(grid)
    background.begin()
    fetched = fetch_attn(grid, offsets, pieces, stage, w_sems)
    loads = load(sources, (q_ref, k_ref, v_ref, m_ref, cos_ref, sin_ref, whole_ref), in_sems)
    sib, over, _ = greet(grid, 2, cycle)
    rows_ref[0] = g_ref[...].astype(bf16)
    spread = Spread(rows_ref, s_sems, sib, over)
    spread.start()
    background.advance()
    end_fetch(grid, fetched, stage, held, wo_ref)

    def work(slot, start, size):
        at = slice(start, start + size)
        made = jnp.dot(rows_ref[slot, at], wo_ref[...], preferred_element_type=f32).astype(bf16)
        for h in range(heads):
            gm_ref[h, slot, at] = made[:, h * HP : (h + 1) * HP]

    key_sum[...] = jnp.zeros_like(key_sum)
    value_sum[...] = jnp.zeros_like(value_sum)
    query_sum[...] = jnp.zeros_like(query_sum)

    def attend_back(i):
        for h in range(heads):
            product = gm_ref[h, i].astype(f32) * m_ref[i, :, h * HP : (h + 1) * HP].astype(f32)
            summed = jnp.sum(product, 1, keepdims=True)
            delta[h] = jnp.transpose(jnp.broadcast_to(summed, (rows, HP)))[:8]

        def block(j):
            allowed = (tokc_ref[j] <= tokr_ref[i]) & (tokc_ref[j] >= from_ref[i])
            for h in range(heads):
                query, upstream = q_ref[h, i], gm_ref[h, i]
                key, value = k_ref[h // 2, j], v_ref[h // 2, j]
                scores = jnp.where(allowed, dot_nt(key, query) * scale, NEVER)
                probs = jnp.exp(scores - l_ref[i, h, 0:1])
                value_sum[h // 2, j] += jnp.dot(
                    probs.astype(bf16), upstream, preferred_element_type=f32
                )
                grad_scores = (probs * (dot_nt(value, upstream) - delta[h, 0:1])).astype(bf16)
                key_sum[h // 2, j] += jnp.dot(grad_scores, query, preferred_element_type=f32)
                query_sum[h, i] += lax.dot_general(
                    grad_scores, key, TN, preferred_element_type=f32
                )

        for j in range(4):
            if i == j:
                block(j)
            else:
                pl.when((ids[j] < ids[i]) & (ids[j] >= ids[i] - 2))(functools.partial(block, j))

    work(0, 0, rows)
    spread.near.wait_recv()
    work(1, 0, rows)
    wait_all(loads[:4])
    attend_back(0)
    attend_back(1)
    background.advance()
    size = rows // PARTS
    for k in range(PARTS):
        spread.pass_on(k)
        work(2, k * size, size)
        spread.relay[k].wait_recv()
        work(3, k * size, size)
    attend_back(2)
    attend_back(3)

    def back(summed, at):
        one = summed * scale
        return (one * cos_ref[at] - swapped(one) * sin_ref[at]).astype(bf16)

    collect = Collect(hold, c_sems, sib, over)
    cuts = pieces_of(rows)
    wait_all(loads[4:])

    def work_back(i):
        for at in range(2 * heads):
            if at < heads:
                made, low = back(query_sum[at, i], i), at // 2 * 4 + at % 2
            elif at < heads + pairs:
                made, low = back(key_sum[at - heads, i], i), (at - heads) * 4 + 2
            else:
                h = at - heads - pairs
                made, low = value_sum[h, i].astype(bf16), h * 4 + 3
            dqkv_ref[i, :, at * HP : (at + 1) * HP] = made
            low_ref[i, :, low * HD : (low + 1) * HD] = made[:, :HD]
        part[...] = dot_nt(dqkv_ref[i], held[...])

    work_back(3)
    for k in range(PARTS):
        collect.give_side(k, part[cuts[k]])
    work_back(2)
    for k in range(PARTS):
        collect.give_over(k, part[cuts[k]])
    work_back(1)
    collect.give_near(part[...])
    work_back(0)
    for i in range(4):
        for h in range(heads):
            low_m[i, :, h * HD : (h + 1) * HD] = m_ref[i, :, h * HP : h * HP + HD]
    weight_terms(whole_out, rows_ref, low_m)
    half = out_term.shape[2]
    for n in range(out_term.shape[0]):
        for j in range(pairs):
            cols = slice(2 * j * HD, 2 * (j + 1) * HD)
            out_term[n, j] = jnp.concatenate(
                [whole_out[(2 * n + k) * half : (2 * n + k + 1) * half, cols] for k in range(2)], 1
            )
    weight_terms(qkv_term, whole_ref, low_ref)
    background.advance()
    grad, gains = norm_back(h_ref[...].astype(f32), gain_ref[...], collect.finish(part[...]))
    out_ref[...] = (g_ref[...] + grad).astype(bf16)
    gains_ref[...] = gains
    background.advance()
    spread.end()
    collect.end()
    background.finish()


def attn_back_call(grid, plan, grad_middle, hidden, gain_row, facts, kept, found):
    whole, query, keys, values, mixed, lse = kept
    rows, width = hidden.shape
    depth = width // (grid.Y * grid.C)
    heads = query.shape[0]
    pairs = heads // 2
    offsets, blocks = apart(found)
    return fused_call(
        grid, functools.partial(attn_back_kernel, grid, heads, offsets), "attn_back", plan,
        (
            grad_middle, hidden, gain_row, lse, facts["tok_col"], facts["tok_row"],
            facts["from_row"], query, keys, values, mixed, facts["cos"], facts["sin"], whole,
            *blocks,
        ),
        [VMEM] * 7 + [ANY] * (7 + len(blocks)),
        shaped(
            ((rows, width), bf16), ((8, width), f32), ((width, 2 * heads * HD), bf16),
            ((width // depth, pairs, depth // 2, BLOCK), bf16),
        ),
        (VMEM,) * 4,
        [
            *attn_weights(grid, found, width),
            pltpu.VMEM((4, rows, width), bf16), Spread.sems,
            pltpu.VMEM((heads, 4, rows, HP), bf16),
            pltpu.VMEM((4, rows, 2 * heads * HP), bf16),
            pltpu.VMEM((4, rows, 2 * heads * HD), bf16),
            pltpu.VMEM((4, rows, heads * HD), bf16),
            pltpu.VMEM((width, heads * HD), bf16),
            pltpu.VMEM((pairs, 4, rows, HP), f32),
            pltpu.VMEM((pairs, 4, rows, HP), f32),
            pltpu.VMEM((heads, 4, rows, HP), f32),
            pltpu.VMEM((heads, 8, rows), f32),
            pltpu.VMEM((rows, width), f32),
        ]
        + Collect.scratch(rows, width)
        + [
            pltpu.VMEM((heads, 4, rows, HP), bf16),
            pltpu.VMEM((pairs, 4, rows, HP), bf16),
            pltpu.VMEM((pairs, 4, rows, HP), bf16),
            pltpu.VMEM((4, rows, heads * HP), bf16),
            pltpu.VMEM((4, rows, HP), f32),
            pltpu.VMEM((4, rows, HP), f32),
            pltpu.VMEM((4, rows, width), bf16),
            pltpu.SemaphoreType.DMA((7,)),
        ],
        80,
    )


def start_kernel(
    grid, joins, early, background, cycle, wq, wk, wv, wo, wg, wu, wd, gains_ref, docs_ref, freq_ref,
    all_gains, cos_ref, sin_ref, tok_row, from_row, tok_col, from_col,
    attn_ref, ffn_ref, sems, local, table, land, t_sems, docs_land, begins, d_sems,
):
    x, y, c, z = grid.me()
    mine = z // (grid.Z // 2) == c
    attn_to = [background.refs[h[0]][h[1]] for h in joins[0]]
    ffn_to = [background.refs[h[0]][h[1]] for h in joins[1]]
    depth, units = ffn_ref.shape[2:]
    share_rows = attn_ref.shape[1]
    rows = pl.ds(pl.multiple_of(c * depth, depth), depth)
    attn_rows = pl.ds(pl.multiple_of(c * share_rows, share_rows), share_rows)

    def pack():
        for side in range(2):
            heads = [wq[0, :, 2 * side * HD : 2 * (side + 1) * HD]]
            heads += [ref[0, :, side * HD : (side + 1) * HD] for ref in (wk, wv)]
            turned = jnp.transpose(wo[0, 2 * side * HD : 2 * (side + 1) * HD].astype(f32)).astype(bf16)
            attn_ref[side, :depth] = jnp.concatenate(heads, 1)
            attn_ref[side, depth:] = jnp.concatenate([turned[: depth // 2], turned[depth // 2 :]], 1)

    others = doubling(grid)
    sib, over, diag = greet(grid, 3, cycle, others, pack)
    everything = []
    for layer in range(2):
        to = attn_to[layer].at[attn_rows]
        moves = [
            (mine, pltpu.make_async_copy(attn_ref.at[layer], to, local.at[0])),
            (~mine, remote(attn_ref.at[layer], to, sems, 0, sib)),
            (mine, remote(attn_ref.at[1 - layer], to, sems, 1, over)),
            (~mine, remote(attn_ref.at[1 - layer], to, sems, 2, diag)),
        ]
        into = ffn_to[layer].at[:, rows]
        quarter = lambda side, core: ffn_ref.at[2 * side + core]
        parts = [
            remote(quarter(1 - layer, c), into, sems, 4, over),
            remote(quarter(1 - layer, 1 - c), into, sems, 5, diag),
            remote(quarter(layer, 1 - c), into, sems, 3, sib),
            pltpu.make_async_copy(quarter(layer, c), into, local.at[1]),
        ]
        everything.append((moves, parts))

        @pl.when(x == layer)
        def _():
            for condition, copy in moves:
                pl.when(condition)(copy.start)

    for q in range(4):
        cols = slice(q * units, (q + 1) * units)
        ffn_ref[q, 0] = wg[0, :, cols]
        ffn_ref[q, 1] = wu[0, :, cols]
        ffn_ref[q, 2] = jnp.transpose(wd[0, cols].astype(f32)).astype(bf16)

    (own, to_sib, to_over, to_diag), parts = [copy for _, copy in moves], parts

    @pl.when(mine)
    def _():
        for copy in (to_sib, to_over, to_diag):
            copy.wait_recv()
        own.wait()
        to_over.wait_send()

    @pl.when(~mine)
    def _():
        to_sib.wait_send()
        to_diag.wait_send()

    background.advance()
    for layer in range(2):
        pl.when(x == layer)(functools.partial(start_all, everything[layer][1]))
    shares = grid.Y * grid.C * grid.Z
    share = gains_ref.shape[2]
    table[0] = jnp.zeros_like(table[0])
    padded = jnp.concatenate([gains_ref[0].astype(f32), jnp.zeros((2, HP - share), f32)], 1)
    table[0, (y * grid.C + c) * grid.Z + z, :2, :] = padded
    docs = remote(docs_ref, docs_land, d_sems, 0, sib)
    docs.start()
    for n in sum_over(table, land, t_sems, [sib] + others):
        if n % 2 == 1 and early:
            background.advance()
            early -= 1
    last = len(others) + 1
    copy = remote(table.at[last], land.at[last], t_sems, last, over)
    copy.start()
    copy.wait()
    docs.wait()
    both = jnp.where(z % grid.C == c, docs_ref[...], docs_land[...])
    doc = jnp.where(z // grid.C == 0, both[0], both[1])
    begin = jnp.zeros_like(doc)
    for value in range(1, DOCS):
        before = jnp.sum((doc < value).astype(f32), (0, 1), keepdims=True).astype(jnp.int32)
        begin = jnp.where(doc == value, before, begin)
    begins[...] = begin
    size = tok_row.shape[2]
    per = size // HP
    lane = lax.broadcasted_iota(jnp.int32, (size, HP), 1)
    for n, quarter in enumerate(place_id(grid)):
        rows_of = [begins[pl.ds(quarter * per + k, 1)] for k in range(per)]
        from_row[n] = jnp.concatenate(rows_of, 1)
        tok_row[n] = quarter * size + lax.broadcasted_iota(jnp.int32, (1, size), 1)
        columns = [
            jnp.transpose(jnp.broadcast_to(row.astype(f32), (HP, HP)))[:, :1] for row in rows_of
        ]
        column = jnp.concatenate(columns, 0)
        token = quarter * size + lax.broadcasted_iota(jnp.int32, (size, 1), 0)
        from_col[n] = column.astype(jnp.int32)
        tok_col[n] = token
        angle = (token.astype(f32) - column) * freq_ref[0:1]
        sine = jnp.sin(angle)
        cos_ref[n] = jnp.where(lane < HD, jnp.cos(angle), 0.0)
        sin_ref[n] = jnp.where(lane < HD // 2, -sine, jnp.where(lane < HD, sine, 0.0))
    for p in range(shares):
        own, other = table[last, p, :2, :share], land[last, p, :2, :share]
        at = slice(p * share, (p + 1) * share)
        all_gains[0, :, at] = jnp.where(x == 0, own, other)
        all_gains[1, :, at] = jnp.where(x == 0, other, own)
    for n in range(early):
        background.advance()
    wait_all(parts)
    background.finish()


def start_call(grid, plan, joins, early, shards, gains, doc_ids, rows):
    depth, width = shards[0].shape[1], grid.Y * grid.C * shards[0].shape[1]
    units = shards[4].shape[2] // 4
    hops = len(doubling(grid)) + 1
    table = (hops + 1, grid.Y * grid.C * grid.Z, 8, HP)
    ladder = np.arange(HP) % (HD // 2)
    frequency = np.power(np.float32(rope_base), (-2.0 * ladder / HD).astype(np.float32))
    frequency = jnp.asarray(np.broadcast_to(frequency.astype(np.float32), (8, HP)))
    docs = doc_ids.reshape(doc_ids.shape[0], -1, HP)
    ints = jnp.int32
    gain_all, cosine, sine_part, tok_row, from_row, tok_col, from_col = fused_call(
        grid, functools.partial(start_kernel, grid, joins, early), "start", plan,
        (*shards, gains, docs, frequency), [VMEM] * 10,
        shaped(
            ((2, 2, width), f32), ((4, rows, HP), f32), ((4, rows, HP), f32), ((4, 1, rows), ints),
            ((4, 1, rows), ints), ((4, rows, 1), ints), ((4, rows, 1), ints),
        ),
        (VMEM,) * 7,
        [
            pltpu.VMEM((2, depth * 3 // 2, BLOCK), bf16),
            pltpu.VMEM((4, 3, depth, units), bf16),
            pltpu.SemaphoreType.DMA((2, 6)),
            pltpu.SemaphoreType.DMA((2,)),
            pltpu.VMEM(table, f32),
            pltpu.VMEM(table, f32),
            pltpu.SemaphoreType.DMA((2, hops + 1)),
            pltpu.VMEM(docs.shape, ints),
            pltpu.VMEM(docs.shape[1:], ints),
            pltpu.SemaphoreType.DMA((2, 1)),
        ],
        70,
    )
    return gain_all, {
        "cos": cosine, "sin": sine_part, "tok_row": tok_row, "from_row": from_row,
        "tok_col": tok_col, "from_col": from_col,
    }


def tail_kernel(
    grid, ready, background, cycle, one_0, two_0, one_1, two_1, ffn_own, ffn_came, attn_own, attn_came,
    gain_out, sems, local, table, land, t_sems,
):
    x, _, c, z = grid.me()
    mine = z // (grid.Z // 2) == c
    depth, share_rows = ffn_own.shape[2], attn_own.shape[0]

    def part_of(core, size):
        return pl.ds(pl.multiple_of(core * size, size), size)

    rows, other = part_of(c, depth), part_of(1 - c, depth)
    attn_rows, attn_other = part_of(c, share_rows), part_of(1 - c, share_rows)
    background.begin()
    others = doubling(grid)
    sib, over, diag = greet(grid, 3, cycle, others)
    background.advance()
    table[0] = jnp.concatenate(
        [jnp.sum(ref[...], 0, keepdims=True) for ref in (one_0, two_0, one_1, two_1)]
        + [jnp.zeros((4, table.shape[2]), f32)],
        0,
    )

    def home(n, layer, heads):
        term, parts, alive = background.totals[n]
        for part in parts:
            background.do(alive, functools.partial(background.put, part, False))
        if heads:
            keep = (term.at[attn_rows], attn_own)
            moves = [
                remote(term.at[attn_other], attn_own, sems, 3, sib),
                remote(term.at[attn_rows], attn_came, sems, 4, over),
                remote(term.at[attn_other], attn_came, sems, 5, diag),
            ]
        else:
            keep = (term.at[:, rows], ffn_own.at[c])
            moves = [
                remote(term.at[:, other], ffn_own.at[c], sems, 0, sib),
                remote(term.at[:, rows], ffn_came.at[c], sems, 1, over),
                remote(term.at[:, other], ffn_came.at[c], sems, 2, diag),
            ]
        stay = pltpu.make_async_copy(*keep, local.at[1 if heads else 0])
        here = x == layer
        there = x != layer
        if heads:
            here, there = here & mine, there & mine

        @pl.when(here)
        def _():
            stay.start()
            moves[0].start()

        @pl.when(there)
        def _():
            moves[1].start()
            moves[2].start()

        return stay, moves

    done = {}
    waiting = [(n, rest) for n, *rest in ready]
    hops = sum_over(table, land, t_sems, [over, sib] + others)
    while waiting or background.now < len(background.stages):
        for n, (layer, heads, stage) in list(waiting):
            if stage < max(0, background.now - 1) or background.now >= len(background.stages):
                background.arrived(stage)
                done[heads] = home(n, layer, heads)
                waiting.remove((n, [layer, heads, stage]))
                break
        next(hops, None)
        next(hops, None)
        if background.now < len(background.stages):
            background.advance()
    for _ in hops:
        pass
    gain_out[...] = table[len(others) + 2]
    background.finish()
    stay, moves = done[False]
    stay.wait()
    for copy in moves:
        copy.wait()
    stay, moves = done[True]

    @pl.when(mine)
    def _():
        stay.wait()
        for copy in moves:
            copy.wait_send()
        moves[1].wait_recv()

    @pl.when(~mine)
    def _():
        moves[0].wait_recv()
        moves[2].wait_recv()


def tail_call(grid, plan, ready, gain_rows, depth, units):
    width = gain_rows[0].shape[1]
    hops = len(doubling(grid)) + 2
    table = (hops + 1, 8, width)
    return fused_call(
        grid, functools.partial(tail_kernel, grid, ready), "tail", plan, gain_rows, [VMEM] * 4,
        shaped(
            *[((2, 3, depth, units), bf16)] * 2, *[((depth * 3 // 2, BLOCK), bf16)] * 2, ((8, width), f32)
        ),
        (ANY,) * 4 + (VMEM,),
        [
            pltpu.SemaphoreType.DMA((2, 6)),
            pltpu.SemaphoreType.DMA((2,)),
            pltpu.VMEM(table, f32),
            pltpu.VMEM(table, f32),
            pltpu.SemaphoreType.DMA((2, hops)),
        ],
        60,
    )


def finish_kernel(
    ffn_own, ffn_came, attn_own, attn_came, out_one, out_two, grad_one, grad_two,
    produced, grads, query, key, value, out, gate, up, down,
):
    x = lax.axis_index("section")
    depth, units = ffn_own.shape[2:]

    def put(side, ffn_ref, attn_ref):
        for core in range(2):
            at = slice((2 * side + core) * units, (2 * side + core + 1) * units)
            gate[:, at] = ffn_ref[core, 0].astype(f32)
            up[:, at] = ffn_ref[core, 1].astype(f32)
            down[at] = jnp.transpose(ffn_ref[core, 2].astype(f32))

        def head(n):
            if n < 4:
                return attn_ref[:depth, n * HD : (n + 1) * HD].astype(f32)
            return jnp.concatenate(
                [attn_ref[depth:, k * HD : (k + 1) * HD].astype(f32) for k in (n - 4, n - 2)], 0
            )

        for h in range(2):
            at = slice((2 * side + h) * HD, (2 * side + h + 1) * HD)
            query[:, at] = head(h)
            out[at] = jnp.transpose(head(4 + h))
        key[side * HD : (side + 1) * HD] = jnp.transpose(head(2))
        value[side * HD : (side + 1) * HD] = jnp.transpose(head(3))

    for layer in range(2):

        @pl.when(x == layer)
        def _():
            put(layer, ffn_own, attn_own)
            put(1 - layer, ffn_came, attn_came)
            produced[layer] = out_one[...]
            produced[1 - layer] = out_two[...]
            grads[layer] = grad_one[...].astype(f32)
            grads[1 - layer] = grad_two[...].astype(f32)


def finish_call(blocks, outs, grads, shards):
    shape = (2,) + outs[0].shape
    shapes = [shard.shape[1:] for shard in shards]
    shapes[1:3] = [shape[::-1] for shape in shapes[1:3]]
    produced, grads, query, key, value, *rest = pl.pallas_call(
        finish_kernel,
        out_shape=shaped((shape, bf16), (shape, f32))
        + tuple(jax.ShapeDtypeStruct(one, f32) for one in shapes),
        in_specs=[VMEM] * 8,
        out_specs=(VMEM,) * 9,
        compiler_params=params(),
        cost_estimate=cost(8),
        name="finish",
    )(*blocks, *outs, *grads)
    return produced, grads, query, key.T, value.T, *rest


def after(value, *others):
    return lax.optimization_barrier((value,) + others)[0]


def layer_forward(grid, hidden_in, attn, ffn, nexts, gain_pair, facts):
    plan = Plan()
    ffn.add(plan, 0)
    whole, query, keys, values, middle, mixed, lse = attn_call(
        grid, plan, hidden_in, gain_pair[0:1], facts, attn.found
    )
    plan = Plan()
    if nexts:
        nexts[0].add(plan, 0)
        nexts[1].add(plan, max(0, len(plan.stages) - 2), 1)
    result, whole2, gate, up, hidden = ffn_call(grid, plan, middle, gain_pair[1:2], ffn.found)
    kept = (hidden_in, (whole, query, keys, values, mixed, lse), middle, whole2, gate, up, hidden)
    return result, kept


def layer_backward(grid, grad_out, kept, attn, ffn, gain_pair, facts, running, sum_ffn, sum_attn, leaving):
    hidden_in, kept_attn, middle, whole2, gate, up, hidden = kept
    plan = Plan()
    for ring in running:
        ring.add(plan, 0, min(4, ring.left()))
    grad_middle, gain_two, terms = ffn_back_call(
        grid, plan, grad_out, middle, gain_pair[1:2], gate, up, hidden, whole2, ffn.found
    )
    sums = sum_ffn(terms)
    running.append(sums)
    plan = Plan()
    sums.add(plan, 0, 3)
    grad_input, gain_one, qkv_term, out_term = attn_back_call(
        grid, plan, grad_middle, hidden_in, after(gain_pair[0:1], *leaving), facts, kept_attn, attn.found
    )
    running.append(sum_attn(qkv_term, out_term))
    return grad_input, (gain_one, gain_two)


def body(grid, inputs, doc_ids, cotangent, wq, wk, wv, wo, wg, wu, wd, gains):
    X, Y, C, Z = grid.X, grid.Y, grid.C, grid.Z
    x, y, c, z = grid.me()
    pos = grid.my_pos()
    micro, rows, width = inputs.shape
    depth = wq.shape[1]
    at_zero = x == 0

    def enter(block):
        def route(m):
            def go(x, y, c, z):
                if z % 2 != (x + m * C + c) % 2:
                    return None
                return (x, y, z // 2, m * C + c)

            return go

        first, last = grid.send(block[0], route(0)), grid.send(block[1], route(1))
        return jnp.where(z // C == 0, first, last)

    def leave(lower_block, upper_block):
        first = z // C == 0

        def route(swap):
            def go(x, y, c, z):
                section = (z // C + swap) % 2
                return (section, y, z % C, 2 * c + (x + z) % 2)

            return go

        same = grid.send(jnp.where(first, lower_block, upper_block), route(0))
        swapped_over = grid.send(jnp.where(first, upper_block, lower_block), route(1))
        return same, swapped_over

    rows_in = enter(inputs)
    halves = Z // 2
    tall = C * depth
    units = wg.shape[2] // 4
    share_rows = depth * 3 // 2
    upper, lower = pl.ds(0, tall // 2), pl.ds(tall // 2, tall // 2)
    cores = [pl.ds(core * share_rows, share_rows) for core in range(2)]
    attn_cuts = [((cores[0],), (cores[0],), None), ((cores[1],), None, (cores[1],))]
    ffn_cuts = [((m,), (m, upper), (m, lower)) for m in range(3)]
    attn = [Gather(grid, (C * share_rows, BLOCK), attn_cuts, True) for _ in range(2)]
    ffn = [Gather(grid, (3, tall, units), ffn_cuts) for _ in range(2)]
    plan = Plan()
    joins = [[ring.begin(plan) for ring in rings] for rings in (attn, ffn)]
    attn[0].add(plan, 0)
    ffn[0].add(plan, max(0, len(plan.stages) - 2), 1)
    shards = (wq, wk, wv, wo, wg, wu, wd)
    gain_all, facts = start_call(
        grid, plan, joins, max(0, len(plan.stages) - 3), shards, gains, doc_ids, rows
    )

    hidden = rows_in
    kept = []
    for s in range(2):
        nexts = (attn[1], ffn[1]) if s == 0 else None
        hidden, keep = layer_forward(grid, hidden, attn[s], ffn[s], nexts, gain_all[s], facts)
        kept.append(keep)
    rows_cot = enter(after(cotangent, kept[1][2]))
    outs = leave(after(kept[1][0], hidden, rows_cot), after(hidden, rows_cot))

    def sum_ffn(terms):
        def block(m):
            return lambda yy, zz: (
                m,
                pl.ds(pl.multiple_of(yy * tall, tall), tall),
                pl.ds(pl.multiple_of(zz * units, units), units),
            )

        parts = [(cuts, [(terms, block(m), (m,))]) for m, cuts in enumerate(ffn_cuts)]
        return Scatter(grid, parts, (3, tall, units))

    def sum_attn(qkv_term, out_term):
        def top(core):
            return lambda yy, zz: (
                pl.ds(pl.multiple_of((yy * C + core) * depth, depth), depth),
                pl.ds(pl.multiple_of(zz % halves * BLOCK, BLOCK), BLOCK),
            )

        def below(core):
            return lambda yy, zz: (yy * C + core, zz % halves)

        parts = []
        for core in range(C):
            first = core * share_rows
            places = [
                (qkv_term, top(core), (pl.ds(first, depth),)),
                (out_term, below(core), (pl.ds(first + depth, depth // 2),)),
            ]
            parts.append((attn_cuts[core], places))
        return Scatter(grid, parts, (C * share_rows, BLOCK), True)

    upstream = rows_cot
    gain_terms, running = [None] * 2, []
    waited, grads = outs, [None] * 2
    for s in (1, 0):
        upstream, gain_terms[s] = layer_backward(
            grid, upstream, kept[s], attn[s], ffn[s], gain_all[s], facts, running, sum_ffn, sum_attn, waited
        )
        grads[s], waited = upstream, ()
    grads_in = leave(*grads)
    plan = Plan()
    ready = []
    for n in (3, 2, 1, 0):
        left = running[n].left()
        running[n].add(plan, 0, left, True)
        ready.append((1 - n // 2, n % 2 == 1, left - 1))
        running[n].total(plan)
    order = sorted(range(4), key=lambda n: ready[n][2])
    ready = [(n,) + ready[n] for n in order]
    *blocks, gain_sum = tail_call(grid, plan, ready, gain_terms[0] + gain_terms[1], depth, units)

    produced, grads_in, *terms = finish_call(blocks, outs, grads_in, shards)
    share = gains.shape[2]
    mine = (y * C + c) * Z + z
    gain_share = lax.dynamic_slice(gain_sum, (2 * x, mine * share), (2, share))[None]
    return (
        produced[None],
        grads_in[None],
        *[term[None] for term in terms],
        gain_share,
    )


def solution(mesh):
    grid = Grid(mesh)

    def run(*arguments):
        grid.calls = 0
        return body(grid, *arguments)

    return jax.shard_map(
        run,
        mesh=mesh,
        in_specs=(
            P(None, ("fsdp", "tensor"), None),
            P(None, "fsdp", None),
            P(None, ("fsdp", "tensor"), None),
            P("section", "fsdp", "tensor"),
            P("section", "fsdp", "tensor"),
            P("section", "fsdp", "tensor"),
            P("section", "tensor", "fsdp"),
            P("section", "fsdp", "tensor"),
            P("section", "fsdp", "tensor"),
            P("section", "tensor", "fsdp"),
            P("section", None, ("fsdp", "tensor")),
        ),
        out_specs=(
            P("section", None, ("fsdp", "tensor"), None),
            P("section", None, ("fsdp", "tensor"), None),
            P("section", "fsdp", "tensor"),
            P("section", "fsdp", "tensor"),
            P("section", "fsdp", "tensor"),
            P("section", "tensor", "fsdp"),
            P("section", "fsdp", "tensor"),
            P("section", "fsdp", "tensor"),
            P("section", "tensor", "fsdp"),
            P("section", None, ("fsdp", "tensor")),
        ),
        check_vma=False,
    )
```

```python
import functools

import jax
import jax.numpy as jnp
import numpy as np
import jax.experimental.pallas as pl
import jax.experimental.pallas.tpu as pltpu
from jax import lax
from jax.sharding import PartitionSpec as P

HD = 96
DOCS = 4
HP = 128
NEVER = -1e30
BLOCK = 4 * HD
epsilon = 1e-05
rope_base = 100000.0
AXES = ("section", "fsdp", "tensor")
bf16 = jnp.bfloat16
f32 = jnp.float32


class Grid:
    def __init__(self, mesh):
        self.calls = 0
        self.X = mesh.shape["section"]
        self.C = 2
        self.Y = mesh.shape["fsdp"] // self.C
        self.Z = mesh.shape["tensor"]
        self.R = self.Y * self.Z
        self.places = [
            (x, y, c, z)
            for x in range(self.X)
            for y in range(self.Y)
            for c in range(self.C)
            for z in range(self.Z)
        ]

    def rank(self, place):
        x, y, c, z = place
        return ((x * self.Y + y) * self.C + c) * self.Z + z

    def send(self, block, route):
        pairs = []
        for place in self.places:
            goal = route(*place)
            if goal is not None:
                pairs.append((self.rank(place), self.rank(goal)))
        return lax.ppermute(block, AXES, pairs)

    def over_x(self, block):
        return self.send(block, lambda x, y, c, z: (1 - x, y, c, z))

    def over_c(self, block):
        return self.send(block, lambda x, y, c, z: (x, y, 1 - c, z))

    def place_of(self, p):
        p = p % self.R
        y, k = p // self.Z, p % self.Z
        return (y, k if y % 2 == 0 else self.Z - 1 - k)

    def pos_of(self, y, z):
        return y * self.Z + (z if y % 2 == 0 else self.Z - 1 - z)

    def neighbour(self, way):
        yy, zz = self.dyn_place(self.my_pos() + way)
        return {"fsdp": yy * self.C + lax.axis_index("fsdp") % self.C, "tensor": zz}

    def me(self):
        x = lax.axis_index("section")
        f = lax.axis_index("fsdp")
        z = lax.axis_index("tensor")
        return x, f // self.C, f % self.C, z

    def my_pos(self):
        x, y, c, z = self.me()
        return y * self.Z + jnp.where(y % 2 == 0, z, self.Z - 1 - z)

    def dyn_place(self, p):
        p = (p + 2 * self.R) % self.R
        y, k = p // self.Z, p % self.Z
        return y, jnp.where(y % 2 == 0, k, self.Z - 1 - k)

def params(limit=56):
    return pltpu.CompilerParams(vmem_limit_bytes=limit * 1024 * 1024)


def whole_vmem(count):
    return [pl.BlockSpec(memory_space=pltpu.VMEM)] * count


def cost(micros):
    return pl.CostEstimate(flops=int(micros * 1.0e9), bytes_accessed=1 << 20, transcendentals=0)


def swapped(values):
    lane = lax.broadcasted_iota(jnp.int32, values.shape, 1)
    half = HD // 2
    return jnp.where(lane < half, pltpu.roll(values, HP - half, 1), pltpu.roll(values, half, 1))


MESH = pl.DeviceIdType.MESH
NT = (((1,), (1,)), ((), ()))
PARTS = 2


def dot_nt(a, b):
    return lax.dot_general(a, b, NT, preferred_element_type=f32)


def partners(grid):
    x, y, c, _ = grid.me()
    return (
        {"fsdp": y * grid.C + 1 - c},
        {"section": 1 - x},
        {"section": 1 - x, "fsdp": y * grid.C + 1 - c},
    )


def doubling(grid):
    _, y, c, z = grid.me()
    found = []
    for bit in range((grid.Y - 1).bit_length()):
        step = 1 << bit
        found.append({"fsdp": (y + step * (1 - 2 * ((y // step) % 2))) * grid.C + c})
    for bit in range((grid.Z - 1).bit_length()):
        step = 1 << bit
        found.append({"tensor": z + step * (1 - 2 * ((z // step) % 2))})
    return found


def greet(grid, sides, cycle, more=(), meanwhile=lambda: None):
    others = list(partners(grid)[:sides]) + list(more)
    if cycle:
        others += [grid.neighbour(1), grid.neighbour(-1)]
    barrier = pltpu.get_barrier_semaphore()
    for other in others:
        pl.semaphore_signal(barrier, inc=1, device_id=other, device_id_type=MESH)
    meanwhile()
    pl.semaphore_wait(barrier, len(others))
    return partners(grid)


def sum_over(table, land, sems, others):
    for n, other in enumerate(others):
        copy = remote(table.at[n], land.at[n], sems, n, other)
        copy.start()
        copy.wait()
        table[n + 1] = table[n] + land[n]
        yield n


def remote(src, dst, sems, n, device):
    return pltpu.make_async_remote_copy(
        src_ref=src, dst_ref=dst, send_sem=sems.at[0, n], recv_sem=sems.at[1, n],
        device_id=device, device_id_type=MESH,
    )


def pieces_of(rows):
    size = rows // PARTS
    return [pl.ds(k * size, size) for k in range(PARTS)]


def start_all(copies):
    for copy in copies:
        copy.start()


def wait_all(copies):
    for copy in copies:
        copy.wait()


class Plan:
    def __init__(self):
        self.inputs, self.outs, self.lands, self.stages, self.hooks = [], [], [], [], []
        self.slots, self.makes, self.totals, self.moves, self.copies = [], [], [], 0, 1

    def give(self, array):
        for n, known in enumerate(self.inputs):
            if known is array:
                return ("in", n)
        self.inputs.append(array)
        return ("in", len(self.inputs) - 1)

    def room(self, shape):
        self.outs.append(jax.ShapeDtypeStruct(shape, bf16))
        return ("out", len(self.outs) - 1)

    def land(self, shape):
        self.lands.append(shape)
        return ("land", len(self.lands) - 1)

    def slot(self, key, shape):
        if (key, shape) not in self.slots:
            self.slots.append((key, shape))
        return self.slots.index((key, shape))

    def make(self, stage, key, shape, parts, offset, owned):
        slot = self.slot(key, shape)
        made = []
        for places, came in parts:
            copies = [(self.give(array), src, dst) for array, src, dst in places]
            joins = [(h if isinstance(h, tuple) else self.give(h), at) for h, at in came]
            made.append((copies, joins))
        self.copies = max(self.copies, sum(len(c) + len(j) for c, j in made))
        self.makes.append((stage, slot, made, offset, owned))
        return ("make", len(self.makes) - 1)

    def move(self, stage, src, dst, way, offset, owned, cut, part=0, needs=None):
        while len(self.stages) <= stage:
            self.stages.append([])
        self.stages[stage].append((self.moves, src, dst, way, offset, owned, cut, part, needs))
        self.moves += 1
        return self.moves - 1

    def scratch(self):
        if not self.moves:
            return []
        held = [pltpu.VMEM(shape, bf16) for _, shape in self.slots for _ in range(2)]
        held += [pltpu.VMEM(shape, bf16) for shape in self.lands]
        sems = [pltpu.SemaphoreType.DMA((2, self.moves))]
        if self.slots:
            sems.append(pltpu.SemaphoreType.DMA((len(self.slots), self.copies)))
        return held + sems

    def settle(self, results):
        for hook in self.hooks:
            hook(lambda handle: self.inputs[handle[1]] if handle[0] == "in" else results[handle[1]])


class Background:
    def __init__(self, grid, plan, ins, outs, rest):
        self.stages, self.totals, self.now, self.sent = [], [], -1, 0
        if not plan.moves:
            return
        pos = grid.my_pos()
        core = lax.axis_index("fsdp") % grid.C
        count = 2 * len(plan.slots)
        held, lands = rest[:count], rest[count : count + len(plan.lands)]
        sems = rest[count + len(plan.lands)]
        local = rest[-1]
        self.refs = {"in": ins, "out": outs, "land": lands}

        def live(owned, offset):
            if not owned:
                return None
            return grid.dyn_place(pos + offset)[1] // (grid.Z // 2) == core

        def built(slot, made, offset, owned):
            term, more = held[2 * slot], held[2 * slot + 1]
            yy, zz = grid.dyn_place(pos + offset)
            n, parts = 0, []
            for copies, joins in made:
                fetches, adds = [], []
                for handle, src, dst in copies:
                    ref = self.refs[handle[0]][handle[1]].at[src(yy, zz)]
                    fetches.append(pltpu.make_async_copy(ref, term.at[dst], local.at[slot, n]))
                    n += 1
                for handle, at in joins:
                    ref = self.refs[handle[0]][handle[1]]
                    if handle[0] == "land":
                        adds.append((None, ref, at))
                    else:
                        copy = pltpu.make_async_copy(ref.at[at], more.at[at], local.at[slot, n])
                        adds.append((copy, more, at))
                    n += 1
                parts.append((fetches, adds, term, handle_early(joins)))
            return parts, live(owned, offset)

        def handle_early(joins):
            return all(handle[0] == "in" for handle, _ in joins)

        self.makes = [[] for _ in plan.stages]
        buffers = []
        for stage, slot, made, offset, owned in plan.makes:
            parts, alive = built(slot, made, offset, owned)
            self.makes[stage].append((parts, alive))
            buffers.append((held[2 * slot], parts, alive))
        for slot, made, owned in plan.totals:
            self.totals.append((held[2 * slot],) + built(slot, made, 0, owned))
        self.all = {}
        for stage in plan.stages:
            row = []
            for number, src, dst, way, offset, owned, cut, part, needs in stage:
                put = None
                if src[0] == "make":
                    src_ref, parts, alive = buffers[src[1]]
                    put = (parts[part], alive)
                else:
                    src_ref = self.refs[src[0]][src[1]]
                dst_ref = self.refs[dst[0]][dst[1]]
                copy = remote(src_ref.at[cut], dst_ref.at[cut], sems, number, grid.neighbour(way))
                self.all[number] = (copy, live(owned, offset), live(owned, offset - way))
                row.append((number, put, needs))
            self.stages.append(row)
        self.come, self.put_done = set(), set()

    @staticmethod
    def do(condition, action):
        if condition is None:
            action()
        else:
            pl.when(condition)(action)

    def fetch(self, stage):
        if stage < len(self.stages):
            for parts, alive in self.makes[stage]:
                for fetches, adds, _, early in parts:
                    copies = fetches + [copy for copy, _, _ in adds if copy is not None and early]
                    self.do(alive, functools.partial(start_all, copies))

    def begin(self):
        self.fetch(0)
        for _, parts, alive in self.totals:
            for fetches, _, _, _ in parts:
                self.do(alive, functools.partial(start_all, fetches))

    @staticmethod
    def put(part, started=True):
        fetches, adds, term, early = part
        wait_all(fetches)
        for copy, ref, at in adds:
            if copy is not None:
                if not (early and started):
                    copy.start()
                copy.wait()
            term[at] = (term[at].astype(f32) + ref[at].astype(f32)).astype(bf16)

    def arrive(self, number):
        if number is not None and number not in self.come:
            self.come.add(number)
            copy, _, come = self.all[number]
            self.do(come, copy.wait_recv)

    def advance(self):
        self.now += 1
        if self.now < len(self.stages):
            for number, put, needs in self.stages[self.now]:
                for need in needs or ():
                    self.arrive(need)
                if put is not None and id(put[0]) not in self.put_done:
                    self.put_done.add(id(put[0]))
                    self.do(put[1], functools.partial(self.put, put[0]))
                copy, go, _ = self.all[number]
                self.do(go, copy.start)
            if self.now + 1 < len(self.stages):
                self.wait_sends(self.now)
                self.fetch(self.now + 1)
        if self.now >= len(self.stages):
            for row in self.stages:
                for number, _, _ in row:
                    self.arrive(number)

    def arrived(self, stage):
        for row in self.stages[: stage + 1]:
            for number, _, _ in row:
                self.arrive(number)

    def wait_sends(self, stage):
        while self.sent < stage:
            for number, _, _ in self.stages[self.sent]:
                copy, go, _ = self.all[number]
                self.do(go, copy.wait_send)
            self.sent += 1

    def finish(self):
        while self.now < len(self.stages):
            self.advance()
        self.wait_sends(len(self.stages))


class Gather:
    def __init__(self, grid, shape, cuts, owned=False):
        self.grid, self.owned, self.shape, self.cuts = grid, owned, shape, cuts
        self.k, self.total = 0, grid.R // 2

    def begin(self, plan):
        room = plan.room(self.shape)
        self.up = self.down = room

        def hook(get):
            self.found = [(0, get(room))]
            if self.k == 0:
                self.up = self.down = get(room)

        plan.hooks.append(hook)
        return room

    def left(self):
        return self.total - self.k

    def add(self, plan, stage, hops=None):
        hops = self.left() if hops is None else min(hops, self.left())
        if hops == 0:
            return
        one = self.up is self.down
        up = self.up if isinstance(self.up, tuple) else plan.give(self.up)
        down = up if one else plan.give(self.down)
        new = []
        before = [(None, None)] * len(self.cuts)
        for n in range(hops):
            self.k += 1
            k = self.k
            last = k == self.total
            to_up = plan.room(self.shape)
            to_down = to_up if last else plan.room(self.shape)
            now = []
            for (cut, first, second), (need_up, need_down) in zip(self.cuts, before):
                pair = (first, second) if last else (cut, cut)
                moved = []
                for src, dst, way, part, need in (
                    (up, to_up, 1, pair[0], need_up), (down, to_down, -1, pair[1], need_down)
                ):
                    moved.append(
                        None
                        if part is None
                        else plan.move(
                            stage + n, src, dst, way, -way * (k - 1), self.owned, part,
                            needs=(need,),
                        )
                    )
                now.append(tuple(moved))
            before = now
            new.append((-k, to_up))
            if not last:
                new.append((k, to_down))
            up, down = to_up, to_down

        def hook(get):
            self.up, self.down = get(up), get(down)
            self.found += [(offset, get(handle)) for offset, handle in new]

        plan.hooks.append(hook)


class Scatter:
    def __init__(self, grid, parts, shape, owned=False):
        self.grid, self.parts, self.shape, self.owned = grid, parts, shape, owned
        self.k = grid.R // 2
        self.held = {1: None, -1: None}

    def left(self):
        return self.k

    def came(self, way, n):
        if self.held[way] is None:
            return []
        block, column = self.held[way]
        at = self.parts[n][0][column]
        return [] if at is None else [(block, at)]

    def add(self, plan, stage, steps=1, final=False):
        steps = min(steps, self.k)
        before = {way: [None] * len(self.parts) for way in (1, -1)}
        for n in range(steps):
            k = self.k
            self.k -= 1
            room = plan.land if n < steps - 1 or final else plan.room
            rooms = {way: room(self.shape) for way in (1, -1)}
            halves = k == self.grid.R // 2
            blocks = {}
            for way in (1, -1):
                if halves and way == -1:
                    blocks[way] = blocks[1]
                    continue
                parts = [(places, self.came(way, m)) for m, (_, places) in enumerate(self.parts)]
                blocks[way] = plan.make(
                    stage + n, (id(self), way, n % 2), self.shape, parts, way * k, self.owned
                )
            now = {1: [], -1: []}
            for m, (cuts, _) in enumerate(self.parts):
                for way in (1, -1):
                    column = (1 if way == 1 else 2) if halves else 0
                    moved = None
                    if cuts[column] is not None:
                        moved = plan.move(
                            stage + n, blocks[way], rooms[way], way, way * k, self.owned, cuts[column],
                            m, (before[way][m],),
                        )
                    now[way].append(moved)
            before = now
            self.held = {
                way: (rooms[way], (1 if way == 1 else 2) if halves else 0) for way in (1, -1)
            }

        def hook(get):
            self.held = {
                way: (get(block), column) if block[0] == "out" else (None, column)
                for way, (block, column) in self.held.items()
            }

        if steps:
            plan.hooks.append(hook)

    def total(self, plan):
        parts = [
            (places, self.came(1, m) + self.came(-1, m)) for m, (_, places) in enumerate(self.parts)
        ]
        slot = plan.slot(("total", id(self)), self.shape)
        made = []
        for places, came in parts:
            copies = [(plan.give(array), src, dst) for array, src, dst in places]
            joins = [(h if isinstance(h, tuple) else plan.give(h), at) for h, at in came]
            made.append((copies, joins))
        plan.copies = max(plan.copies, sum(len(c) + len(j) for c, j in made))
        plan.totals.append((slot, made, self.owned))


def fused_call(grid, kernel, name, plan, inputs, in_specs, outs, out_specs, scratch, micros):
    plan = Plan() if plan is None else plan
    a, b, c, d = len(inputs), len(plan.inputs), len(outs), len(plan.outs)
    moves = plan.moves

    def whole(*refs):
        fg_in, bg_in = refs[:a], refs[a : a + b]
        fg_out, bg_out = refs[a + b : a + b + c], refs[a + b + c : a + b + c + d]
        rest = refs[a + b + c + d :]
        own = len(scratch)
        background = Background(grid, plan, bg_in, bg_out, rest[own:])
        kernel(background, bool(moves), *fg_in, *fg_out, *rest[:own])

    number = grid.calls
    grid.calls += 1
    results = pl.pallas_call(
        whole,
        out_shape=tuple(outs) + tuple(plan.outs),
        in_specs=list(in_specs) + [ANY] * b,
        out_specs=tuple(out_specs) + (ANY,) * d,
        scratch_shapes=list(scratch) + plan.scratch(),
        compiler_params=remote_params(number),
        cost_estimate=cost(micros),
        name=name,
    )(*inputs, *plan.inputs)
    plan.settle(results[c:])
    return results[:c]


def load(sources, places, sems):
    copies = [
        pltpu.make_async_copy(src, dst, sems.at[n]) for n, (src, dst) in enumerate(zip(sources, places))
    ]
    start_all(copies)
    return copies


class Spread:
    sems = pltpu.SemaphoreType.DMA((2, 1 + 2 * PARTS))

    def __init__(self, rows_ref, sems, sib, over):
        cuts = pieces_of(rows_ref.shape[1])
        self.near = remote(rows_ref.at[0], rows_ref.at[1], sems, 0, sib)
        self.far = [
            remote(rows_ref.at[0, at], rows_ref.at[2, at], sems, 1 + k, over)
            for k, at in enumerate(cuts)
        ]
        self.relay = [
            remote(rows_ref.at[2, at], rows_ref.at[3, at], sems, 1 + PARTS + k, sib)
            for k, at in enumerate(cuts)
        ]

    def start(self):
        for copy in self.far:
            copy.start()
        self.near.start()

    def pass_on(self, k):
        self.far[k].wait_recv()
        self.relay[k].start()

    def end(self):
        self.near.wait_send()
        for copy in self.far + self.relay:
            copy.wait_send()


class Collect:
    sems = pltpu.SemaphoreType.DMA((2, 1 + 2 * PARTS))

    @staticmethod
    def scratch(rows, width):
        return [pltpu.VMEM((6, rows, width), bf16), Collect.sems]

    def __init__(self, hold, sems, sib, over):
        self.hold = hold
        self.cuts = pieces_of(hold.shape[1])
        self.near = remote(hold.at[0], hold.at[2], sems, 0, sib)
        self.side = [
            remote(hold.at[1, at], hold.at[3, at], sems, 1 + k, sib)
            for k, at in enumerate(self.cuts)
        ]
        self.over = [
            remote(hold.at[4, at], hold.at[5, at], sems, 1 + PARTS + k, over)
            for k, at in enumerate(self.cuts)
        ]

    def give_near(self, part):
        self.hold[0] = part.astype(bf16)
        self.near.start()

    def give_side(self, k, part):
        self.hold[1, self.cuts[k]] = part.astype(bf16)
        self.side[k].start()

    def give_over(self, k, part):
        self.side[k].wait_recv()
        self.hold[4, self.cuts[k]] = (part + self.hold[3, self.cuts[k]].astype(f32)).astype(bf16)
        self.over[k].start()

    def finish(self, part):
        self.near.wait_recv()
        part = part + self.hold[2].astype(f32)
        for copy in self.over:
            copy.wait_recv()
        return part + self.hold[5].astype(f32)

    def end(self):
        self.near.wait_send()
        for copy in self.side + self.over:
            copy.wait_send()


def normed_rows(values, gain_row):
    return values * lax.rsqrt(jnp.mean(values * values, -1, keepdims=True) + epsilon) * gain_row


def norm_back(values, gain_row, upstream):
    scale = lax.rsqrt(jnp.mean(values * values, -1, keepdims=True) + epsilon)
    unit = values * scale
    moved = upstream * gain_row
    grad = scale * (moved - unit * jnp.mean(moved * unit, -1, keepdims=True))
    gains = upstream * unit
    return grad, jnp.sum(gains.reshape(-1, 8, gains.shape[-1]), 0)


def remote_params(number, limit=58):
    return pltpu.CompilerParams(
        vmem_limit_bytes=limit * 1024 * 1024, collective_id=number, has_side_effects=True
    )


def shaped(*pairs):
    return tuple(jax.ShapeDtypeStruct(shape, dtype) for shape, dtype in pairs)


ANY = pl.BlockSpec(memory_space=pl.ANY)
VMEM = pl.BlockSpec(memory_space=pltpu.VMEM)


def attn_kernel(
    grid, heads, offsets, background, cycle, h_ref, gain_ref, cos_ref, sin_ref, tokk_ref, tokq_ref,
    from_ref, *refs,
):
    pieces = refs[: len(offsets)]
    (
        all_ref, q_ref, k_ref, v_ref, mid_ref, mixed_ref, lse_ref,
        stage, w_sems, held, wo_ref, rows_ref, s_sems, out_sem, top, total, acc, part, hold, c_sems,
    ) = refs[len(offsets) :]
    rows = h_ref.shape[0]
    halves = heads // 2
    scale = HD ** (-0.5)
    ids = place_id(grid)
    background.begin()
    fetched = fetch_attn(grid, offsets, pieces, stage, w_sems)
    sib, over, _ = greet(grid, 2, cycle)
    rows_ref[0] = normed_rows(h_ref[...].astype(f32), gain_ref[...]).astype(bf16)
    spread = Spread(rows_ref, s_sems, sib, over)
    spread.start()
    background.advance()
    end_fetch(grid, fetched, stage, held, wo_ref)

    def work(slot, start, size):
        cosine, sine_part = cos_ref[slot, start : start + size], sin_ref[slot, start : start + size]
        at = slice(start, start + size)
        made = jnp.dot(rows_ref[slot, at], held[...], preferred_element_type=f32)
        for h in range(3 * halves):
            one = made[:, h * HP : (h + 1) * HP]
            turned = (one * cosine + swapped(one) * sine_part).astype(bf16)
            if h < 2 * halves:
                q_ref[h, slot, at] = turned
            else:
                k_ref[h - 2 * halves, slot, at] = turned
        for h in range(halves):
            v_ref[h, slot, at] = made[:, (3 * halves + h) * HP : (3 * halves + h + 1) * HP].astype(bf16)

    work(0, 0, rows)
    spread.near.wait_recv()
    work(1, 0, rows)
    size = rows // PARTS
    for k in range(PARTS):
        spread.pass_on(k)
        work(2, k * size, size)
        spread.relay[k].wait_recv()
        work(3, k * size, size)
    out = pltpu.make_async_copy(rows_ref, all_ref, out_sem)
    out.start()
    collect = Collect(hold, c_sems, sib, over)

    def attend(i):
        tok_q, begin = tokq_ref[i], from_ref[i]

        def block(j, first):
            tok_k = tokk_ref[j]
            allowed = (tok_k <= tok_q) & (tok_k >= begin)
            for h in range(heads):
                scores = dot_nt(q_ref[h, i], k_ref[h // 2, j])
                scores = jnp.where(allowed, scores * scale, NEVER)
                peak = jnp.max(scores, 1, keepdims=True)
                if not first:
                    before = top[h]
                    peak = jnp.maximum(peak, before)
                raised = jnp.exp(scores - peak)
                summed = jnp.sum(raised, 1, keepdims=True)
                got = jnp.dot(raised.astype(bf16), v_ref[h // 2, j], preferred_element_type=f32)
                if first:
                    total[h] = summed
                    acc[h] = got
                else:
                    shrink = jnp.exp(before - peak)
                    total[h] = total[h] * shrink + summed
                    acc[h] = acc[h] * shrink + got
                top[h] = peak

        block(i, True)
        for j in range(4):
            if j != i:
                pl.when((ids[j] < ids[i]) & (ids[j] >= ids[i] - 2))(functools.partial(block, j, False))
        for h in range(heads):
            mixed_ref[i, :, h * HP : (h + 1) * HP] = (acc[h] / total[h]).astype(bf16)
            log_total = top[h] + jnp.log(total[h])
            lse_ref[i, h] = jnp.transpose(jnp.broadcast_to(log_total, (rows, HP)))[:8]
        part[...] = dot_nt(mixed_ref[i], wo_ref[...])

    cuts = pieces_of(rows)
    attend(3)
    for k in range(PARTS):
        collect.give_side(k, part[cuts[k]])
    background.advance()
    attend(2)
    for k in range(PARTS):
        collect.give_over(k, part[cuts[k]])
    attend(1)
    collect.give_near(part[...])
    attend(0)
    mid_ref[...] = collect.finish(part[...] + h_ref[...].astype(f32))
    background.advance()
    out.wait()
    spread.end()
    collect.end()
    background.finish()


def attn_call(grid, plan, hidden, gain_row, facts, found):
    rows, width = hidden.shape
    halves = grid.Z // 2
    heads = 2 * halves
    offsets, blocks = apart(found)
    shape = (halves, 4, rows, HP)
    return fused_call(
        grid, functools.partial(attn_kernel, grid, heads, offsets), "attn", plan,
        (
            hidden, gain_row, facts["cos"], facts["sin"], facts["tok_row"], facts["tok_col"],
            facts["from_col"], *blocks,
        ),
        [VMEM] * 7 + [ANY] * len(blocks),
        shaped(
            ((4, rows, width), bf16), ((heads,) + shape[1:], bf16), (shape, bf16), (shape, bf16),
            ((rows, width), f32), ((4, rows, heads * HP), bf16), ((4, heads, 8, rows), f32),
        ),
        (ANY,) + (VMEM,) * 6,
        [
            *attn_weights(grid, found, width),
            pltpu.VMEM((4, rows, width), bf16), Spread.sems, pltpu.SemaphoreType.DMA,
            pltpu.VMEM((heads, rows, 1), f32),
            pltpu.VMEM((heads, rows, 1), f32),
            pltpu.VMEM((heads, rows, HP), f32),
            pltpu.VMEM((rows, width), f32),
        ]
        + Collect.scratch(rows, width),
        60,
    )


def fetch_attn(grid, offsets, pieces, stage, sems):
    pos = grid.my_pos()
    core = lax.axis_index("fsdp") % grid.C
    halves = grid.Z // 2
    fetched = []
    for i, offset in enumerate(offsets):
        yy, zz = grid.dyn_place(pos + offset)
        copy = pltpu.make_async_copy(pieces[i], stage.at[yy * halves + zz % halves], sems.at[i])
        live = zz // halves == core
        pl.when(live)(copy.start)
        fetched.append((live, copy))
    return fetched


def end_fetch(grid, fetched, stage, qkv, out):
    for live, copy in fetched:
        pl.when(live)(copy.wait)
    halves = grid.Z // 2
    share_rows = stage.shape[1] // grid.C
    depth = share_rows * 2 // 3
    half = depth // 2

    def put(ref, first, count, at, head):
        blank = jnp.zeros((count, HP - HD), bf16)
        ref[first : first + count, at * HP : (at + 1) * HP] = jnp.concatenate([head, blank], 1)

    for yy in range(grid.Y):
        for j in range(halves):
            block = stage.at[yy * halves + j]
            for core in range(grid.C):
                first, base = (yy * grid.C + core) * depth, core * share_rows
                for n, at in enumerate((2 * j, 2 * j + 1, 2 * halves + j, 3 * halves + j)):
                    put(qkv, first, depth, at, block[base : base + depth, n * HD : (n + 1) * HD])
                for n in range(4):
                    head = block[base + depth : base + share_rows, n * HD : (n + 1) * HD]
                    put(out, first + n // 2 * half, half, 2 * j + n % 2, head)


def attn_weights(grid, found, width):
    tall, halves = found[0][1].shape[0], grid.Z // 2
    return [
        pltpu.VMEM((grid.Y * halves, tall, BLOCK), bf16),
        pltpu.SemaphoreType.DMA((len(found),)),
        pltpu.VMEM((width, 4 * halves * HP), bf16),
        pltpu.VMEM((width, 2 * halves * HP), bf16),
    ]


def apart(found):
    return [offset for offset, _ in found], [block for _, block in found]


def place_id(grid):
    x, _, c, z = grid.me()
    return [2 * cc + (xx + z) % 2 for xx, cc in ((x, c), (x, 1 - c), (1 - x, c), (1 - x, 1 - c))]


def fetch_ffn(grid, offsets, pieces, held, sems):
    pos = grid.my_pos()
    _, tall, units = pieces[0].shape
    copies = []
    for i, offset in enumerate(offsets):
        yy, zz = grid.dyn_place(pos + offset)
        rows = pl.ds(pl.multiple_of(yy * tall, tall), tall)
        cols = pl.ds(pl.multiple_of(zz * units, units), units)
        copy = pltpu.make_async_copy(pieces[i], held.at[:, rows, cols], sems.at[i])
        copy.start()
        copies.append(copy)
    return copies


STEP = 512


def ffn_kernel(grid, offsets, background, cycle, mid_ref, gain_ref, *refs):
    count = len(offsets)
    pieces = refs[:count]
    (
        out_ref, all_ref, *stored,
        held, w_sems, rows_ref, s_sems, part, own, hold, c_sems, out_sem,
        gate_ref, up_ref, hid_ref, g_sems,
    ) = refs[count:]
    rows, width = mid_ref.shape
    hidden = gate_ref.shape[2]
    writes = []

    def store(slot):
        for n, (src, dst) in enumerate(zip((gate_ref, up_ref, hid_ref), stored)):
            writes.append(pltpu.make_async_copy(src.at[slot], dst.at[slot], g_sems.at[n, slot]))
            writes[-1].start()

    background.begin()
    fetched = fetch_ffn(grid, offsets, pieces, held, w_sems)
    sib, over, _ = greet(grid, 2, cycle)
    rows_ref[0] = normed_rows(mid_ref[...], gain_ref[...]).astype(bf16)
    spread = Spread(rows_ref, s_sems, sib, over)
    collect = Collect(hold, c_sems, sib, over)
    spread.start()
    background.advance()
    for copy in fetched:
        copy.wait()

    def work(slots, start, size):
        at = pl.ds(start, size)
        tall = size * len(slots)

        def rows_of(ref):
            return jnp.concatenate([ref[slot, at] for slot in slots], 0)

        def put(ref, cols, values):
            for n, slot in enumerate(slots):
                ref[slot, at, cols] = values[n * size : (n + 1) * size].astype(bf16)

        def tile(n, carry):
            cols = pl.ds(pl.multiple_of(n * STEP, STEP), STEP)
            some = rows_of(rows_ref)
            gate = jnp.dot(some, held[0, :, cols], preferred_element_type=f32)
            up = jnp.dot(some, held[1, :, cols], preferred_element_type=f32)
            put(gate_ref, cols, gate)
            put(up_ref, cols, up)
            put(hid_ref, cols, gate * jax.nn.sigmoid(gate) * up)
            return carry

        lax.fori_loop(0, hidden // STEP, tile, 0)

        def tile_down(n, carry):
            cols = pl.ds(pl.multiple_of(n * STEP, STEP), STEP)
            part[:tall, cols] = dot_nt(rows_of(hid_ref), held[2, cols])
            return carry

        lax.fori_loop(0, width // STEP, tile_down, 0)

    work((0,), 0, rows)
    store(0)
    own[...] = mid_ref[...] + part[...]
    spread.near.wait_recv()
    work((1,), 0, rows)
    store(1)
    collect.give_near(part[...])
    background.advance()
    cuts = pieces_of(rows)
    size = rows // PARTS
    for k in range(PARTS):
        spread.pass_on(k)
        if k:
            background.advance()
        spread.relay[k].wait_recv()
        work((3, 2), k * size, size)
        collect.give_side(k, part[:size])
        collect.give_over(k, part[size : 2 * size])
    store(2)
    store(3)
    background.advance()
    out = pltpu.make_async_copy(rows_ref, all_ref, out_sem)
    out.start()
    out_ref[...] = collect.finish(own[...]).astype(bf16)
    out.wait()
    wait_all(writes)
    spread.end()
    collect.end()
    background.finish()


def ffn_call(grid, plan, middle, gain_row, found):
    rows, width = middle.shape
    offsets, blocks = [o for o, _ in found], [b for _, b in found]
    hidden = grid.Z * blocks[0].shape[2]
    return fused_call(
        grid, functools.partial(ffn_kernel, grid, offsets), "ffn", plan,
        (middle, gain_row, *blocks), [VMEM] * 2 + [ANY] * len(blocks),
        shaped(((rows, width), bf16), ((4, rows, width), bf16), *[((4, rows, hidden), bf16)] * 3),
        (VMEM,) + (ANY,) * 4,
        [
            pltpu.VMEM((3, width, hidden), bf16),
            pltpu.SemaphoreType.DMA((len(blocks),)),
            pltpu.VMEM((4, rows, width), bf16),
            Spread.sems,
            pltpu.VMEM((rows, width), f32),
            pltpu.VMEM((rows, width), f32),
        ]
        + Collect.scratch(rows, width)
        + [pltpu.SemaphoreType.DMA]
        + [pltpu.VMEM((4, rows, hidden), bf16)] * 3
        + [pltpu.SemaphoreType.DMA((3, 4))],
        44,
    )


TN = (((0,), (0,)), ((), ()))


def weight_terms(out, left, right, step=512):
    whole = right[...].reshape(-1, right.shape[-1])

    def tile(n, carry):
        cols = pl.ds(pl.multiple_of(n * step, step), step)
        some = left[:, :, cols].reshape(-1, step)
        out[cols, :] = lax.dot_general(some, whole, TN, preferred_element_type=f32).astype(bf16)
        return carry

    lax.fori_loop(0, left.shape[-1] // step, tile, 0)


def ffn_back_kernel(
    grid, offsets, background, cycle, g_ref, mid_ref, gain_ref, *refs
):
    count = len(offsets)
    sources, pieces = refs[:4], refs[4 : 4 + count]
    (
        out_ref, gains_ref, terms_ref,
        held, w_sems, rows_ref, s_sems, dgate_ref, dup_ref, part, own, hold, c_sems, out_sems,
        gate_ref, up_ref, hid_ref, whole_ref, in_sems,
    ) = refs[4 + count :]
    rows, width = mid_ref.shape
    hidden = gate_ref.shape[2]
    loads = load(sources, (gate_ref, up_ref, hid_ref, whole_ref), in_sems)
    background.begin()
    fetched = fetch_ffn(grid, offsets, pieces, held, w_sems)
    sib, over, _ = greet(grid, 2, cycle)
    rows_ref[0] = g_ref[...]
    spread = Spread(rows_ref, s_sems, sib, over)
    collect = Collect(hold, c_sems, sib, over)
    spread.start()
    background.advance()
    wait_all(fetched + loads[:2])

    def work(slots, start, size):
        at = pl.ds(start, size)
        tall = size * len(slots)

        def rows_of(ref, cols=slice(None)):
            return jnp.concatenate([ref[slot, at, cols] for slot in slots], 0)

        def put(ref, cols, values):
            for n, slot in enumerate(slots):
                ref[slot, at, cols] = values[n * size : (n + 1) * size].astype(bf16)

        def tile(n, carry):
            cols = pl.ds(pl.multiple_of(n * STEP, STEP), STEP)
            grad = jnp.dot(rows_of(rows_ref), held[2, :, cols], preferred_element_type=f32)
            gate = rows_of(gate_ref, cols).astype(f32)
            up = rows_of(up_ref, cols).astype(f32)
            sig = jax.nn.sigmoid(gate)
            put(dgate_ref, cols, grad * up * sig * (1.0 + gate * (1.0 - sig)))
            put(dup_ref, cols, grad * gate * sig)
            return carry

        lax.fori_loop(0, hidden // STEP, tile, 0)

        def tile_back(n, carry):
            cols = pl.ds(pl.multiple_of(n * STEP, STEP), STEP)
            part[:tall, cols] = dot_nt(rows_of(dgate_ref), held[0, cols]) + dot_nt(
                rows_of(dup_ref), held[1, cols]
            )
            return carry

        lax.fori_loop(0, width // STEP, tile_back, 0)

    work((0,), 0, rows)
    own[...] = part[...]
    spread.near.wait_recv()
    work((1,), 0, rows)
    collect.give_near(part[...])
    background.advance()
    cuts = pieces_of(rows)
    size = rows // PARTS
    for k in range(PARTS):
        spread.pass_on(k)
        if k:
            background.advance()
        spread.relay[k].wait_recv()
        work((3, 2), k * size, size)
        collect.give_side(k, part[:size])
        collect.give_over(k, part[size : 2 * size])
    background.advance()
    wait_all(loads[2:])
    outs = []
    for m, (left, right) in enumerate(
        ((rows_ref, hid_ref), (whole_ref, dgate_ref), (whole_ref, dup_ref))
    ):
        n = (m + 2) % 3
        weight_terms(held.at[n], left, right)
        outs.append(pltpu.make_async_copy(held.at[n], terms_ref.at[n], out_sems.at[n]))
        outs[-1].start()
    second = collect.finish(own[...])
    grad, gains = norm_back(mid_ref[...], gain_ref[...], second)
    out_ref[...] = g_ref[...].astype(f32) + grad
    gains_ref[...] = gains
    background.advance()
    wait_all(outs)
    spread.end()
    collect.end()
    background.finish()


def ffn_back_call(grid, plan, grad_out, middle, gain_row, gate, up, hidden_low, whole, found):
    rows, width = middle.shape
    offsets, blocks = apart(found)
    hidden = gate.shape[2]
    return fused_call(
        grid, functools.partial(ffn_back_kernel, grid, offsets), "ffn_back", plan,
        (grad_out, middle, gain_row, gate, up, hidden_low, whole, *blocks),
        [VMEM] * 3 + [ANY] * (4 + len(blocks)),
        shaped(((rows, width), f32), ((8, width), f32), ((3, width, hidden), bf16)),
        (VMEM, VMEM, ANY),
        [
            pltpu.VMEM((3, width, hidden), bf16),
            pltpu.SemaphoreType.DMA((len(blocks),)),
            pltpu.VMEM((4, rows, width), bf16),
            Spread.sems,
            pltpu.VMEM((4, rows, hidden), bf16),
            pltpu.VMEM((4, rows, hidden), bf16),
            pltpu.VMEM((rows, width), f32),
            pltpu.VMEM((rows, width), f32),
        ]
        + Collect.scratch(rows, width)
        + [pltpu.SemaphoreType.DMA((3,))]
        + [pltpu.VMEM((4, rows, hidden), bf16)] * 3
        + [pltpu.VMEM((4, rows, width), bf16), pltpu.SemaphoreType.DMA((4,))],
        60,
    )


def attn_back_kernel(
    grid, heads, offsets, background, cycle, g_ref, h_ref, gain_ref, l_ref, tokc_ref, tokr_ref,
    from_ref, *refs,
):
    sources, pieces = refs[:7], refs[7 : 7 + len(offsets)]
    (
        out_ref, gains_ref, qkv_term, out_term,
        stage, w_sems, held, wo_ref, rows_ref, s_sems, gm_ref, dqkv_ref, low_ref, low_m, whole_out,
        key_sum, value_sum, query_sum, delta, part, hold, c_sems,
        q_ref, k_ref, v_ref, m_ref, cos_ref, sin_ref, whole_ref, in_sems,
    ) = refs[7 + len(offsets) :]
    rows = g_ref.shape[0]
    pairs = heads // 2
    scale = HD ** (-0.5)
    ids = place_id(grid)
    background.begin()
    fetched = fetch_attn(grid, offsets, pieces, stage, w_sems)
    loads = load(sources, (q_ref, k_ref, v_ref, m_ref, cos_ref, sin_ref, whole_ref), in_sems)
    sib, over, _ = greet(grid, 2, cycle)
    rows_ref[0] = g_ref[...].astype(bf16)
    spread = Spread(rows_ref, s_sems, sib, over)
    spread.start()
    background.advance()
    end_fetch(grid, fetched, stage, held, wo_ref)

    def work(slot, start, size):
        at = slice(start, start + size)
        made = jnp.dot(rows_ref[slot, at], wo_ref[...], preferred_element_type=f32).astype(bf16)
        for h in range(heads):
            gm_ref[h, slot, at] = made[:, h * HP : (h + 1) * HP]

    key_sum[...] = jnp.zeros_like(key_sum)
    value_sum[...] = jnp.zeros_like(value_sum)
    query_sum[...] = jnp.zeros_like(query_sum)

    def attend_back(i):
        for h in range(heads):
            product = gm_ref[h, i].astype(f32) * m_ref[i, :, h * HP : (h + 1) * HP].astype(f32)
            summed = jnp.sum(product, 1, keepdims=True)
            delta[h] = jnp.transpose(jnp.broadcast_to(summed, (rows, HP)))[:8]

        def block(j):
            allowed = (tokc_ref[j] <= tokr_ref[i]) & (tokc_ref[j] >= from_ref[i])
            for h in range(heads):
                query, upstream = q_ref[h, i], gm_ref[h, i]
                key, value = k_ref[h // 2, j], v_ref[h // 2, j]
                scores = jnp.where(allowed, dot_nt(key, query) * scale, NEVER)
                probs = jnp.exp(scores - l_ref[i, h, 0:1])
                value_sum[h // 2, j] += jnp.dot(
                    probs.astype(bf16), upstream, preferred_element_type=f32
                )
                grad_scores = (probs * (dot_nt(value, upstream) - delta[h, 0:1])).astype(bf16)
                key_sum[h // 2, j] += jnp.dot(grad_scores, query, preferred_element_type=f32)
                query_sum[h, i] += lax.dot_general(
                    grad_scores, key, TN, preferred_element_type=f32
                )

        for j in range(4):
            if i == j:
                block(j)
            else:
                pl.when((ids[j] < ids[i]) & (ids[j] >= ids[i] - 2))(functools.partial(block, j))

    work(0, 0, rows)
    spread.near.wait_recv()
    work(1, 0, rows)
    wait_all(loads[:4])
    attend_back(0)
    attend_back(1)
    background.advance()
    size = rows // PARTS
    for k in range(PARTS):
        spread.pass_on(k)
        work(2, k * size, size)
        spread.relay[k].wait_recv()
        work(3, k * size, size)
    attend_back(2)
    attend_back(3)

    def back(summed, at):
        one = summed * scale
        return (one * cos_ref[at] - swapped(one) * sin_ref[at]).astype(bf16)

    collect = Collect(hold, c_sems, sib, over)
    cuts = pieces_of(rows)
    wait_all(loads[4:])

    def work_back(i):
        for at in range(2 * heads):
            if at < heads:
                made, low = back(query_sum[at, i], i), at // 2 * 4 + at % 2
            elif at < heads + pairs:
                made, low = back(key_sum[at - heads, i], i), (at - heads) * 4 + 2
            else:
                h = at - heads - pairs
                made, low = value_sum[h, i].astype(bf16), h * 4 + 3
            dqkv_ref[i, :, at * HP : (at + 1) * HP] = made
            low_ref[i, :, low * HD : (low + 1) * HD] = made[:, :HD]
        part[...] = dot_nt(dqkv_ref[i], held[...])

    work_back(3)
    for k in range(PARTS):
        collect.give_side(k, part[cuts[k]])
    work_back(2)
    for k in range(PARTS):
        collect.give_over(k, part[cuts[k]])
    work_back(1)
    collect.give_near(part[...])
    work_back(0)
    for i in range(4):
        for h in range(heads):
            low_m[i, :, h * HD : (h + 1) * HD] = m_ref[i, :, h * HP : h * HP + HD]
    weight_terms(whole_out, rows_ref, low_m)
    half = out_term.shape[2]
    for n in range(out_term.shape[0]):
        for j in range(pairs):
            cols = slice(2 * j * HD, 2 * (j + 1) * HD)
            out_term[n, j] = jnp.concatenate(
                [whole_out[(2 * n + k) * half : (2 * n + k + 1) * half, cols] for k in range(2)], 1
            )
    weight_terms(qkv_term, whole_ref, low_ref)
    background.advance()
    grad, gains = norm_back(h_ref[...].astype(f32), gain_ref[...], collect.finish(part[...]))
    out_ref[...] = (g_ref[...] + grad).astype(bf16)
    gains_ref[...] = gains
    background.advance()
    spread.end()
    collect.end()
    background.finish()


def attn_back_call(grid, plan, grad_middle, hidden, gain_row, facts, kept, found):
    whole, query, keys, values, mixed, lse = kept
    rows, width = hidden.shape
    depth = width // (grid.Y * grid.C)
    heads = query.shape[0]
    pairs = heads // 2
    offsets, blocks = apart(found)
    return fused_call(
        grid, functools.partial(attn_back_kernel, grid, heads, offsets), "attn_back", plan,
        (
            grad_middle, hidden, gain_row, lse, facts["tok_col"], facts["tok_row"],
            facts["from_row"], query, keys, values, mixed, facts["cos"], facts["sin"], whole,
            *blocks,
        ),
        [VMEM] * 7 + [ANY] * (7 + len(blocks)),
        shaped(
            ((rows, width), bf16), ((8, width), f32), ((width, 2 * heads * HD), bf16),
            ((width // depth, pairs, depth // 2, BLOCK), bf16),
        ),
        (VMEM,) * 4,
        [
            *attn_weights(grid, found, width),
            pltpu.VMEM((4, rows, width), bf16), Spread.sems,
            pltpu.VMEM((heads, 4, rows, HP), bf16),
            pltpu.VMEM((4, rows, 2 * heads * HP), bf16),
            pltpu.VMEM((4, rows, 2 * heads * HD), bf16),
            pltpu.VMEM((4, rows, heads * HD), bf16),
            pltpu.VMEM((width, heads * HD), bf16),
            pltpu.VMEM((pairs, 4, rows, HP), f32),
            pltpu.VMEM((pairs, 4, rows, HP), f32),
            pltpu.VMEM((heads, 4, rows, HP), f32),
            pltpu.VMEM((heads, 8, rows), f32),
            pltpu.VMEM((rows, width), f32),
        ]
        + Collect.scratch(rows, width)
        + [
            pltpu.VMEM((heads, 4, rows, HP), bf16),
            pltpu.VMEM((pairs, 4, rows, HP), bf16),
            pltpu.VMEM((pairs, 4, rows, HP), bf16),
            pltpu.VMEM((4, rows, heads * HP), bf16),
            pltpu.VMEM((4, rows, HP), f32),
            pltpu.VMEM((4, rows, HP), f32),
            pltpu.VMEM((4, rows, width), bf16),
            pltpu.SemaphoreType.DMA((7,)),
        ],
        80,
    )


def start_kernel(
    grid, joins, early, background, cycle, wq, wk, wv, wo, wg, wu, wd, gains_ref, docs_ref, freq_ref,
    all_gains, cos_ref, sin_ref, tok_row, from_row, tok_col, from_col,
    attn_ref, ffn_ref, sems, local, table, land, t_sems, docs_land, begins, d_sems,
):
    x, y, c, z = grid.me()
    mine = z // (grid.Z // 2) == c
    attn_to = [background.refs[h[0]][h[1]] for h in joins[0]]
    ffn_to = [background.refs[h[0]][h[1]] for h in joins[1]]
    depth, units = ffn_ref.shape[2:]
    share_rows = attn_ref.shape[1]
    rows = pl.ds(pl.multiple_of(c * depth, depth), depth)
    attn_rows = pl.ds(pl.multiple_of(c * share_rows, share_rows), share_rows)

    def pack():
        for side in range(2):
            heads = [wq[0, :, 2 * side * HD : 2 * (side + 1) * HD]]
            heads += [ref[0, :, side * HD : (side + 1) * HD] for ref in (wk, wv)]
            turned = jnp.transpose(wo[0, 2 * side * HD : 2 * (side + 1) * HD].astype(f32)).astype(bf16)
            attn_ref[side, :depth] = jnp.concatenate(heads, 1)
            attn_ref[side, depth:] = jnp.concatenate([turned[: depth // 2], turned[depth // 2 :]], 1)

    others = doubling(grid)
    sib, over, diag = greet(grid, 3, cycle, others, pack)
    everything = []
    for layer in range(2):
        to = attn_to[layer].at[attn_rows]
        moves = [
            (mine, pltpu.make_async_copy(attn_ref.at[layer], to, local.at[0])),
            (~mine, remote(attn_ref.at[layer], to, sems, 0, sib)),
            (mine, remote(attn_ref.at[1 - layer], to, sems, 1, over)),
            (~mine, remote(attn_ref.at[1 - layer], to, sems, 2, diag)),
        ]
        into = ffn_to[layer].at[:, rows]
        quarter = lambda side, core: ffn_ref.at[2 * side + core]
        parts = [
            remote(quarter(1 - layer, c), into, sems, 4, over),
            remote(quarter(1 - layer, 1 - c), into, sems, 5, diag),
            remote(quarter(layer, 1 - c), into, sems, 3, sib),
            pltpu.make_async_copy(quarter(layer, c), into, local.at[1]),
        ]
        everything.append((moves, parts))

        @pl.when(x == layer)
        def _():
            for condition, copy in moves:
                pl.when(condition)(copy.start)

    for q in range(4):
        cols = slice(q * units, (q + 1) * units)
        ffn_ref[q, 0] = wg[0, :, cols]
        ffn_ref[q, 1] = wu[0, :, cols]
        ffn_ref[q, 2] = jnp.transpose(wd[0, cols].astype(f32)).astype(bf16)

    (own, to_sib, to_over, to_diag), parts = [copy for _, copy in moves], parts

    @pl.when(mine)
    def _():
        for copy in (to_sib, to_over, to_diag):
            copy.wait_recv()
        own.wait()
        to_over.wait_send()

    @pl.when(~mine)
    def _():
        to_sib.wait_send()
        to_diag.wait_send()

    background.advance()
    for layer in range(2):
        pl.when(x == layer)(functools.partial(start_all, everything[layer][1]))
    shares = grid.Y * grid.C * grid.Z
    share = gains_ref.shape[2]
    table[0] = jnp.zeros_like(table[0])
    padded = jnp.concatenate([gains_ref[0].astype(f32), jnp.zeros((2, HP - share), f32)], 1)
    table[0, (y * grid.C + c) * grid.Z + z, :2, :] = padded
    docs = remote(docs_ref, docs_land, d_sems, 0, sib)
    docs.start()
    for n in sum_over(table, land, t_sems, [sib] + others):
        if n % 2 == 1 and early:
            background.advance()
            early -= 1
    last = len(others) + 1
    copy = remote(table.at[last], land.at[last], t_sems, last, over)
    copy.start()
    copy.wait()
    docs.wait()
    both = jnp.where(z % grid.C == c, docs_ref[...], docs_land[...])
    doc = jnp.where(z // grid.C == 0, both[0], both[1])
    begin = jnp.zeros_like(doc)
    for value in range(1, DOCS):
        before = jnp.sum((doc < value).astype(f32), (0, 1), keepdims=True).astype(jnp.int32)
        begin = jnp.where(doc == value, before, begin)
    begins[...] = begin
    size = tok_row.shape[2]
    per = size // HP
    lane = lax.broadcasted_iota(jnp.int32, (size, HP), 1)
    for n, quarter in enumerate(place_id(grid)):
        rows_of = [begins[pl.ds(quarter * per + k, 1)] for k in range(per)]
        from_row[n] = jnp.concatenate(rows_of, 1)
        tok_row[n] = quarter * size + lax.broadcasted_iota(jnp.int32, (1, size), 1)
        columns = [
            jnp.transpose(jnp.broadcast_to(row.astype(f32), (HP, HP)))[:, :1] for row in rows_of
        ]
        column = jnp.concatenate(columns, 0)
        token = quarter * size + lax.broadcasted_iota(jnp.int32, (size, 1), 0)
        from_col[n] = column.astype(jnp.int32)
        tok_col[n] = token
        angle = (token.astype(f32) - column) * freq_ref[0:1]
        sine = jnp.sin(angle)
        cos_ref[n] = jnp.where(lane < HD, jnp.cos(angle), 0.0)
        sin_ref[n] = jnp.where(lane < HD // 2, -sine, jnp.where(lane < HD, sine, 0.0))
    for p in range(shares):
        own, other = table[last, p, :2, :share], land[last, p, :2, :share]
        at = slice(p * share, (p + 1) * share)
        all_gains[0, :, at] = jnp.where(x == 0, own, other)
        all_gains[1, :, at] = jnp.where(x == 0, other, own)
    for n in range(early):
        background.advance()
    wait_all(parts)
    background.finish()


def start_call(grid, plan, joins, early, shards, gains, doc_ids, rows):
    depth, width = shards[0].shape[1], grid.Y * grid.C * shards[0].shape[1]
    units = shards[4].shape[2] // 4
    hops = len(doubling(grid)) + 1
    table = (hops + 1, grid.Y * grid.C * grid.Z, 8, HP)
    ladder = np.arange(HP) % (HD // 2)
    frequency = np.power(np.float32(rope_base), (-2.0 * ladder / HD).astype(np.float32))
    frequency = jnp.asarray(np.broadcast_to(frequency.astype(np.float32), (8, HP)))
    docs = doc_ids.reshape(doc_ids.shape[0], -1, HP)
    ints = jnp.int32
    gain_all, cosine, sine_part, tok_row, from_row, tok_col, from_col = fused_call(
        grid, functools.partial(start_kernel, grid, joins, early), "start", plan,
        (*shards, gains, docs, frequency), [VMEM] * 10,
        shaped(
            ((2, 2, width), f32), ((4, rows, HP), f32), ((4, rows, HP), f32), ((4, 1, rows), ints),
            ((4, 1, rows), ints), ((4, rows, 1), ints), ((4, rows, 1), ints),
        ),
        (VMEM,) * 7,
        [
            pltpu.VMEM((2, depth * 3 // 2, BLOCK), bf16),
            pltpu.VMEM((4, 3, depth, units), bf16),
            pltpu.SemaphoreType.DMA((2, 6)),
            pltpu.SemaphoreType.DMA((2,)),
            pltpu.VMEM(table, f32),
            pltpu.VMEM(table, f32),
            pltpu.SemaphoreType.DMA((2, hops + 1)),
            pltpu.VMEM(docs.shape, ints),
            pltpu.VMEM(docs.shape[1:], ints),
            pltpu.SemaphoreType.DMA((2, 1)),
        ],
        70,
    )
    return gain_all, {
        "cos": cosine, "sin": sine_part, "tok_row": tok_row, "from_row": from_row,
        "tok_col": tok_col, "from_col": from_col,
    }


def tail_kernel(
    grid, ready, background, cycle, one_0, two_0, one_1, two_1, ffn_own, ffn_came, attn_own, attn_came,
    gain_out, sems, local, table, land, t_sems,
):
    x, _, c, z = grid.me()
    mine = z // (grid.Z // 2) == c
    depth, share_rows = ffn_own.shape[2], attn_own.shape[0]

    def part_of(core, size):
        return pl.ds(pl.multiple_of(core * size, size), size)

    rows, other = part_of(c, depth), part_of(1 - c, depth)
    attn_rows, attn_other = part_of(c, share_rows), part_of(1 - c, share_rows)
    background.begin()
    others = doubling(grid)
    sib, over, diag = greet(grid, 3, cycle, others)
    background.advance()
    table[0] = jnp.concatenate(
        [jnp.sum(ref[...], 0, keepdims=True) for ref in (one_0, two_0, one_1, two_1)]
        + [jnp.zeros((4, table.shape[2]), f32)],
        0,
    )

    def home(n, layer, heads):
        term, parts, alive = background.totals[n]
        for part in parts:
            background.do(alive, functools.partial(background.put, part, False))
        if heads:
            keep = (term.at[attn_rows], attn_own)
            moves = [
                remote(term.at[attn_other], attn_own, sems, 3, sib),
                remote(term.at[attn_rows], attn_came, sems, 4, over),
                remote(term.at[attn_other], attn_came, sems, 5, diag),
            ]
        else:
            keep = (term.at[:, rows], ffn_own.at[c])
            moves = [
                remote(term.at[:, other], ffn_own.at[c], sems, 0, sib),
                remote(term.at[:, rows], ffn_came.at[c], sems, 1, over),
                remote(term.at[:, other], ffn_came.at[c], sems, 2, diag),
            ]
        stay = pltpu.make_async_copy(*keep, local.at[1 if heads else 0])
        here = x == layer
        there = x != layer
        if heads:
            here, there = here & mine, there & mine

        @pl.when(here)
        def _():
            stay.start()
            moves[0].start()

        @pl.when(there)
        def _():
            moves[1].start()
            moves[2].start()

        return stay, moves

    done = {}
    waiting = [(n, rest) for n, *rest in ready]
    hops = sum_over(table, land, t_sems, [over, sib] + others)
    while waiting or background.now < len(background.stages):
        for n, (layer, heads, stage) in list(waiting):
            if stage < max(0, background.now - 1) or background.now >= len(background.stages):
                background.arrived(stage)
                done[heads] = home(n, layer, heads)
                waiting.remove((n, [layer, heads, stage]))
                break
        next(hops, None)
        next(hops, None)
        if background.now < len(background.stages):
            background.advance()
    for _ in hops:
        pass
    gain_out[...] = table[len(others) + 2]
    background.finish()
    stay, moves = done[False]
    stay.wait()
    for copy in moves:
        copy.wait()
    stay, moves = done[True]

    @pl.when(mine)
    def _():
        stay.wait()
        for copy in moves:
            copy.wait_send()
        moves[1].wait_recv()

    @pl.when(~mine)
    def _():
        moves[0].wait_recv()
        moves[2].wait_recv()


def tail_call(grid, plan, ready, gain_rows, depth, units):
    width = gain_rows[0].shape[1]
    hops = len(doubling(grid)) + 2
    table = (hops + 1, 8, width)
    return fused_call(
        grid, functools.partial(tail_kernel, grid, ready), "tail", plan, gain_rows, [VMEM] * 4,
        shaped(
            *[((2, 3, depth, units), bf16)] * 2, *[((depth * 3 // 2, BLOCK), bf16)] * 2, ((8, width), f32)
        ),
        (ANY,) * 4 + (VMEM,),
        [
            pltpu.SemaphoreType.DMA((2, 6)),
            pltpu.SemaphoreType.DMA((2,)),
            pltpu.VMEM(table, f32),
            pltpu.VMEM(table, f32),
            pltpu.SemaphoreType.DMA((2, hops)),
        ],
        60,
    )


def finish_kernel(
    ffn_own, ffn_came, attn_own, attn_came, out_one, out_two, grad_one, grad_two,
    produced, grads, query, key, value, out, gate, up, down,
):
    x = lax.axis_index("section")
    depth, units = ffn_own.shape[2:]

    def put(side, ffn_ref, attn_ref):
        for core in range(2):
            at = slice((2 * side + core) * units, (2 * side + core + 1) * units)
            gate[:, at] = ffn_ref[core, 0].astype(f32)
            up[:, at] = ffn_ref[core, 1].astype(f32)
            down[at] = jnp.transpose(ffn_ref[core, 2].astype(f32))

        def head(n):
            if n < 4:
                return attn_ref[:depth, n * HD : (n + 1) * HD].astype(f32)
            return jnp.concatenate(
                [attn_ref[depth:, k * HD : (k + 1) * HD].astype(f32) for k in (n - 4, n - 2)], 0
            )

        for h in range(2):
            at = slice((2 * side + h) * HD, (2 * side + h + 1) * HD)
            query[:, at] = head(h)
            out[at] = jnp.transpose(head(4 + h))
        key[side * HD : (side + 1) * HD] = jnp.transpose(head(2))
        value[side * HD : (side + 1) * HD] = jnp.transpose(head(3))

    for layer in range(2):

        @pl.when(x == layer)
        def _():
            put(layer, ffn_own, attn_own)
            put(1 - layer, ffn_came, attn_came)
            produced[layer] = out_one[...]
            produced[1 - layer] = out_two[...]
            grads[layer] = grad_one[...].astype(f32)
            grads[1 - layer] = grad_two[...].astype(f32)


def finish_call(blocks, outs, grads, shards):
    shape = (2,) + outs[0].shape
    shapes = [shard.shape[1:] for shard in shards]
    shapes[1:3] = [shape[::-1] for shape in shapes[1:3]]
    produced, grads, query, key, value, *rest = pl.pallas_call(
        finish_kernel,
        out_shape=shaped((shape, bf16), (shape, f32))
        + tuple(jax.ShapeDtypeStruct(one, f32) for one in shapes),
        in_specs=[VMEM] * 8,
        out_specs=(VMEM,) * 9,
        compiler_params=params(),
        cost_estimate=cost(8),
        name="finish",
    )(*blocks, *outs, *grads)
    return produced, grads, query, key.T, value.T, *rest


def after(value, *others):
    return lax.optimization_barrier((value,) + others)[0]


def layer_forward(grid, hidden_in, attn, ffn, nexts, gain_pair, facts):
    plan = Plan()
    ffn.add(plan, 0)
    whole, query, keys, values, middle, mixed, lse = attn_call(
        grid, plan, hidden_in, gain_pair[0:1], facts, attn.found
    )
    plan = Plan()
    if nexts:
        nexts[0].add(plan, 0)
        nexts[1].add(plan, max(0, len(plan.stages) - 2), 1)
    result, whole2, gate, up, hidden = ffn_call(grid, plan, middle, gain_pair[1:2], ffn.found)
    kept = (hidden_in, (whole, query, keys, values, mixed, lse), middle, whole2, gate, up, hidden)
    return result, kept


def layer_backward(grid, grad_out, kept, attn, ffn, gain_pair, facts, running, sum_ffn, sum_attn, leaving):
    hidden_in, kept_attn, middle, whole2, gate, up, hidden = kept
    plan = Plan()
    for ring in running:
        ring.add(plan, 0, min(4, ring.left()))
    grad_middle, gain_two, terms = ffn_back_call(
        grid, plan, grad_out, middle, gain_pair[1:2], gate, up, hidden, whole2, ffn.found
    )
    sums = sum_ffn(terms)
    running.append(sums)
    plan = Plan()
    sums.add(plan, 0, 3)
    grad_input, gain_one, qkv_term, out_term = attn_back_call(
        grid, plan, grad_middle, hidden_in, after(gain_pair[0:1], *leaving), facts, kept_attn, attn.found
    )
    running.append(sum_attn(qkv_term, out_term))
    return grad_input, (gain_one, gain_two)


def body(grid, inputs, doc_ids, cotangent, wq, wk, wv, wo, wg, wu, wd, gains):
    X, Y, C, Z = grid.X, grid.Y, grid.C, grid.Z
    x, y, c, z = grid.me()
    pos = grid.my_pos()
    micro, rows, width = inputs.shape
    depth = wq.shape[1]
    at_zero = x == 0

    def enter(block):
        def route(m):
            def go(x, y, c, z):
                if z % 2 != (x + m * C + c) % 2:
                    return None
                return (x, y, z // 2, m * C + c)

            return go

        first, last = grid.send(block[0], route(0)), grid.send(block[1], route(1))
        return jnp.where(z // C == 0, first, last)

    def leave(lower_block, upper_block):
        first = z // C == 0

        def route(swap):
            def go(x, y, c, z):
                section = (z // C + swap) % 2
                return (section, y, z % C, 2 * c + (x + z) % 2)

            return go

        same = grid.send(jnp.where(first, lower_block, upper_block), route(0))
        swapped_over = grid.send(jnp.where(first, upper_block, lower_block), route(1))
        return same, swapped_over

    rows_in = enter(inputs)
    halves = Z // 2
    tall = C * depth
    units = wg.shape[2] // 4
    share_rows = depth * 3 // 2
    upper, lower = pl.ds(0, tall // 2), pl.ds(tall // 2, tall // 2)
    cores = [pl.ds(core * share_rows, share_rows) for core in range(2)]
    attn_cuts = [((cores[0],), (cores[0],), None), ((cores[1],), None, (cores[1],))]
    ffn_cuts = [((m,), (m, upper), (m, lower)) for m in range(3)]
    attn = [Gather(grid, (C * share_rows, BLOCK), attn_cuts, True) for _ in range(2)]
    ffn = [Gather(grid, (3, tall, units), ffn_cuts) for _ in range(2)]
    plan = Plan()
    joins = [[ring.begin(plan) for ring in rings] for rings in (attn, ffn)]
    attn[0].add(plan, 0)
    ffn[0].add(plan, max(0, len(plan.stages) - 2), 1)
    shards = (wq, wk, wv, wo, wg, wu, wd)
    gain_all, facts = start_call(
        grid, plan, joins, max(0, len(plan.stages) - 3), shards, gains, doc_ids, rows
    )

    hidden = rows_in
    kept = []
    for s in range(2):
        nexts = (attn[1], ffn[1]) if s == 0 else None
        hidden, keep = layer_forward(grid, hidden, attn[s], ffn[s], nexts, gain_all[s], facts)
        kept.append(keep)
    rows_cot = enter(after(cotangent, kept[1][2]))
    outs = leave(after(kept[1][0], hidden, rows_cot), after(hidden, rows_cot))

    def sum_ffn(terms):
        def block(m):
            return lambda yy, zz: (
                m,
                pl.ds(pl.multiple_of(yy * tall, tall), tall),
                pl.ds(pl.multiple_of(zz * units, units), units),
            )

        parts = [(cuts, [(terms, block(m), (m,))]) for m, cuts in enumerate(ffn_cuts)]
        return Scatter(grid, parts, (3, tall, units))

    def sum_attn(qkv_term, out_term):
        def top(core):
            return lambda yy, zz: (
                pl.ds(pl.multiple_of((yy * C + core) * depth, depth), depth),
                pl.ds(pl.multiple_of(zz % halves * BLOCK, BLOCK), BLOCK),
            )

        def below(core):
            return lambda yy, zz: (yy * C + core, zz % halves)

        parts = []
        for core in range(C):
            first = core * share_rows
            places = [
                (qkv_term, top(core), (pl.ds(first, depth),)),
                (out_term, below(core), (pl.ds(first + depth, depth // 2),)),
            ]
            parts.append((attn_cuts[core], places))
        return Scatter(grid, parts, (C * share_rows, BLOCK), True)

    upstream = rows_cot
    gain_terms, running = [None] * 2, []
    waited, grads = outs, [None] * 2
    for s in (1, 0):
        upstream, gain_terms[s] = layer_backward(
            grid, upstream, kept[s], attn[s], ffn[s], gain_all[s], facts, running, sum_ffn, sum_attn, waited
        )
        grads[s], waited = upstream, ()
    grads_in = leave(*grads)
    plan = Plan()
    ready = []
    for n in (3, 2, 1, 0):
        left = running[n].left()
        running[n].add(plan, 0, left, True)
        ready.append((1 - n // 2, n % 2 == 1, left - 1))
        running[n].total(plan)
    order = sorted(range(4), key=lambda n: ready[n][2])
    ready = [(n,) + ready[n] for n in order]
    *blocks, gain_sum = tail_call(grid, plan, ready, gain_terms[0] + gain_terms[1], depth, units)

    produced, grads_in, *terms = finish_call(blocks, outs, grads_in, shards)
    share = gains.shape[2]
    mine = (y * C + c) * Z + z
    gain_share = lax.dynamic_slice(gain_sum, (2 * x, mine * share), (2, share))[None]
    return (
        produced[None],
        grads_in[None],
        *[term[None] for term in terms],
        gain_share,
    )


def solution(mesh):
    grid = Grid(mesh)

    def run(*arguments):
        grid.calls = 0
        return body(grid, *arguments)

    return jax.shard_map(
        run,
        mesh=mesh,
        in_specs=(
            P(None, ("fsdp", "tensor"), None),
            P(None, "fsdp", None),
            P(None, ("fsdp", "tensor"), None),
            P("section", "fsdp", "tensor"),
            P("section", "fsdp", "tensor"),
            P("section", "fsdp", "tensor"),
            P("section", "tensor", "fsdp"),
            P("section", "fsdp", "tensor"),
            P("section", "fsdp", "tensor"),
            P("section", "tensor", "fsdp"),
            P("section", None, ("fsdp", "tensor")),
        ),
        out_specs=(
            P("section", None, ("fsdp", "tensor"), None),
            P("section", None, ("fsdp", "tensor"), None),
            P("section", "fsdp", "tensor"),
            P("section", "fsdp", "tensor"),
            P("section", "fsdp", "tensor"),
            P("section", "tensor", "fsdp"),
            P("section", "fsdp", "tensor"),
            P("section", "fsdp", "tensor"),
            P("section", "tensor", "fsdp"),
            P("section", None, ("fsdp", "tensor")),
        ),
        check_vma=False,
    )
```

```python
import functools

import jax
import jax.numpy as jnp
import numpy as np
import jax.experimental.pallas as pl
import jax.experimental.pallas.tpu as pltpu
from jax import lax
from jax.sharding import PartitionSpec as P

HD = 96
DOCS = 4
HP = 128
NEVER = -1e30
BLOCK = 4 * HD
epsilon = 1e-05
rope_base = 100000.0
AXES = ("section", "fsdp", "tensor")
bf16 = jnp.bfloat16
f32 = jnp.float32


class Grid:
    def __init__(self, mesh):
        self.calls = 0
        self.X = mesh.shape["section"]
        self.C = 2
        self.Y = mesh.shape["fsdp"] // self.C
        self.Z = mesh.shape["tensor"]
        self.R = self.Y * self.Z
        self.places = [
            (x, y, c, z)
            for x in range(self.X)
            for y in range(self.Y)
            for c in range(self.C)
            for z in range(self.Z)
        ]

    def rank(self, place):
        x, y, c, z = place
        return ((x * self.Y + y) * self.C + c) * self.Z + z

    def send(self, block, route):
        pairs = []
        for place in self.places:
            goal = route(*place)
            if goal is not None:
                pairs.append((self.rank(place), self.rank(goal)))
        return lax.ppermute(block, AXES, pairs)

    def over_x(self, block):
        return self.send(block, lambda x, y, c, z: (1 - x, y, c, z))

    def over_c(self, block):
        return self.send(block, lambda x, y, c, z: (x, y, 1 - c, z))

    def place_of(self, p):
        p = p % self.R
        y, k = p // self.Z, p % self.Z
        return (y, k if y % 2 == 0 else self.Z - 1 - k)

    def pos_of(self, y, z):
        return y * self.Z + (z if y % 2 == 0 else self.Z - 1 - z)

    def neighbour(self, way):
        yy, zz = self.dyn_place(self.my_pos() + way)
        return {"fsdp": yy * self.C + lax.axis_index("fsdp") % self.C, "tensor": zz}

    def me(self):
        x = lax.axis_index("section")
        f = lax.axis_index("fsdp")
        z = lax.axis_index("tensor")
        return x, f // self.C, f % self.C, z

    def my_pos(self):
        x, y, c, z = self.me()
        return y * self.Z + jnp.where(y % 2 == 0, z, self.Z - 1 - z)

    def dyn_place(self, p):
        p = (p + 2 * self.R) % self.R
        y, k = p // self.Z, p % self.Z
        return y, jnp.where(y % 2 == 0, k, self.Z - 1 - k)

def params(limit=56):
    return pltpu.CompilerParams(vmem_limit_bytes=limit * 1024 * 1024)


def whole_vmem(count):
    return [pl.BlockSpec(memory_space=pltpu.VMEM)] * count


def cost(micros):
    return pl.CostEstimate(flops=int(micros * 1.0e9), bytes_accessed=1 << 20, transcendentals=0)


def swapped(values):
    lane = lax.broadcasted_iota(jnp.int32, values.shape, 1)
    half = HD // 2
    return jnp.where(lane < half, pltpu.roll(values, HP - half, 1), pltpu.roll(values, half, 1))


MESH = pl.DeviceIdType.MESH
NT = (((1,), (1,)), ((), ()))
PARTS = 2


def dot_nt(a, b):
    return lax.dot_general(a, b, NT, preferred_element_type=f32)


def partners(grid):
    x, y, c, _ = grid.me()
    return (
        {"fsdp": y * grid.C + 1 - c},
        {"section": 1 - x},
        {"section": 1 - x, "fsdp": y * grid.C + 1 - c},
    )


def doubling(grid):
    _, y, c, z = grid.me()
    found = []
    for bit in range((grid.Y - 1).bit_length()):
        step = 1 << bit
        found.append({"fsdp": (y + step * (1 - 2 * ((y // step) % 2))) * grid.C + c})
    for bit in range((grid.Z - 1).bit_length()):
        step = 1 << bit
        found.append({"tensor": z + step * (1 - 2 * ((z // step) % 2))})
    return found


def greet(grid, sides, cycle, more=(), meanwhile=lambda: None):
    others = list(partners(grid)[:sides]) + list(more)
    if cycle:
        others += [grid.neighbour(1), grid.neighbour(-1)]
    barrier = pltpu.get_barrier_semaphore()
    for other in others:
        pl.semaphore_signal(barrier, inc=1, device_id=other, device_id_type=MESH)
    meanwhile()
    pl.semaphore_wait(barrier, len(others))
    return partners(grid)


def sum_over(table, land, sems, others):
    for n, other in enumerate(others):
        copy = remote(table.at[n], land.at[n], sems, n, other)
        copy.start()
        copy.wait()
        table[n + 1] = table[n] + land[n]
        yield n


def remote(src, dst, sems, n, device):
    return pltpu.make_async_remote_copy(
        src_ref=src, dst_ref=dst, send_sem=sems.at[0, n], recv_sem=sems.at[1, n],
        device_id=device, device_id_type=MESH,
    )


def pieces_of(rows):
    size = rows // PARTS
    return [pl.ds(k * size, size) for k in range(PARTS)]


def start_all(copies):
    for copy in copies:
        copy.start()


def wait_all(copies):
    for copy in copies:
        copy.wait()


class Plan:
    def __init__(self):
        self.inputs, self.outs, self.lands, self.stages, self.hooks = [], [], [], [], []
        self.slots, self.makes, self.totals, self.moves, self.copies = [], [], [], 0, 1

    def give(self, array):
        for n, known in enumerate(self.inputs):
            if known is array:
                return ("in", n)
        self.inputs.append(array)
        return ("in", len(self.inputs) - 1)

    def room(self, shape):
        self.outs.append(jax.ShapeDtypeStruct(shape, bf16))
        return ("out", len(self.outs) - 1)

    def land(self, shape):
        self.lands.append(shape)
        return ("land", len(self.lands) - 1)

    def slot(self, key, shape):
        if (key, shape) not in self.slots:
            self.slots.append((key, shape))
        return self.slots.index((key, shape))

    def make(self, stage, key, shape, parts, offset, owned):
        slot = self.slot(key, shape)
        made = []
        for places, came in parts:
            copies = [(self.give(array), src, dst) for array, src, dst in places]
            joins = [(h if isinstance(h, tuple) else self.give(h), at) for h, at in came]
            made.append((copies, joins))
        self.copies = max(self.copies, sum(len(c) + len(j) for c, j in made))
        self.makes.append((stage, slot, made, offset, owned))
        return ("make", len(self.makes) - 1)

    def move(self, stage, src, dst, way, offset, owned, cut, part=0, needs=None):
        while len(self.stages) <= stage:
            self.stages.append([])
        self.stages[stage].append((self.moves, src, dst, way, offset, owned, cut, part, needs))
        self.moves += 1
        return self.moves - 1

    def scratch(self):
        if not self.moves:
            return []
        held = [pltpu.VMEM(shape, bf16) for _, shape in self.slots for _ in range(2)]
        held += [pltpu.VMEM(shape, bf16) for shape in self.lands]
        sems = [pltpu.SemaphoreType.DMA((2, self.moves))]
        if self.slots:
            sems.append(pltpu.SemaphoreType.DMA((len(self.slots), self.copies)))
        return held + sems

    def settle(self, results):
        for hook in self.hooks:
            hook(lambda handle: self.inputs[handle[1]] if handle[0] == "in" else results[handle[1]])


class Background:
    def __init__(self, grid, plan, ins, outs, rest):
        self.stages, self.totals, self.now, self.sent = [], [], -1, 0
        if not plan.moves:
            return
        pos = grid.my_pos()
        core = lax.axis_index("fsdp") % grid.C
        count = 2 * len(plan.slots)
        held, lands = rest[:count], rest[count : count + len(plan.lands)]
        sems = rest[count + len(plan.lands)]
        local = rest[-1]
        self.refs = {"in": ins, "out": outs, "land": lands}

        def live(owned, offset):
            if not owned:
                return None
            return grid.dyn_place(pos + offset)[1] // (grid.Z // 2) == core

        def built(slot, made, offset, owned):
            term, more = held[2 * slot], held[2 * slot + 1]
            yy, zz = grid.dyn_place(pos + offset)
            n, parts = 0, []
            for copies, joins in made:
                fetches, adds = [], []
                for handle, src, dst in copies:
                    ref = self.refs[handle[0]][handle[1]].at[src(yy, zz)]
                    fetches.append(pltpu.make_async_copy(ref, term.at[dst], local.at[slot, n]))
                    n += 1
                for handle, at in joins:
                    ref = self.refs[handle[0]][handle[1]]
                    if handle[0] == "land":
                        adds.append((None, ref, at))
                    else:
                        copy = pltpu.make_async_copy(ref.at[at], more.at[at], local.at[slot, n])
                        adds.append((copy, more, at))
                    n += 1
                parts.append((fetches, adds, term, handle_early(joins)))
            return parts, live(owned, offset)

        def handle_early(joins):
            return all(handle[0] == "in" for handle, _ in joins)

        self.makes = [[] for _ in plan.stages]
        buffers = []
        for stage, slot, made, offset, owned in plan.makes:
            parts, alive = built(slot, made, offset, owned)
            self.makes[stage].append((parts, alive))
            buffers.append((held[2 * slot], parts, alive))
        for slot, made, owned in plan.totals:
            self.totals.append((held[2 * slot],) + built(slot, made, 0, owned))
        self.all = {}
        for stage in plan.stages:
            row = []
            for number, src, dst, way, offset, owned, cut, part, needs in stage:
                put = None
                if src[0] == "make":
                    src_ref, parts, alive = buffers[src[1]]
                    put = (parts[part], alive)
                else:
                    src_ref = self.refs[src[0]][src[1]]
                dst_ref = self.refs[dst[0]][dst[1]]
                copy = remote(src_ref.at[cut], dst_ref.at[cut], sems, number, grid.neighbour(way))
                self.all[number] = (copy, live(owned, offset), live(owned, offset - way))
                row.append((number, put, needs))
            self.stages.append(row)
        self.come, self.put_done = set(), set()

    @staticmethod
    def do(condition, action):
        if condition is None:
            action()
        else:
            pl.when(condition)(action)

    def fetch(self, stage):
        if stage < len(self.stages):
            for parts, alive in self.makes[stage]:
                for fetches, adds, _, early in parts:
                    copies = fetches + [copy for copy, _, _ in adds if copy is not None and early]
                    self.do(alive, functools.partial(start_all, copies))

    def begin(self):
        self.fetch(0)
        for _, parts, alive in self.totals:
            for fetches, _, _, _ in parts:
                self.do(alive, functools.partial(start_all, fetches))

    @staticmethod
    def put(part, started=True):
        fetches, adds, term, early = part
        wait_all(fetches)
        for copy, ref, at in adds:
            if copy is not None:
                if not (early and started):
                    copy.start()
                copy.wait()
            term[at] = (term[at].astype(f32) + ref[at].astype(f32)).astype(bf16)

    def arrive(self, number):
        if number is not None and number not in self.come:
            self.come.add(number)
            copy, _, come = self.all[number]
            self.do(come, copy.wait_recv)

    def advance(self):
        self.now += 1
        if self.now < len(self.stages):
            for number, put, needs in self.stages[self.now]:
                for need in needs or ():
                    self.arrive(need)
                if put is not None and id(put[0]) not in self.put_done:
                    self.put_done.add(id(put[0]))
                    self.do(put[1], functools.partial(self.put, put[0]))
                copy, go, _ = self.all[number]
                self.do(go, copy.start)
            if self.now + 1 < len(self.stages):
                self.wait_sends(self.now)
                self.fetch(self.now + 1)
        if self.now >= len(self.stages):
            for row in self.stages:
                for number, _, _ in row:
                    self.arrive(number)

    def arrived(self, stage):
        for row in self.stages[: stage + 1]:
            for number, _, _ in row:
                self.arrive(number)

    def wait_sends(self, stage):
        while self.sent < stage:
            for number, _, _ in self.stages[self.sent]:
                copy, go, _ = self.all[number]
                self.do(go, copy.wait_send)
            self.sent += 1

    def finish(self):
        while self.now < len(self.stages):
            self.advance()
        self.wait_sends(len(self.stages))


class Gather:
    def __init__(self, grid, shape, cuts, owned=False):
        self.grid, self.owned, self.shape, self.cuts = grid, owned, shape, cuts
        self.k, self.total = 0, grid.R // 2

    def begin(self, plan):
        room = plan.room(self.shape)
        self.up = self.down = room

        def hook(get):
            self.found = [(0, get(room))]
            if self.k == 0:
                self.up = self.down = get(room)

        plan.hooks.append(hook)
        return room

    def left(self):
        return self.total - self.k

    def add(self, plan, stage, hops=None):
        hops = self.left() if hops is None else min(hops, self.left())
        if hops == 0:
            return
        one = self.up is self.down
        up = self.up if isinstance(self.up, tuple) else plan.give(self.up)
        down = up if one else plan.give(self.down)
        new = []
        before = [(None, None)] * len(self.cuts)
        for n in range(hops):
            self.k += 1
            k = self.k
            last = k == self.total
            to_up = plan.room(self.shape)
            to_down = to_up if last else plan.room(self.shape)
            now = []
            for (cut, first, second), (need_up, need_down) in zip(self.cuts, before):
                pair = (first, second) if last else (cut, cut)
                moved = []
                for src, dst, way, part, need in (
                    (up, to_up, 1, pair[0], need_up), (down, to_down, -1, pair[1], need_down)
                ):
                    moved.append(
                        None
                        if part is None
                        else plan.move(
                            stage + n, src, dst, way, -way * (k - 1), self.owned, part,
                            needs=(need,),
                        )
                    )
                now.append(tuple(moved))
            before = now
            new.append((-k, to_up))
            if not last:
                new.append((k, to_down))
            up, down = to_up, to_down

        def hook(get):
            self.up, self.down = get(up), get(down)
            self.found += [(offset, get(handle)) for offset, handle in new]

        plan.hooks.append(hook)


class Scatter:
    def __init__(self, grid, parts, shape, owned=False):
        self.grid, self.parts, self.shape, self.owned = grid, parts, shape, owned
        self.k = grid.R // 2
        self.held = {1: None, -1: None}

    def left(self):
        return self.k

    def came(self, way, n):
        if self.held[way] is None:
            return []
        block, column = self.held[way]
        at = self.parts[n][0][column]
        return [] if at is None else [(block, at)]

    def add(self, plan, stage, steps=1, final=False):
        steps = min(steps, self.k)
        before = {way: [None] * len(self.parts) for way in (1, -1)}
        for n in range(steps):
            k = self.k
            self.k -= 1
            room = plan.land if n < steps - 1 or final else plan.room
            rooms = {way: room(self.shape) for way in (1, -1)}
            halves = k == self.grid.R // 2
            blocks = {}
            for way in (1, -1):
                if halves and way == -1:
                    blocks[way] = blocks[1]
                    continue
                parts = [(places, self.came(way, m)) for m, (_, places) in enumerate(self.parts)]
                blocks[way] = plan.make(
                    stage + n, (id(self), way, n % 2), self.shape, parts, way * k, self.owned
                )
            now = {1: [], -1: []}
            for m, (cuts, _) in enumerate(self.parts):
                for way in (1, -1):
                    column = (1 if way == 1 else 2) if halves else 0
                    moved = None
                    if cuts[column] is not None:
                        moved = plan.move(
                            stage + n, blocks[way], rooms[way], way, way * k, self.owned, cuts[column],
                            m, (before[way][m],),
                        )
                    now[way].append(moved)
            before = now
            self.held = {
                way: (rooms[way], (1 if way == 1 else 2) if halves else 0) for way in (1, -1)
            }

        def hook(get):
            self.held = {
                way: (get(block), column) if block[0] == "out" else (None, column)
                for way, (block, column) in self.held.items()
            }

        if steps:
            plan.hooks.append(hook)

    def total(self, plan):
        parts = [
            (places, self.came(1, m) + self.came(-1, m)) for m, (_, places) in enumerate(self.parts)
        ]
        slot = plan.slot(("total", id(self)), self.shape)
        made = []
        for places, came in parts:
            copies = [(plan.give(array), src, dst) for array, src, dst in places]
            joins = [(h if isinstance(h, tuple) else plan.give(h), at) for h, at in came]
            made.append((copies, joins))
        plan.copies = max(plan.copies, sum(len(c) + len(j) for c, j in made))
        plan.totals.append((slot, made, self.owned))


def fused_call(grid, kernel, name, plan, inputs, in_specs, outs, out_specs, scratch, micros):
    plan = Plan() if plan is None else plan
    a, b, c, d = len(inputs), len(plan.inputs), len(outs), len(plan.outs)
    moves = plan.moves

    def whole(*refs):
        fg_in, bg_in = refs[:a], refs[a : a + b]
        fg_out, bg_out = refs[a + b : a + b + c], refs[a + b + c : a + b + c + d]
        rest = refs[a + b + c + d :]
        own = len(scratch)
        background = Background(grid, plan, bg_in, bg_out, rest[own:])
        kernel(background, bool(moves), *fg_in, *fg_out, *rest[:own])

    number = grid.calls
    grid.calls += 1
    results = pl.pallas_call(
        whole,
        out_shape=tuple(outs) + tuple(plan.outs),
        in_specs=list(in_specs) + [ANY] * b,
        out_specs=tuple(out_specs) + (ANY,) * d,
        scratch_shapes=list(scratch) + plan.scratch(),
        compiler_params=remote_params(number),
        cost_estimate=cost(micros),
        name=name,
    )(*inputs, *plan.inputs)
    plan.settle(results[c:])
    return results[:c]


def load(sources, places, sems):
    copies = [
        pltpu.make_async_copy(src, dst, sems.at[n]) for n, (src, dst) in enumerate(zip(sources, places))
    ]
    start_all(copies)
    return copies


class Spread:
    sems = pltpu.SemaphoreType.DMA((2, 1 + 2 * PARTS))

    def __init__(self, rows_ref, sems, sib, over):
        cuts = pieces_of(rows_ref.shape[1])
        self.near = remote(rows_ref.at[0], rows_ref.at[1], sems, 0, sib)
        self.far = [
            remote(rows_ref.at[0, at], rows_ref.at[2, at], sems, 1 + k, over)
            for k, at in enumerate(cuts)
        ]
        self.relay = [
            remote(rows_ref.at[2, at], rows_ref.at[3, at], sems, 1 + PARTS + k, sib)
            for k, at in enumerate(cuts)
        ]

    def start(self):
        for copy in self.far:
            copy.start()
        self.near.start()

    def pass_on(self, k):
        self.far[k].wait_recv()
        self.relay[k].start()

    def end(self):
        self.near.wait_send()
        for copy in self.far + self.relay:
            copy.wait_send()


class Collect:
    sems = pltpu.SemaphoreType.DMA((2, 1 + 2 * PARTS))

    @staticmethod
    def scratch(rows, width):
        return [pltpu.VMEM((6, rows, width), bf16), Collect.sems]

    def __init__(self, hold, sems, sib, over):
        self.hold = hold
        self.cuts = pieces_of(hold.shape[1])
        self.near = remote(hold.at[0], hold.at[2], sems, 0, sib)
        self.side = [
            remote(hold.at[1, at], hold.at[3, at], sems, 1 + k, sib)
            for k, at in enumerate(self.cuts)
        ]
        self.over = [
            remote(hold.at[4, at], hold.at[5, at], sems, 1 + PARTS + k, over)
            for k, at in enumerate(self.cuts)
        ]

    def give_near(self, part):
        self.hold[0] = part.astype(bf16)
        self.near.start()

    def give_side(self, k, part):
        self.hold[1, self.cuts[k]] = part.astype(bf16)
        self.side[k].start()

    def give_over(self, k, part):
        self.side[k].wait_recv()
        self.hold[4, self.cuts[k]] = (part + self.hold[3, self.cuts[k]].astype(f32)).astype(bf16)
        self.over[k].start()

    def finish(self, part):
        self.near.wait_recv()
        part = part + self.hold[2].astype(f32)
        for copy in self.over:
            copy.wait_recv()
        return part + self.hold[5].astype(f32)

    def end(self):
        self.near.wait_send()
        for copy in self.side + self.over:
            copy.wait_send()


def normed_rows(values, gain_row):
    return values * lax.rsqrt(jnp.mean(values * values, -1, keepdims=True) + epsilon) * gain_row


def norm_back(values, gain_row, upstream):
    scale = lax.rsqrt(jnp.mean(values * values, -1, keepdims=True) + epsilon)
    unit = values * scale
    moved = upstream * gain_row
    grad = scale * (moved - unit * jnp.mean(moved * unit, -1, keepdims=True))
    gains = upstream * unit
    return grad, jnp.sum(gains.reshape(-1, 8, gains.shape[-1]), 0)


def remote_params(number, limit=58):
    return pltpu.CompilerParams(
        vmem_limit_bytes=limit * 1024 * 1024, collective_id=number, has_side_effects=True
    )


def shaped(*pairs):
    return tuple(jax.ShapeDtypeStruct(shape, dtype) for shape, dtype in pairs)


ANY = pl.BlockSpec(memory_space=pl.ANY)
VMEM = pl.BlockSpec(memory_space=pltpu.VMEM)


def attn_kernel(
    grid, heads, offsets, background, cycle, h_ref, gain_ref, cos_ref, sin_ref, tokk_ref, tokq_ref,
    from_ref, *refs,
):
    pieces = refs[: len(offsets)]
    (
        all_ref, q_ref, k_ref, v_ref, mid_ref, mixed_ref, lse_ref,
        stage, w_sems, held, wo_ref, rows_ref, s_sems, out_sem, top, total, acc, part, hold, c_sems,
    ) = refs[len(offsets) :]
    rows = h_ref.shape[0]
    halves = heads // 2
    scale = HD ** (-0.5)
    ids = place_id(grid)
    background.begin()
    fetched = fetch_attn(grid, offsets, pieces, stage, w_sems)
    sib, over, _ = greet(grid, 2, cycle)
    rows_ref[0] = normed_rows(h_ref[...].astype(f32), gain_ref[...]).astype(bf16)
    spread = Spread(rows_ref, s_sems, sib, over)
    spread.start()
    background.advance()
    end_fetch(grid, fetched, stage, held, wo_ref)

    def work(slot, start, size):
        cosine, sine_part = cos_ref[slot, start : start + size], sin_ref[slot, start : start + size]
        at = slice(start, start + size)
        made = jnp.dot(rows_ref[slot, at], held[...], preferred_element_type=f32)
        for h in range(3 * halves):
            one = made[:, h * HP : (h + 1) * HP]
            turned = (one * cosine + swapped(one) * sine_part).astype(bf16)
            if h < 2 * halves:
                q_ref[h, slot, at] = turned
            else:
                k_ref[h - 2 * halves, slot, at] = turned
        for h in range(halves):
            v_ref[h, slot, at] = made[:, (3 * halves + h) * HP : (3 * halves + h + 1) * HP].astype(bf16)

    work(0, 0, rows)
    spread.near.wait_recv()
    work(1, 0, rows)
    size = rows // PARTS
    for k in range(PARTS):
        spread.pass_on(k)
        work(2, k * size, size)
        spread.relay[k].wait_recv()
        work(3, k * size, size)
    out = pltpu.make_async_copy(rows_ref, all_ref, out_sem)
    out.start()
    collect = Collect(hold, c_sems, sib, over)

    def attend(i):
        tok_q, begin = tokq_ref[i], from_ref[i]

        def block(j, first):
            tok_k = tokk_ref[j]
            allowed = (tok_k <= tok_q) & (tok_k >= begin)
            for h in range(heads):
                scores = dot_nt(q_ref[h, i], k_ref[h // 2, j])
                scores = jnp.where(allowed, scores * scale, NEVER)
                peak = jnp.max(scores, 1, keepdims=True)
                if not first:
                    before = top[h]
                    peak = jnp.maximum(peak, before)
                raised = jnp.exp(scores - peak)
                summed = jnp.sum(raised, 1, keepdims=True)
                got = jnp.dot(raised.astype(bf16), v_ref[h // 2, j], preferred_element_type=f32)
                if first:
                    total[h] = summed
                    acc[h] = got
                else:
                    shrink = jnp.exp(before - peak)
                    total[h] = total[h] * shrink + summed
                    acc[h] = acc[h] * shrink + got
                top[h] = peak

        block(i, True)
        for j in range(4):
            if j != i:
                pl.when((ids[j] < ids[i]) & (ids[j] >= ids[i] - 2))(functools.partial(block, j, False))
        for h in range(heads):
            mixed_ref[i, :, h * HP : (h + 1) * HP] = (acc[h] / total[h]).astype(bf16)
            log_total = top[h] + jnp.log(total[h])
            lse_ref[i, h] = jnp.transpose(jnp.broadcast_to(log_total, (rows, HP)))[:8]
        part[...] = dot_nt(mixed_ref[i], wo_ref[...])

    cuts = pieces_of(rows)
    attend(3)
    for k in range(PARTS):
        collect.give_side(k, part[cuts[k]])
    background.advance()
    attend(2)
    for k in range(PARTS):
        collect.give_over(k, part[cuts[k]])
    attend(1)
    collect.give_near(part[...])
    attend(0)
    mid_ref[...] = collect.finish(part[...] + h_ref[...].astype(f32))
    background.advance()
    out.wait()
    spread.end()
    collect.end()
    background.finish()


def attn_call(grid, plan, hidden, gain_row, facts, found):
    rows, width = hidden.shape
    halves = grid.Z // 2
    heads = 2 * halves
    offsets, blocks = apart(found)
    shape = (halves, 4, rows, HP)
    return fused_call(
        grid, functools.partial(attn_kernel, grid, heads, offsets), "attn", plan,
        (
            hidden, gain_row, facts["cos"], facts["sin"], facts["tok_row"], facts["tok_col"],
            facts["from_col"], *blocks,
        ),
        [VMEM] * 7 + [ANY] * len(blocks),
        shaped(
            ((4, rows, width), bf16), ((heads,) + shape[1:], bf16), (shape, bf16), (shape, bf16),
            ((rows, width), f32), ((4, rows, heads * HP), bf16), ((4, heads, 8, rows), f32),
        ),
        (ANY,) + (VMEM,) * 6,
        [
            *attn_weights(grid, found, width),
            pltpu.VMEM((4, rows, width), bf16), Spread.sems, pltpu.SemaphoreType.DMA,
            pltpu.VMEM((heads, rows, 1), f32),
            pltpu.VMEM((heads, rows, 1), f32),
            pltpu.VMEM((heads, rows, HP), f32),
            pltpu.VMEM((rows, width), f32),
        ]
        + Collect.scratch(rows, width),
        60,
    )


def fetch_attn(grid, offsets, pieces, stage, sems):
    pos = grid.my_pos()
    core = lax.axis_index("fsdp") % grid.C
    halves = grid.Z // 2
    fetched = []
    for i, offset in enumerate(offsets):
        yy, zz = grid.dyn_place(pos + offset)
        copy = pltpu.make_async_copy(pieces[i], stage.at[yy * halves + zz % halves], sems.at[i])
        live = zz // halves == core
        pl.when(live)(copy.start)
        fetched.append((live, copy))
    return fetched


def end_fetch(grid, fetched, stage, qkv, out):
    for live, copy in fetched:
        pl.when(live)(copy.wait)
    halves = grid.Z // 2
    share_rows = stage.shape[1] // grid.C
    depth = share_rows * 2 // 3
    half = depth // 2

    def put(ref, first, count, at, head):
        blank = jnp.zeros((count, HP - HD), bf16)
        ref[first : first + count, at * HP : (at + 1) * HP] = jnp.concatenate([head, blank], 1)

    for yy in range(grid.Y):
        for j in range(halves):
            block = stage.at[yy * halves + j]
            for core in range(grid.C):
                first, base = (yy * grid.C + core) * depth, core * share_rows
                for n, at in enumerate((2 * j, 2 * j + 1, 2 * halves + j, 3 * halves + j)):
                    put(qkv, first, depth, at, block[base : base + depth, n * HD : (n + 1) * HD])
                for n in range(4):
                    head = block[base + depth : base + share_rows, n * HD : (n + 1) * HD]
                    put(out, first + n // 2 * half, half, 2 * j + n % 2, head)


def attn_weights(grid, found, width):
    tall, halves = found[0][1].shape[0], grid.Z // 2
    return [
        pltpu.VMEM((grid.Y * halves, tall, BLOCK), bf16),
        pltpu.SemaphoreType.DMA((len(found),)),
        pltpu.VMEM((width, 4 * halves * HP), bf16),
        pltpu.VMEM((width, 2 * halves * HP), bf16),
    ]


def apart(found):
    return [offset for offset, _ in found], [block for _, block in found]


def place_id(grid):
    x, _, c, z = grid.me()
    return [2 * cc + (xx + z) % 2 for xx, cc in ((x, c), (x, 1 - c), (1 - x, c), (1 - x, 1 - c))]


def fetch_ffn(grid, offsets, pieces, held, sems):
    pos = grid.my_pos()
    _, tall, units = pieces[0].shape
    copies = []
    for i, offset in enumerate(offsets):
        yy, zz = grid.dyn_place(pos + offset)
        rows = pl.ds(pl.multiple_of(yy * tall, tall), tall)
        cols = pl.ds(pl.multiple_of(zz * units, units), units)
        copy = pltpu.make_async_copy(pieces[i], held.at[:, rows, cols], sems.at[i])
        copy.start()
        copies.append(copy)
    return copies


STEP = 512


def ffn_kernel(grid, offsets, background, cycle, mid_ref, gain_ref, *refs):
    count = len(offsets)
    pieces = refs[:count]
    (
        out_ref, all_ref, *stored,
        held, w_sems, rows_ref, s_sems, part, own, hold, c_sems, out_sem,
        gate_ref, up_ref, hid_ref, g_sems,
    ) = refs[count:]
    rows, width = mid_ref.shape
    hidden = gate_ref.shape[2]
    writes = []

    def store(slot):
        for n, (src, dst) in enumerate(zip((gate_ref, up_ref, hid_ref), stored)):
            writes.append(pltpu.make_async_copy(src.at[slot], dst.at[slot], g_sems.at[n, slot]))
            writes[-1].start()

    background.begin()
    fetched = fetch_ffn(grid, offsets, pieces, held, w_sems)
    sib, over, _ = greet(grid, 2, cycle)
    rows_ref[0] = normed_rows(mid_ref[...], gain_ref[...]).astype(bf16)
    spread = Spread(rows_ref, s_sems, sib, over)
    collect = Collect(hold, c_sems, sib, over)
    spread.start()
    background.advance()
    for copy in fetched:
        copy.wait()

    def work(slots, start, size):
        at = pl.ds(start, size)
        tall = size * len(slots)

        def rows_of(ref):
            return jnp.concatenate([ref[slot, at] for slot in slots], 0)

        def put(ref, cols, values):
            for n, slot in enumerate(slots):
                ref[slot, at, cols] = values[n * size : (n + 1) * size].astype(bf16)

        def tile(n, carry):
            cols = pl.ds(pl.multiple_of(n * STEP, STEP), STEP)
            some = rows_of(rows_ref)
            gate = jnp.dot(some, held[0, :, cols], preferred_element_type=f32)
            up = jnp.dot(some, held[1, :, cols], preferred_element_type=f32)
            put(gate_ref, cols, gate)
            put(up_ref, cols, up)
            put(hid_ref, cols, gate * jax.nn.sigmoid(gate) * up)
            return carry

        lax.fori_loop(0, hidden // STEP, tile, 0)

        def tile_down(n, carry):
            cols = pl.ds(pl.multiple_of(n * STEP, STEP), STEP)
            part[:tall, cols] = dot_nt(rows_of(hid_ref), held[2, cols])
            return carry

        lax.fori_loop(0, width // STEP, tile_down, 0)

    work((0,), 0, rows)
    store(0)
    own[...] = mid_ref[...] + part[...]
    spread.near.wait_recv()
    work((1,), 0, rows)
    store(1)
    collect.give_near(part[...])
    background.advance()
    cuts = pieces_of(rows)
    size = rows // PARTS
    for k in range(PARTS):
        spread.pass_on(k)
        if k:
            background.advance()
        spread.relay[k].wait_recv()
        work((3, 2), k * size, size)
        collect.give_side(k, part[:size])
        collect.give_over(k, part[size : 2 * size])
    store(2)
    store(3)
    background.advance()
    out = pltpu.make_async_copy(rows_ref, all_ref, out_sem)
    out.start()
    out_ref[...] = collect.finish(own[...]).astype(bf16)
    out.wait()
    wait_all(writes)
    spread.end()
    collect.end()
    background.finish()


def ffn_call(grid, plan, middle, gain_row, found):
    rows, width = middle.shape
    offsets, blocks = [o for o, _ in found], [b for _, b in found]
    hidden = grid.Z * blocks[0].shape[2]
    return fused_call(
        grid, functools.partial(ffn_kernel, grid, offsets), "ffn", plan,
        (middle, gain_row, *blocks), [VMEM] * 2 + [ANY] * len(blocks),
        shaped(((rows, width), bf16), ((4, rows, width), bf16), *[((4, rows, hidden), bf16)] * 3),
        (VMEM,) + (ANY,) * 4,
        [
            pltpu.VMEM((3, width, hidden), bf16),
            pltpu.SemaphoreType.DMA((len(blocks),)),
            pltpu.VMEM((4, rows, width), bf16),
            Spread.sems,
            pltpu.VMEM((rows, width), f32),
            pltpu.VMEM((rows, width), f32),
        ]
        + Collect.scratch(rows, width)
        + [pltpu.SemaphoreType.DMA]
        + [pltpu.VMEM((4, rows, hidden), bf16)] * 3
        + [pltpu.SemaphoreType.DMA((3, 4))],
        44,
    )


TN = (((0,), (0,)), ((), ()))


def weight_terms(out, left, right, step=512):
    whole = right[...].reshape(-1, right.shape[-1])

    def tile(n, carry):
        cols = pl.ds(pl.multiple_of(n * step, step), step)
        some = left[:, :, cols].reshape(-1, step)
        out[cols, :] = lax.dot_general(some, whole, TN, preferred_element_type=f32).astype(bf16)
        return carry

    lax.fori_loop(0, left.shape[-1] // step, tile, 0)


def ffn_back_kernel(
    grid, offsets, background, cycle, g_ref, mid_ref, gain_ref, *refs
):
    count = len(offsets)
    sources, pieces = refs[:4], refs[4 : 4 + count]
    (
        out_ref, gains_ref, terms_ref,
        held, w_sems, rows_ref, s_sems, dgate_ref, dup_ref, part, own, hold, c_sems, out_sems,
        gate_ref, up_ref, hid_ref, whole_ref, in_sems,
    ) = refs[4 + count :]
    rows, width = mid_ref.shape
    hidden = gate_ref.shape[2]
    loads = load(sources, (gate_ref, up_ref, hid_ref, whole_ref), in_sems)
    background.begin()
    fetched = fetch_ffn(grid, offsets, pieces, held, w_sems)
    sib, over, _ = greet(grid, 2, cycle)
    rows_ref[0] = g_ref[...]
    spread = Spread(rows_ref, s_sems, sib, over)
    collect = Collect(hold, c_sems, sib, over)
    spread.start()
    background.advance()
    wait_all(fetched + loads[:2])

    def work(slots, start, size):
        at = pl.ds(start, size)
        tall = size * len(slots)

        def rows_of(ref, cols=slice(None)):
            return jnp.concatenate([ref[slot, at, cols] for slot in slots], 0)

        def put(ref, cols, values):
            for n, slot in enumerate(slots):
                ref[slot, at, cols] = values[n * size : (n + 1) * size].astype(bf16)

        def tile(n, carry):
            cols = pl.ds(pl.multiple_of(n * STEP, STEP), STEP)
            grad = jnp.dot(rows_of(rows_ref), held[2, :, cols], preferred_element_type=f32)
            gate = rows_of(gate_ref, cols).astype(f32)
            up = rows_of(up_ref, cols).astype(f32)
            sig = jax.nn.sigmoid(gate)
            put(dgate_ref, cols, grad * up * sig * (1.0 + gate * (1.0 - sig)))
            put(dup_ref, cols, grad * gate * sig)
            return carry

        lax.fori_loop(0, hidden // STEP, tile, 0)

        def tile_back(n, carry):
            cols = pl.ds(pl.multiple_of(n * STEP, STEP), STEP)
            part[:tall, cols] = dot_nt(rows_of(dgate_ref), held[0, cols]) + dot_nt(
                rows_of(dup_ref), held[1, cols]
            )
            return carry

        lax.fori_loop(0, width // STEP, tile_back, 0)

    work((0,), 0, rows)
    own[...] = part[...]
    spread.near.wait_recv()
    work((1,), 0, rows)
    collect.give_near(part[...])
    background.advance()
    cuts = pieces_of(rows)
    size = rows // PARTS
    for k in range(PARTS):
        spread.pass_on(k)
        if k:
            background.advance()
        spread.relay[k].wait_recv()
        work((3, 2), k * size, size)
        collect.give_side(k, part[:size])
        collect.give_over(k, part[size : 2 * size])
    background.advance()
    wait_all(loads[2:])
    outs = []
    for m, (left, right) in enumerate(
        ((rows_ref, hid_ref), (whole_ref, dgate_ref), (whole_ref, dup_ref))
    ):
        n = (m + 2) % 3
        weight_terms(held.at[n], left, right)
        outs.append(pltpu.make_async_copy(held.at[n], terms_ref.at[n], out_sems.at[n]))
        outs[-1].start()
    second = collect.finish(own[...])
    grad, gains = norm_back(mid_ref[...], gain_ref[...], second)
    out_ref[...] = g_ref[...].astype(f32) + grad
    gains_ref[...] = gains
    background.advance()
    wait_all(outs)
    spread.end()
    collect.end()
    background.finish()


def ffn_back_call(grid, plan, grad_out, middle, gain_row, gate, up, hidden_low, whole, found):
    rows, width = middle.shape
    offsets, blocks = apart(found)
    hidden = gate.shape[2]
    return fused_call(
        grid, functools.partial(ffn_back_kernel, grid, offsets), "ffn_back", plan,
        (grad_out, middle, gain_row, gate, up, hidden_low, whole, *blocks),
        [VMEM] * 3 + [ANY] * (4 + len(blocks)),
        shaped(((rows, width), f32), ((8, width), f32), ((3, width, hidden), bf16)),
        (VMEM, VMEM, ANY),
        [
            pltpu.VMEM((3, width, hidden), bf16),
            pltpu.SemaphoreType.DMA((len(blocks),)),
            pltpu.VMEM((4, rows, width), bf16),
            Spread.sems,
            pltpu.VMEM((4, rows, hidden), bf16),
            pltpu.VMEM((4, rows, hidden), bf16),
            pltpu.VMEM((rows, width), f32),
            pltpu.VMEM((rows, width), f32),
        ]
        + Collect.scratch(rows, width)
        + [pltpu.SemaphoreType.DMA((3,))]
        + [pltpu.VMEM((4, rows, hidden), bf16)] * 3
        + [pltpu.VMEM((4, rows, width), bf16), pltpu.SemaphoreType.DMA((4,))],
        60,
    )


def attn_back_kernel(
    grid, heads, offsets, background, cycle, g_ref, h_ref, gain_ref, l_ref, tokc_ref, tokr_ref,
    from_ref, *refs,
):
    sources, pieces = refs[:7], refs[7 : 7 + len(offsets)]
    (
        out_ref, gains_ref, qkv_term, out_term,
        stage, w_sems, held, wo_ref, rows_ref, s_sems, gm_ref, dqkv_ref, low_ref, low_m, whole_out,
        key_sum, value_sum, query_sum, delta, part, hold, c_sems,
        q_ref, k_ref, v_ref, m_ref, cos_ref, sin_ref, whole_ref, in_sems,
    ) = refs[7 + len(offsets) :]
    rows = g_ref.shape[0]
    pairs = heads // 2
    scale = HD ** (-0.5)
    ids = place_id(grid)
    background.begin()
    fetched = fetch_attn(grid, offsets, pieces, stage, w_sems)
    loads = load(sources, (q_ref, k_ref, v_ref, m_ref, cos_ref, sin_ref, whole_ref), in_sems)
    sib, over, _ = greet(grid, 2, cycle)
    rows_ref[0] = g_ref[...].astype(bf16)
    spread = Spread(rows_ref, s_sems, sib, over)
    spread.start()
    background.advance()
    end_fetch(grid, fetched, stage, held, wo_ref)

    def work(slot, start, size):
        at = slice(start, start + size)
        made = jnp.dot(rows_ref[slot, at], wo_ref[...], preferred_element_type=f32).astype(bf16)
        for h in range(heads):
            gm_ref[h, slot, at] = made[:, h * HP : (h + 1) * HP]

    key_sum[...] = jnp.zeros_like(key_sum)
    value_sum[...] = jnp.zeros_like(value_sum)
    query_sum[...] = jnp.zeros_like(query_sum)

    def attend_back(i):
        for h in range(heads):
            product = gm_ref[h, i].astype(f32) * m_ref[i, :, h * HP : (h + 1) * HP].astype(f32)
            summed = jnp.sum(product, 1, keepdims=True)
            delta[h] = jnp.transpose(jnp.broadcast_to(summed, (rows, HP)))[:8]

        def block(j):
            allowed = (tokc_ref[j] <= tokr_ref[i]) & (tokc_ref[j] >= from_ref[i])
            for h in range(heads):
                query, upstream = q_ref[h, i], gm_ref[h, i]
                key, value = k_ref[h // 2, j], v_ref[h // 2, j]
                scores = jnp.where(allowed, dot_nt(key, query) * scale, NEVER)
                probs = jnp.exp(scores - l_ref[i, h, 0:1])
                value_sum[h // 2, j] += jnp.dot(
                    probs.astype(bf16), upstream, preferred_element_type=f32
                )
                grad_scores = (probs * (dot_nt(value, upstream) - delta[h, 0:1])).astype(bf16)
                key_sum[h // 2, j] += jnp.dot(grad_scores, query, preferred_element_type=f32)
                query_sum[h, i] += lax.dot_general(
                    grad_scores, key, TN, preferred_element_type=f32
                )

        for j in range(4):
            if i == j:
                block(j)
            else:
                pl.when((ids[j] < ids[i]) & (ids[j] >= ids[i] - 2))(functools.partial(block, j))

    work(0, 0, rows)
    spread.near.wait_recv()
    work(1, 0, rows)
    wait_all(loads[:4])
    attend_back(0)
    attend_back(1)
    background.advance()
    size = rows // PARTS
    for k in range(PARTS):
        spread.pass_on(k)
        work(2, k * size, size)
        spread.relay[k].wait_recv()
        work(3, k * size, size)
    attend_back(2)
    attend_back(3)

    def back(summed, at):
        one = summed * scale
        return (one * cos_ref[at] - swapped(one) * sin_ref[at]).astype(bf16)

    collect = Collect(hold, c_sems, sib, over)
    cuts = pieces_of(rows)
    wait_all(loads[4:])

    def work_back(i):
        for at in range(2 * heads):
            if at < heads:
                made, low = back(query_sum[at, i], i), at // 2 * 4 + at % 2
            elif at < heads + pairs:
                made, low = back(key_sum[at - heads, i], i), (at - heads) * 4 + 2
            else:
                h = at - heads - pairs
                made, low = value_sum[h, i].astype(bf16), h * 4 + 3
            dqkv_ref[i, :, at * HP : (at + 1) * HP] = made
            low_ref[i, :, low * HD : (low + 1) * HD] = made[:, :HD]
        part[...] = dot_nt(dqkv_ref[i], held[...])

    work_back(3)
    for k in range(PARTS):
        collect.give_side(k, part[cuts[k]])
    work_back(2)
    for k in range(PARTS):
        collect.give_over(k, part[cuts[k]])
    work_back(1)
    collect.give_near(part[...])
    work_back(0)
    for i in range(4):
        for h in range(heads):
            low_m[i, :, h * HD : (h + 1) * HD] = m_ref[i, :, h * HP : h * HP + HD]
    weight_terms(whole_out, rows_ref, low_m)
    half = out_term.shape[2]
    for n in range(out_term.shape[0]):
        for j in range(pairs):
            cols = slice(2 * j * HD, 2 * (j + 1) * HD)
            out_term[n, j] = jnp.concatenate(
                [whole_out[(2 * n + k) * half : (2 * n + k + 1) * half, cols] for k in range(2)], 1
            )
    weight_terms(qkv_term, whole_ref, low_ref)
    background.advance()
    grad, gains = norm_back(h_ref[...].astype(f32), gain_ref[...], collect.finish(part[...]))
    out_ref[...] = (g_ref[...] + grad).astype(bf16)
    gains_ref[...] = gains
    background.advance()
    spread.end()
    collect.end()
    background.finish()


def attn_back_call(grid, plan, grad_middle, hidden, gain_row, facts, kept, found):
    whole, query, keys, values, mixed, lse = kept
    rows, width = hidden.shape
    depth = width // (grid.Y * grid.C)
    heads = query.shape[0]
    pairs = heads // 2
    offsets, blocks = apart(found)
    return fused_call(
        grid, functools.partial(attn_back_kernel, grid, heads, offsets), "attn_back", plan,
        (
            grad_middle, hidden, gain_row, lse, facts["tok_col"], facts["tok_row"],
            facts["from_row"], query, keys, values, mixed, facts["cos"], facts["sin"], whole,
            *blocks,
        ),
        [VMEM] * 7 + [ANY] * (7 + len(blocks)),
        shaped(
            ((rows, width), bf16), ((8, width), f32), ((width, 2 * heads * HD), bf16),
            ((width // depth, pairs, depth // 2, BLOCK), bf16),
        ),
        (VMEM,) * 4,
        [
            *attn_weights(grid, found, width),
            pltpu.VMEM((4, rows, width), bf16), Spread.sems,
            pltpu.VMEM((heads, 4, rows, HP), bf16),
            pltpu.VMEM((4, rows, 2 * heads * HP), bf16),
            pltpu.VMEM((4, rows, 2 * heads * HD), bf16),
            pltpu.VMEM((4, rows, heads * HD), bf16),
            pltpu.VMEM((width, heads * HD), bf16),
            pltpu.VMEM((pairs, 4, rows, HP), f32),
            pltpu.VMEM((pairs, 4, rows, HP), f32),
            pltpu.VMEM((heads, 4, rows, HP), f32),
            pltpu.VMEM((heads, 8, rows), f32),
            pltpu.VMEM((rows, width), f32),
        ]
        + Collect.scratch(rows, width)
        + [
            pltpu.VMEM((heads, 4, rows, HP), bf16),
            pltpu.VMEM((pairs, 4, rows, HP), bf16),
            pltpu.VMEM((pairs, 4, rows, HP), bf16),
            pltpu.VMEM((4, rows, heads * HP), bf16),
            pltpu.VMEM((4, rows, HP), f32),
            pltpu.VMEM((4, rows, HP), f32),
            pltpu.VMEM((4, rows, width), bf16),
            pltpu.SemaphoreType.DMA((7,)),
        ],
        80,
    )


def start_kernel(
    grid, joins, early, background, cycle, wq, wk, wv, wo, wg, wu, wd, gains_ref, docs_ref, freq_ref,
    all_gains, cos_ref, sin_ref, tok_row, from_row, tok_col, from_col,
    attn_ref, ffn_ref, sems, local, table, land, t_sems, docs_land, begins, d_sems,
):
    x, y, c, z = grid.me()
    mine = z // (grid.Z // 2) == c
    attn_to = [background.refs[h[0]][h[1]] for h in joins[0]]
    ffn_to = [background.refs[h[0]][h[1]] for h in joins[1]]
    depth, units = ffn_ref.shape[2:]
    share_rows = attn_ref.shape[1]
    rows = pl.ds(pl.multiple_of(c * depth, depth), depth)
    attn_rows = pl.ds(pl.multiple_of(c * share_rows, share_rows), share_rows)

    def pack():
        for side in range(2):
            heads = [wq[0, :, 2 * side * HD : 2 * (side + 1) * HD]]
            heads += [ref[0, :, side * HD : (side + 1) * HD] for ref in (wk, wv)]
            turned = jnp.transpose(wo[0, 2 * side * HD : 2 * (side + 1) * HD].astype(f32)).astype(bf16)
            attn_ref[side, :depth] = jnp.concatenate(heads, 1)
            attn_ref[side, depth:] = jnp.concatenate([turned[: depth // 2], turned[depth // 2 :]], 1)

    others = doubling(grid)
    sib, over, diag = greet(grid, 3, cycle, others, pack)
    everything = []
    for layer in range(2):
        to = attn_to[layer].at[attn_rows]
        moves = [
            (mine, pltpu.make_async_copy(attn_ref.at[layer], to, local.at[0])),
            (~mine, remote(attn_ref.at[layer], to, sems, 0, sib)),
            (mine, remote(attn_ref.at[1 - layer], to, sems, 1, over)),
            (~mine, remote(attn_ref.at[1 - layer], to, sems, 2, diag)),
        ]
        into = ffn_to[layer].at[:, rows]
        quarter = lambda side, core: ffn_ref.at[2 * side + core]
        parts = [
            remote(quarter(1 - layer, c), into, sems, 4, over),
            remote(quarter(1 - layer, 1 - c), into, sems, 5, diag),
            remote(quarter(layer, 1 - c), into, sems, 3, sib),
            pltpu.make_async_copy(quarter(layer, c), into, local.at[1]),
        ]
        everything.append((moves, parts))

        @pl.when(x == layer)
        def _():
            for condition, copy in moves:
                pl.when(condition)(copy.start)

    for q in range(4):
        cols = slice(q * units, (q + 1) * units)
        ffn_ref[q, 0] = wg[0, :, cols]
        ffn_ref[q, 1] = wu[0, :, cols]
        ffn_ref[q, 2] = jnp.transpose(wd[0, cols].astype(f32)).astype(bf16)

    (own, to_sib, to_over, to_diag), parts = [copy for _, copy in moves], parts

    @pl.when(mine)
    def _():
        for copy in (to_sib, to_over, to_diag):
            copy.wait_recv()
        own.wait()
        to_over.wait_send()

    @pl.when(~mine)
    def _():
        to_sib.wait_send()
        to_diag.wait_send()

    background.advance()
    for layer in range(2):
        pl.when(x == layer)(functools.partial(start_all, everything[layer][1]))
    shares = grid.Y * grid.C * grid.Z
    share = gains_ref.shape[2]
    table[0] = jnp.zeros_like(table[0])
    padded = jnp.concatenate([gains_ref[0].astype(f32), jnp.zeros((2, HP - share), f32)], 1)
    table[0, (y * grid.C + c) * grid.Z + z, :2, :] = padded
    docs = remote(docs_ref, docs_land, d_sems, 0, sib)
    docs.start()
    for n in sum_over(table, land, t_sems, [sib] + others):
        if n % 2 == 1 and early:
            background.advance()
            early -= 1
    last = len(others) + 1
    copy = remote(table.at[last], land.at[last], t_sems, last, over)
    copy.start()
    copy.wait()
    docs.wait()
    both = jnp.where(z % grid.C == c, docs_ref[...], docs_land[...])
    doc = jnp.where(z // grid.C == 0, both[0], both[1])
    begin = jnp.zeros_like(doc)
    for value in range(1, DOCS):
        before = jnp.sum((doc < value).astype(f32), (0, 1), keepdims=True).astype(jnp.int32)
        begin = jnp.where(doc == value, before, begin)
    begins[...] = begin
    size = tok_row.shape[2]
    per = size // HP
    lane = lax.broadcasted_iota(jnp.int32, (size, HP), 1)
    for n, quarter in enumerate(place_id(grid)):
        rows_of = [begins[pl.ds(quarter * per + k, 1)] for k in range(per)]
        from_row[n] = jnp.concatenate(rows_of, 1)
        tok_row[n] = quarter * size + lax.broadcasted_iota(jnp.int32, (1, size), 1)
        columns = [
            jnp.transpose(jnp.broadcast_to(row.astype(f32), (HP, HP)))[:, :1] for row in rows_of
        ]
        column = jnp.concatenate(columns, 0)
        token = quarter * size + lax.broadcasted_iota(jnp.int32, (size, 1), 0)
        from_col[n] = column.astype(jnp.int32)
        tok_col[n] = token
        angle = (token.astype(f32) - column) * freq_ref[0:1]
        sine = jnp.sin(angle)
        cos_ref[n] = jnp.where(lane < HD, jnp.cos(angle), 0.0)
        sin_ref[n] = jnp.where(lane < HD // 2, -sine, jnp.where(lane < HD, sine, 0.0))
    for p in range(shares):
        own, other = table[last, p, :2, :share], land[last, p, :2, :share]
        at = slice(p * share, (p + 1) * share)
        all_gains[0, :, at] = jnp.where(x == 0, own, other)
        all_gains[1, :, at] = jnp.where(x == 0, other, own)
    for n in range(early):
        background.advance()
    wait_all(parts)
    background.finish()


def start_call(grid, plan, joins, early, shards, gains, doc_ids, rows):
    depth, width = shards[0].shape[1], grid.Y * grid.C * shards[0].shape[1]
    units = shards[4].shape[2] // 4
    hops = len(doubling(grid)) + 1
    table = (hops + 1, grid.Y * grid.C * grid.Z, 8, HP)
    ladder = np.arange(HP) % (HD // 2)
    frequency = np.power(np.float32(rope_base), (-2.0 * ladder / HD).astype(np.float32))
    frequency = jnp.asarray(np.broadcast_to(frequency.astype(np.float32), (8, HP)))
    docs = doc_ids.reshape(doc_ids.shape[0], -1, HP)
    ints = jnp.int32
    gain_all, cosine, sine_part, tok_row, from_row, tok_col, from_col = fused_call(
        grid, functools.partial(start_kernel, grid, joins, early), "start", plan,
        (*shards, gains, docs, frequency), [VMEM] * 10,
        shaped(
            ((2, 2, width), f32), ((4, rows, HP), f32), ((4, rows, HP), f32), ((4, 1, rows), ints),
            ((4, 1, rows), ints), ((4, rows, 1), ints), ((4, rows, 1), ints),
        ),
        (VMEM,) * 7,
        [
            pltpu.VMEM((2, depth * 3 // 2, BLOCK), bf16),
            pltpu.VMEM((4, 3, depth, units), bf16),
            pltpu.SemaphoreType.DMA((2, 6)),
            pltpu.SemaphoreType.DMA((2,)),
            pltpu.VMEM(table, f32),
            pltpu.VMEM(table, f32),
            pltpu.SemaphoreType.DMA((2, hops + 1)),
            pltpu.VMEM(docs.shape, ints),
            pltpu.VMEM(docs.shape[1:], ints),
            pltpu.SemaphoreType.DMA((2, 1)),
        ],
        70,
    )
    return gain_all, {
        "cos": cosine, "sin": sine_part, "tok_row": tok_row, "from_row": from_row,
        "tok_col": tok_col, "from_col": from_col,
    }


def tail_kernel(
    grid, ready, background, cycle, one_0, two_0, one_1, two_1, ffn_own, ffn_came, attn_own, attn_came,
    gain_out, sems, local, table, land, t_sems,
):
    x, _, c, z = grid.me()
    mine = z // (grid.Z // 2) == c
    depth, share_rows = ffn_own.shape[2], attn_own.shape[0]

    def part_of(core, size):
        return pl.ds(pl.multiple_of(core * size, size), size)

    rows, other = part_of(c, depth), part_of(1 - c, depth)
    attn_rows, attn_other = part_of(c, share_rows), part_of(1 - c, share_rows)
    background.begin()
    others = doubling(grid)
    sib, over, diag = greet(grid, 3, cycle, others)
    background.advance()
    table[0] = jnp.concatenate(
        [jnp.sum(ref[...], 0, keepdims=True) for ref in (one_0, two_0, one_1, two_1)]
        + [jnp.zeros((4, table.shape[2]), f32)],
        0,
    )

    def home(n, layer, heads):
        term, parts, alive = background.totals[n]
        for part in parts:
            background.do(alive, functools.partial(background.put, part, False))
        if heads:
            keep = (term.at[attn_rows], attn_own)
            moves = [
                remote(term.at[attn_other], attn_own, sems, 3, sib),
                remote(term.at[attn_rows], attn_came, sems, 4, over),
                remote(term.at[attn_other], attn_came, sems, 5, diag),
            ]
        else:
            keep = (term.at[:, rows], ffn_own.at[c])
            moves = [
                remote(term.at[:, other], ffn_own.at[c], sems, 0, sib),
                remote(term.at[:, rows], ffn_came.at[c], sems, 1, over),
                remote(term.at[:, other], ffn_came.at[c], sems, 2, diag),
            ]
        stay = pltpu.make_async_copy(*keep, local.at[1 if heads else 0])
        here = x == layer
        there = x != layer
        if heads:
            here, there = here & mine, there & mine

        @pl.when(here)
        def _():
            stay.start()
            moves[0].start()

        @pl.when(there)
        def _():
            moves[1].start()
            moves[2].start()

        return stay, moves

    done = {}
    waiting = [(n, rest) for n, *rest in ready]
    hops = sum_over(table, land, t_sems, [over, sib] + others)
    while waiting or background.now < len(background.stages):
        for n, (layer, heads, stage) in list(waiting):
            if stage < max(0, background.now - 1) or background.now >= len(background.stages):
                background.arrived(stage)
                done[heads] = home(n, layer, heads)
                waiting.remove((n, [layer, heads, stage]))
                break
        next(hops, None)
        next(hops, None)
        if background.now < len(background.stages):
            background.advance()
    for _ in hops:
        pass
    gain_out[...] = table[len(others) + 2]
    background.finish()
    stay, moves = done[False]
    stay.wait()
    for copy in moves:
        copy.wait()
    stay, moves = done[True]

    @pl.when(mine)
    def _():
        stay.wait()
        for copy in moves:
            copy.wait_send()
        moves[1].wait_recv()

    @pl.when(~mine)
    def _():
        moves[0].wait_recv()
        moves[2].wait_recv()


def tail_call(grid, plan, ready, gain_rows, depth, units):
    width = gain_rows[0].shape[1]
    hops = len(doubling(grid)) + 2
    table = (hops + 1, 8, width)
    return fused_call(
        grid, functools.partial(tail_kernel, grid, ready), "tail", plan, gain_rows, [VMEM] * 4,
        shaped(
            *[((2, 3, depth, units), bf16)] * 2, *[((depth * 3 // 2, BLOCK), bf16)] * 2, ((8, width), f32)
        ),
        (ANY,) * 4 + (VMEM,),
        [
            pltpu.SemaphoreType.DMA((2, 6)),
            pltpu.SemaphoreType.DMA((2,)),
            pltpu.VMEM(table, f32),
            pltpu.VMEM(table, f32),
            pltpu.SemaphoreType.DMA((2, hops)),
        ],
        60,
    )


def finish_kernel(
    ffn_own, ffn_came, attn_own, attn_came, out_one, out_two, grad_one, grad_two,
    produced, grads, query, key, value, out, gate, up, down,
):
    x = lax.axis_index("section")
    depth, units = ffn_own.shape[2:]

    def put(side, ffn_ref, attn_ref):
        for core in range(2):
            at = slice((2 * side + core) * units, (2 * side + core + 1) * units)
            gate[:, at] = ffn_ref[core, 0].astype(f32)
            up[:, at] = ffn_ref[core, 1].astype(f32)
            down[at] = jnp.transpose(ffn_ref[core, 2].astype(f32))

        def head(n):
            if n < 4:
                return attn_ref[:depth, n * HD : (n + 1) * HD].astype(f32)
            return jnp.concatenate(
                [attn_ref[depth:, k * HD : (k + 1) * HD].astype(f32) for k in (n - 4, n - 2)], 0
            )

        for h in range(2):
            at = slice((2 * side + h) * HD, (2 * side + h + 1) * HD)
            query[:, at] = head(h)
            out[at] = jnp.transpose(head(4 + h))
        key[side * HD : (side + 1) * HD] = jnp.transpose(head(2))
        value[side * HD : (side + 1) * HD] = jnp.transpose(head(3))

    for layer in range(2):

        @pl.when(x == layer)
        def _():
            put(layer, ffn_own, attn_own)
            put(1 - layer, ffn_came, attn_came)
            produced[layer] = out_one[...]
            produced[1 - layer] = out_two[...]
            grads[layer] = grad_one[...].astype(f32)
            grads[1 - layer] = grad_two[...].astype(f32)


def finish_call(blocks, outs, grads, shards):
    shape = (2,) + outs[0].shape
    shapes = [shard.shape[1:] for shard in shards]
    shapes[1:3] = [shape[::-1] for shape in shapes[1:3]]
    produced, grads, query, key, value, *rest = pl.pallas_call(
        finish_kernel,
        out_shape=shaped((shape, bf16), (shape, f32))
        + tuple(jax.ShapeDtypeStruct(one, f32) for one in shapes),
        in_specs=[VMEM] * 8,
        out_specs=(VMEM,) * 9,
        compiler_params=params(),
        cost_estimate=cost(8),
        name="finish",
    )(*blocks, *outs, *grads)
    return produced, grads, query, key.T, value.T, *rest


def after(value, *others):
    return lax.optimization_barrier((value,) + others)[0]


def layer_forward(grid, hidden_in, attn, ffn, nexts, gain_pair, facts):
    plan = Plan()
    ffn.add(plan, 0)
    whole, query, keys, values, middle, mixed, lse = attn_call(
        grid, plan, hidden_in, gain_pair[0:1], facts, attn.found
    )
    plan = Plan()
    if nexts:
        nexts[0].add(plan, 0)
        nexts[1].add(plan, max(0, len(plan.stages) - 2), 1)
    result, whole2, gate, up, hidden = ffn_call(grid, plan, middle, gain_pair[1:2], ffn.found)
    kept = (hidden_in, (whole, query, keys, values, mixed, lse), middle, whole2, gate, up, hidden)
    return result, kept


def layer_backward(grid, grad_out, kept, attn, ffn, gain_pair, facts, running, sum_ffn, sum_attn, leaving):
    hidden_in, kept_attn, middle, whole2, gate, up, hidden = kept
    plan = Plan()
    for ring in reversed(running):
        ring.add(plan, 0, min(4, ring.left()))
    grad_middle, gain_two, terms = ffn_back_call(
        grid, plan, grad_out, middle, gain_pair[1:2], gate, up, hidden, whole2, ffn.found
    )
    sums = sum_ffn(terms)
    running.append(sums)
    plan = Plan()
    sums.add(plan, 0, 3)
    grad_input, gain_one, qkv_term, out_term = attn_back_call(
        grid, plan, grad_middle, hidden_in, after(gain_pair[0:1], *leaving), facts, kept_attn, attn.found
    )
    running.append(sum_attn(qkv_term, out_term))
    return grad_input, (gain_one, gain_two)


def body(grid, inputs, doc_ids, cotangent, wq, wk, wv, wo, wg, wu, wd, gains):
    X, Y, C, Z = grid.X, grid.Y, grid.C, grid.Z
    x, y, c, z = grid.me()
    pos = grid.my_pos()
    micro, rows, width = inputs.shape
    depth = wq.shape[1]
    at_zero = x == 0

    def enter(block):
        def route(m):
            def go(x, y, c, z):
                if z % 2 != (x + m * C + c) % 2:
                    return None
                return (x, y, z // 2, m * C + c)

            return go

        first, last = grid.send(block[0], route(0)), grid.send(block[1], route(1))
        return jnp.where(z // C == 0, first, last)

    def leave(lower_block, upper_block):
        first = z // C == 0

        def route(swap):
            def go(x, y, c, z):
                section = (z // C + swap) % 2
                return (section, y, z % C, 2 * c + (x + z) % 2)

            return go

        same = grid.send(jnp.where(first, lower_block, upper_block), route(0))
        swapped_over = grid.send(jnp.where(first, upper_block, lower_block), route(1))
        return same, swapped_over

    rows_in = enter(inputs)
    halves = Z // 2
    tall = C * depth
    units = wg.shape[2] // 4
    share_rows = depth * 3 // 2
    upper, lower = pl.ds(0, tall // 2), pl.ds(tall // 2, tall // 2)
    cores = [pl.ds(core * share_rows, share_rows) for core in range(2)]
    attn_cuts = [((cores[0],), (cores[0],), None), ((cores[1],), None, (cores[1],))]
    ffn_cuts = [((m,), (m, upper), (m, lower)) for m in range(3)]
    attn = [Gather(grid, (C * share_rows, BLOCK), attn_cuts, True) for _ in range(2)]
    ffn = [Gather(grid, (3, tall, units), ffn_cuts) for _ in range(2)]
    plan = Plan()
    joins = [[ring.begin(plan) for ring in rings] for rings in (attn, ffn)]
    attn[0].add(plan, 0)
    ffn[0].add(plan, max(0, len(plan.stages) - 2), 1)
    shards = (wq, wk, wv, wo, wg, wu, wd)
    gain_all, facts = start_call(
        grid, plan, joins, max(0, len(plan.stages) - 3), shards, gains, doc_ids, rows
    )

    hidden = rows_in
    kept = []
    for s in range(2):
        nexts = (attn[1], ffn[1]) if s == 0 else None
        hidden, keep = layer_forward(grid, hidden, attn[s], ffn[s], nexts, gain_all[s], facts)
        kept.append(keep)
    rows_cot = enter(after(cotangent, kept[1][2]))
    outs = leave(after(kept[1][0], hidden, rows_cot), after(hidden, rows_cot))

    def sum_ffn(terms):
        def block(m):
            return lambda yy, zz: (
                m,
                pl.ds(pl.multiple_of(yy * tall, tall), tall),
                pl.ds(pl.multiple_of(zz * units, units), units),
            )

        parts = [(cuts, [(terms, block(m), (m,))]) for m, cuts in enumerate(ffn_cuts)]
        return Scatter(grid, parts, (3, tall, units))

    def sum_attn(qkv_term, out_term):
        def top(core):
            return lambda yy, zz: (
                pl.ds(pl.multiple_of((yy * C + core) * depth, depth), depth),
                pl.ds(pl.multiple_of(zz % halves * BLOCK, BLOCK), BLOCK),
            )

        def below(core):
            return lambda yy, zz: (yy * C + core, zz % halves)

        parts = []
        for core in range(C):
            first = core * share_rows
            places = [
                (qkv_term, top(core), (pl.ds(first, depth),)),
                (out_term, below(core), (pl.ds(first + depth, depth // 2),)),
            ]
            parts.append((attn_cuts[core], places))
        return Scatter(grid, parts, (C * share_rows, BLOCK), True)

    upstream = rows_cot
    gain_terms, running = [None] * 2, []
    waited, grads = outs, [None] * 2
    for s in (1, 0):
        upstream, gain_terms[s] = layer_backward(
            grid, upstream, kept[s], attn[s], ffn[s], gain_all[s], facts, running, sum_ffn, sum_attn, waited
        )
        grads[s], waited = upstream, ()
    grads_in = leave(*grads)
    plan = Plan()
    ready = []
    for n in (3, 2, 1, 0):
        left = running[n].left()
        running[n].add(plan, 0, left, True)
        ready.append((1 - n // 2, n % 2 == 1, left - 1))
        running[n].total(plan)
    order = sorted(range(4), key=lambda n: ready[n][2])
    ready = [(n,) + ready[n] for n in order]
    *blocks, gain_sum = tail_call(grid, plan, ready, gain_terms[0] + gain_terms[1], depth, units)

    produced, grads_in, *terms = finish_call(blocks, outs, grads_in, shards)
    share = gains.shape[2]
    mine = (y * C + c) * Z + z
    gain_share = lax.dynamic_slice(gain_sum, (2 * x, mine * share), (2, share))[None]
    return (
        produced[None],
        grads_in[None],
        *[term[None] for term in terms],
        gain_share,
    )


def solution(mesh):
    grid = Grid(mesh)

    def run(*arguments):
        grid.calls = 0
        return body(grid, *arguments)

    return jax.shard_map(
        run,
        mesh=mesh,
        in_specs=(
            P(None, ("fsdp", "tensor"), None),
            P(None, "fsdp", None),
            P(None, ("fsdp", "tensor"), None),
            P("section", "fsdp", "tensor"),
            P("section", "fsdp", "tensor"),
            P("section", "fsdp", "tensor"),
            P("section", "tensor", "fsdp"),
            P("section", "fsdp", "tensor"),
            P("section", "fsdp", "tensor"),
            P("section", "tensor", "fsdp"),
            P("section", None, ("fsdp", "tensor")),
        ),
        out_specs=(
            P("section", None, ("fsdp", "tensor"), None),
            P("section", None, ("fsdp", "tensor"), None),
            P("section", "fsdp", "tensor"),
            P("section", "fsdp", "tensor"),
            P("section", "fsdp", "tensor"),
            P("section", "tensor", "fsdp"),
            P("section", "fsdp", "tensor"),
            P("section", "fsdp", "tensor"),
            P("section", "tensor", "fsdp"),
            P("section", None, ("fsdp", "tensor")),
        ),
        check_vma=False,
    )
```
